32 devices in a mesh: facet: 16 (over z, x, core), band: 2 (over y).
Axes of the slice: x: 2, y: 2, z: 4, core: 2. Of those that a mesh axis runs over, the one named last changes fastest.
Arguments:
- facet_strips: float32 [2, 16, 2, 8, 4096], P('band', 'facet'), may hold values from -6 to 6
- subgrid_offsets: int32 [2, 16], replicated, may hold values from 0 to 4095
- sample_cells: int32 [2, 2, 16, 2, 512], P('band', None, 'facet'), may hold values from 0 to 511, as said below
- sample_values: float32 [2, 2, 16, 2, 512], P('band', None, 'facet'), may hold values from -6 to 6
- sample_weights: float32 [2, 2, 16, 512], P('band', None, 'facet'), may hold values from 0.1 to 1
- sample_flags: int32 [2, 2, 16, 512], P('band', None, 'facet'), may hold values 0 or 1
Outputs:
- residual_strips: float32 [16, 8, 2, 4096], P('facet', 'band')
The draws below stay inside these ranges and needn't reach their ends.
Inputs may be any that keep to these rules, and one draw needn't show every extreme that they name: `sample_cells`: slot 0 holds a row of 0 to (16 // 8) * 8 - 1, slot 1 a column of 0 to 512 - 1; every subgrid of every sub-band and front has a sample at its last row and last column.
All inputs are finite; a program needn't handle non-finite values. No bound on the sum of `sample_flags` on one device may be relied on, other than what follows from the above.
Results may differ from the reference program's by a relative error of at most 0.006.
Values may be sent and summed in bfloat16 or wider, within the bound.
No kernel may reach another device: no remote copies, remote signals or barrier semaphores. Data moves between devices by JAX's collectives and lax.ppermute only.
A program may use at most 64 MiB of HBM per device.

```python
import math
import jax
import jax.numpy as jnp
from jax import lax

FN = 4096
CONTRIB = 64
FACET_ROWS = 8
COLS = 8
FRONTS = 2
VIS = 512
FACETS = 16
BANDS = 2
SG = 512
CELLS = 8192


def draw_sample_cells(key, part):
    row_total = FACETS // FACET_ROWS * COLS
    key_row = jax.random.fold_in(key, 11)
    key_col = jax.random.fold_in(key, 23)
    row_draw = jax.random.randint(key_row, (BANDS, FRONTS, FACETS, 1, VIS), 0, row_total, dtype=jnp.int32)
    col_draw = jax.random.randint(key_col, (BANDS, FRONTS, FACETS, 1, VIS), 0, SG, dtype=jnp.int32)
    row_draw = row_draw.at[..., 0].set(row_total - 1).at[..., 1].set(0)
    col_draw = col_draw.at[..., 0].set(SG - 1).at[..., 1].set(0)
    return jnp.concatenate([row_draw, col_draw], axis=3).astype(jnp.int32)


def place_ends(result, stream_key, least, high):
    spot = [jax.random.randint(jax.random.fold_in(stream_key, axis), (), 0, length) for axis, length in enumerate(result.shape)]
    widest = result.shape.index(max(result.shape))
    beside = spot[:widest] + [(spot[widest] + 1) % result.shape[widest]] + spot[widest + 1:]
    return result.at[tuple(spot)].set(least).at[tuple(beside)].set(high)


def shard_levels(own_key, extent, shards, low, top_value):
    loudness, own = 1.0, jax.random.fold_in(own_key, 6)
    for position, blocks in shards:
        steps = jnp.exp(jax.random.uniform(jax.random.fold_in(own, position), (blocks,), jnp.float32, low / len(shards), top_value / len(shards)))
        loudness = loudness * jnp.repeat(steps, extent[position] // blocks).reshape([-1 if axis == position else 1 for axis in range(len(extent))])
    return loudness


def noise(key, shape, deviation, most, cuts=(), held_as=jnp.bfloat16):
    level = shard_levels(key, shape, cuts, -0.22, 0.18) if cuts else 1.0
    array = jax.random.normal(key, shape, jnp.float32) * deviation * level
    return jnp.minimum(jnp.maximum(array, -most), most).astype(held_as)


def setup_inputs(seed: int = 0) -> dict:
    splits = jax.random.split(jax.random.key(seed), 7)
    facet_strips = noise(splits[0], (BANDS, FACETS, 2, COLS, FN), 1.0, 6.0, ((0, 2), (1, 16)), jnp.float32)
    subgrid_offsets = place_ends(jax.random.randint(splits[1], (FRONTS, FACETS), 0, FN), jax.random.fold_in(splits[1], 1), 0, FN - 1).astype(jnp.int32)
    sample_cells = draw_sample_cells(jax.random.fold_in(splits[6], 71), 0)
    sample_values = noise(splits[3], (BANDS, FRONTS, FACETS, 2, VIS), 1.0, 6.0, ((0, 2), (2, 16)), jnp.float32)
    sample_weights = jnp.clip(jnp.exp(math.log(1.0) - 2.3025851 * jax.random.uniform(splits[4], (BANDS, FRONTS, FACETS, VIS), jnp.float32) ** shard_levels(splits[4], (BANDS, FRONTS, FACETS, VIS), ((0, 2), (2, 16)), -0.2, 0.2)), 0.1, 1.0)
    sample_flags = place_ends((jax.random.randint(splits[5], (BANDS, FRONTS, FACETS, VIS), 0, 8) < 7).astype(jnp.int32), jax.random.fold_in(splits[5], 1), 0, 1)
    return {"facet_strips": facet_strips, "subgrid_offsets": subgrid_offsets, "sample_cells": sample_cells, "sample_values": sample_values, "sample_weights": sample_weights, "sample_flags": sample_flags}


def to_complex(real_part, imag_part):
    return lax.complex(real_part, imag_part)


def rounded(values):
    real_part = lax.optimization_barrier(jnp.real(values).astype(jnp.bfloat16)).astype(jnp.float32)
    imag_part = lax.optimization_barrier(jnp.imag(values).astype(jnp.bfloat16)).astype(jnp.float32)
    return to_complex(real_part, imag_part)


def reference(facet_strips, subgrid_offsets, sample_cells, sample_values, sample_weights, sample_flags):
    facet_count = FACETS
    col_groups = facet_count // FACET_ROWS
    subgrid_len = SG
    counter = jnp.arange(FN).astype(jnp.float32)
    window = 1.0 + 0.5 * jnp.cos(counter * (2.0 * math.pi / FN))
    positions = (subgrid_offsets[:, :, None] + jnp.arange(CONTRIB, dtype=jnp.int32)[None, None, :]) % FN

    def one_band(running, inputs):
        strips, cell_pairs, observed, weights, flagged = inputs
        cell_index = (cell_pairs[:, :, 0] * subgrid_len + cell_pairs[:, :, 1]).astype(jnp.int32)
        signal = to_complex(strips[:, 0], strips[:, 1]) * window
        spectrum = jnp.fft.fft(signal, axis=-1) * FN ** -0.5
        cutout = spectrum[:, :, positions]
        pieces = rounded(jnp.fft.ifft(cutout, axis=-1) * CONTRIB ** 0.5)
        sky_image = pieces.reshape(col_groups, FACET_ROWS, COLS, FRONTS, facet_count, CONTRIB)
        sky_image = jnp.transpose(sky_image, (3, 4, 0, 2, 1, 5)).reshape(FRONTS, facet_count, col_groups * COLS, subgrid_len)
        model_grid = (jnp.fft.fft(sky_image, axis=-1) * subgrid_len ** -0.5).reshape(FRONTS, facet_count, CELLS)
        predicted = jnp.take_along_axis(model_grid, cell_index, axis=2)
        factor = weights * flagged.astype(jnp.float32)
        residual = to_complex(factor * (observed[:, :, 0] - jnp.real(predicted)), factor * (observed[:, :, 1] - jnp.imag(predicted)))
        slot_index = cell_index + jnp.arange(FRONTS * facet_count, dtype=jnp.int32).reshape(FRONTS, facet_count, 1) * CELLS
        slot_index = slot_index.reshape(-1)
        grid_real = jax.ops.segment_sum(jnp.real(residual).reshape(-1), slot_index, num_segments=FRONTS * facet_count * CELLS)
        grid_imag = jax.ops.segment_sum(jnp.imag(residual).reshape(-1), slot_index, num_segments=FRONTS * facet_count * CELLS)
        grid = to_complex(grid_real, grid_imag).reshape(FRONTS, facet_count, col_groups * COLS, subgrid_len)
        returned = jnp.fft.ifft(grid, axis=-1) * subgrid_len ** 0.5
        returned = returned.reshape(FRONTS, facet_count, col_groups, COLS, FACET_ROWS, CONTRIB)
        returned = jnp.transpose(returned, (2, 4, 3, 0, 1, 5)).reshape(facet_count, COLS, FRONTS, facet_count, CONTRIB)
        return running + rounded(returned), None

    zeros = jnp.zeros((facet_count, COLS, FRONTS, facet_count, CONTRIB), jnp.float32)
    start_value = to_complex(zeros, zeros)
    summed = lax.scan(one_band, start_value, (facet_strips, sample_cells, sample_values, sample_weights, sample_flags))[0]
    partial_value = jnp.fft.fft(summed, axis=-1) * CONTRIB ** -0.5
    spread = jnp.zeros((facet_count, COLS, FN), partial_value.dtype).at[:, :, positions].add(partial_value)
    lines = jnp.fft.ifft(spread, axis=-1) * FN ** 0.5 * window
    return jnp.stack([jnp.real(lines), jnp.imag(lines)], axis=2)
```

```python
import functools
import math

import jax
import jax.numpy as jnp
import ml_dtypes
import numpy as np
from jax import lax
from jax.experimental import pallas as pl
from jax.experimental.pallas import tpu as pltpu
from jax.sharding import PartitionSpec as P

CONTRIB = 64
FACET_ROWS = 8
LANES = 128
HALF = LANES // 2
VMEM_LIMIT = 48 * 1024 * 1024
F32 = jnp.float32
BF16 = jnp.bfloat16


def phases(rows, cols, length, rotation):
    product = np.outer(rows, cols) % length
    return np.exp(rotation * 2j * np.pi * product / length)


def from_left(matrix):
    return np.block([[matrix.real, -matrix.imag], [matrix.imag, matrix.real]])


def from_right(matrix):
    return np.block([[matrix.real, matrix.imag], [-matrix.imag, matrix.real]])


def high_low(table):
    high = table.astype(ml_dtypes.bfloat16)
    low = (table - high.astype(np.float64)).astype(ml_dtypes.bfloat16)
    return np.stack([high, low])


def side_by_side(values):
    straight = np.concatenate([values.real, values.real], axis=-1)
    crossed = np.concatenate([-values.imag, values.imag], axis=-1)
    return np.stack([straight, crossed]).astype(np.float32)


def tables(length):
    blocks = length // CONTRIB
    short = np.arange(CONTRIB)
    outer = np.concatenate([np.arange(0, blocks, 2), np.arange(1, blocks, 2)])
    window = 1.0 + 0.5 * np.cos(np.arange(length) * (2.0 * math.pi / length))
    turn = np.tile(phases(short, short, length, -1), (1, 2))
    pair = np.eye(2)
    subgrid_len = FACET_ROWS * CONTRIB
    return dict(
        window=(window * length**-0.5).reshape(length // LANES, LANES).astype(np.float32),
        turn=np.stack([turn.real, turn.imag]).astype(np.float32),
        shift=side_by_side(phases(short, short, CONTRIB, -1)),
        outer_minus=high_low(from_left(phases(short, outer, blocks, -1))),
        inner_minus=high_low(from_right(np.kron(pair, phases(short, short, CONTRIB, -1)))),
        piece=high_low(from_right(phases(short, short, CONTRIB, 1)) * CONTRIB**-0.5),
        inner_plus=high_low(from_right(np.kron(pair, phases(short, short, CONTRIB, 1)))),
        outer_plus=high_low(from_left(phases(outer, short, blocks, 1))),
        partial=high_low(from_right(phases(short, short, CONTRIB, -1)).T * CONTRIB**-0.5),
        grid_turn=side_by_side(phases(np.arange(FACET_ROWS), short, subgrid_len, -1)),
        model=high_low(from_right(phases(short, short, CONTRIB, -1)).T * subgrid_len**-0.5),
        back=high_low(from_right(phases(short, short, CONTRIB, 1)) * subgrid_len**-0.5),
    )


def split(values):
    high = values.astype(BF16)
    return high, (values - high.astype(F32)).astype(BF16)


def dot(left, right, dims=((1,), (0,))):
    return lax.dot_general(left, right, (dims, ((), ())), preferred_element_type=F32)


def times_table(values, table, dims=((1,), (0,))):
    high, low = split(values)
    return dot(high, table[0], dims) + dot(low, table[0], dims) + dot(high, table[1], dims)


def table_times(table, values, dims=((1,), (0,))):
    high, low = split(values)
    return dot(table[0], high, dims) + dot(table[0], low, dims) + dot(table[1], high, dims)


def iota(shape, dimension):
    return lax.broadcasted_iota(jnp.int32, shape, dimension)


def swap_halves(values):
    return pltpu.roll(values, HALF, 1)


def offsets_on_lanes(offsets_ref, columns):
    fronts, owners = offsets_ref.shape
    lane = iota((1, fronts * owners * columns), 1)
    spread = jnp.zeros_like(lane)
    for place in range(fronts * owners):
        begin = place * columns
        here = (lane >= begin) & (lane < begin + columns)
        spread = jnp.where(here, offsets_ref[place % fronts, place // fronts], spread)
    return lane, spread


def place_shifts(offsets_ref, shift_ref, straight_ref, crossed_ref, columns):
    fronts, owners = offsets_ref.shape
    for place in range(fronts * owners):
        residue = offsets_ref[place % fronts, place // fronts] % CONTRIB
        rows = pl.ds(place * columns, columns)
        straight_ref[rows, :] = jnp.broadcast_to(
            shift_ref[0, pl.ds(residue, 1), :], (columns, LANES)
        )
        crossed_ref[rows, :] = jnp.broadcast_to(
            shift_ref[1, pl.ds(residue, 1), :], (columns, LANES)
        )


def one_hot(shape, targets):
    return jnp.where(iota(shape, 0) == targets, 1.0, 0.0).astype(BF16)


def turned_eighths(values, rotation):
    sign = jnp.where(iota(values[0].shape, 1) < HALF, -rotation, rotation).astype(F32)

    def quarter_turn(value):
        return swap_halves(value) * sign

    def four(a, b, c, d):
        even_sum, even_diff = a + c, a - c
        odd_sum, odd_diff = b + d, quarter_turn(b - d)
        return even_sum + odd_sum, even_diff + odd_diff, even_sum - odd_sum, even_diff - odd_diff

    even = four(*values[0::2])
    odd = four(*values[1::2])
    root = math.sqrt(0.5)
    turned = (
        odd[0],
        (odd[1] + quarter_turn(odd[1])) * root,
        quarter_turn(odd[2]),
        (quarter_turn(odd[3]) - odd[3]) * root,
    )
    return [e + o for e, o in zip(even, turned)] + [e - o for e, o in zip(even, turned)]


def predict_kernel(
    offsets_ref, strips_ref, window_ref, turn_ref, shift_ref, outer_ref, inner_ref, piece_ref,
    out_ref, real_ref, imag_ref, straight_ref, crossed_ref,
):
    columns, length = strips_ref.shape[1:]
    groups = length // LANES
    pairs = columns // 2
    place_shifts(offsets_ref, shift_ref, straight_ref, crossed_ref, columns)
    window = window_ref[...]
    low_half = iota((groups, LANES), 1) < HALF
    sections = []
    for part, held in enumerate((real_ref, imag_ref)):
        for group in range(groups):
            held[group * columns : (group + 1) * columns, :] = strips_ref[
                part, :, group * LANES : (group + 1) * LANES
            ]
        even, odd = [], []
        for pair in range(pairs):
            first = held[pl.ds(2 * pair, groups, stride=columns), :] * window
            second = held[pl.ds(2 * pair + 1, groups, stride=columns), :] * window
            even.append(jnp.where(low_half, first, swap_halves(second)))
            odd.append(jnp.where(low_half, swap_halves(first), second))
        sections += [jnp.concatenate(even, axis=1), jnp.concatenate(odd, axis=1)]
    section = table_times(outer_ref, jnp.concatenate(sections, axis=0))
    turned = []
    for pair in range(pairs):
        lanes = slice(pair * LANES, (pair + 1) * LANES)
        real, imag = section[:CONTRIB, lanes], section[CONTRIB:, lanes]
        turned.append(
            jnp.concatenate(
                [
                    real * turn_ref[0] - imag * turn_ref[1],
                    real * turn_ref[1] + imag * turn_ref[0],
                ],
                axis=1,
            )
        )
    inner = times_table(jnp.concatenate(turned, axis=0), inner_ref)
    spectrum = jnp.concatenate(
        [
            jnp.concatenate(
                [
                    inner[pair * CONTRIB : (pair + 1) * CONTRIB, part * LANES : (part + 1) * LANES]
                    for pair in range(pairs)
                ],
                axis=1,
            )
            for part in range(2)
        ],
        axis=0,
    )
    blocks = length // CONTRIB
    lane, spread = offsets_on_lanes(offsets_ref, columns)
    first_block, residue = spread // CONTRIB, spread % CONTRIB
    base = lane % columns * blocks
    width = lane.shape[1]
    shape = (columns * blocks, width)
    high, low = split(spectrum)
    pick = one_hot(shape, base + first_block)
    inside = dot(high, pick) + dot(low, pick)
    pick = one_hot(shape, base + (first_block + 1) % blocks)
    beyond = dot(high, pick) + dot(low, pick)
    kappa = iota((2 * CONTRIB, width), 0) % CONTRIB
    cutout = jnp.where(kappa >= residue, inside, beyond)
    piece = times_table(cutout.T, piece_ref)
    out_ref[...] = (piece * straight_ref[...] + swap_halves(piece) * crossed_ref[...]).astype(BF16)


def subgrid_kernel(
    pieces_ref, cells_ref, values_ref, weights_ref, flags_ref, turn_ref, model_ref, back_ref,
    out_ref, held_ref, *, columns, bands,
):
    fronts, _, samples = cells_ref.shape
    facets = pieces_ref.shape[0] // (fronts * columns)
    groups = facets // FACET_ROWS
    rows = groups * columns
    depth = FACET_ROWS * rows
    share = columns // bands
    pieces = pieces_ref[...].astype(F32)

    def block(facet, front):
        begin = (facet * fronts + front) * columns
        return pieces[begin : begin + columns, :]

    sky = [
        jnp.concatenate(
            [block(j * FACET_ROWS + i, t) for t in range(fronts) for j in range(groups)], axis=0
        )
        for i in range(FACET_ROWS)
    ]
    sky = turned_eighths(sky, -1.0)
    sky = [
        value * turn_ref[0, i : i + 1, :] + swap_halves(value) * turn_ref[1, i : i + 1, :]
        for i, value in enumerate(sky)
    ]
    stacked = jnp.concatenate(
        [value[t * rows : (t + 1) * rows, :] for t in range(fronts) for value in sky], axis=0
    )
    model = table_times(model_ref, stacked, ((1,), (1,)))
    grids = []
    for t in range(fronts):
        row, col = cells_ref[t, 0:1, :], cells_ref[t, 1:2, :]
        pick = one_hot((depth, samples), col % FACET_ROWS * rows + row)
        high, low = split(model[:, t * depth : (t + 1) * depth])
        line = dot(high, pick) + dot(low, pick)
        mask = iota((HALF, samples), 0) == col // FACET_ROWS
        factor = weights_ref[t] * flags_ref[t].astype(F32)
        highs, lows = [], []
        for part in range(2):
            predicted = jnp.sum(
                jnp.where(mask, line[part * HALF : (part + 1) * HALF, :], 0.0),
                axis=0,
                keepdims=True,
            )
            residual = factor * (values_ref[t, part : part + 1, :] - predicted)
            high = residual.astype(BF16).astype(F32)
            highs.append(jnp.where(mask, high, 0.0).astype(BF16))
            lows.append(jnp.where(mask, residual - high, 0.0).astype(BF16))
        grids.append(
            dot(pick, jnp.concatenate(highs, axis=0), ((1,), (1,)))
            + dot(pick, jnp.concatenate(lows, axis=0), ((1,), (1,)))
        )
    back = times_table(jnp.concatenate(grids, axis=0), back_ref)
    lines = []
    for i in range(FACET_ROWS):
        value = jnp.concatenate(
            [
                back[t * depth + i * rows : t * depth + (i + 1) * rows, :]
                for t in range(fronts)
            ],
            axis=0,
        )
        lines.append(
            value * turn_ref[0, i : i + 1, :] - swap_halves(value) * turn_ref[1, i : i + 1, :]
        )
    lines = turned_eighths(lines, 1.0)
    for i in range(FACET_ROWS):
        for t in range(fronts):
            for j in range(groups):
                for b in range(bands):
                    source = (t * groups + j) * columns + b * share
                    target = ((b * facets + j * FACET_ROWS + i) * fronts + t) * share
                    held_ref[target : target + share, :] = lines[i][source : source + share, :]
    out_ref[...] = held_ref[...].astype(BF16)


def return_kernel(
    offsets_ref, pieces_ref, window_ref, turn_ref, shift_ref, partial_ref, inner_ref, outer_ref,
    out_ref, straight_ref, crossed_ref, *line_refs, bands,
):
    columns, _, length = out_ref.shape
    blocks = length // CONTRIB
    groups = length // LANES
    pairs = (columns + 1) // 2
    place_shifts(offsets_ref, shift_ref, straight_ref, crossed_ref, columns)
    width = pieces_ref.shape[0] // bands
    summed = pieces_ref[0:width, :].astype(F32)
    for b in range(1, bands):
        summed += pieces_ref[b * width : (b + 1) * width, :].astype(F32)
    summed = summed * straight_ref[...] - swap_halves(summed) * crossed_ref[...]
    residues = table_times(partial_ref, summed, ((1,), (1,)))
    lane, spread = offsets_on_lanes(offsets_ref, columns)
    first_block, residue = spread // CONTRIB, spread % CONTRIB
    base = lane % columns * blocks
    kappa = iota((2 * CONTRIB, width), 0) % CONTRIB
    inside = kappa >= residue
    both = jnp.concatenate(
        [jnp.where(inside, residues, 0.0), jnp.where(inside, 0.0, residues)], axis=1
    )
    targets = jnp.concatenate(
        [base + first_block, base + (first_block + 1) % blocks], axis=1
    )
    put = one_hot((2 * pairs * blocks, 2 * width), targets)
    high, low = split(both)
    spectrum = dot(high, put, ((1,), (1,))) + dot(low, put, ((1,), (1,)))
    inner = times_table(
        jnp.concatenate(
            [
                jnp.concatenate(
                    [
                        spectrum[:CONTRIB, pair * LANES : (pair + 1) * LANES],
                        spectrum[CONTRIB:, pair * LANES : (pair + 1) * LANES],
                    ],
                    axis=1,
                )
                for pair in range(pairs)
            ],
            axis=0,
        ),
        inner_ref,
    )
    reals, imags = [], []
    for pair in range(pairs):
        rows = slice(pair * CONTRIB, (pair + 1) * CONTRIB)
        real, imag = inner[rows, :LANES], inner[rows, LANES:]
        reals.append(real * turn_ref[0] + imag * turn_ref[1])
        imags.append(imag * turn_ref[0] - real * turn_ref[1])
    lines = table_times(
        outer_ref,
        jnp.concatenate(
            [jnp.concatenate(reals, axis=1), jnp.concatenate(imags, axis=1)], axis=0
        ),
    )
    window = window_ref[...]
    low_half = iota((groups, LANES), 1) < HALF
    for part in range(2):
        for pair in range(pairs):
            lanes = slice(pair * LANES, (pair + 1) * LANES)
            begin = part * blocks
            even = lines[begin : begin + groups, lanes]
            odd = lines[begin + groups : begin + blocks, lanes]
            line_refs[2 * pair][pl.ds(part, groups, stride=2), :] = (
                jnp.where(low_half, even, swap_halves(odd)) * window
            )
            if 2 * pair + 1 < columns:
                line_refs[2 * pair + 1][pl.ds(part, groups, stride=2), :] = (
                    jnp.where(low_half, swap_halves(even), odd) * window
                )
    for column in range(columns):
        for group in range(groups):
            out_ref[column, :, group * LANES : (group + 1) * LANES] = line_refs[column][
                2 * group : 2 * group + 2, :
            ]


def kernel_call(kernel, name, out_shape, in_smem, scratch, *operands):
    smem = pl.BlockSpec(memory_space=pltpu.SMEM)
    vmem = pl.BlockSpec(memory_space=pltpu.VMEM)
    specs = [smem if index < in_smem else vmem for index in range(len(operands))]
    return pl.pallas_call(
        kernel,
        out_shape=out_shape,
        in_specs=specs,
        out_specs=vmem,
        scratch_shapes=[pltpu.VMEM(shape, F32) for shape in scratch],
        compiler_params=pltpu.CompilerParams(vmem_limit_bytes=VMEM_LIMIT),
        name=name,
    )(*operands)


def local(facets, bands, strips, offsets, cells, values, weights, flags):
    columns, length = strips.shape[-2:]
    fronts = offsets.shape[0]
    share = columns // bands
    made = {key: jnp.asarray(value) for key, value in tables(length).items()}
    rows = facets * fronts * columns
    held = length // LANES * columns
    pieces = kernel_call(
        predict_kernel, "predict", jax.ShapeDtypeStruct((rows, LANES), BF16), 1,
        [(held, LANES)] * 2 + [(rows, LANES)] * 2,
        offsets, strips[0, 0], made["window"], made["turn"], made["shift"],
        made["outer_minus"], made["inner_minus"], made["piece"],
    )
    arrived = lax.all_to_all(pieces, "facet", split_axis=0, concat_axis=0, tiled=True)
    returned = kernel_call(
        functools.partial(subgrid_kernel, columns=columns, bands=bands), "subgrid",
        jax.ShapeDtypeStruct((rows, LANES), BF16), 0, [(rows, LANES)],
        arrived, cells[0, :, 0], values[0, :, 0], weights[0], flags[0],
        made["grid_turn"], made["model"], made["back"],
    )
    delivered = lax.all_to_all(
        returned, ("band", "facet"), split_axis=0, concat_axis=0, tiled=True
    )
    width = facets * fronts * share
    lines = kernel_call(
        functools.partial(return_kernel, bands=bands), "lines",
        jax.ShapeDtypeStruct((share, 2, length), F32), 1,
        [(width, LANES)] * 2 + [(2 * length // LANES, LANES)] * share,
        offsets, delivered, made["window"], made["turn"], made["shift"],
        made["partial"], made["inner_plus"], made["outer_plus"],
    )
    return lines[None]


def solution(mesh):
    placed = (
        P("band", "facet", None, None, None),
        P(),
        P("band", None, "facet", None, None),
        P("band", None, "facet", None, None),
        P("band", None, "facet", None),
        P("band", None, "facet", None),
    )
    return jax.shard_map(
        functools.partial(local, mesh.shape["facet"], mesh.shape["band"]),
        mesh=mesh,
        in_specs=placed,
        out_specs=P("facet", "band", None, None),
        check_vma=False,
    )
```

```python
import functools
import math

import jax
import jax.numpy as jnp
import ml_dtypes
import numpy as np
from jax import lax
from jax.experimental import pallas as pl
from jax.experimental.pallas import tpu as pltpu
from jax.sharding import PartitionSpec as P

CONTRIB = 64
FACET_ROWS = 8
LANES = 128
HALF = LANES // 2
VMEM_LIMIT = 48 * 1024 * 1024
F32 = jnp.float32
BF16 = jnp.bfloat16


def phases(rows, cols, length, rotation):
    product = np.outer(rows, cols) % length
    return np.exp(rotation * 2j * np.pi * product / length)


def from_left(matrix):
    return np.block([[matrix.real, -matrix.imag], [matrix.imag, matrix.real]])


def from_right(matrix):
    return np.block([[matrix.real, matrix.imag], [-matrix.imag, matrix.real]])


def high_low(table):
    high = table.astype(ml_dtypes.bfloat16)
    low = (table - high.astype(np.float64)).astype(ml_dtypes.bfloat16)
    return np.stack([high, low])


def side_by_side(values):
    straight = np.concatenate([values.real, values.real], axis=-1)
    crossed = np.concatenate([-values.imag, values.imag], axis=-1)
    return np.stack([straight, crossed]).astype(np.float32)


def tables(length):
    blocks = length // CONTRIB
    short = np.arange(CONTRIB)
    outer = np.concatenate([np.arange(0, blocks, 2), np.arange(1, blocks, 2)])
    window = 1.0 + 0.5 * np.cos(np.arange(length) * (2.0 * math.pi / length))
    turn = np.tile(phases(short, short, length, -1), (1, 2))
    pair = np.eye(2)
    subgrid_len = FACET_ROWS * CONTRIB
    return dict(
        window=(window * length**-0.5).reshape(length // LANES, LANES).astype(np.float32),
        turn=np.stack([turn.real, turn.imag]).astype(np.float32),
        shift=side_by_side(phases(short, short, CONTRIB, -1)),
        outer_minus=high_low(from_left(phases(short, outer, blocks, -1))),
        inner_minus=high_low(from_right(np.kron(pair, phases(short, short, CONTRIB, -1)))),
        piece=high_low(from_right(phases(short, short, CONTRIB, 1)) * CONTRIB**-0.5),
        inner_plus=high_low(from_right(np.kron(pair, phases(short, short, CONTRIB, 1)))),
        outer_plus=high_low(from_left(phases(outer, short, blocks, 1))),
        partial=high_low(from_right(phases(short, short, CONTRIB, -1)).T * CONTRIB**-0.5),
        grid_turn=side_by_side(phases(np.arange(FACET_ROWS), short, subgrid_len, -1)),
        model=high_low(from_right(phases(short, short, CONTRIB, -1)).T * subgrid_len**-0.5),
        back=high_low(from_right(phases(short, short, CONTRIB, 1)) * subgrid_len**-0.5),
    )


def split(values):
    high = values.astype(BF16)
    return high, (values - high.astype(F32)).astype(BF16)


def dot(left, right, dims=((1,), (0,))):
    return lax.dot_general(left, right, (dims, ((), ())), preferred_element_type=F32)


def times_table(values, table, dims=((1,), (0,))):
    high, low = split(values)
    return dot(high, table[0], dims) + dot(low, table[0], dims) + dot(high, table[1], dims)


def table_times(table, values, dims=((1,), (0,))):
    high, low = split(values)
    return dot(table[0], high, dims) + dot(table[0], low, dims) + dot(table[1], high, dims)


def iota(shape, dimension):
    return lax.broadcasted_iota(jnp.int32, shape, dimension)


def swap_halves(values):
    return pltpu.roll(values, HALF, 1)


def offsets_on_lanes(offsets_ref, columns):
    fronts, owners = offsets_ref.shape
    lane = iota((1, fronts * owners * columns), 1)
    spread = jnp.zeros_like(lane)
    for place in range(fronts * owners):
        begin = place * columns
        here = (lane >= begin) & (lane < begin + columns)
        spread = jnp.where(here, offsets_ref[place % fronts, place // fronts], spread)
    return lane, spread


def place_shifts(offsets_ref, shift_ref, straight_ref, crossed_ref, columns):
    fronts, owners = offsets_ref.shape
    for place in range(fronts * owners):
        residue = offsets_ref[place % fronts, place // fronts] % CONTRIB
        rows = pl.ds(place * columns, columns)
        straight_ref[rows, :] = jnp.broadcast_to(
            shift_ref[0, pl.ds(residue, 1), :], (columns, LANES)
        )
        crossed_ref[rows, :] = jnp.broadcast_to(
            shift_ref[1, pl.ds(residue, 1), :], (columns, LANES)
        )


def one_hot(shape, targets):
    return jnp.where(iota(shape, 0) == targets, 1.0, 0.0).astype(BF16)


def turned_eighths(values, rotation):
    sign = jnp.where(iota(values[0].shape, 1) < HALF, -rotation, rotation).astype(F32)

    def quarter_turn(value):
        return swap_halves(value) * sign

    def four(a, b, c, d):
        even_sum, even_diff = a + c, a - c
        odd_sum, odd_diff = b + d, quarter_turn(b - d)
        return even_sum + odd_sum, even_diff + odd_diff, even_sum - odd_sum, even_diff - odd_diff

    even = four(*values[0::2])
    odd = four(*values[1::2])
    root = math.sqrt(0.5)
    turned = (
        odd[0],
        (odd[1] + quarter_turn(odd[1])) * root,
        quarter_turn(odd[2]),
        (quarter_turn(odd[3]) - odd[3]) * root,
    )
    return [e + o for e, o in zip(even, turned)] + [e - o for e, o in zip(even, turned)]


def predict_kernel(*refs):
    count = 8
    copies = [
        pltpu.make_async_copy(refs[i], refs[count + 1 + i], refs[-1].at[i]) for i in range(count)
    ]
    for copy in copies:
        copy.start()
    out_ref = refs[count]
    strips_ref, window_ref, outer_ref, turn_ref, inner_ref, offsets_ref, shift_ref, piece_ref = (
        refs[count + 1 : 2 * count + 1]
    )
    real_ref, imag_ref, straight_ref, crossed_ref = refs[2 * count + 1 : -1]
    columns, length = strips_ref.shape[1:]
    groups = length // LANES
    pairs = columns // 2
    copies[0].wait()
    copies[1].wait()
    window = window_ref[...]
    low_half = iota((groups, LANES), 1) < HALF
    sections = []
    for part, held in enumerate((real_ref, imag_ref)):
        for group in range(groups):
            held[group * columns : (group + 1) * columns, :] = strips_ref[
                part, :, group * LANES : (group + 1) * LANES
            ]
        even, odd = [], []
        for pair in range(pairs):
            first = held[pl.ds(2 * pair, groups, stride=columns), :] * window
            second = held[pl.ds(2 * pair + 1, groups, stride=columns), :] * window
            even.append(jnp.where(low_half, first, swap_halves(second)))
            odd.append(jnp.where(low_half, swap_halves(first), second))
        sections += [jnp.concatenate(even, axis=1), jnp.concatenate(odd, axis=1)]
    for copy in copies[2:]:
        copy.wait()
    place_shifts(offsets_ref, shift_ref, straight_ref, crossed_ref, columns)
    section = table_times(outer_ref, jnp.concatenate(sections, axis=0))
    turned = []
    for pair in range(pairs):
        lanes = slice(pair * LANES, (pair + 1) * LANES)
        real, imag = section[:CONTRIB, lanes], section[CONTRIB:, lanes]
        turned.append(
            jnp.concatenate(
                [
                    real * turn_ref[0] - imag * turn_ref[1],
                    real * turn_ref[1] + imag * turn_ref[0],
                ],
                axis=1,
            )
        )
    inner = times_table(jnp.concatenate(turned, axis=0), inner_ref)
    spectrum = jnp.concatenate(
        [
            jnp.concatenate(
                [
                    inner[pair * CONTRIB : (pair + 1) * CONTRIB, part * LANES : (part + 1) * LANES]
                    for pair in range(pairs)
                ],
                axis=1,
            )
            for part in range(2)
        ],
        axis=0,
    )
    blocks = length // CONTRIB
    lane, spread = offsets_on_lanes(offsets_ref, columns)
    first_block, residue = spread // CONTRIB, spread % CONTRIB
    base = lane % columns * blocks
    width = lane.shape[1]
    shape = (columns * blocks, width)
    high, low = split(spectrum)
    pick = one_hot(shape, base + first_block)
    inside = dot(high, pick) + dot(low, pick)
    pick = one_hot(shape, base + (first_block + 1) % blocks)
    beyond = dot(high, pick) + dot(low, pick)
    kappa = iota((2 * CONTRIB, width), 0) % CONTRIB
    cutout = jnp.where(kappa >= residue, inside, beyond)
    piece = times_table(cutout.T, piece_ref)
    out_ref[...] = (piece * straight_ref[...] + swap_halves(piece) * crossed_ref[...]).astype(BF16)


def subgrid_kernel(
    pieces_ref, cells_ref, values_ref, weights_ref, flags_ref, turn_ref, model_ref, back_ref,
    out_ref, held_ref, *, columns, bands,
):
    fronts, _, samples = cells_ref.shape
    facets = pieces_ref.shape[0] // (fronts * columns)
    groups = facets // FACET_ROWS
    rows = groups * columns
    depth = FACET_ROWS * rows
    share = columns // bands
    pieces = pieces_ref[...].astype(F32)

    def block(facet, front):
        begin = (facet * fronts + front) * columns
        return pieces[begin : begin + columns, :]

    sky = [
        jnp.concatenate(
            [block(j * FACET_ROWS + i, t) for t in range(fronts) for j in range(groups)], axis=0
        )
        for i in range(FACET_ROWS)
    ]
    sky = turned_eighths(sky, -1.0)
    sky = [
        value * turn_ref[0, i : i + 1, :] + swap_halves(value) * turn_ref[1, i : i + 1, :]
        for i, value in enumerate(sky)
    ]
    stacked = jnp.concatenate(
        [value[t * rows : (t + 1) * rows, :] for t in range(fronts) for value in sky], axis=0
    )
    model = table_times(model_ref, stacked, ((1,), (1,)))
    grids = []
    for t in range(fronts):
        row, col = cells_ref[t, 0:1, :], cells_ref[t, 1:2, :]
        pick = one_hot((depth, samples), col % FACET_ROWS * rows + row)
        high, low = split(model[:, t * depth : (t + 1) * depth])
        line = dot(high, pick) + dot(low, pick)
        mask = iota((HALF, samples), 0) == col // FACET_ROWS
        factor = weights_ref[t] * flags_ref[t].astype(F32)
        highs, lows = [], []
        for part in range(2):
            predicted = jnp.sum(
                jnp.where(mask, line[part * HALF : (part + 1) * HALF, :], 0.0),
                axis=0,
                keepdims=True,
            )
            residual = factor * (values_ref[t, part : part + 1, :] - predicted)
            high = residual.astype(BF16).astype(F32)
            highs.append(jnp.where(mask, high, 0.0).astype(BF16))
            lows.append(jnp.where(mask, residual - high, 0.0).astype(BF16))
        grids.append(
            dot(pick, jnp.concatenate(highs, axis=0), ((1,), (1,)))
            + dot(pick, jnp.concatenate(lows, axis=0), ((1,), (1,)))
        )
    back = times_table(jnp.concatenate(grids, axis=0), back_ref)
    lines = []
    for i in range(FACET_ROWS):
        value = jnp.concatenate(
            [
                back[t * depth + i * rows : t * depth + (i + 1) * rows, :]
                for t in range(fronts)
            ],
            axis=0,
        )
        lines.append(
            value * turn_ref[0, i : i + 1, :] - swap_halves(value) * turn_ref[1, i : i + 1, :]
        )
    lines = turned_eighths(lines, 1.0)
    for i in range(FACET_ROWS):
        for t in range(fronts):
            for j in range(groups):
                for b in range(bands):
                    source = (t * groups + j) * columns + b * share
                    target = ((b * facets + j * FACET_ROWS + i) * fronts + t) * share
                    held_ref[target : target + share, :] = lines[i][source : source + share, :]
    out_ref[...] = held_ref[...].astype(BF16)


def return_kernel(
    offsets_ref, pieces_ref, window_ref, turn_ref, shift_ref, partial_ref, inner_ref, outer_ref,
    out_ref, straight_ref, crossed_ref, *line_refs, bands,
):
    columns, _, length = out_ref.shape
    blocks = length // CONTRIB
    groups = length // LANES
    pairs = (columns + 1) // 2
    place_shifts(offsets_ref, shift_ref, straight_ref, crossed_ref, columns)
    width = pieces_ref.shape[0] // bands
    summed = pieces_ref[0:width, :].astype(F32)
    for b in range(1, bands):
        summed += pieces_ref[b * width : (b + 1) * width, :].astype(F32)
    summed = summed * straight_ref[...] - swap_halves(summed) * crossed_ref[...]
    residues = table_times(partial_ref, summed, ((1,), (1,)))
    lane, spread = offsets_on_lanes(offsets_ref, columns)
    first_block, residue = spread // CONTRIB, spread % CONTRIB
    base = lane % columns * blocks
    kappa = iota((2 * CONTRIB, width), 0) % CONTRIB
    inside = kappa >= residue
    both = jnp.concatenate(
        [jnp.where(inside, residues, 0.0), jnp.where(inside, 0.0, residues)], axis=1
    )
    targets = jnp.concatenate(
        [base + first_block, base + (first_block + 1) % blocks], axis=1
    )
    put = one_hot((2 * pairs * blocks, 2 * width), targets)
    high, low = split(both)
    spectrum = dot(high, put, ((1,), (1,))) + dot(low, put, ((1,), (1,)))
    inner = times_table(
        jnp.concatenate(
            [
                jnp.concatenate(
                    [
                        spectrum[:CONTRIB, pair * LANES : (pair + 1) * LANES],
                        spectrum[CONTRIB:, pair * LANES : (pair + 1) * LANES],
                    ],
                    axis=1,
                )
                for pair in range(pairs)
            ],
            axis=0,
        ),
        inner_ref,
    )
    reals, imags = [], []
    for pair in range(pairs):
        rows = slice(pair * CONTRIB, (pair + 1) * CONTRIB)
        real, imag = inner[rows, :LANES], inner[rows, LANES:]
        reals.append(real * turn_ref[0] + imag * turn_ref[1])
        imags.append(imag * turn_ref[0] - real * turn_ref[1])
    lines = table_times(
        outer_ref,
        jnp.concatenate(
            [jnp.concatenate(reals, axis=1), jnp.concatenate(imags, axis=1)], axis=0
        ),
    )
    window = window_ref[...]
    low_half = iota((groups, LANES), 1) < HALF
    for part in range(2):
        for pair in range(pairs):
            lanes = slice(pair * LANES, (pair + 1) * LANES)
            begin = part * blocks
            even = lines[begin : begin + groups, lanes]
            odd = lines[begin + groups : begin + blocks, lanes]
            line_refs[2 * pair][pl.ds(part, groups, stride=2), :] = (
                jnp.where(low_half, even, swap_halves(odd)) * window
            )
            if 2 * pair + 1 < columns:
                line_refs[2 * pair + 1][pl.ds(part, groups, stride=2), :] = (
                    jnp.where(low_half, swap_halves(even), odd) * window
                )
    for column in range(columns):
        for group in range(groups):
            out_ref[column, :, group * LANES : (group + 1) * LANES] = line_refs[column][
                2 * group : 2 * group + 2, :
            ]


def kernel_call(kernel, name, out_shape, spaces, scratch, *operands):
    return pl.pallas_call(
        kernel,
        out_shape=out_shape,
        in_specs=[pl.BlockSpec(memory_space=space) for space in spaces],
        out_specs=pl.BlockSpec(memory_space=pltpu.VMEM),
        scratch_shapes=scratch,
        compiler_params=pltpu.CompilerParams(vmem_limit_bytes=VMEM_LIMIT),
        name=name,
    )(*operands)


def wide(rows):
    return pltpu.VMEM((rows, LANES), F32)


def local(facets, bands, strips, offsets, cells, values, weights, flags):
    columns, length = strips.shape[-2:]
    fronts = offsets.shape[0]
    share = columns // bands
    made = {key: jnp.asarray(value) for key, value in tables(length).items()}
    rows = facets * fronts * columns
    held = length // LANES * columns
    fetched = [
        strips[0, 0], made["window"], made["outer_minus"], made["turn"], made["inner_minus"],
        offsets, made["shift"], made["piece"],
    ]
    is_scalar = [array is offsets for array in fetched]
    fetched = [pltpu.with_memory_space_constraint(array, pltpu.HBM) for array in fetched]
    pieces = kernel_call(
        predict_kernel, "predict", jax.ShapeDtypeStruct((rows, LANES), BF16),
        [pltpu.HBM] * len(fetched),
        [
            (pltpu.SMEM if scalar else pltpu.VMEM)(array.shape, array.dtype)
            for array, scalar in zip(fetched, is_scalar)
        ]
        + [wide(held)] * 2
        + [wide(rows)] * 2
        + [pltpu.SemaphoreType.DMA((len(fetched),))],
        *fetched,
    )
    arrived = lax.all_to_all(pieces, "facet", split_axis=0, concat_axis=0, tiled=True)
    returned = kernel_call(
        functools.partial(subgrid_kernel, columns=columns, bands=bands), "subgrid",
        jax.ShapeDtypeStruct((rows, LANES), BF16), [pltpu.VMEM] * 8, [wide(rows)],
        arrived, cells[0, :, 0], values[0, :, 0], weights[0], flags[0],
        made["grid_turn"], made["model"], made["back"],
    )
    delivered = lax.all_to_all(
        returned, ("band", "facet"), split_axis=0, concat_axis=0, tiled=True
    )
    width = facets * fronts * share
    lines = kernel_call(
        functools.partial(return_kernel, bands=bands), "lines",
        jax.ShapeDtypeStruct((share, 2, length), F32), [pltpu.SMEM] + [pltpu.VMEM] * 7,
        [wide(width)] * 2 + [wide(2 * length // LANES)] * share,
        offsets, delivered, made["window"], made["turn"], made["shift"],
        made["partial"], made["inner_plus"], made["outer_plus"],
    )
    return lines[None]


def solution(mesh):
    placed = (
        P("band", "facet", None, None, None),
        P(),
        P("band", None, "facet", None, None),
        P("band", None, "facet", None, None),
        P("band", None, "facet", None),
        P("band", None, "facet", None),
    )
    return jax.shard_map(
        functools.partial(local, mesh.shape["facet"], mesh.shape["band"]),
        mesh=mesh,
        in_specs=placed,
        out_specs=P("facet", "band", None, None),
        check_vma=False,
    )
```

```python
import functools
import math

import jax
import jax.numpy as jnp
import ml_dtypes
import numpy as np
from jax import lax
from jax.experimental import pallas as pl
from jax.experimental.pallas import tpu as pltpu
from jax.sharding import PartitionSpec as P

CONTRIB = 64
FACET_ROWS = 8
LANES = 128
HALF = LANES // 2
MOST_STEPS = 32
VMEM_LIMIT = 48 * 1024 * 1024
F32 = jnp.float32
BF16 = jnp.bfloat16


def phases(rows, cols, length, rotation):
    product = np.outer(rows, cols) % length
    return np.exp(rotation * 2j * np.pi * product / length)


def from_left(matrix):
    return np.block([[matrix.real, -matrix.imag], [matrix.imag, matrix.real]])


def from_right(matrix):
    return np.block([[matrix.real, matrix.imag], [-matrix.imag, matrix.real]])


def high_low(table):
    high = table.astype(ml_dtypes.bfloat16)
    low = (table - high.astype(np.float64)).astype(ml_dtypes.bfloat16)
    return np.stack([high, low])


def side_by_side(values):
    straight = np.concatenate([values.real, values.real], axis=-1)
    crossed = np.concatenate([-values.imag, values.imag], axis=-1)
    return np.stack([straight, crossed]).astype(np.float32)


def tables(length):
    blocks = length // CONTRIB
    short = np.arange(CONTRIB)
    outer = np.concatenate([np.arange(0, blocks, 2), np.arange(1, blocks, 2)])
    window = 1.0 + 0.5 * np.cos(np.arange(length) * (2.0 * math.pi / length))
    turn = np.tile(phases(short, short, length, -1), (1, 2))
    pair = np.eye(2)
    subgrid_len = FACET_ROWS * CONTRIB
    return dict(
        window=(window * length**-0.5).reshape(length // LANES, LANES).astype(np.float32),
        turn=np.stack([turn.real, turn.imag]).astype(np.float32),
        shift=side_by_side(phases(short, short, CONTRIB, -1)),
        outer_minus=high_low(from_left(phases(short, outer, blocks, -1))),
        inner_minus=high_low(from_right(np.kron(pair, phases(short, short, CONTRIB, -1)))),
        piece=high_low(from_right(phases(short, short, CONTRIB, 1)) * CONTRIB**-0.5),
        inner_plus=high_low(from_right(np.kron(pair, phases(short, short, CONTRIB, 1)))),
        outer_plus=high_low(from_left(phases(outer, short, blocks, 1))),
        partial=high_low(from_right(phases(short, short, CONTRIB, -1)).T * CONTRIB**-0.5),
        grid_turn=side_by_side(phases(np.arange(FACET_ROWS), short, subgrid_len, -1)),
        model=high_low(from_right(phases(short, short, CONTRIB, -1)).T * subgrid_len**-0.5),
        back=high_low(from_right(phases(short, short, CONTRIB, 1)) * subgrid_len**-0.5),
    )


def split(values):
    high = values.astype(BF16)
    return high, (values - high.astype(F32)).astype(BF16)


def dot(left, right, dims=((1,), (0,))):
    return lax.dot_general(left, right, (dims, ((), ())), preferred_element_type=F32)


def times_table(values, table, dims=((1,), (0,))):
    high, low = split(values)
    return dot(high, table[0], dims) + dot(low, table[0], dims) + dot(high, table[1], dims)


def table_times(table, values, dims=((1,), (0,))):
    high, low = split(values)
    return dot(table[0], high, dims) + dot(table[0], low, dims) + dot(table[1], high, dims)


def iota(shape, dimension):
    return lax.broadcasted_iota(jnp.int32, shape, dimension)


def swap_halves(values):
    return pltpu.roll(values, HALF, 1)


def offsets_on_lanes(offsets_ref, columns):
    fronts, owners = offsets_ref.shape
    lane = iota((1, fronts * owners * columns), 1)
    spread = jnp.zeros_like(lane)
    for place in range(fronts * owners):
        begin = place * columns
        here = (lane >= begin) & (lane < begin + columns)
        spread = jnp.where(here, offsets_ref[place % fronts, place // fronts], spread)
    return lane, spread


def place_shifts(offsets_ref, shift_ref, straight_ref, crossed_ref, columns):
    fronts, owners = offsets_ref.shape
    for place in range(fronts * owners):
        residue = offsets_ref[place % fronts, place // fronts] % CONTRIB
        rows = pl.ds(place * columns, columns)
        straight_ref[rows, :] = jnp.broadcast_to(
            shift_ref[0, pl.ds(residue, 1), :], (columns, LANES)
        )
        crossed_ref[rows, :] = jnp.broadcast_to(
            shift_ref[1, pl.ds(residue, 1), :], (columns, LANES)
        )


def one_hot(shape, targets):
    return jnp.where(iota(shape, 0) == targets, 1.0, 0.0).astype(BF16)


def turned_eighths(values, rotation):
    sign = jnp.where(iota(values[0].shape, 1) < HALF, -rotation, rotation).astype(F32)

    def quarter_turn(value):
        return swap_halves(value) * sign

    def four(a, b, c, d):
        even_sum, even_diff = a + c, a - c
        odd_sum, odd_diff = b + d, quarter_turn(b - d)
        return even_sum + odd_sum, even_diff + odd_diff, even_sum - odd_sum, even_diff - odd_diff

    even = four(*values[0::2])
    odd = four(*values[1::2])
    root = math.sqrt(0.5)
    turned = (
        odd[0],
        (odd[1] + quarter_turn(odd[1])) * root,
        quarter_turn(odd[2]),
        (quarter_turn(odd[3]) - odd[3]) * root,
    )
    return [e + o for e, o in zip(even, turned)] + [e - o for e, o in zip(even, turned)]


def predict_kernel(*refs, outs):
    count = 8
    sources, out_refs, targets = refs[:count], refs[count : count + outs], refs[count + outs :]
    copies = [
        pltpu.make_async_copy(sources[i], targets[i], refs[-1].at[i]) for i in range(count)
    ]
    for copy in copies:
        copy.start()
    strips_ref, window_ref, outer_ref, turn_ref, inner_ref, offsets_ref, shift_ref, piece_ref = (
        targets[:count]
    )
    real_ref, imag_ref, straight_ref, crossed_ref, held_ref = targets[count:-1]
    columns, length = strips_ref.shape[1:]
    groups = length // LANES
    pairs = columns // 2
    copies[0].wait()
    copies[1].wait()
    window = window_ref[...]
    low_half = iota((groups, LANES), 1) < HALF
    sections = []
    for part, held in enumerate((real_ref, imag_ref)):
        for group in range(groups):
            held[group * columns : (group + 1) * columns, :] = strips_ref[
                part, :, group * LANES : (group + 1) * LANES
            ]
        even, odd = [], []
        for pair in range(pairs):
            first = held[pl.ds(2 * pair, groups, stride=columns), :] * window
            second = held[pl.ds(2 * pair + 1, groups, stride=columns), :] * window
            even.append(jnp.where(low_half, first, swap_halves(second)))
            odd.append(jnp.where(low_half, swap_halves(first), second))
        sections += [jnp.concatenate(even, axis=1), jnp.concatenate(odd, axis=1)]
    for copy in copies[2:]:
        copy.wait()
    place_shifts(offsets_ref, shift_ref, straight_ref, crossed_ref, columns)
    section = table_times(outer_ref, jnp.concatenate(sections, axis=0))
    turned = []
    for pair in range(pairs):
        lanes = slice(pair * LANES, (pair + 1) * LANES)
        real, imag = section[:CONTRIB, lanes], section[CONTRIB:, lanes]
        turned.append(
            jnp.concatenate(
                [
                    real * turn_ref[0] - imag * turn_ref[1],
                    real * turn_ref[1] + imag * turn_ref[0],
                ],
                axis=1,
            )
        )
    inner = times_table(jnp.concatenate(turned, axis=0), inner_ref)
    spectrum = jnp.concatenate(
        [
            jnp.concatenate(
                [
                    inner[pair * CONTRIB : (pair + 1) * CONTRIB, part * LANES : (part + 1) * LANES]
                    for pair in range(pairs)
                ],
                axis=1,
            )
            for part in range(2)
        ],
        axis=0,
    )
    blocks = length // CONTRIB
    lane, spread = offsets_on_lanes(offsets_ref, columns)
    first_block, residue = spread // CONTRIB, spread % CONTRIB
    base = lane % columns * blocks
    width = lane.shape[1]
    shape = (columns * blocks, width)
    high, low = split(spectrum)
    pick = one_hot(shape, base + first_block)
    inside = dot(high, pick) + dot(low, pick)
    pick = one_hot(shape, base + (first_block + 1) % blocks)
    beyond = dot(high, pick) + dot(low, pick)
    kappa = iota((2 * CONTRIB, width), 0) % CONTRIB
    cutout = jnp.where(kappa >= residue, inside, beyond)
    piece = times_table(cutout.T, piece_ref)
    piece = piece * straight_ref[...] + swap_halves(piece) * crossed_ref[...]
    if outs == 1:
        out_refs[0][...] = piece.astype(BF16)
        return
    held_ref[...] = piece
    me = lax.axis_index("facet")
    for step, out_ref in enumerate(out_refs):
        rows = out_ref.shape[0]
        begin = pl.multiple_of((me ^ step) * rows, rows)
        out_ref[...] = held_ref[pl.ds(begin, rows), :].astype(BF16)


def subgrid_kernel(*refs, columns, bands, facets, parts):
    cells_ref, values_ref, weights_ref, flags_ref, turn_ref, model_ref, back_ref = refs[parts:-2]
    out_ref, held_ref = refs[-2:]
    fronts, _, samples = cells_ref.shape
    groups = facets // FACET_ROWS
    rows = groups * columns
    depth = FACET_ROWS * rows
    share = columns // bands
    if parts == 1:
        pieces = refs[0][...].astype(F32)
    else:
        me = lax.axis_index("facet")
        for step, part_ref in enumerate(refs[:parts]):
            begin = pl.multiple_of((me ^ step) * part_ref.shape[0], part_ref.shape[0])
            held_ref[pl.ds(begin, part_ref.shape[0]), :] = part_ref[...].astype(F32)
        pieces = held_ref[...]

    def block(facet, front):
        begin = (facet * fronts + front) * columns
        return pieces[begin : begin + columns, :]

    sky = [
        jnp.concatenate(
            [block(j * FACET_ROWS + i, t) for t in range(fronts) for j in range(groups)], axis=0
        )
        for i in range(FACET_ROWS)
    ]
    sky = turned_eighths(sky, -1.0)
    sky = [
        value * turn_ref[0, i : i + 1, :] + swap_halves(value) * turn_ref[1, i : i + 1, :]
        for i, value in enumerate(sky)
    ]
    stacked = jnp.concatenate(
        [value[t * rows : (t + 1) * rows, :] for t in range(fronts) for value in sky], axis=0
    )
    model = table_times(model_ref, stacked, ((1,), (1,)))
    grids = []
    for t in range(fronts):
        row, col = cells_ref[t, 0:1, :], cells_ref[t, 1:2, :]
        pick = one_hot((depth, samples), col % FACET_ROWS * rows + row)
        high, low = split(model[:, t * depth : (t + 1) * depth])
        line = dot(high, pick) + dot(low, pick)
        mask = iota((HALF, samples), 0) == col // FACET_ROWS
        factor = weights_ref[t] * flags_ref[t].astype(F32)
        highs, lows = [], []
        for part in range(2):
            predicted = jnp.sum(
                jnp.where(mask, line[part * HALF : (part + 1) * HALF, :], 0.0),
                axis=0,
                keepdims=True,
            )
            residual = factor * (values_ref[t, part : part + 1, :] - predicted)
            high = residual.astype(BF16).astype(F32)
            highs.append(jnp.where(mask, high, 0.0).astype(BF16))
            lows.append(jnp.where(mask, residual - high, 0.0).astype(BF16))
        grids.append(
            dot(pick, jnp.concatenate(highs, axis=0), ((1,), (1,)))
            + dot(pick, jnp.concatenate(lows, axis=0), ((1,), (1,)))
        )
    back = times_table(jnp.concatenate(grids, axis=0), back_ref)
    lines = []
    for i in range(FACET_ROWS):
        value = jnp.concatenate(
            [
                back[t * depth + i * rows : t * depth + (i + 1) * rows, :]
                for t in range(fronts)
            ],
            axis=0,
        )
        lines.append(
            value * turn_ref[0, i : i + 1, :] - swap_halves(value) * turn_ref[1, i : i + 1, :]
        )
    lines = turned_eighths(lines, 1.0)
    for i in range(FACET_ROWS):
        for t in range(fronts):
            for j in range(groups):
                for b in range(bands):
                    source = (t * groups + j) * columns + b * share
                    target = ((b * facets + j * FACET_ROWS + i) * fronts + t) * share
                    held_ref[target : target + share, :] = lines[i][source : source + share, :]
    out_ref[...] = held_ref[...].astype(BF16)


def return_kernel(
    offsets_ref, pieces_ref, window_ref, turn_ref, shift_ref, partial_ref, inner_ref, outer_ref,
    out_ref, straight_ref, crossed_ref, *line_refs, bands,
):
    columns, _, length = out_ref.shape
    blocks = length // CONTRIB
    groups = length // LANES
    pairs = (columns + 1) // 2
    place_shifts(offsets_ref, shift_ref, straight_ref, crossed_ref, columns)
    width = pieces_ref.shape[0] // bands
    summed = pieces_ref[0:width, :].astype(F32)
    for b in range(1, bands):
        summed += pieces_ref[b * width : (b + 1) * width, :].astype(F32)
    summed = summed * straight_ref[...] - swap_halves(summed) * crossed_ref[...]
    residues = table_times(partial_ref, summed, ((1,), (1,)))
    lane, spread = offsets_on_lanes(offsets_ref, columns)
    first_block, residue = spread // CONTRIB, spread % CONTRIB
    base = lane % columns * blocks
    kappa = iota((2 * CONTRIB, width), 0) % CONTRIB
    inside = kappa >= residue
    both = jnp.concatenate(
        [jnp.where(inside, residues, 0.0), jnp.where(inside, 0.0, residues)], axis=1
    )
    targets = jnp.concatenate(
        [base + first_block, base + (first_block + 1) % blocks], axis=1
    )
    put = one_hot((2 * pairs * blocks, 2 * width), targets)
    high, low = split(both)
    spectrum = dot(high, put, ((1,), (1,))) + dot(low, put, ((1,), (1,)))
    inner = times_table(
        jnp.concatenate(
            [
                jnp.concatenate(
                    [
                        spectrum[:CONTRIB, pair * LANES : (pair + 1) * LANES],
                        spectrum[CONTRIB:, pair * LANES : (pair + 1) * LANES],
                    ],
                    axis=1,
                )
                for pair in range(pairs)
            ],
            axis=0,
        ),
        inner_ref,
    )
    reals, imags = [], []
    for pair in range(pairs):
        rows = slice(pair * CONTRIB, (pair + 1) * CONTRIB)
        real, imag = inner[rows, :LANES], inner[rows, LANES:]
        reals.append(real * turn_ref[0] + imag * turn_ref[1])
        imags.append(imag * turn_ref[0] - real * turn_ref[1])
    lines = table_times(
        outer_ref,
        jnp.concatenate(
            [jnp.concatenate(reals, axis=1), jnp.concatenate(imags, axis=1)], axis=0
        ),
    )
    window = window_ref[...]
    low_half = iota((groups, LANES), 1) < HALF
    for part in range(2):
        for pair in range(pairs):
            lanes = slice(pair * LANES, (pair + 1) * LANES)
            begin = part * blocks
            even = lines[begin : begin + groups, lanes]
            odd = lines[begin + groups : begin + blocks, lanes]
            line_refs[2 * pair][pl.ds(part, groups, stride=2), :] = (
                jnp.where(low_half, even, swap_halves(odd)) * window
            )
            if 2 * pair + 1 < columns:
                line_refs[2 * pair + 1][pl.ds(part, groups, stride=2), :] = (
                    jnp.where(low_half, swap_halves(even), odd) * window
                )
    for column in range(columns):
        for group in range(groups):
            out_ref[column, :, group * LANES : (group + 1) * LANES] = line_refs[column][
                2 * group : 2 * group + 2, :
            ]


def kernel_call(kernel, name, out_shape, spaces, scratch, *operands):
    return pl.pallas_call(
        kernel,
        out_shape=out_shape,
        in_specs=[pl.BlockSpec(memory_space=space) for space in spaces],
        out_specs=jax.tree.map(lambda _: pl.BlockSpec(memory_space=pltpu.VMEM), out_shape),
        scratch_shapes=scratch,
        compiler_params=pltpu.CompilerParams(vmem_limit_bytes=VMEM_LIMIT),
        name=name,
    )(*operands)


def wide(rows):
    return pltpu.VMEM((rows, LANES), F32)


def local(facets, bands, strips, offsets, cells, values, weights, flags):
    columns, length = strips.shape[-2:]
    fronts = offsets.shape[0]
    share = columns // bands
    made = {key: jnp.asarray(value) for key, value in tables(length).items()}
    rows = facets * fronts * columns
    held = length // LANES * columns
    fetched = [
        strips[0, 0], made["window"], made["outer_minus"], made["turn"], made["inner_minus"],
        offsets, made["shift"], made["piece"],
    ]
    is_scalar = [array is offsets for array in fetched]
    fetched = [pltpu.with_memory_space_constraint(array, pltpu.HBM) for array in fetched]
    parts = facets if facets <= MOST_STEPS and facets & (facets - 1) == 0 else 1
    pieces = kernel_call(
        functools.partial(predict_kernel, outs=parts), "predict",
        [jax.ShapeDtypeStruct((rows // parts, LANES), BF16)] * parts,
        [pltpu.HBM] * len(fetched),
        [
            (pltpu.SMEM if scalar else pltpu.VMEM)(array.shape, array.dtype)
            for array, scalar in zip(fetched, is_scalar)
        ]
        + [wide(held)] * 2
        + [wide(rows)] * 3
        + [pltpu.SemaphoreType.DMA((len(fetched),))],
        *fetched,
    )
    if parts == 1:
        arrived = [lax.all_to_all(pieces[0], "facet", split_axis=0, concat_axis=0, tiled=True)]
    else:
        arrived = [pieces[0]] + [
            lax.ppermute(pieces[step], "facet", [(i, i ^ step) for i in range(facets)])
            for step in range(1, facets)
        ]
    returned = kernel_call(
        functools.partial(
            subgrid_kernel, columns=columns, bands=bands, facets=facets, parts=parts
        ),
        "subgrid",
        jax.ShapeDtypeStruct((rows, LANES), BF16), [pltpu.VMEM] * (7 + parts), [wide(rows)],
        *arrived, cells[0, :, 0], values[0, :, 0], weights[0], flags[0],
        made["grid_turn"], made["model"], made["back"],
    )
    delivered = lax.all_to_all(
        returned, ("band", "facet"), split_axis=0, concat_axis=0, tiled=True
    )
    width = facets * fronts * share
    lines = kernel_call(
        functools.partial(return_kernel, bands=bands), "lines",
        jax.ShapeDtypeStruct((share, 2, length), F32), [pltpu.SMEM] + [pltpu.VMEM] * 7,
        [wide(width)] * 2 + [wide(2 * length // LANES)] * share,
        offsets, delivered, made["window"], made["turn"], made["shift"],
        made["partial"], made["inner_plus"], made["outer_plus"],
    )
    return lines[None]


def solution(mesh):
    placed = (
        P("band", "facet", None, None, None),
        P(),
        P("band", None, "facet", None, None),
        P("band", None, "facet", None, None),
        P("band", None, "facet", None),
        P("band", None, "facet", None),
    )
    return jax.shard_map(
        functools.partial(local, mesh.shape["facet"], mesh.shape["band"]),
        mesh=mesh,
        in_specs=placed,
        out_specs=P("facet", "band", None, None),
        check_vma=False,
    )
```

```python
import functools
import math

import jax
import jax.numpy as jnp
import ml_dtypes
import numpy as np
from jax import lax
from jax.experimental import pallas as pl
from jax.experimental.pallas import tpu as pltpu
from jax.sharding import Mesh
from jax.sharding import PartitionSpec as P

CONTRIB = 64
FACET_ROWS = 8
LANES = 128
HALF = LANES // 2
VMEM_LIMIT = 48 * 1024 * 1024
F32 = jnp.float32
BF16 = jnp.bfloat16


def phases(rows, cols, length, rotation):
    product = np.outer(rows, cols) % length
    return np.exp(rotation * 2j * np.pi * product / length)


def from_left(matrix):
    return np.block([[matrix.real, -matrix.imag], [matrix.imag, matrix.real]])


def from_right(matrix):
    return np.block([[matrix.real, matrix.imag], [-matrix.imag, matrix.real]])


def high_low(table):
    high = table.astype(ml_dtypes.bfloat16)
    low = (table - high.astype(np.float64)).astype(ml_dtypes.bfloat16)
    return np.stack([high, low])


def side_by_side(values):
    straight = np.concatenate([values.real, values.real], axis=-1)
    crossed = np.concatenate([-values.imag, values.imag], axis=-1)
    return np.stack([straight, crossed]).astype(np.float32)


def tables(length):
    blocks = length // CONTRIB
    short = np.arange(CONTRIB)
    outer = np.concatenate([np.arange(0, blocks, 2), np.arange(1, blocks, 2)])
    window = 1.0 + 0.5 * np.cos(np.arange(length) * (2.0 * math.pi / length))
    turn = np.tile(phases(short, short, length, -1), (1, 2))
    pair = np.eye(2)
    subgrid_len = FACET_ROWS * CONTRIB
    return dict(
        window=(window * length**-0.5).reshape(length // LANES, LANES).astype(np.float32),
        turn=np.stack([turn.real, turn.imag]).astype(np.float32),
        shift=side_by_side(phases(short, short, CONTRIB, -1)),
        outer_minus=high_low(from_left(phases(short, outer, blocks, -1))),
        inner_minus=high_low(from_right(np.kron(pair, phases(short, short, CONTRIB, -1)))),
        piece=high_low(from_right(phases(short, short, CONTRIB, 1)) * CONTRIB**-0.5),
        inner_plus=high_low(from_right(np.kron(pair, phases(short, short, CONTRIB, 1)))),
        outer_plus=high_low(from_left(phases(outer, short, blocks, 1))),
        partial=high_low(from_right(phases(short, short, CONTRIB, -1)).T * CONTRIB**-0.5),
        grid_turn=side_by_side(phases(np.arange(FACET_ROWS), short, subgrid_len, -1)),
        model=high_low(from_right(phases(short, short, CONTRIB, -1)) * subgrid_len**-0.5),
        back=high_low(from_right(phases(short, short, CONTRIB, 1)) * subgrid_len**-0.5),
    )


def split(values):
    high = values.astype(BF16)
    return high, (values - high.astype(F32)).astype(BF16)


def dot(left, right, dims=((1,), (0,))):
    return lax.dot_general(left, right, (dims, ((), ())), preferred_element_type=F32)


def times_table(values, table, dims=((1,), (0,))):
    high, low = split(values)
    return dot(high, table[0], dims) + dot(low, table[0], dims) + dot(high, table[1], dims)


def table_times(table, values, dims=((1,), (0,))):
    high, low = split(values)
    return dot(table[0], high, dims) + dot(table[0], low, dims) + dot(table[1], high, dims)


def iota(shape, dimension):
    return lax.broadcasted_iota(jnp.int32, shape, dimension)


def swap_halves(values):
    return pltpu.roll(values, HALF, 1)


def place_offsets(offsets_ref):
    fronts, owners = offsets_ref.shape
    groups = owners // FACET_ROWS
    own = lax.axis_index("group")
    return [
        offsets_ref[t, lax.rem(own + step, groups) * FACET_ROWS + member]
        for member in range(FACET_ROWS)
        for step in range(groups)
        for t in range(fronts)
    ]


def offsets_on_lanes(offsets, columns):
    lane = iota((1, len(offsets) * columns), 1)
    spread = jnp.zeros_like(lane)
    for place, offset in enumerate(offsets):
        begin = place * columns
        here = (lane >= begin) & (lane < begin + columns)
        spread = jnp.where(here, offset, spread)
    return lane, spread


def place_shifts(offsets, shift_ref, straight_ref, crossed_ref, columns):
    for place, offset in enumerate(offsets):
        residue = offset % CONTRIB
        rows = pl.ds(place * columns, columns)
        straight_ref[rows, :] = jnp.broadcast_to(
            shift_ref[0, pl.ds(residue, 1), :], (columns, LANES)
        )
        crossed_ref[rows, :] = jnp.broadcast_to(
            shift_ref[1, pl.ds(residue, 1), :], (columns, LANES)
        )


def one_hot(shape, targets):
    return jnp.where(iota(shape, 0) == targets, 1.0, 0.0).astype(BF16)


def turned_eighths(values, rotation):
    sign = jnp.where(iota(values[0].shape, 1) < HALF, -rotation, rotation).astype(F32)

    def quarter_turn(value):
        return swap_halves(value) * sign

    def four(a, b, c, d):
        even_sum, even_diff = a + c, a - c
        odd_sum, odd_diff = b + d, quarter_turn(b - d)
        return even_sum + odd_sum, even_diff + odd_diff, even_sum - odd_sum, even_diff - odd_diff

    even = four(*values[0::2])
    odd = four(*values[1::2])
    root = math.sqrt(0.5)
    turned = (
        odd[0],
        (odd[1] + quarter_turn(odd[1])) * root,
        quarter_turn(odd[2]),
        (quarter_turn(odd[3]) - odd[3]) * root,
    )
    return [e + o for e, o in zip(even, turned)] + [e - o for e, o in zip(even, turned)]


def predict_kernel(*refs):
    count = 8
    copies = [
        pltpu.make_async_copy(refs[i], refs[count + 1 + i], refs[-1].at[i]) for i in range(count)
    ]
    for copy in copies:
        copy.start()
    out_ref = refs[count]
    strips_ref, window_ref, outer_ref, turn_ref, inner_ref, offsets_ref, shift_ref, piece_ref = (
        refs[count + 1 : 2 * count + 1]
    )
    real_ref, imag_ref, straight_ref, crossed_ref = refs[2 * count + 1 : -1]
    columns, length = strips_ref.shape[1:]
    groups = length // LANES
    pairs = columns // 2
    copies[0].wait()
    copies[1].wait()
    window = window_ref[...]
    low_half = iota((groups, LANES), 1) < HALF
    sections = []
    for part, held in enumerate((real_ref, imag_ref)):
        for group in range(groups):
            held[group * columns : (group + 1) * columns, :] = strips_ref[
                part, :, group * LANES : (group + 1) * LANES
            ]
        even, odd = [], []
        for pair in range(pairs):
            first = held[pl.ds(2 * pair, groups, stride=columns), :] * window
            second = held[pl.ds(2 * pair + 1, groups, stride=columns), :] * window
            even.append(jnp.where(low_half, first, swap_halves(second)))
            odd.append(jnp.where(low_half, swap_halves(first), second))
        sections += [jnp.concatenate(even, axis=1), jnp.concatenate(odd, axis=1)]
    for copy in copies[2:]:
        copy.wait()
    offsets = place_offsets(offsets_ref)
    place_shifts(offsets, shift_ref, straight_ref, crossed_ref, columns)
    section = table_times(outer_ref, jnp.concatenate(sections, axis=0))
    turned = []
    for pair in range(pairs):
        lanes = slice(pair * LANES, (pair + 1) * LANES)
        real, imag = section[:CONTRIB, lanes], section[CONTRIB:, lanes]
        turned.append(
            jnp.concatenate(
                [
                    real * turn_ref[0] - imag * turn_ref[1],
                    real * turn_ref[1] + imag * turn_ref[0],
                ],
                axis=1,
            )
        )
    inner = times_table(jnp.concatenate(turned, axis=0), inner_ref)
    spectrum = jnp.concatenate(
        [
            jnp.concatenate(
                [
                    inner[pair * CONTRIB : (pair + 1) * CONTRIB, part * LANES : (part + 1) * LANES]
                    for pair in range(pairs)
                ],
                axis=1,
            )
            for part in range(2)
        ],
        axis=0,
    )
    blocks = length // CONTRIB
    lane, spread = offsets_on_lanes(offsets, columns)
    first_block, residue = spread // CONTRIB, spread % CONTRIB
    base = lane % columns * blocks
    width = lane.shape[1]
    shape = (columns * blocks, width)
    high, low = split(spectrum)
    pick = one_hot(shape, base + first_block)
    inside = dot(high, pick) + dot(low, pick)
    pick = one_hot(shape, base + (first_block + 1) % blocks)
    beyond = dot(high, pick) + dot(low, pick)
    kappa = iota((2 * CONTRIB, width), 0) % CONTRIB
    cutout = jnp.where(kappa >= residue, inside, beyond)
    piece = times_table(cutout.T, piece_ref)
    out_ref[...] = (piece * straight_ref[...] + swap_halves(piece) * crossed_ref[...]).astype(BF16)


def subgrid_kernel(pieces_ref, turn_ref, model_ref, back_ref, *refs, columns, bands):
    samples_refs, (out_ref, held_ref) = refs[:-2], refs[-2:]
    groups = len(samples_refs) // 4
    fronts, _, samples = samples_refs[0].shape
    own = lax.axis_index("group")
    rows = pieces_ref.shape[0] // FACET_ROWS
    depth = FACET_ROWS * columns
    share = columns // bands
    pieces = pieces_ref[...].astype(F32)
    sky = turned_eighths(
        [pieces[i * rows : (i + 1) * rows, :] for i in range(FACET_ROWS)], -1.0
    )
    sky = [
        value * turn_ref[0, i : i + 1, :] + swap_halves(value) * turn_ref[1, i : i + 1, :]
        for i, value in enumerate(sky)
    ]
    spots = range(groups * fronts)
    stacked = jnp.concatenate(
        [value[spot * columns : (spot + 1) * columns, :] for spot in spots for value in sky],
        axis=0,
    )
    model = times_table(stacked, model_ref)
    grids = []
    for spot in spots:
        step, t = spot // fronts, spot % fronts
        cells_ref, values_ref, weights_ref, flags_ref = samples_refs[4 * step : 4 * step + 4]
        row, col = cells_ref[t, 0:1, :] - own * columns, cells_ref[t, 1:2, :]
        inside = (row >= 0) & (row < columns)
        target = jnp.where(inside, col % FACET_ROWS * columns + row, -1)
        pick = one_hot((depth, samples), target)
        high, low = split(model[spot * depth : (spot + 1) * depth, :].T)
        line = dot(high, pick) + dot(low, pick)
        mask = iota((HALF, samples), 0) == col // FACET_ROWS
        factor = weights_ref[t] * flags_ref[t].astype(F32)
        highs, lows = [], []
        for part in range(2):
            predicted = jnp.sum(
                jnp.where(mask, line[part * HALF : (part + 1) * HALF, :], 0.0),
                axis=0,
                keepdims=True,
            )
            residual = factor * (values_ref[t, part : part + 1, :] - predicted)
            high = residual.astype(BF16).astype(F32)
            highs.append(jnp.where(mask, high, 0.0).astype(BF16))
            lows.append(jnp.where(mask, residual - high, 0.0).astype(BF16))
        grids.append(
            dot(pick, jnp.concatenate(highs, axis=0), ((1,), (1,)))
            + dot(pick, jnp.concatenate(lows, axis=0), ((1,), (1,)))
        )
    back = times_table(jnp.concatenate(grids, axis=0), back_ref)
    lines = []
    for i in range(FACET_ROWS):
        value = jnp.concatenate(
            [
                back[spot * depth + i * columns : spot * depth + (i + 1) * columns, :]
                for spot in spots
            ],
            axis=0,
        )
        lines.append(
            value * turn_ref[0, i : i + 1, :] - swap_halves(value) * turn_ref[1, i : i + 1, :]
        )
    lines = turned_eighths(lines, 1.0)
    for i in range(FACET_ROWS):
        for spot in spots:
            for b in range(bands):
                source = spot * columns + b * share
                target = ((b * FACET_ROWS + i) * len(spots) + spot) * share
                held_ref[target : target + share, :] = lines[i][source : source + share, :]
    out_ref[...] = held_ref[...].astype(BF16)


def return_kernel(
    offsets_ref, pieces_ref, window_ref, turn_ref, shift_ref, partial_ref, inner_ref, outer_ref,
    out_ref, straight_ref, crossed_ref, *line_refs, bands,
):
    columns, _, length = out_ref.shape
    blocks = length // CONTRIB
    groups = length // LANES
    pairs = (columns + 1) // 2
    offsets = place_offsets(offsets_ref)
    place_shifts(offsets, shift_ref, straight_ref, crossed_ref, columns)
    width = pieces_ref.shape[0] // bands
    summed = pieces_ref[0:width, :].astype(F32)
    for b in range(1, bands):
        summed += pieces_ref[b * width : (b + 1) * width, :].astype(F32)
    summed = summed * straight_ref[...] - swap_halves(summed) * crossed_ref[...]
    residues = table_times(partial_ref, summed, ((1,), (1,)))
    lane, spread = offsets_on_lanes(offsets, columns)
    first_block, residue = spread // CONTRIB, spread % CONTRIB
    base = lane % columns * blocks
    kappa = iota((2 * CONTRIB, width), 0) % CONTRIB
    inside = kappa >= residue
    both = jnp.concatenate(
        [jnp.where(inside, residues, 0.0), jnp.where(inside, 0.0, residues)], axis=1
    )
    targets = jnp.concatenate(
        [base + first_block, base + (first_block + 1) % blocks], axis=1
    )
    put = one_hot((2 * pairs * blocks, 2 * width), targets)
    high, low = split(both)
    spectrum = dot(high, put, ((1,), (1,))) + dot(low, put, ((1,), (1,)))
    inner = times_table(
        jnp.concatenate(
            [
                jnp.concatenate(
                    [
                        spectrum[:CONTRIB, pair * LANES : (pair + 1) * LANES],
                        spectrum[CONTRIB:, pair * LANES : (pair + 1) * LANES],
                    ],
                    axis=1,
                )
                for pair in range(pairs)
            ],
            axis=0,
        ),
        inner_ref,
    )
    reals, imags = [], []
    for pair in range(pairs):
        rows = slice(pair * CONTRIB, (pair + 1) * CONTRIB)
        real, imag = inner[rows, :LANES], inner[rows, LANES:]
        reals.append(real * turn_ref[0] + imag * turn_ref[1])
        imags.append(imag * turn_ref[0] - real * turn_ref[1])
    lines = table_times(
        outer_ref,
        jnp.concatenate(
            [jnp.concatenate(reals, axis=1), jnp.concatenate(imags, axis=1)], axis=0
        ),
    )
    window = window_ref[...]
    low_half = iota((groups, LANES), 1) < HALF
    for part in range(2):
        for pair in range(pairs):
            lanes = slice(pair * LANES, (pair + 1) * LANES)
            begin = part * blocks
            even = lines[begin : begin + groups, lanes]
            odd = lines[begin + groups : begin + blocks, lanes]
            line_refs[2 * pair][pl.ds(part, groups, stride=2), :] = (
                jnp.where(low_half, even, swap_halves(odd)) * window
            )
            if 2 * pair + 1 < columns:
                line_refs[2 * pair + 1][pl.ds(part, groups, stride=2), :] = (
                    jnp.where(low_half, swap_halves(even), odd) * window
                )
    for column in range(columns):
        for group in range(groups):
            out_ref[column, :, group * LANES : (group + 1) * LANES] = line_refs[column][
                2 * group : 2 * group + 2, :
            ]


def kernel_call(kernel, name, out_shape, spaces, scratch, *operands):
    return pl.pallas_call(
        kernel,
        out_shape=out_shape,
        in_specs=[pl.BlockSpec(memory_space=space) for space in spaces],
        out_specs=pl.BlockSpec(memory_space=pltpu.VMEM),
        scratch_shapes=scratch,
        compiler_params=pltpu.CompilerParams(vmem_limit_bytes=VMEM_LIMIT),
        name=name,
    )(*operands)


def wide(rows):
    return pltpu.VMEM((rows, LANES), F32)


def local(groups, bands, strips, offsets, cells, values, weights, flags):
    columns, length = strips.shape[-2:]
    fronts = offsets.shape[0]
    share = columns // bands
    made = {key: jnp.asarray(value) for key, value in tables(length).items()}
    facets = groups * FACET_ROWS
    rows = facets * fronts * columns
    held = length // LANES * columns
    fetched = [
        strips[0, 0], made["window"], made["outer_minus"], made["turn"], made["inner_minus"],
        offsets, made["shift"], made["piece"],
    ]
    is_scalar = [array is offsets for array in fetched]
    fetched = [pltpu.with_memory_space_constraint(array, pltpu.HBM) for array in fetched]
    pieces = kernel_call(
        predict_kernel, "predict", jax.ShapeDtypeStruct((rows, LANES), BF16),
        [pltpu.HBM] * len(fetched),
        [
            (pltpu.SMEM if scalar else pltpu.VMEM)(array.shape, array.dtype)
            for array, scalar in zip(fetched, is_scalar)
        ]
        + [wide(held)] * 2
        + [wide(rows)] * 2
        + [pltpu.SemaphoreType.DMA((len(fetched),))],
        *fetched,
    )
    samples = [cells[0, :, 0], values[0, :, 0], weights[0], flags[0]]
    gathered = list(samples)
    for step in range(1, groups):
        moves = [((group + step) % groups, group) for group in range(groups)]
        gathered += [lax.ppermute(array, "group", moves) for array in samples]
    arrived = lax.all_to_all(pieces, "member", split_axis=0, concat_axis=0, tiled=True)
    returned = kernel_call(
        functools.partial(subgrid_kernel, columns=columns, bands=bands), "subgrid",
        jax.ShapeDtypeStruct((rows, LANES), BF16), [pltpu.VMEM] * (4 + len(gathered)),
        [wide(rows)],
        arrived, made["grid_turn"], made["model"], made["back"], *gathered,
    )
    delivered = lax.all_to_all(
        returned, ("band", "member"), split_axis=0, concat_axis=0, tiled=True
    )
    width = facets * fronts * share
    lines = kernel_call(
        functools.partial(return_kernel, bands=bands), "lines",
        jax.ShapeDtypeStruct((share, 2, length), F32), [pltpu.SMEM] + [pltpu.VMEM] * 7,
        [wide(width)] * 2 + [wide(2 * length // LANES)] * share,
        offsets, delivered, made["window"], made["turn"], made["shift"],
        made["partial"], made["inner_plus"], made["outer_plus"],
    )
    return lines[None]


def solution(mesh):
    bands = mesh.shape["band"]
    groups = mesh.shape["facet"] // FACET_ROWS
    split_mesh = Mesh(
        mesh.devices.reshape(groups, FACET_ROWS, bands), ("group", "member", "band")
    )
    facet = ("group", "member")
    placed = (
        P("band", facet, None, None, None),
        P(),
        P("band", None, facet, None, None),
        P("band", None, facet, None, None),
        P("band", None, facet, None),
        P("band", None, facet, None),
    )
    return jax.shard_map(
        functools.partial(local, groups, bands),
        mesh=split_mesh,
        in_specs=placed,
        out_specs=P(facet, "band", None, None),
        check_vma=False,
    )
```

```python
import functools
import math

import jax
import jax.numpy as jnp
import ml_dtypes
import numpy as np
from jax import lax
from jax.experimental import pallas as pl
from jax.experimental.pallas import tpu as pltpu
from jax.sharding import Mesh
from jax.sharding import PartitionSpec as P

CONTRIB = 64
FACET_ROWS = 8
SUBGRID = FACET_ROWS * CONTRIB
LANES = 128
HALF = LANES // 2
VMEM_LIMIT = 48 * 1024 * 1024
F32 = jnp.float32
BF16 = jnp.bfloat16


def phases(rows, cols, length, rotation):
    product = np.outer(rows, cols) % length
    return np.exp(rotation * 2j * np.pi * product / length)


def from_left(matrix):
    return np.block([[matrix.real, -matrix.imag], [matrix.imag, matrix.real]])


def from_right(matrix):
    return np.block([[matrix.real, matrix.imag], [-matrix.imag, matrix.real]])


def high_low(table):
    high = table.astype(ml_dtypes.bfloat16)
    low = (table - high.astype(np.float64)).astype(ml_dtypes.bfloat16)
    return np.stack([high, low])


def side_by_side(values):
    straight = np.concatenate([values.real, values.real], axis=-1)
    crossed = np.concatenate([-values.imag, values.imag], axis=-1)
    return np.stack([straight, crossed]).astype(np.float32)


def tables(length):
    blocks = length // CONTRIB
    short = np.arange(CONTRIB)
    outer = np.concatenate([np.arange(0, blocks, 2), np.arange(1, blocks, 2)])
    window = 1.0 + 0.5 * np.cos(np.arange(length) * (2.0 * math.pi / length))
    turn = np.tile(phases(short, short, length, -1), (1, 2))
    pair = np.eye(2)
    return dict(
        window=(window * length**-0.5).reshape(length // LANES, LANES).astype(np.float32),
        turn=np.stack([turn.real, turn.imag]).astype(np.float32),
        shift=side_by_side(phases(short, short, CONTRIB, -1)),
        outer_minus=high_low(from_left(phases(short, outer, blocks, -1))),
        inner_minus=high_low(from_right(np.kron(pair, phases(short, short, CONTRIB, -1)))),
        piece=high_low(from_right(phases(short, short, CONTRIB, 1)) * CONTRIB**-0.5),
        inner_plus=high_low(from_right(np.kron(pair, phases(short, short, CONTRIB, 1)))),
        outer_plus=high_low(from_left(phases(outer, short, blocks, 1))),
        partial=high_low(from_right(phases(short, short, CONTRIB, -1)).T * CONTRIB**-0.5),
        grid_turn=side_by_side(phases(np.arange(FACET_ROWS), short, SUBGRID, -1)),
        model=high_low(from_right(phases(short, short, CONTRIB, -1)) * SUBGRID**-0.5),
        back=high_low(from_right(phases(short, short, CONTRIB, 1)) * SUBGRID**-0.5),
    )


def split(values):
    high = values.astype(BF16)
    return high, (values - high.astype(F32)).astype(BF16)


def dot(left, right, dims=((1,), (0,))):
    return lax.dot_general(left, right, (dims, ((), ())), preferred_element_type=F32)


def times_table(values, table, dims=((1,), (0,))):
    high, low = split(values)
    return dot(high, table[0], dims) + dot(low, table[0], dims) + dot(high, table[1], dims)


def table_times(table, values, dims=((1,), (0,))):
    high, low = split(values)
    return dot(table[0], high, dims) + dot(table[0], low, dims) + dot(table[1], high, dims)


def iota(shape, dimension):
    return lax.broadcasted_iota(jnp.int32, shape, dimension)


def swap_halves(values):
    return pltpu.roll(values, HALF, 1)


def place_offsets(offsets_ref):
    fronts, owners = offsets_ref.shape
    groups = owners // FACET_ROWS
    own = lax.axis_index("group")
    return [
        offsets_ref[t, lax.rem(own + step, groups) * FACET_ROWS + member]
        for member in range(FACET_ROWS)
        for step in range(groups)
        for t in range(fronts)
    ]


def offsets_on_lanes(offsets, columns):
    lane = iota((1, len(offsets) * columns), 1)
    spread = jnp.zeros_like(lane)
    for place, offset in enumerate(offsets):
        begin = place * columns
        here = (lane >= begin) & (lane < begin + columns)
        spread = jnp.where(here, offset, spread)
    return lane, spread


def place_shifts(offsets, shift_ref, straight_ref, crossed_ref, columns):
    for place, offset in enumerate(offsets):
        residue = offset % CONTRIB
        rows = pl.ds(place * columns, columns)
        straight_ref[rows, :] = jnp.broadcast_to(
            shift_ref[0, pl.ds(residue, 1), :], (columns, LANES)
        )
        crossed_ref[rows, :] = jnp.broadcast_to(
            shift_ref[1, pl.ds(residue, 1), :], (columns, LANES)
        )


def one_hot(shape, targets):
    return jnp.where(iota(shape, 0) == targets, 1.0, 0.0).astype(BF16)


def turned_eighths(values, rotation):
    sign = jnp.where(iota(values[0].shape, 1) < HALF, -rotation, rotation).astype(F32)

    def quarter_turn(value):
        return swap_halves(value) * sign

    def four(a, b, c, d):
        even_sum, even_diff = a + c, a - c
        odd_sum, odd_diff = b + d, quarter_turn(b - d)
        return even_sum + odd_sum, even_diff + odd_diff, even_sum - odd_sum, even_diff - odd_diff

    even = four(*values[0::2])
    odd = four(*values[1::2])
    root = math.sqrt(0.5)
    turned = (
        odd[0],
        (odd[1] + quarter_turn(odd[1])) * root,
        quarter_turn(odd[2]),
        (quarter_turn(odd[3]) - odd[3]) * root,
    )
    return [e + o for e, o in zip(even, turned)] + [e - o for e, o in zip(even, turned)]


def pack_samples(cells_ref, values_ref, weights_ref, flags_ref, out_ref):
    for t in range(cells_ref.shape[0]):
        rows = [
            cells_ref[t, 0:1, :].astype(F32) * SUBGRID + cells_ref[t, 1:2, :].astype(F32),
            weights_ref[t] * flags_ref[t].astype(F32),
            values_ref[t],
        ]
        out_ref[4 * t : 4 * t + 4, :] = jnp.concatenate(rows, axis=0)


def predict_kernel(*refs):
    count = 12
    sources, outs, targets = refs[:count], refs[count : count + 2], refs[count + 2 :]
    copies = [
        pltpu.make_async_copy(sources[i], targets[i], refs[-1].at[i]) for i in range(count)
    ]
    for copy in copies:
        copy.start()
    out_ref, packed_ref = outs
    offsets_ref, shift_ref, strips_ref, window_ref = targets[:4]
    outer_ref, turn_ref, inner_ref, piece_ref = targets[8:count]
    real_ref, imag_ref, straight_ref, crossed_ref = targets[count:-1]
    columns, length = strips_ref.shape[1:]
    groups = length // LANES
    pairs = columns // 2
    blocks = length // CONTRIB
    for copy in copies[:2]:
        copy.wait()
    offsets = place_offsets(offsets_ref)
    place_shifts(offsets, shift_ref, straight_ref, crossed_ref, columns)
    lane, spread = offsets_on_lanes(offsets, columns)
    first_block, residue = spread // CONTRIB, spread % CONTRIB
    base = lane % columns * blocks
    width = lane.shape[1]
    shape = (columns * blocks, width)
    pick_inside = one_hot(shape, base + first_block)
    pick_beyond = one_hot(shape, base + (first_block + 1) % blocks)
    for copy in copies[4:8]:
        copy.wait()
    pack_samples(*targets[4:8], packed_ref)
    copies[2].wait()
    copies[3].wait()
    window = window_ref[...]
    low_half = iota((groups, LANES), 1) < HALF
    sections = []
    for part, held in enumerate((real_ref, imag_ref)):
        for group in range(groups):
            held[group * columns : (group + 1) * columns, :] = strips_ref[
                part, :, group * LANES : (group + 1) * LANES
            ]
        even, odd = [], []
        for pair in range(pairs):
            first = held[pl.ds(2 * pair, groups, stride=columns), :] * window
            second = held[pl.ds(2 * pair + 1, groups, stride=columns), :] * window
            even.append(jnp.where(low_half, first, swap_halves(second)))
            odd.append(jnp.where(low_half, swap_halves(first), second))
        sections += [jnp.concatenate(even, axis=1), jnp.concatenate(odd, axis=1)]
    for copy in copies[8:]:
        copy.wait()
    section = table_times(outer_ref, jnp.concatenate(sections, axis=0))
    turned = []
    for pair in range(pairs):
        lanes = slice(pair * LANES, (pair + 1) * LANES)
        real, imag = section[:CONTRIB, lanes], section[CONTRIB:, lanes]
        turned.append(
            jnp.concatenate(
                [
                    real * turn_ref[0] - imag * turn_ref[1],
                    real * turn_ref[1] + imag * turn_ref[0],
                ],
                axis=1,
            )
        )
    inner = times_table(jnp.concatenate(turned, axis=0), inner_ref)
    spectrum = jnp.concatenate(
        [
            jnp.concatenate(
                [
                    inner[pair * CONTRIB : (pair + 1) * CONTRIB, part * LANES : (part + 1) * LANES]
                    for pair in range(pairs)
                ],
                axis=1,
            )
            for part in range(2)
        ],
        axis=0,
    )
    high, low = split(spectrum)
    inside = dot(high, pick_inside) + dot(low, pick_inside)
    beyond = dot(high, pick_beyond) + dot(low, pick_beyond)
    kappa = iota((2 * CONTRIB, width), 0) % CONTRIB
    cutout = jnp.where(kappa >= residue, inside, beyond)
    piece = times_table(cutout.T, piece_ref)
    out_ref[...] = (piece * straight_ref[...] + swap_halves(piece) * crossed_ref[...]).astype(BF16)


def subgrid_kernel(pieces_ref, turn_ref, model_ref, back_ref, *refs, columns, bands):
    samples_refs, (out_ref, held_ref) = refs[:-2], refs[-2:]
    groups = len(samples_refs)
    fronts, samples = samples_refs[0].shape[0] // 4, samples_refs[0].shape[1]
    own = lax.axis_index("group")
    rows = pieces_ref.shape[0] // FACET_ROWS
    depth = FACET_ROWS * columns
    share = columns // bands
    pieces = pieces_ref[...].astype(F32)
    sky = turned_eighths(
        [pieces[i * rows : (i + 1) * rows, :] for i in range(FACET_ROWS)], -1.0
    )
    sky = [
        value * turn_ref[0, i : i + 1, :] + swap_halves(value) * turn_ref[1, i : i + 1, :]
        for i, value in enumerate(sky)
    ]
    spots = range(groups * fronts)
    stacked = jnp.concatenate(
        [value[spot * columns : (spot + 1) * columns, :] for spot in spots for value in sky],
        axis=0,
    )
    model = times_table(stacked, model_ref)
    grids = []
    for spot in spots:
        step, t = spot // fronts, spot % fronts
        sample = samples_refs[step][4 * t : 4 * t + 4, :]
        cell = sample[0:1, :].astype(jnp.int32)
        row, col = cell // SUBGRID - own * columns, cell % SUBGRID
        inside = (row >= 0) & (row < columns)
        target = jnp.where(inside, col % FACET_ROWS * columns + row, -1)
        pick = one_hot((depth, samples), target)
        high, low = split(model[spot * depth : (spot + 1) * depth, :].T)
        line = dot(high, pick) + dot(low, pick)
        mask = iota((HALF, samples), 0) == col // FACET_ROWS
        highs, lows = [], []
        for part in range(2):
            predicted = jnp.sum(
                jnp.where(mask, line[part * HALF : (part + 1) * HALF, :], 0.0),
                axis=0,
                keepdims=True,
            )
            residual = sample[1:2, :] * (sample[2 + part : 3 + part, :] - predicted)
            high = residual.astype(BF16).astype(F32)
            highs.append(jnp.where(mask, high, 0.0).astype(BF16))
            lows.append(jnp.where(mask, residual - high, 0.0).astype(BF16))
        grids.append(
            dot(pick, jnp.concatenate(highs, axis=0), ((1,), (1,)))
            + dot(pick, jnp.concatenate(lows, axis=0), ((1,), (1,)))
        )
    back = times_table(jnp.concatenate(grids, axis=0), back_ref)
    lines = []
    for i in range(FACET_ROWS):
        value = jnp.concatenate(
            [
                back[spot * depth + i * columns : spot * depth + (i + 1) * columns, :]
                for spot in spots
            ],
            axis=0,
        )
        lines.append(
            value * turn_ref[0, i : i + 1, :] - swap_halves(value) * turn_ref[1, i : i + 1, :]
        )
    lines = turned_eighths(lines, 1.0)
    for i in range(FACET_ROWS):
        for spot in spots:
            for b in range(bands):
                source = spot * columns + b * share
                target = ((b * FACET_ROWS + i) * len(spots) + spot) * share
                held_ref[target : target + share, :] = lines[i][source : source + share, :]
    out_ref[...] = held_ref[...].astype(BF16)


def return_kernel(
    offsets_ref, pieces_ref, window_ref, turn_ref, shift_ref, partial_ref, inner_ref, outer_ref,
    out_ref, straight_ref, crossed_ref, *line_refs, bands,
):
    columns, _, length = out_ref.shape
    blocks = length // CONTRIB
    groups = length // LANES
    pairs = (columns + 1) // 2
    offsets = place_offsets(offsets_ref)
    place_shifts(offsets, shift_ref, straight_ref, crossed_ref, columns)
    width = pieces_ref.shape[0] // bands
    summed = pieces_ref[0:width, :].astype(F32)
    for b in range(1, bands):
        summed += pieces_ref[b * width : (b + 1) * width, :].astype(F32)
    summed = summed * straight_ref[...] - swap_halves(summed) * crossed_ref[...]
    residues = table_times(partial_ref, summed, ((1,), (1,)))
    lane, spread = offsets_on_lanes(offsets, columns)
    first_block, residue = spread // CONTRIB, spread % CONTRIB
    base = lane % columns * blocks
    kappa = iota((2 * CONTRIB, width), 0) % CONTRIB
    inside = kappa >= residue
    both = jnp.concatenate(
        [jnp.where(inside, residues, 0.0), jnp.where(inside, 0.0, residues)], axis=1
    )
    targets = jnp.concatenate(
        [base + first_block, base + (first_block + 1) % blocks], axis=1
    )
    put = one_hot((2 * pairs * blocks, 2 * width), targets)
    high, low = split(both)
    spectrum = dot(high, put, ((1,), (1,))) + dot(low, put, ((1,), (1,)))
    inner = times_table(
        jnp.concatenate(
            [
                jnp.concatenate(
                    [
                        spectrum[:CONTRIB, pair * LANES : (pair + 1) * LANES],
                        spectrum[CONTRIB:, pair * LANES : (pair + 1) * LANES],
                    ],
                    axis=1,
                )
                for pair in range(pairs)
            ],
            axis=0,
        ),
        inner_ref,
    )
    reals, imags = [], []
    for pair in range(pairs):
        rows = slice(pair * CONTRIB, (pair + 1) * CONTRIB)
        real, imag = inner[rows, :LANES], inner[rows, LANES:]
        reals.append(real * turn_ref[0] + imag * turn_ref[1])
        imags.append(imag * turn_ref[0] - real * turn_ref[1])
    lines = table_times(
        outer_ref,
        jnp.concatenate(
            [jnp.concatenate(reals, axis=1), jnp.concatenate(imags, axis=1)], axis=0
        ),
    )
    window = window_ref[...]
    low_half = iota((groups, LANES), 1) < HALF
    for part in range(2):
        for pair in range(pairs):
            lanes = slice(pair * LANES, (pair + 1) * LANES)
            begin = part * blocks
            even = lines[begin : begin + groups, lanes]
            odd = lines[begin + groups : begin + blocks, lanes]
            line_refs[2 * pair][pl.ds(part, groups, stride=2), :] = (
                jnp.where(low_half, even, swap_halves(odd)) * window
            )
            if 2 * pair + 1 < columns:
                line_refs[2 * pair + 1][pl.ds(part, groups, stride=2), :] = (
                    jnp.where(low_half, swap_halves(even), odd) * window
                )
    for column in range(columns):
        for group in range(groups):
            out_ref[column, :, group * LANES : (group + 1) * LANES] = line_refs[column][
                2 * group : 2 * group + 2, :
            ]


def kernel_call(kernel, name, out_shape, spaces, scratch, *operands):
    return pl.pallas_call(
        kernel,
        out_shape=out_shape,
        in_specs=[pl.BlockSpec(memory_space=space) for space in spaces],
        out_specs=jax.tree.map(lambda _: pl.BlockSpec(memory_space=pltpu.VMEM), out_shape),
        scratch_shapes=scratch,
        compiler_params=pltpu.CompilerParams(vmem_limit_bytes=VMEM_LIMIT),
        name=name,
    )(*operands)


def wide(rows):
    return pltpu.VMEM((rows, LANES), F32)


def local(groups, bands, strips, offsets, cells, values, weights, flags):
    columns, length = strips.shape[-2:]
    fronts = offsets.shape[0]
    share = columns // bands
    made = {key: jnp.asarray(value) for key, value in tables(length).items()}
    facets = groups * FACET_ROWS
    rows = facets * fronts * columns
    held = length // LANES * columns
    fetched = [
        offsets, made["shift"], strips[0, 0], made["window"],
        cells[0, :, 0], values[0, :, 0], weights[0], flags[0],
        made["outer_minus"], made["turn"], made["inner_minus"], made["piece"],
    ]
    landing = [pltpu.VMEM(array.shape, array.dtype) for array in fetched]
    landing[0] = pltpu.SMEM(offsets.shape, offsets.dtype)
    pieces, packed = kernel_call(
        predict_kernel, "predict",
        [
            jax.ShapeDtypeStruct((rows, LANES), BF16),
            jax.ShapeDtypeStruct((4 * fronts, cells.shape[-1]), F32),
        ],
        [pltpu.HBM] * len(fetched),
        landing
        + [wide(held)] * 2
        + [wide(rows)] * 2
        + [pltpu.SemaphoreType.DMA((len(fetched),))],
        *[pltpu.with_memory_space_constraint(array, pltpu.HBM) for array in fetched],
    )
    gathered = [packed]
    for step in range(1, groups):
        moves = [((group + step) % groups, group) for group in range(groups)]
        gathered.append(lax.ppermute(packed, "group", moves))
    arrived = lax.all_to_all(pieces, "member", split_axis=0, concat_axis=0, tiled=True)
    returned = kernel_call(
        functools.partial(subgrid_kernel, columns=columns, bands=bands), "subgrid",
        jax.ShapeDtypeStruct((rows, LANES), BF16), [pltpu.VMEM] * (4 + len(gathered)),
        [wide(rows)],
        arrived, made["grid_turn"], made["model"], made["back"], *gathered,
    )
    delivered = lax.all_to_all(
        returned, ("band", "member"), split_axis=0, concat_axis=0, tiled=True
    )
    width = facets * fronts * share
    lines = kernel_call(
        functools.partial(return_kernel, bands=bands), "lines",
        jax.ShapeDtypeStruct((share, 2, length), F32), [pltpu.SMEM] + [pltpu.VMEM] * 7,
        [wide(width)] * 2 + [wide(2 * length // LANES)] * share,
        offsets, delivered, made["window"], made["turn"], made["shift"],
        made["partial"], made["inner_plus"], made["outer_plus"],
    )
    return lines[None]


def solution(mesh):
    bands = mesh.shape["band"]
    groups = mesh.shape["facet"] // FACET_ROWS
    split_mesh = Mesh(
        mesh.devices.reshape(groups, FACET_ROWS, bands), ("group", "member", "band")
    )
    facet = ("group", "member")
    placed = (
        P("band", facet, None, None, None),
        P(),
        P("band", None, facet, None, None),
        P("band", None, facet, None, None),
        P("band", None, facet, None),
        P("band", None, facet, None),
    )
    return jax.shard_map(
        functools.partial(local, groups, bands),
        mesh=split_mesh,
        in_specs=placed,
        out_specs=P(facet, "band", None, None),
        check_vma=False,
    )
```

```python
import functools
import math

import jax
import jax.numpy as jnp
import ml_dtypes
import numpy as np
from jax import lax
from jax.experimental import pallas as pl
from jax.experimental.pallas import tpu as pltpu
from jax.sharding import Mesh
from jax.sharding import PartitionSpec as P

CONTRIB = 64
FACET_ROWS = 8
SUBGRID = FACET_ROWS * CONTRIB
LANES = 128
HALF = LANES // 2
VMEM_LIMIT = 48 * 1024 * 1024
F32 = jnp.float32
BF16 = jnp.bfloat16


def phases(rows, cols, length, rotation):
    product = np.outer(rows, cols) % length
    return np.exp(rotation * 2j * np.pi * product / length)


def from_left(matrix):
    return np.block([[matrix.real, -matrix.imag], [matrix.imag, matrix.real]])


def from_right(matrix):
    return np.block([[matrix.real, matrix.imag], [-matrix.imag, matrix.real]])


def high_low(table):
    high = table.astype(ml_dtypes.bfloat16)
    low = (table - high.astype(np.float64)).astype(ml_dtypes.bfloat16)
    return np.stack([high, low])


def side_by_side(values):
    straight = np.concatenate([values.real, values.real], axis=-1)
    crossed = np.concatenate([-values.imag, values.imag], axis=-1)
    return np.stack([straight, crossed])


def stack_tables(named):
    places, blocks, begin = {}, [], 0
    for name, table in named.items():
        count = table.shape[1] // LANES
        places[name] = (begin, table.shape[0], count)
        blocks += [table[:, i * LANES : (i + 1) * LANES] for i in range(count)]
        begin += table.shape[0] * count
    return np.concatenate(blocks, axis=0), places


def stack_pairs(named):
    return stack_tables(
        {(name, i): table for name, pair in named.items() for i, table in enumerate(pair)}
    )


def tables(length):
    blocks = length // CONTRIB
    short = np.arange(CONTRIB)
    outer = np.concatenate([np.arange(0, blocks, 2), np.arange(1, blocks, 2)])
    window = 1.0 + 0.5 * np.cos(np.arange(length) * (2.0 * math.pi / length))
    window = (window * length**-0.5).reshape(length // LANES, LANES).astype(np.float32)
    turn = np.tile(phases(short, short, length, -1), (1, 2))
    turn = np.stack([turn.real, turn.imag]).astype(np.float32)
    pair = np.eye(2)
    shift = high_low(np.concatenate(side_by_side(phases(short, short, CONTRIB, -1)), axis=1))
    outer_minus = from_left(phases(short, outer, blocks, -1))
    inner_minus = from_right(np.kron(pair, phases(short, short, CONTRIB, -1)))
    piece = from_right(phases(short, short, CONTRIB, 1)) * CONTRIB**-0.5
    return dict(
        plain=stack_tables(dict(window=window, real=turn[0], imag=turn[1])),
        paired=stack_pairs(
            dict(
                shift=shift,
                outer=high_low(outer_minus),
                inner=high_low(inner_minus),
                piece=high_low(piece),
            )
        ),
        window=window,
        turn=turn,
        shift=shift,
        inner_plus=high_low(from_right(np.kron(pair, phases(short, short, CONTRIB, 1)))),
        outer_plus=high_low(from_left(phases(outer, short, blocks, 1))),
        partial=high_low(from_right(phases(short, short, CONTRIB, -1)).T * CONTRIB**-0.5),
        grid_turn=side_by_side(phases(np.arange(FACET_ROWS), short, SUBGRID, -1)).astype(
            np.float32
        ),
        model=high_low(from_right(phases(short, short, CONTRIB, -1)) * SUBGRID**-0.5),
        back=high_low(from_right(phases(short, short, CONTRIB, 1)) * SUBGRID**-0.5),
    )


def split(values):
    high = values.astype(BF16)
    return high, (values - high.astype(F32)).astype(BF16)


def dot(left, right, dims=((1,), (0,))):
    return lax.dot_general(left, right, (dims, ((), ())), preferred_element_type=F32)


def times_table(values, table, dims=((1,), (0,))):
    high, low = split(values)
    return dot(high, table[0], dims) + dot(low, table[0], dims) + dot(high, table[1], dims)


def table_times(table, values, dims=((1,), (0,))):
    high, low = split(values)
    return dot(table[0], high, dims) + dot(table[0], low, dims) + dot(table[1], high, dims)


def iota(shape, dimension):
    return lax.broadcasted_iota(jnp.int32, shape, dimension)


def swap_halves(values):
    return pltpu.roll(values, HALF, 1)


def table_at(ref, place):
    begin, rows, blocks = place
    parts = [ref[begin + i * rows : begin + (i + 1) * rows, :] for i in range(blocks)]
    return parts[0] if blocks == 1 else jnp.concatenate(parts, axis=1)


def offsets_on_lanes(offsets_ref, columns):
    fronts, owners = offsets_ref.shape
    groups = owners // FACET_ROWS
    own = lax.axis_index("group")
    begins = []
    for step in range(groups):
        group = own + step
        begins.append(jnp.where(group >= groups, group - groups, group) * FACET_ROWS)
    spread = iota((1, fronts * owners * columns), 1)
    place_of = spread // columns
    for place in range(fronts * owners):
        t, step, member = place % fronts, place // fronts % groups, place // (fronts * groups)
        spread = jnp.where(place_of == place, offsets_ref[t, begins[step] + member], spread)
    return spread


def shift_rows(residue, table):
    pick = jnp.where(iota((CONTRIB, residue.shape[1]), 0) == residue, 1.0, 0.0).T.astype(BF16)
    rows = dot(pick, table[0]) + dot(pick, table[1])
    return rows[:, :LANES], rows[:, LANES:]


def one_hot(shape, targets):
    return jnp.where(iota(shape, 0) == targets, 1.0, 0.0).astype(BF16)


def turned_eighths(values, rotation):
    sign = jnp.where(iota(values[0].shape, 1) < HALF, -rotation, rotation).astype(F32)

    def quarter_turn(value):
        return swap_halves(value) * sign

    def four(a, b, c, d):
        even_sum, even_diff = a + c, a - c
        odd_sum, odd_diff = b + d, quarter_turn(b - d)
        return even_sum + odd_sum, even_diff + odd_diff, even_sum - odd_sum, even_diff - odd_diff

    even = four(*values[0::2])
    odd = four(*values[1::2])
    root = math.sqrt(0.5)
    turned = (
        odd[0],
        (odd[1] + quarter_turn(odd[1])) * root,
        quarter_turn(odd[2]),
        (quarter_turn(odd[3]) - odd[3]) * root,
    )
    return [e + o for e, o in zip(even, turned)] + [e - o for e, o in zip(even, turned)]


def pack_samples(cells_ref, values_ref, weights_ref, flags_ref, out_ref):
    for t in range(cells_ref.shape[0]):
        rows = [
            cells_ref[t, 0:1, :].astype(F32) * SUBGRID + cells_ref[t, 1:2, :].astype(F32),
            weights_ref[t] * flags_ref[t].astype(F32),
            values_ref[t],
        ]
        out_ref[4 * t : 4 * t + 4, :] = jnp.concatenate(rows, axis=0)


def start_all(sources, targets, semaphores):
    copies = [
        pltpu.make_async_copy(source, target, semaphores.at[i])
        for i, (source, target) in enumerate(zip(sources, targets))
    ]
    for copy in copies:
        copy.start()
    return copies


def predict(spread, copies, strips_ref, plain_ref, paired_ref, held_refs, out_ref, plain, paired):
    columns, length = strips_ref.shape[1:]
    groups = length // LANES
    pairs = columns // 2
    blocks = length // CONTRIB
    width = spread.shape[1]
    first_block, residue = spread // CONTRIB, spread % CONTRIB
    base = iota(spread.shape, 1) % columns * blocks
    shape = (columns * blocks, width)
    pick_inside = one_hot(shape, base + first_block)
    pick_beyond = one_hot(shape, base + (first_block + 1) % blocks)
    for copy in copies:
        copy.wait()

    def pair_at(name):
        return [table_at(paired_ref, paired[name, i]) for i in range(2)]

    window = table_at(plain_ref, plain["window"])
    turn_real, turn_imag = table_at(plain_ref, plain["real"]), table_at(plain_ref, plain["imag"])
    low_half = iota((groups, LANES), 1) < HALF
    sections = []
    for part, held in enumerate(held_refs):
        for group in range(groups):
            held[group * columns : (group + 1) * columns, :] = strips_ref[
                part, :, group * LANES : (group + 1) * LANES
            ]
        even, odd = [], []
        for pair in range(pairs):
            first = held[pl.ds(2 * pair, groups, stride=columns), :] * window
            second = held[pl.ds(2 * pair + 1, groups, stride=columns), :] * window
            even.append(jnp.where(low_half, first, swap_halves(second)))
            odd.append(jnp.where(low_half, swap_halves(first), second))
        sections += [jnp.concatenate(even, axis=1), jnp.concatenate(odd, axis=1)]
    section = table_times(pair_at("outer"), jnp.concatenate(sections, axis=0))
    turned = []
    for pair in range(pairs):
        lanes = slice(pair * LANES, (pair + 1) * LANES)
        real, imag = section[:CONTRIB, lanes], section[CONTRIB:, lanes]
        turned.append(
            jnp.concatenate(
                [real * turn_real - imag * turn_imag, real * turn_imag + imag * turn_real],
                axis=1,
            )
        )
    inner = times_table(jnp.concatenate(turned, axis=0), pair_at("inner"))
    spectrum = jnp.concatenate(
        [
            jnp.concatenate(
                [
                    inner[pair * CONTRIB : (pair + 1) * CONTRIB, part * LANES : (part + 1) * LANES]
                    for pair in range(pairs)
                ],
                axis=1,
            )
            for part in range(2)
        ],
        axis=0,
    )
    high, low = split(spectrum)
    inside = dot(high, pick_inside) + dot(low, pick_inside)
    beyond = dot(high, pick_beyond) + dot(low, pick_beyond)
    kappa = iota((2 * CONTRIB, width), 0) % CONTRIB
    cutout = jnp.where(kappa >= residue, inside, beyond)
    piece = times_table(cutout.T, pair_at("piece"))
    straight, crossed = shift_rows(residue, pair_at("shift"))
    out_ref[...] = (piece * straight + swap_halves(piece) * crossed).astype(BF16)


def in_first_half():
    return 2 * lax.axis_index("group") < lax.axis_size("group")


def early_kernel(
    offsets, cells, values, weights, flags, strips, plain_table, paired_table,
    out_ref, packed_ref, places_ref,
    offsets_ref, cells_ref, values_ref, weights_ref, flags_ref, strips_ref, plain_ref, paired_ref,
    real_ref, imag_ref, small_semaphores, semaphores, *, plain, paired, share,
):
    columns = strips_ref.shape[1]
    small = start_all(
        (offsets, cells, values, weights, flags),
        (offsets_ref, cells_ref, values_ref, weights_ref, flags_ref),
        small_semaphores,
    )

    def large():
        sources, targets = (strips, plain_table, paired_table), (strips_ref, plain_ref, paired_ref)
        return [
            pltpu.make_async_copy(source, target, semaphores.at[i])
            for i, (source, target) in enumerate(zip(sources, targets))
        ]

    @pl.when(in_first_half())
    def _():
        for copy in large():
            copy.start()

    for copy in small:
        copy.wait()
    for t in range(cells_ref.shape[0]):
        rows = [
            cells_ref[t, 0:1, :].astype(F32) * SUBGRID + cells_ref[t, 1:2, :].astype(F32),
            weights_ref[t] * flags_ref[t].astype(F32),
            values_ref[t],
        ]
        packed_ref[4 * t : 4 * t + 4, :] = jnp.concatenate(rows, axis=0)
    places_ref[...] = offsets_on_lanes(offsets_ref, share)

    @pl.when(in_first_half())
    def _():
        spread = offsets_on_lanes(offsets_ref, columns)
        predict(
            spread, large(), strips_ref, plain_ref, paired_ref, (real_ref, imag_ref), out_ref,
            plain, paired,
        )


def late_kernel(
    early_ref, offsets, strips, plain_table, paired_table, out_ref,
    offsets_ref, strips_ref, plain_ref, paired_ref, real_ref, imag_ref, semaphores,
    *, plain, paired,
):
    @pl.when(in_first_half())
    def _():
        out_ref[...] = early_ref[...]

    @pl.when(jnp.logical_not(in_first_half()))
    def _():
        copies = start_all(
            (offsets, strips, plain_table, paired_table),
            (offsets_ref, strips_ref, plain_ref, paired_ref),
            semaphores,
        )
        copies[0].wait()
        spread = offsets_on_lanes(offsets_ref, strips_ref.shape[1])
        predict(
            spread, copies[1:], strips_ref, plain_ref, paired_ref, (real_ref, imag_ref), out_ref,
            plain, paired,
        )


def subgrid_kernel(pieces_ref, turn_ref, model_ref, back_ref, *refs, columns, bands):
    samples_refs, (out_ref, held_ref) = refs[:-2], refs[-2:]
    groups = len(samples_refs)
    fronts, samples = samples_refs[0].shape[0] // 4, samples_refs[0].shape[1]
    own = lax.axis_index("group")
    rows = pieces_ref.shape[0] // FACET_ROWS
    depth = FACET_ROWS * columns
    share = columns // bands
    pieces = pieces_ref[...].astype(F32)
    sky = turned_eighths(
        [pieces[i * rows : (i + 1) * rows, :] for i in range(FACET_ROWS)], -1.0
    )
    sky = [
        value * turn_ref[0, i : i + 1, :] + swap_halves(value) * turn_ref[1, i : i + 1, :]
        for i, value in enumerate(sky)
    ]
    spots = range(groups * fronts)
    stacked = jnp.concatenate(
        [value[spot * columns : (spot + 1) * columns, :] for spot in spots for value in sky],
        axis=0,
    )
    model = times_table(stacked, model_ref)
    grids = []
    for spot in spots:
        step, t = spot // fronts, spot % fronts
        sample = samples_refs[step][4 * t : 4 * t + 4, :]
        cell = sample[0:1, :].astype(jnp.int32)
        row, col = cell // SUBGRID - own * columns, cell % SUBGRID
        inside = (row >= 0) & (row < columns)
        target = jnp.where(inside, col % FACET_ROWS * columns + row, -1)
        pick = one_hot((depth, samples), target)
        high, low = split(model[spot * depth : (spot + 1) * depth, :].T)
        line = dot(high, pick) + dot(low, pick)
        mask = iota((HALF, samples), 0) == col // FACET_ROWS
        highs, lows = [], []
        for part in range(2):
            predicted = jnp.sum(
                jnp.where(mask, line[part * HALF : (part + 1) * HALF, :], 0.0),
                axis=0,
                keepdims=True,
            )
            residual = sample[1:2, :] * (sample[2 + part : 3 + part, :] - predicted)
            high = residual.astype(BF16).astype(F32)
            highs.append(jnp.where(mask, high, 0.0).astype(BF16))
            lows.append(jnp.where(mask, residual - high, 0.0).astype(BF16))
        grids.append(
            dot(pick, jnp.concatenate(highs, axis=0), ((1,), (1,)))
            + dot(pick, jnp.concatenate(lows, axis=0), ((1,), (1,)))
        )
    back = times_table(jnp.concatenate(grids, axis=0), back_ref)
    lines = []
    for i in range(FACET_ROWS):
        value = jnp.concatenate(
            [
                back[spot * depth + i * columns : spot * depth + (i + 1) * columns, :]
                for spot in spots
            ],
            axis=0,
        )
        lines.append(
            value * turn_ref[0, i : i + 1, :] - swap_halves(value) * turn_ref[1, i : i + 1, :]
        )
    lines = turned_eighths(lines, 1.0)
    for i in range(FACET_ROWS):
        for spot in spots:
            for b in range(bands):
                source = spot * columns + b * share
                target = ((b * FACET_ROWS + i) * len(spots) + spot) * share
                held_ref[target : target + share, :] = lines[i][source : source + share, :]
    out_ref[...] = held_ref[...].astype(BF16)


def return_kernel(
    places_ref, pieces_ref, window_ref, turn_ref, shift_ref, partial_ref, inner_ref, outer_ref,
    out_ref, *line_refs, bands,
):
    columns, _, length = out_ref.shape
    blocks = length // CONTRIB
    groups = length // LANES
    pairs = (columns + 1) // 2
    spread = places_ref[...]
    first_block, residue = spread // CONTRIB, spread % CONTRIB
    straight, crossed = shift_rows(residue, shift_ref)
    width = pieces_ref.shape[0] // bands
    summed = pieces_ref[0:width, :].astype(F32)
    for b in range(1, bands):
        summed += pieces_ref[b * width : (b + 1) * width, :].astype(F32)
    summed = summed * straight - swap_halves(summed) * crossed
    residues = table_times(partial_ref, summed, ((1,), (1,)))
    base = iota(spread.shape, 1) % columns * blocks
    kappa = iota((2 * CONTRIB, width), 0) % CONTRIB
    inside = kappa >= residue
    both = jnp.concatenate(
        [jnp.where(inside, residues, 0.0), jnp.where(inside, 0.0, residues)], axis=1
    )
    targets = jnp.concatenate(
        [base + first_block, base + (first_block + 1) % blocks], axis=1
    )
    put = one_hot((2 * pairs * blocks, 2 * width), targets)
    high, low = split(both)
    spectrum = dot(high, put, ((1,), (1,))) + dot(low, put, ((1,), (1,)))
    inner = times_table(
        jnp.concatenate(
            [
                jnp.concatenate(
                    [
                        spectrum[:CONTRIB, pair * LANES : (pair + 1) * LANES],
                        spectrum[CONTRIB:, pair * LANES : (pair + 1) * LANES],
                    ],
                    axis=1,
                )
                for pair in range(pairs)
            ],
            axis=0,
        ),
        inner_ref,
    )
    reals, imags = [], []
    for pair in range(pairs):
        rows = slice(pair * CONTRIB, (pair + 1) * CONTRIB)
        real, imag = inner[rows, :LANES], inner[rows, LANES:]
        reals.append(real * turn_ref[0] + imag * turn_ref[1])
        imags.append(imag * turn_ref[0] - real * turn_ref[1])
    lines = table_times(
        outer_ref,
        jnp.concatenate(
            [jnp.concatenate(reals, axis=1), jnp.concatenate(imags, axis=1)], axis=0
        ),
    )
    window = window_ref[...]
    low_half = iota((groups, LANES), 1) < HALF
    for part in range(2):
        for pair in range(pairs):
            lanes = slice(pair * LANES, (pair + 1) * LANES)
            begin = part * blocks
            even = lines[begin : begin + groups, lanes]
            odd = lines[begin + groups : begin + blocks, lanes]
            line_refs[2 * pair][pl.ds(part, groups, stride=2), :] = (
                jnp.where(low_half, even, swap_halves(odd)) * window
            )
            if 2 * pair + 1 < columns:
                line_refs[2 * pair + 1][pl.ds(part, groups, stride=2), :] = (
                    jnp.where(low_half, swap_halves(even), odd) * window
                )
    for column in range(columns):
        for group in range(groups):
            out_ref[column, :, group * LANES : (group + 1) * LANES] = line_refs[column][
                2 * group : 2 * group + 2, :
            ]


def kernel_call(kernel, name, out_shape, spaces, scratch, *operands):
    return pl.pallas_call(
        kernel,
        out_shape=out_shape,
        in_specs=[pl.BlockSpec(memory_space=space) for space in spaces],
        out_specs=jax.tree.map(lambda _: pl.BlockSpec(memory_space=pltpu.VMEM), out_shape),
        scratch_shapes=scratch,
        compiler_params=pltpu.CompilerParams(vmem_limit_bytes=VMEM_LIMIT),
        name=name,
    )(*operands)


def wide(rows):
    return pltpu.VMEM((rows, LANES), F32)


def local(groups, bands, strips, offsets, cells, values, weights, flags):
    columns, length = strips.shape[-2:]
    fronts = offsets.shape[0]
    share = columns // bands
    facets = groups * FACET_ROWS
    rows = facets * fronts * columns
    width = facets * fronts * share
    made = tables(length)
    plain, plain_places = made.pop("plain")
    paired, paired_places = made.pop("paired")
    made = {key: jnp.asarray(value) for key, value in made.items()}
    held = length // LANES * columns
    small = [offsets, cells[0, :, 0], values[0, :, 0], weights[0], flags[0]]
    large = [strips[0, 0], jnp.asarray(plain), jnp.asarray(paired)]

    def landing(arrays):
        return [
            (pltpu.SMEM if array is offsets else pltpu.VMEM)(array.shape, array.dtype)
            for array in arrays
        ]

    def in_hbm(arrays):
        return [pltpu.with_memory_space_constraint(array, pltpu.HBM) for array in arrays]

    def semaphores(count):
        return pltpu.SemaphoreType.DMA((count,))

    early, packed, places = kernel_call(
        functools.partial(early_kernel, plain=plain_places, paired=paired_places, share=share),
        "early",
        [
            jax.ShapeDtypeStruct((rows, LANES), BF16),
            jax.ShapeDtypeStruct((4 * fronts, cells.shape[-1]), F32),
            jax.ShapeDtypeStruct((1, width), jnp.int32),
        ],
        [pltpu.HBM] * 8,
        landing(small + large) + [wide(held)] * 2 + [semaphores(5), semaphores(3)],
        *in_hbm(small + large),
    )
    pieces = kernel_call(
        functools.partial(late_kernel, plain=plain_places, paired=paired_places), "late",
        jax.ShapeDtypeStruct((rows, LANES), BF16), [pltpu.VMEM] + [pltpu.HBM] * 4,
        landing([offsets] + large) + [wide(held)] * 2 + [semaphores(4)],
        early, *in_hbm([offsets] + large),
    )
    gathered = [packed]
    for step in range(1, groups):
        moves = [((group + step) % groups, group) for group in range(groups)]
        gathered.append(lax.ppermute(packed, "group", moves))
    arrived = lax.all_to_all(pieces, "member", split_axis=0, concat_axis=0, tiled=True)
    returned = kernel_call(
        functools.partial(subgrid_kernel, columns=columns, bands=bands), "subgrid",
        jax.ShapeDtypeStruct((rows, LANES), BF16), [pltpu.VMEM] * (4 + len(gathered)),
        [wide(rows)],
        arrived, made["grid_turn"], made["model"], made["back"], *gathered,
    )
    delivered = lax.all_to_all(
        returned, ("band", "member"), split_axis=0, concat_axis=0, tiled=True
    )
    lines = kernel_call(
        functools.partial(return_kernel, bands=bands), "lines",
        jax.ShapeDtypeStruct((share, 2, length), F32), [pltpu.VMEM] * 8,
        [wide(2 * length // LANES)] * share,
        places, delivered, made["window"], made["turn"], made["shift"],
        made["partial"], made["inner_plus"], made["outer_plus"],
    )
    return lines[None]


def solution(mesh):
    bands = mesh.shape["band"]
    groups = mesh.shape["facet"] // FACET_ROWS
    split_mesh = Mesh(
        mesh.devices.reshape(groups, FACET_ROWS, bands), ("group", "member", "band")
    )
    facet = ("group", "member")
    placed = (
        P("band", facet, None, None, None),
        P(),
        P("band", None, facet, None, None),
        P("band", None, facet, None, None),
        P("band", None, facet, None),
        P("band", None, facet, None),
    )
    return jax.shard_map(
        functools.partial(local, groups, bands),
        mesh=split_mesh,
        in_specs=placed,
        out_specs=P(facet, "band", None, None),
        check_vma=False,
    )
```

```python
import functools
import math

import jax
import jax.numpy as jnp
import ml_dtypes
import numpy as np
from jax import lax
from jax.experimental import pallas as pl
from jax.experimental.pallas import tpu as pltpu
from jax.sharding import Mesh
from jax.sharding import PartitionSpec as P

CONTRIB = 64
FACET_ROWS = 8
SUBGRID = FACET_ROWS * CONTRIB
LANES = 128
HALF = LANES // 2
LATE_FLOPS = 10**10
PREPARE_FLOPS = 2 * 10**10
VMEM_LIMIT = 48 * 1024 * 1024
F32 = jnp.float32
BF16 = jnp.bfloat16


def phases(rows, cols, length, rotation):
    product = np.outer(rows, cols) % length
    return np.exp(rotation * 2j * np.pi * product / length)


def from_left(matrix):
    return np.block([[matrix.real, -matrix.imag], [matrix.imag, matrix.real]])


def from_right(matrix):
    return np.block([[matrix.real, matrix.imag], [-matrix.imag, matrix.real]])


def high_low(table):
    high = table.astype(ml_dtypes.bfloat16)
    low = (table - high.astype(np.float64)).astype(ml_dtypes.bfloat16)
    return np.stack([high, low])


def side_by_side(values):
    straight = np.concatenate([values.real, values.real], axis=-1)
    crossed = np.concatenate([-values.imag, values.imag], axis=-1)
    return np.stack([straight, crossed])


def stack_tables(named):
    places, blocks, begin = {}, [], 0
    for name, table in named.items():
        count = table.shape[1] // LANES
        places[name] = (begin, table.shape[0], count)
        blocks += [table[:, i * LANES : (i + 1) * LANES] for i in range(count)]
        begin += table.shape[0] * count
    return np.concatenate(blocks, axis=0), places


def stack_pairs(named):
    return stack_tables(
        {(name, i): table for name, pair in named.items() for i, table in enumerate(pair)}
    )


def tables(length):
    blocks = length // CONTRIB
    short = np.arange(CONTRIB)
    outer = np.concatenate([np.arange(0, blocks, 2), np.arange(1, blocks, 2)])
    window = 1.0 + 0.5 * np.cos(np.arange(length) * (2.0 * math.pi / length))
    window = (window * length**-0.5).reshape(length // LANES, LANES).astype(np.float32)
    turn = np.tile(phases(short, short, length, -1), (1, 2))
    turn = np.stack([turn.real, turn.imag]).astype(np.float32)
    pair = np.eye(2)
    shift = high_low(np.concatenate(side_by_side(phases(short, short, CONTRIB, -1)), axis=1))
    outer_minus = from_left(phases(short, outer, blocks, -1))
    inner_minus = from_right(np.kron(pair, phases(short, short, CONTRIB, -1)))
    piece = from_right(phases(short, short, CONTRIB, 1)) * CONTRIB**-0.5
    return dict(
        plain=stack_tables(dict(window=window, real=turn[0], imag=turn[1])),
        paired=stack_pairs(
            dict(
                shift=shift,
                outer=high_low(outer_minus),
                inner=high_low(inner_minus),
                piece=high_low(piece),
            )
        ),
        window=window,
        turn=turn,
        shift=shift,
        inner_plus=high_low(from_right(np.kron(pair, phases(short, short, CONTRIB, 1)))),
        outer_plus=high_low(from_left(phases(outer, short, blocks, 1))),
        partial=high_low(from_right(phases(short, short, CONTRIB, -1)).T * CONTRIB**-0.5),
        grid_turn=side_by_side(phases(np.arange(FACET_ROWS), short, SUBGRID, -1)).astype(
            np.float32
        ),
        model=high_low(from_right(phases(short, short, CONTRIB, -1)) * SUBGRID**-0.5),
        back=high_low(from_right(phases(short, short, CONTRIB, 1)) * SUBGRID**-0.5),
    )


def split(values):
    high = values.astype(BF16)
    return high, (values - high.astype(F32)).astype(BF16)


def dot(left, right, dims=((1,), (0,))):
    return lax.dot_general(left, right, (dims, ((), ())), preferred_element_type=F32)


def times_table(values, table, dims=((1,), (0,))):
    high, low = split(values)
    return dot(high, table[0], dims) + dot(low, table[0], dims) + dot(high, table[1], dims)


def table_times(table, values, dims=((1,), (0,))):
    high, low = split(values)
    return dot(table[0], high, dims) + dot(table[0], low, dims) + dot(table[1], high, dims)


def iota(shape, dimension):
    return lax.broadcasted_iota(jnp.int32, shape, dimension)


def swap_halves(values):
    return pltpu.roll(values, HALF, 1)


def table_at(ref, place):
    begin, rows, blocks = place
    parts = [ref[begin + i * rows : begin + (i + 1) * rows, :] for i in range(blocks)]
    return parts[0] if blocks == 1 else jnp.concatenate(parts, axis=1)


def offsets_on_lanes(offsets_ref, columns):
    fronts, owners = offsets_ref.shape
    groups = owners // FACET_ROWS
    own = lax.axis_index("group")
    begins = []
    for step in range(groups):
        group = own + step
        begins.append(jnp.where(group >= groups, group - groups, group) * FACET_ROWS)
    spread = iota((1, fronts * owners * columns), 1)
    place_of = spread // columns
    for place in range(fronts * owners):
        t, step, member = place % fronts, place // fronts % groups, place // (fronts * groups)
        spread = jnp.where(place_of == place, offsets_ref[t, begins[step] + member], spread)
    return spread


def shift_rows(residue, table):
    pick = jnp.where(iota((CONTRIB, residue.shape[1]), 0) == residue, 1.0, 0.0).T.astype(BF16)
    rows = dot(pick, table[0]) + dot(pick, table[1])
    return rows[:, :LANES], rows[:, LANES:]


def one_hot(shape, targets):
    return jnp.where(iota(shape, 0) == targets, 1.0, 0.0).astype(BF16)


def turned_eighths(values, rotation):
    sign = jnp.where(iota(values[0].shape, 1) < HALF, -rotation, rotation).astype(F32)

    def quarter_turn(value):
        return swap_halves(value) * sign

    def four(a, b, c, d):
        even_sum, even_diff = a + c, a - c
        odd_sum, odd_diff = b + d, quarter_turn(b - d)
        return even_sum + odd_sum, even_diff + odd_diff, even_sum - odd_sum, even_diff - odd_diff

    even = four(*values[0::2])
    odd = four(*values[1::2])
    root = math.sqrt(0.5)
    turned = (
        odd[0],
        (odd[1] + quarter_turn(odd[1])) * root,
        quarter_turn(odd[2]),
        (quarter_turn(odd[3]) - odd[3]) * root,
    )
    return [e + o for e, o in zip(even, turned)] + [e - o for e, o in zip(even, turned)]


def pack_samples(cells_ref, values_ref, weights_ref, flags_ref, out_ref):
    for t in range(cells_ref.shape[0]):
        rows = [
            cells_ref[t, 0:1, :].astype(F32) * SUBGRID + cells_ref[t, 1:2, :].astype(F32),
            weights_ref[t] * flags_ref[t].astype(F32),
            values_ref[t],
        ]
        out_ref[4 * t : 4 * t + 4, :] = jnp.concatenate(rows, axis=0)


def start_all(sources, targets, semaphores):
    copies = [
        pltpu.make_async_copy(source, target, semaphores.at[i])
        for i, (source, target) in enumerate(zip(sources, targets))
    ]
    for copy in copies:
        copy.start()
    return copies


def predict(spread, copies, strips_ref, plain_ref, paired_ref, held_refs, out_ref, plain, paired):
    columns, length = strips_ref.shape[1:]
    groups = length // LANES
    pairs = columns // 2
    blocks = length // CONTRIB
    width = spread.shape[1]
    first_block, residue = spread // CONTRIB, spread % CONTRIB
    base = iota(spread.shape, 1) % columns * blocks
    shape = (columns * blocks, width)
    pick_inside = one_hot(shape, base + first_block)
    pick_beyond = one_hot(shape, base + (first_block + 1) % blocks)
    for copy in copies:
        copy.wait()

    def pair_at(name):
        return [table_at(paired_ref, paired[name, i]) for i in range(2)]

    window = table_at(plain_ref, plain["window"])
    turn_real, turn_imag = table_at(plain_ref, plain["real"]), table_at(plain_ref, plain["imag"])
    low_half = iota((groups, LANES), 1) < HALF
    sections = []
    for part, held in enumerate(held_refs):
        for group in range(groups):
            held[group * columns : (group + 1) * columns, :] = strips_ref[
                part, :, group * LANES : (group + 1) * LANES
            ]
        even, odd = [], []
        for pair in range(pairs):
            first = held[pl.ds(2 * pair, groups, stride=columns), :] * window
            second = held[pl.ds(2 * pair + 1, groups, stride=columns), :] * window
            even.append(jnp.where(low_half, first, swap_halves(second)))
            odd.append(jnp.where(low_half, swap_halves(first), second))
        sections += [jnp.concatenate(even, axis=1), jnp.concatenate(odd, axis=1)]
    section = table_times(pair_at("outer"), jnp.concatenate(sections, axis=0))
    turned = []
    for pair in range(pairs):
        lanes = slice(pair * LANES, (pair + 1) * LANES)
        real, imag = section[:CONTRIB, lanes], section[CONTRIB:, lanes]
        turned.append(
            jnp.concatenate(
                [real * turn_real - imag * turn_imag, real * turn_imag + imag * turn_real],
                axis=1,
            )
        )
    inner = times_table(jnp.concatenate(turned, axis=0), pair_at("inner"))
    spectrum = jnp.concatenate(
        [
            jnp.concatenate(
                [
                    inner[pair * CONTRIB : (pair + 1) * CONTRIB, part * LANES : (part + 1) * LANES]
                    for pair in range(pairs)
                ],
                axis=1,
            )
            for part in range(2)
        ],
        axis=0,
    )
    high, low = split(spectrum)
    inside = dot(high, pick_inside) + dot(low, pick_inside)
    beyond = dot(high, pick_beyond) + dot(low, pick_beyond)
    kappa = iota((2 * CONTRIB, width), 0) % CONTRIB
    cutout = jnp.where(kappa >= residue, inside, beyond)
    piece = times_table(cutout.T, pair_at("piece"))
    straight, crossed = shift_rows(residue, pair_at("shift"))
    out_ref[...] = (piece * straight + swap_halves(piece) * crossed).astype(BF16)


def in_first_half():
    return 2 * lax.axis_index("group") < lax.axis_size("group")


def early_kernel(
    offsets, cells, values, weights, flags, strips, plain_table, paired_table,
    out_ref, packed_ref, places_ref,
    offsets_ref, cells_ref, values_ref, weights_ref, flags_ref, strips_ref, plain_ref, paired_ref,
    real_ref, imag_ref, small_semaphores, semaphores, *, plain, paired, share,
):
    columns = strips_ref.shape[1]
    small = start_all(
        (offsets, cells, values, weights, flags),
        (offsets_ref, cells_ref, values_ref, weights_ref, flags_ref),
        small_semaphores,
    )

    def large():
        sources, targets = (strips, plain_table, paired_table), (strips_ref, plain_ref, paired_ref)
        return [
            pltpu.make_async_copy(source, target, semaphores.at[i])
            for i, (source, target) in enumerate(zip(sources, targets))
        ]

    @pl.when(in_first_half())
    def _():
        for copy in large():
            copy.start()

    for copy in small:
        copy.wait()
    for t in range(cells_ref.shape[0]):
        rows = [
            cells_ref[t, 0:1, :].astype(F32) * SUBGRID + cells_ref[t, 1:2, :].astype(F32),
            weights_ref[t] * flags_ref[t].astype(F32),
            values_ref[t],
        ]
        packed_ref[4 * t : 4 * t + 4, :] = jnp.concatenate(rows, axis=0)
    places_ref[...] = offsets_on_lanes(offsets_ref, share)

    @pl.when(in_first_half())
    def _():
        spread = offsets_on_lanes(offsets_ref, columns)
        predict(
            spread, large(), strips_ref, plain_ref, paired_ref, (real_ref, imag_ref), out_ref,
            plain, paired,
        )


def late_kernel(
    early_ref, offsets, strips, plain_table, paired_table, out_ref,
    offsets_ref, strips_ref, plain_ref, paired_ref, real_ref, imag_ref, semaphores,
    *, plain, paired,
):
    @pl.when(in_first_half())
    def _():
        out_ref[...] = early_ref[...]

    @pl.when(jnp.logical_not(in_first_half()))
    def _():
        copies = start_all(
            (offsets, strips, plain_table, paired_table),
            (offsets_ref, strips_ref, plain_ref, paired_ref),
            semaphores,
        )
        copies[0].wait()
        spread = offsets_on_lanes(offsets_ref, strips_ref.shape[1])
        predict(
            spread, copies[1:], strips_ref, plain_ref, paired_ref, (real_ref, imag_ref), out_ref,
            plain, paired,
        )


def prepare_kernel(places_ref, shift_ref, *refs, columns, share, blocks):
    samples_refs, outs = refs[:-5], refs[-5:]
    value_ref, weight_ref, put_ref, straight_ref, crossed_ref = outs
    fronts, samples = samples_refs[0].shape[0] // 4, samples_refs[0].shape[1]
    own = lax.axis_index("group")
    depth = FACET_ROWS * columns
    for spot in range(len(samples_refs) * fronts):
        step, t = spot // fronts, spot % fronts
        sample = samples_refs[step][4 * t : 4 * t + 4, :]
        cell = sample[0:1, :].astype(jnp.int32)
        row, col = cell // SUBGRID - own * columns, cell % SUBGRID
        inside = (row >= 0) & (row < columns)
        target = jnp.where(inside, col % FACET_ROWS * columns + row, -1)
        pick = one_hot((depth, samples), target)
        mask = iota((HALF, samples), 0) == col // FACET_ROWS
        factor = sample[1:2, :]
        highs, lows = [], []
        for term in (factor * sample[2:3, :], factor * sample[3:4, :], factor):
            high = term.astype(BF16).astype(F32)
            highs.append(jnp.where(mask, high, 0.0).astype(BF16))
            lows.append(jnp.where(mask, term - high, 0.0).astype(BF16))
        highs, lows = highs + highs[2:], lows + lows[2:]
        grid = dot(pick, jnp.concatenate(highs, axis=0), ((1,), (1,))) + dot(
            pick, jnp.concatenate(lows, axis=0), ((1,), (1,))
        )
        rows = slice(spot * depth, (spot + 1) * depth)
        value_ref[rows, :] = grid[:, :LANES]
        weight_ref[rows, :] = grid[:, LANES:]
    spread = places_ref[...]
    first_block, residue = spread // CONTRIB, spread % CONTRIB
    straight_ref[...], crossed_ref[...] = shift_rows(residue, shift_ref)
    base = iota(spread.shape, 1) % share * blocks
    targets = jnp.concatenate([base + first_block, base + (first_block + 1) % blocks], axis=1)
    put_ref[...] = one_hot(put_ref.shape, targets)


def subgrid_kernel(
    pieces_ref, value_ref, weight_ref, turn_ref, model_ref, back_ref, out_ref, held_ref,
    *, columns, bands,
):
    rows = pieces_ref.shape[0] // FACET_ROWS
    spots = range(rows // columns)
    depth = FACET_ROWS * columns
    share = columns // bands
    pieces = pieces_ref[...].astype(F32)
    sky = turned_eighths(
        [pieces[i * rows : (i + 1) * rows, :] for i in range(FACET_ROWS)], -1.0
    )
    sky = [
        value * turn_ref[0, i : i + 1, :] + swap_halves(value) * turn_ref[1, i : i + 1, :]
        for i, value in enumerate(sky)
    ]
    stacked = jnp.concatenate(
        [value[spot * columns : (spot + 1) * columns, :] for spot in spots for value in sky],
        axis=0,
    )
    grid = value_ref[...] - weight_ref[...] * times_table(stacked, model_ref)
    back = times_table(grid, back_ref)
    lines = []
    for i in range(FACET_ROWS):
        value = jnp.concatenate(
            [
                back[spot * depth + i * columns : spot * depth + (i + 1) * columns, :]
                for spot in spots
            ],
            axis=0,
        )
        lines.append(
            value * turn_ref[0, i : i + 1, :] - swap_halves(value) * turn_ref[1, i : i + 1, :]
        )
    lines = turned_eighths(lines, 1.0)
    for i in range(FACET_ROWS):
        for spot in spots:
            for b in range(bands):
                source = spot * columns + b * share
                target = ((b * FACET_ROWS + i) * len(spots) + spot) * share
                held_ref[target : target + share, :] = lines[i][source : source + share, :]
    out_ref[...] = held_ref[...].astype(BF16)


def return_kernel(
    places_ref, pieces_ref, straight_ref, crossed_ref, put_ref, window_ref, turn_ref, partial_ref,
    inner_ref, outer_ref, out_ref, *line_refs, bands,
):
    columns, _, length = out_ref.shape
    blocks = length // CONTRIB
    groups = length // LANES
    pairs = (columns + 1) // 2
    width = pieces_ref.shape[0] // bands
    summed = pieces_ref[0:width, :].astype(F32)
    for b in range(1, bands):
        summed += pieces_ref[b * width : (b + 1) * width, :].astype(F32)
    summed = summed * straight_ref[...] - swap_halves(summed) * crossed_ref[...]
    residues = table_times(partial_ref, summed, ((1,), (1,)))
    kappa = iota((2 * CONTRIB, width), 0) % CONTRIB
    inside = kappa >= places_ref[...] % CONTRIB
    both = jnp.concatenate(
        [jnp.where(inside, residues, 0.0), jnp.where(inside, 0.0, residues)], axis=1
    )
    put = put_ref[...]
    high, low = split(both)
    spectrum = dot(high, put, ((1,), (1,))) + dot(low, put, ((1,), (1,)))
    inner = times_table(
        jnp.concatenate(
            [
                jnp.concatenate(
                    [
                        spectrum[:CONTRIB, pair * LANES : (pair + 1) * LANES],
                        spectrum[CONTRIB:, pair * LANES : (pair + 1) * LANES],
                    ],
                    axis=1,
                )
                for pair in range(pairs)
            ],
            axis=0,
        ),
        inner_ref,
    )
    reals, imags = [], []
    for pair in range(pairs):
        rows = slice(pair * CONTRIB, (pair + 1) * CONTRIB)
        real, imag = inner[rows, :LANES], inner[rows, LANES:]
        reals.append(real * turn_ref[0] + imag * turn_ref[1])
        imags.append(imag * turn_ref[0] - real * turn_ref[1])
    lines = table_times(
        outer_ref,
        jnp.concatenate(
            [jnp.concatenate(reals, axis=1), jnp.concatenate(imags, axis=1)], axis=0
        ),
    )
    window = window_ref[...]
    low_half = iota((groups, LANES), 1) < HALF
    for part in range(2):
        for pair in range(pairs):
            lanes = slice(pair * LANES, (pair + 1) * LANES)
            begin = part * blocks
            even = lines[begin : begin + groups, lanes]
            odd = lines[begin + groups : begin + blocks, lanes]
            line_refs[2 * pair][pl.ds(part, groups, stride=2), :] = (
                jnp.where(low_half, even, swap_halves(odd)) * window
            )
            if 2 * pair + 1 < columns:
                line_refs[2 * pair + 1][pl.ds(part, groups, stride=2), :] = (
                    jnp.where(low_half, swap_halves(even), odd) * window
                )
    for column in range(columns):
        for group in range(groups):
            out_ref[column, :, group * LANES : (group + 1) * LANES] = line_refs[column][
                2 * group : 2 * group + 2, :
            ]


def kernel_call(kernel, name, out_shape, spaces, scratch, *operands, flops=0):
    return pl.pallas_call(
        kernel,
        out_shape=out_shape,
        in_specs=[pl.BlockSpec(memory_space=space) for space in spaces],
        out_specs=jax.tree.map(lambda _: pl.BlockSpec(memory_space=pltpu.VMEM), out_shape),
        scratch_shapes=scratch,
        compiler_params=pltpu.CompilerParams(vmem_limit_bytes=VMEM_LIMIT),
        cost_estimate=pl.CostEstimate(flops=flops, bytes_accessed=0, transcendentals=0)
        if flops
        else None,
        name=name,
    )(*operands)


def wide(rows):
    return pltpu.VMEM((rows, LANES), F32)


def local(groups, bands, strips, offsets, cells, values, weights, flags):
    columns, length = strips.shape[-2:]
    fronts = offsets.shape[0]
    share = columns // bands
    facets = groups * FACET_ROWS
    rows = facets * fronts * columns
    width = facets * fronts * share
    made = tables(length)
    plain, plain_places = made.pop("plain")
    paired, paired_places = made.pop("paired")
    made = {key: jnp.asarray(value) for key, value in made.items()}
    held = length // LANES * columns
    small = [offsets, cells[0, :, 0], values[0, :, 0], weights[0], flags[0]]
    large = [strips[0, 0], jnp.asarray(plain), jnp.asarray(paired)]

    def landing(arrays):
        return [
            (pltpu.SMEM if array is offsets else pltpu.VMEM)(array.shape, array.dtype)
            for array in arrays
        ]

    def in_hbm(arrays):
        return [pltpu.with_memory_space_constraint(array, pltpu.HBM) for array in arrays]

    def semaphores(count):
        return pltpu.SemaphoreType.DMA((count,))

    early, packed, places = kernel_call(
        functools.partial(early_kernel, plain=plain_places, paired=paired_places, share=share),
        "early",
        [
            jax.ShapeDtypeStruct((rows, LANES), BF16),
            jax.ShapeDtypeStruct((4 * fronts, cells.shape[-1]), F32),
            jax.ShapeDtypeStruct((1, width), jnp.int32),
        ],
        [pltpu.HBM] * 8,
        landing(small + large) + [wide(held)] * 2 + [semaphores(5), semaphores(3)],
        *in_hbm(small + large),
    )
    pieces = kernel_call(
        functools.partial(late_kernel, plain=plain_places, paired=paired_places), "late",
        jax.ShapeDtypeStruct((rows, LANES), BF16), [pltpu.VMEM] + [pltpu.HBM] * 4,
        landing([offsets] + large) + [wide(held)] * 2 + [semaphores(4)],
        early, *in_hbm([offsets] + large), flops=LATE_FLOPS,
    )
    gathered = [packed]
    for step in range(1, groups):
        moves = [((group + step) % groups, group) for group in range(groups)]
        gathered.append(lax.ppermute(packed, "group", moves))
    arrived = lax.all_to_all(pieces, "member", split_axis=0, concat_axis=0, tiled=True)
    blocks = length // CONTRIB
    value, weight, put, straight, crossed = kernel_call(
        functools.partial(prepare_kernel, columns=columns, share=share, blocks=blocks), "prepare",
        [jax.ShapeDtypeStruct((rows, LANES), F32)] * 2
        + [jax.ShapeDtypeStruct(((share + share % 2) * blocks, 2 * width), BF16)]
        + [jax.ShapeDtypeStruct((width, LANES), F32)] * 2,
        [pltpu.VMEM] * (2 + len(gathered)), [],
        places, made["shift"], *gathered, flops=PREPARE_FLOPS,
    )
    returned = kernel_call(
        functools.partial(subgrid_kernel, columns=columns, bands=bands), "subgrid",
        jax.ShapeDtypeStruct((rows, LANES), BF16), [pltpu.VMEM] * 6, [wide(rows)],
        arrived, value, weight, made["grid_turn"], made["model"], made["back"],
    )
    delivered = lax.all_to_all(
        returned, ("band", "member"), split_axis=0, concat_axis=0, tiled=True
    )
    lines = kernel_call(
        functools.partial(return_kernel, bands=bands), "lines",
        jax.ShapeDtypeStruct((share, 2, length), F32), [pltpu.VMEM] * 10,
        [wide(2 * length // LANES)] * share,
        places, delivered, straight, crossed, put, made["window"], made["turn"],
        made["partial"], made["inner_plus"], made["outer_plus"],
    )
    return lines[None]


def solution(mesh):
    bands = mesh.shape["band"]
    groups = mesh.shape["facet"] // FACET_ROWS
    split_mesh = Mesh(
        mesh.devices.reshape(groups, FACET_ROWS, bands), ("group", "member", "band")
    )
    facet = ("group", "member")
    placed = (
        P("band", facet, None, None, None),
        P(),
        P("band", None, facet, None, None),
        P("band", None, facet, None, None),
        P("band", None, facet, None),
        P("band", None, facet, None),
    )
    return jax.shard_map(
        functools.partial(local, groups, bands),
        mesh=split_mesh,
        in_specs=placed,
        out_specs=P(facet, "band", None, None),
        check_vma=False,
    )
```

```python
import functools
import math

import jax
import jax.numpy as jnp
import ml_dtypes
import numpy as np
from jax import lax
from jax.experimental import pallas as pl
from jax.experimental.pallas import tpu as pltpu
from jax.sharding import Mesh
from jax.sharding import PartitionSpec as P

CONTRIB = 64
FACET_ROWS = 8
SUBGRID = FACET_ROWS * CONTRIB
LANES = 128
HALF = LANES // 2
PREDICT_FLOPS = 10**10
PREPARE_FLOPS = 10**8
VMEM_LIMIT = 48 * 1024 * 1024
F32 = jnp.float32
BF16 = jnp.bfloat16


def phases(rows, cols, length, rotation):
    product = np.outer(rows, cols) % length
    return np.exp(rotation * 2j * np.pi * product / length)


def from_left(matrix):
    return np.block([[matrix.real, -matrix.imag], [matrix.imag, matrix.real]])


def from_right(matrix):
    return np.block([[matrix.real, matrix.imag], [-matrix.imag, matrix.real]])


def high_low(table):
    high = table.astype(ml_dtypes.bfloat16)
    low = (table - high.astype(np.float64)).astype(ml_dtypes.bfloat16)
    return np.stack([high, low])


def side_by_side(values):
    straight = np.concatenate([values.real, values.real], axis=-1)
    crossed = np.concatenate([-values.imag, values.imag], axis=-1)
    return np.stack([straight, crossed])


def stack_tables(named):
    places, blocks, begin = {}, [], 0
    for name, table in named.items():
        count = table.shape[1] // LANES
        places[name] = (begin, table.shape[0], count)
        blocks += [table[:, i * LANES : (i + 1) * LANES] for i in range(count)]
        begin += table.shape[0] * count
    return np.concatenate(blocks, axis=0), places


def stack_pairs(named):
    return stack_tables(
        {(name, i): table for name, pair in named.items() for i, table in enumerate(pair)}
    )


def tables(length):
    blocks = length // CONTRIB
    short = np.arange(CONTRIB)
    outer = np.concatenate([np.arange(0, blocks, 2), np.arange(1, blocks, 2)])
    window = 1.0 + 0.5 * np.cos(np.arange(length) * (2.0 * math.pi / length))
    window = (window * length**-0.5).reshape(length // LANES, LANES).astype(np.float32)
    turn = np.tile(phases(short, short, length, -1), (1, 2))
    turn = np.stack([turn.real, turn.imag]).astype(np.float32)
    pair = np.eye(2)
    shift = high_low(np.concatenate(side_by_side(phases(short, short, CONTRIB, -1)), axis=1))
    outer_minus = from_left(phases(short, outer, blocks, -1))
    inner_minus = from_right(np.kron(pair, phases(short, short, CONTRIB, -1)))
    piece = from_right(phases(short, short, CONTRIB, 1)) * CONTRIB**-0.5
    return dict(
        plain=stack_tables(dict(window=window, real=turn[0], imag=turn[1])),
        paired=stack_pairs(
            dict(
                shift=shift,
                outer=high_low(outer_minus),
                inner=high_low(inner_minus),
                piece=high_low(piece),
            )
        ),
        window=window,
        turn=turn,
        shift=shift,
        inner_plus=high_low(from_right(np.kron(pair, phases(short, short, CONTRIB, 1)))),
        outer_plus=high_low(from_left(phases(outer, short, blocks, 1))),
        partial=high_low(from_right(phases(short, short, CONTRIB, -1)).T * CONTRIB**-0.5),
        grid_turn=side_by_side(phases(np.arange(FACET_ROWS), short, SUBGRID, -1)).astype(
            np.float32
        ),
        model=high_low(from_right(phases(short, short, CONTRIB, -1)) * SUBGRID**-0.5),
        back=high_low(from_right(phases(short, short, CONTRIB, 1)) * SUBGRID**-0.5),
    )


def split(values):
    high = values.astype(BF16)
    return high, (values - high.astype(F32)).astype(BF16)


def dot(left, right, dims=((1,), (0,))):
    return lax.dot_general(left, right, (dims, ((), ())), preferred_element_type=F32)


def times_table(values, table, dims=((1,), (0,))):
    high, low = split(values)
    return dot(high, table[0], dims) + dot(low, table[0], dims) + dot(high, table[1], dims)


def table_times(table, values, dims=((1,), (0,))):
    high, low = split(values)
    return dot(table[0], high, dims) + dot(table[0], low, dims) + dot(table[1], high, dims)


def iota(shape, dimension):
    return lax.broadcasted_iota(jnp.int32, shape, dimension)


def swap_halves(values):
    return pltpu.roll(values, HALF, 1)


def table_at(ref, place):
    begin, rows, blocks = place
    parts = [ref[begin + i * rows : begin + (i + 1) * rows, :] for i in range(blocks)]
    return parts[0] if blocks == 1 else jnp.concatenate(parts, axis=1)


def offsets_on_lanes(offsets_ref, columns):
    fronts, owners = offsets_ref.shape
    groups = owners // FACET_ROWS
    own = lax.axis_index("group")
    begins = []
    for step in range(groups):
        group = own + step
        begins.append(jnp.where(group >= groups, group - groups, group) * FACET_ROWS)
    spread = iota((1, fronts * owners * columns), 1)
    place_of = spread // columns
    for place in range(fronts * owners):
        t, step, member = place % fronts, place // fronts % groups, place // (fronts * groups)
        spread = jnp.where(place_of == place, offsets_ref[t, begins[step] + member], spread)
    return spread


def shift_rows(residue, table):
    pick = jnp.where(iota((CONTRIB, residue.shape[1]), 0) == residue, 1.0, 0.0).T.astype(BF16)
    rows = dot(pick, table[0]) + dot(pick, table[1])
    return rows[:, :LANES], rows[:, LANES:]


def one_hot(shape, targets):
    return jnp.where(iota(shape, 0) == targets, 1.0, 0.0).astype(BF16)


def turned_eighths(values, rotation):
    sign = jnp.where(iota(values[0].shape, 1) < HALF, -rotation, rotation).astype(F32)

    def quarter_turn(value):
        return swap_halves(value) * sign

    def four(a, b, c, d):
        even_sum, even_diff = a + c, a - c
        odd_sum, odd_diff = b + d, quarter_turn(b - d)
        return even_sum + odd_sum, even_diff + odd_diff, even_sum - odd_sum, even_diff - odd_diff

    even = four(*values[0::2])
    odd = four(*values[1::2])
    root = math.sqrt(0.5)
    turned = (
        odd[0],
        (odd[1] + quarter_turn(odd[1])) * root,
        quarter_turn(odd[2]),
        (quarter_turn(odd[3]) - odd[3]) * root,
    )
    return [e + o for e, o in zip(even, turned)] + [e - o for e, o in zip(even, turned)]


def pack_samples(cells_ref, values_ref, weights_ref, flags_ref, out_ref):
    for t in range(cells_ref.shape[0]):
        rows = [
            cells_ref[t, 0:1, :].astype(F32) * SUBGRID + cells_ref[t, 1:2, :].astype(F32),
            weights_ref[t] * flags_ref[t].astype(F32),
            values_ref[t],
        ]
        out_ref[4 * t : 4 * t + 4, :] = jnp.concatenate(rows, axis=0)


def start_all(sources, targets, semaphores):
    copies = [
        pltpu.make_async_copy(source, target, semaphores.at[i])
        for i, (source, target) in enumerate(zip(sources, targets))
    ]
    for copy in copies:
        copy.start()
    return copies


def predict(spread, copies, strips_ref, plain_ref, paired_ref, held_refs, out_ref, plain, paired):
    columns, length = strips_ref.shape[1:]
    groups = length // LANES
    pairs = columns // 2
    blocks = length // CONTRIB
    width = spread.shape[1]
    first_block, residue = spread // CONTRIB, spread % CONTRIB
    base = iota(spread.shape, 1) % columns * blocks
    shape = (columns * blocks, width)
    pick_inside = one_hot(shape, base + first_block)
    pick_beyond = one_hot(shape, base + (first_block + 1) % blocks)
    for copy in copies:
        copy.wait()

    def pair_at(name):
        return [table_at(paired_ref, paired[name, i]) for i in range(2)]

    window = table_at(plain_ref, plain["window"])
    turn_real, turn_imag = table_at(plain_ref, plain["real"]), table_at(plain_ref, plain["imag"])
    low_half = iota((groups, LANES), 1) < HALF
    sections = []
    for part, held in enumerate(held_refs):
        for group in range(groups):
            held[group * columns : (group + 1) * columns, :] = strips_ref[
                part, :, group * LANES : (group + 1) * LANES
            ]
        even, odd = [], []
        for pair in range(pairs):
            first = held[pl.ds(2 * pair, groups, stride=columns), :] * window
            second = held[pl.ds(2 * pair + 1, groups, stride=columns), :] * window
            even.append(jnp.where(low_half, first, swap_halves(second)))
            odd.append(jnp.where(low_half, swap_halves(first), second))
        sections += [jnp.concatenate(even, axis=1), jnp.concatenate(odd, axis=1)]
    section = table_times(pair_at("outer"), jnp.concatenate(sections, axis=0))
    turned = []
    for pair in range(pairs):
        lanes = slice(pair * LANES, (pair + 1) * LANES)
        real, imag = section[:CONTRIB, lanes], section[CONTRIB:, lanes]
        turned.append(
            jnp.concatenate(
                [real * turn_real - imag * turn_imag, real * turn_imag + imag * turn_real],
                axis=1,
            )
        )
    inner = times_table(jnp.concatenate(turned, axis=0), pair_at("inner"))
    spectrum = jnp.concatenate(
        [
            jnp.concatenate(
                [
                    inner[pair * CONTRIB : (pair + 1) * CONTRIB, part * LANES : (part + 1) * LANES]
                    for pair in range(pairs)
                ],
                axis=1,
            )
            for part in range(2)
        ],
        axis=0,
    )
    high, low = split(spectrum)
    inside = dot(high, pick_inside) + dot(low, pick_inside)
    beyond = dot(high, pick_beyond) + dot(low, pick_beyond)
    kappa = iota((2 * CONTRIB, width), 0) % CONTRIB
    cutout = jnp.where(kappa >= residue, inside, beyond)
    piece = times_table(cutout.T, pair_at("piece"))
    straight, crossed = shift_rows(residue, pair_at("shift"))
    out_ref[...] = (piece * straight + swap_halves(piece) * crossed).astype(BF16)


def in_first_half():
    return 2 * lax.axis_index("group") < lax.axis_size("group")


def pack_rows(cells_ref, values_ref, weights_ref, flags_ref, packed_ref):
    for t in range(cells_ref.shape[0]):
        rows = [
            cells_ref[t, 0:1, :].astype(F32) * SUBGRID + cells_ref[t, 1:2, :].astype(F32),
            weights_ref[t] * flags_ref[t].astype(F32),
            values_ref[t],
        ]
        packed_ref[4 * t : 4 * t + 4, :] = jnp.concatenate(rows, axis=0)


def pack_kernel(*refs):
    sources, packed_ref, targets, semaphores = refs[:4], refs[4], refs[5:9], refs[9]

    @pl.when(in_first_half())
    def _():
        packed_ref[...] = jnp.zeros_like(packed_ref)

    @pl.when(jnp.logical_not(in_first_half()))
    def _():
        for copy in start_all(sources, targets, semaphores):
            copy.wait()
        pack_rows(*targets, packed_ref)


def predict_kernel(*refs, plain, paired, share):
    sources, outs, targets, refs = refs[:8], refs[8:11], refs[11:19], refs[19:]
    out_ref, packed_ref, places_ref = outs
    offsets_ref, samples_refs = targets[0], targets[1:5]
    strips_ref, plain_ref, paired_ref = targets[5:8]
    copies = start_all(sources, targets, refs[2])
    copies[0].wait()
    spread = offsets_on_lanes(offsets_ref, strips_ref.shape[1])
    places_ref[...] = offsets_on_lanes(offsets_ref, share)
    for copy in copies[1:5]:
        copy.wait()
    pack_rows(*samples_refs, packed_ref)
    predict(
        spread, copies[5:], strips_ref, plain_ref, paired_ref, refs[:2], out_ref, plain, paired
    )


def prepare_kernel(places_ref, shift_ref, *refs, columns, share, blocks):
    samples_refs, outs = refs[:-5], refs[-5:]
    value_ref, weight_ref, put_ref, straight_ref, crossed_ref = outs
    fronts, samples = samples_refs[0].shape[0] // 4, samples_refs[0].shape[1]
    groups = (len(samples_refs) + 1) // 2
    own = lax.axis_index("group")
    depth = FACET_ROWS * columns
    for spot in range(groups * fronts):
        step, t = spot // fronts, spot % fronts
        rows = slice(4 * t, 4 * t + 4)
        if step == 0:
            sample = samples_refs[0][rows, :]
        else:
            sample = samples_refs[2 * step - 1][rows, :] + samples_refs[2 * step][rows, :]
        cell = sample[0:1, :].astype(jnp.int32)
        row, col = cell // SUBGRID - own * columns, cell % SUBGRID
        inside = (row >= 0) & (row < columns)
        target = jnp.where(inside, col % FACET_ROWS * columns + row, -1)
        pick = one_hot((depth, samples), target)
        mask = iota((HALF, samples), 0) == col // FACET_ROWS
        factor = sample[1:2, :]
        highs, lows = [], []
        for term in (factor * sample[2:3, :], factor * sample[3:4, :], factor):
            high = term.astype(BF16).astype(F32)
            highs.append(jnp.where(mask, high, 0.0).astype(BF16))
            lows.append(jnp.where(mask, term - high, 0.0).astype(BF16))
        highs, lows = highs + highs[2:], lows + lows[2:]
        grid = dot(pick, jnp.concatenate(highs, axis=0), ((1,), (1,))) + dot(
            pick, jnp.concatenate(lows, axis=0), ((1,), (1,))
        )
        rows = slice(spot * depth, (spot + 1) * depth)
        value_ref[rows, :] = grid[:, :LANES]
        weight_ref[rows, :] = grid[:, LANES:]
    spread = places_ref[...]
    first_block, residue = spread // CONTRIB, spread % CONTRIB
    straight_ref[...], crossed_ref[...] = shift_rows(residue, shift_ref)
    base = iota(spread.shape, 1) % share * blocks
    targets = jnp.concatenate([base + first_block, base + (first_block + 1) % blocks], axis=1)
    put_ref[...] = one_hot(put_ref.shape, targets)


def subgrid_kernel(
    pieces_ref, value_ref, weight_ref, turn_ref, model_ref, back_ref, out_ref, held_ref,
    *, columns, bands,
):
    rows = pieces_ref.shape[0] // FACET_ROWS
    spots = range(rows // columns)
    depth = FACET_ROWS * columns
    share = columns // bands
    pieces = pieces_ref[...].astype(F32)
    sky = turned_eighths(
        [pieces[i * rows : (i + 1) * rows, :] for i in range(FACET_ROWS)], -1.0
    )
    sky = [
        value * turn_ref[0, i : i + 1, :] + swap_halves(value) * turn_ref[1, i : i + 1, :]
        for i, value in enumerate(sky)
    ]
    stacked = jnp.concatenate(
        [value[spot * columns : (spot + 1) * columns, :] for spot in spots for value in sky],
        axis=0,
    )
    grid = value_ref[...] - weight_ref[...] * times_table(stacked, model_ref)
    back = times_table(grid, back_ref)
    lines = []
    for i in range(FACET_ROWS):
        value = jnp.concatenate(
            [
                back[spot * depth + i * columns : spot * depth + (i + 1) * columns, :]
                for spot in spots
            ],
            axis=0,
        )
        lines.append(
            value * turn_ref[0, i : i + 1, :] - swap_halves(value) * turn_ref[1, i : i + 1, :]
        )
    lines = turned_eighths(lines, 1.0)
    for i in range(FACET_ROWS):
        for spot in spots:
            for b in range(bands):
                source = spot * columns + b * share
                target = ((b * FACET_ROWS + i) * len(spots) + spot) * share
                held_ref[target : target + share, :] = lines[i][source : source + share, :]
    out_ref[...] = held_ref[...].astype(BF16)


def return_kernel(
    places_ref, pieces_ref, straight_ref, crossed_ref, put_ref, window_ref, turn_ref, partial_ref,
    inner_ref, outer_ref, out_ref, *line_refs, bands,
):
    columns, _, length = out_ref.shape
    blocks = length // CONTRIB
    groups = length // LANES
    pairs = (columns + 1) // 2
    width = pieces_ref.shape[0] // bands
    summed = pieces_ref[0:width, :].astype(F32)
    for b in range(1, bands):
        summed += pieces_ref[b * width : (b + 1) * width, :].astype(F32)
    summed = summed * straight_ref[...] - swap_halves(summed) * crossed_ref[...]
    residues = table_times(partial_ref, summed, ((1,), (1,)))
    kappa = iota((2 * CONTRIB, width), 0) % CONTRIB
    inside = kappa >= places_ref[...] % CONTRIB
    both = jnp.concatenate(
        [jnp.where(inside, residues, 0.0), jnp.where(inside, 0.0, residues)], axis=1
    )
    put = put_ref[...]
    high, low = split(both)
    spectrum = dot(high, put, ((1,), (1,))) + dot(low, put, ((1,), (1,)))
    inner = times_table(
        jnp.concatenate(
            [
                jnp.concatenate(
                    [
                        spectrum[:CONTRIB, pair * LANES : (pair + 1) * LANES],
                        spectrum[CONTRIB:, pair * LANES : (pair + 1) * LANES],
                    ],
                    axis=1,
                )
                for pair in range(pairs)
            ],
            axis=0,
        ),
        inner_ref,
    )
    reals, imags = [], []
    for pair in range(pairs):
        rows = slice(pair * CONTRIB, (pair + 1) * CONTRIB)
        real, imag = inner[rows, :LANES], inner[rows, LANES:]
        reals.append(real * turn_ref[0] + imag * turn_ref[1])
        imags.append(imag * turn_ref[0] - real * turn_ref[1])
    lines = table_times(
        outer_ref,
        jnp.concatenate(
            [jnp.concatenate(reals, axis=1), jnp.concatenate(imags, axis=1)], axis=0
        ),
    )
    window = window_ref[...]
    low_half = iota((groups, LANES), 1) < HALF
    for part in range(2):
        for pair in range(pairs):
            lanes = slice(pair * LANES, (pair + 1) * LANES)
            begin = part * blocks
            even = lines[begin : begin + groups, lanes]
            odd = lines[begin + groups : begin + blocks, lanes]
            line_refs[2 * pair][pl.ds(part, groups, stride=2), :] = (
                jnp.where(low_half, even, swap_halves(odd)) * window
            )
            if 2 * pair + 1 < columns:
                line_refs[2 * pair + 1][pl.ds(part, groups, stride=2), :] = (
                    jnp.where(low_half, swap_halves(even), odd) * window
                )
    for column in range(columns):
        for group in range(groups):
            out_ref[column, :, group * LANES : (group + 1) * LANES] = line_refs[column][
                2 * group : 2 * group + 2, :
            ]


def kernel_call(kernel, name, out_shape, spaces, scratch, *operands, flops=0):
    return pl.pallas_call(
        kernel,
        out_shape=out_shape,
        in_specs=[pl.BlockSpec(memory_space=space) for space in spaces],
        out_specs=jax.tree.map(lambda _: pl.BlockSpec(memory_space=pltpu.VMEM), out_shape),
        scratch_shapes=scratch,
        compiler_params=pltpu.CompilerParams(vmem_limit_bytes=VMEM_LIMIT),
        cost_estimate=pl.CostEstimate(flops=flops, bytes_accessed=0, transcendentals=0)
        if flops
        else None,
        name=name,
    )(*operands)


def wide(rows):
    return pltpu.VMEM((rows, LANES), F32)


def local(groups, bands, strips, offsets, cells, values, weights, flags):
    columns, length = strips.shape[-2:]
    fronts = offsets.shape[0]
    share = columns // bands
    facets = groups * FACET_ROWS
    rows = facets * fronts * columns
    width = facets * fronts * share
    made = tables(length)
    plain, plain_places = made.pop("plain")
    paired, paired_places = made.pop("paired")
    made = {key: jnp.asarray(value) for key, value in made.items()}
    held = length // LANES * columns
    small = [offsets, cells[0, :, 0], values[0, :, 0], weights[0], flags[0]]
    large = [strips[0, 0], jnp.asarray(plain), jnp.asarray(paired)]

    def landing(arrays):
        return [
            (pltpu.SMEM if array is offsets else pltpu.VMEM)(array.shape, array.dtype)
            for array in arrays
        ]

    def in_hbm(arrays):
        return [pltpu.with_memory_space_constraint(array, pltpu.HBM) for array in arrays]

    def semaphores(count):
        return pltpu.SemaphoreType.DMA((count,))

    shape = jax.ShapeDtypeStruct((4 * fronts, cells.shape[-1]), F32)
    first = kernel_call(
        pack_kernel, "pack", shape, [pltpu.HBM] * 4,
        landing(small[1:]) + [semaphores(4)], *in_hbm(small[1:]),
    )
    pieces, packed, places = kernel_call(
        functools.partial(predict_kernel, plain=plain_places, paired=paired_places, share=share),
        "predict",
        [
            jax.ShapeDtypeStruct((rows, LANES), BF16),
            shape,
            jax.ShapeDtypeStruct((1, width), jnp.int32),
        ],
        [pltpu.HBM] * 8,
        landing(small + large) + [wide(held)] * 2 + [semaphores(8)],
        *in_hbm(small + large), flops=PREDICT_FLOPS,
    )
    gathered = [packed]
    for step in range(1, groups):
        moves = [((group + step) % groups, group) for group in range(groups)]
        gathered += [
            lax.ppermute(first, "group", [move for move in moves if 2 * move[0] >= groups]),
            lax.ppermute(packed, "group", [move for move in moves if 2 * move[0] < groups]),
        ]
    arrived = lax.all_to_all(pieces, "member", split_axis=0, concat_axis=0, tiled=True)
    blocks = length // CONTRIB
    value, weight, put, straight, crossed = kernel_call(
        functools.partial(prepare_kernel, columns=columns, share=share, blocks=blocks), "prepare",
        [jax.ShapeDtypeStruct((rows, LANES), F32)] * 2
        + [jax.ShapeDtypeStruct(((share + share % 2) * blocks, 2 * width), BF16)]
        + [jax.ShapeDtypeStruct((width, LANES), F32)] * 2,
        [pltpu.VMEM] * (2 + len(gathered)), [],
        places, made["shift"], *gathered, flops=PREPARE_FLOPS,
    )
    returned = kernel_call(
        functools.partial(subgrid_kernel, columns=columns, bands=bands), "subgrid",
        jax.ShapeDtypeStruct((rows, LANES), BF16), [pltpu.VMEM] * 6, [wide(rows)],
        arrived, value, weight, made["grid_turn"], made["model"], made["back"],
    )
    delivered = lax.all_to_all(
        returned, ("band", "member"), split_axis=0, concat_axis=0, tiled=True
    )
    lines = kernel_call(
        functools.partial(return_kernel, bands=bands), "lines",
        jax.ShapeDtypeStruct((share, 2, length), F32), [pltpu.VMEM] * 10,
        [wide(2 * length // LANES)] * share,
        places, delivered, straight, crossed, put, made["window"], made["turn"],
        made["partial"], made["inner_plus"], made["outer_plus"],
    )
    return lines[None]


def solution(mesh):
    bands = mesh.shape["band"]
    groups = mesh.shape["facet"] // FACET_ROWS
    split_mesh = Mesh(
        mesh.devices.reshape(groups, FACET_ROWS, bands), ("group", "member", "band")
    )
    facet = ("group", "member")
    placed = (
        P("band", facet, None, None, None),
        P(),
        P("band", None, facet, None, None),
        P("band", None, facet, None, None),
        P("band", None, facet, None),
        P("band", None, facet, None),
    )
    return jax.shard_map(
        functools.partial(local, groups, bands),
        mesh=split_mesh,
        in_specs=placed,
        out_specs=P(facet, "band", None, None),
        check_vma=False,
    )
```

```python
import functools
import math

import jax
import jax.numpy as jnp
import ml_dtypes
import numpy as np
from jax import lax
from jax.experimental import pallas as pl
from jax.experimental.pallas import tpu as pltpu
from jax.sharding import Mesh
from jax.sharding import PartitionSpec as P

CONTRIB = 64
FACET_ROWS = 8
SUBGRID = FACET_ROWS * CONTRIB
LANES = 128
HALF = LANES // 2
LATE_FLOPS = 10**10
PREPARE_FLOPS = 2 * 10**10
VMEM_LIMIT = 48 * 1024 * 1024
F32 = jnp.float32
BF16 = jnp.bfloat16


def phases(rows, cols, length, rotation):
    product = np.outer(rows, cols) % length
    return np.exp(rotation * 2j * np.pi * product / length)


def from_left(matrix):
    return np.block([[matrix.real, -matrix.imag], [matrix.imag, matrix.real]])


def from_right(matrix):
    return np.block([[matrix.real, matrix.imag], [-matrix.imag, matrix.real]])


def high_low(table):
    high = table.astype(ml_dtypes.bfloat16)
    low = (table - high.astype(np.float64)).astype(ml_dtypes.bfloat16)
    return np.stack([high, low])


def side_by_side(values):
    straight = np.concatenate([values.real, values.real], axis=-1)
    crossed = np.concatenate([-values.imag, values.imag], axis=-1)
    return np.stack([straight, crossed])


def stack_tables(named):
    places, blocks, begin = {}, [], 0
    for name, table in named.items():
        count = table.shape[1] // LANES
        places[name] = (begin, table.shape[0], count)
        blocks += [table[:, i * LANES : (i + 1) * LANES] for i in range(count)]
        begin += table.shape[0] * count
    return np.concatenate(blocks, axis=0), places


def stack_pairs(named):
    return stack_tables(
        {(name, i): table for name, pair in named.items() for i, table in enumerate(pair)}
    )


def tables(length):
    blocks = length // CONTRIB
    short = np.arange(CONTRIB)
    outer = np.concatenate([np.arange(0, blocks, 2), np.arange(1, blocks, 2)])
    window = 1.0 + 0.5 * np.cos(np.arange(length) * (2.0 * math.pi / length))
    window = (window * length**-0.5).reshape(length // LANES, LANES).astype(np.float32)
    turn = np.tile(phases(short, short, length, -1), (1, 2))
    turn = np.stack([turn.real, turn.imag]).astype(np.float32)
    pair = np.eye(2)
    shift = high_low(np.concatenate(side_by_side(phases(short, short, CONTRIB, -1)), axis=1))
    outer_minus = from_left(phases(short, outer, blocks, -1))
    inner_minus = from_right(np.kron(pair, phases(short, short, CONTRIB, -1)))
    piece = from_right(phases(short, short, CONTRIB, 1)) * CONTRIB**-0.5
    return dict(
        plain=stack_tables(dict(window=window, real=turn[0], imag=turn[1])),
        paired=stack_pairs(
            dict(
                shift=shift,
                outer=high_low(outer_minus),
                inner=high_low(inner_minus),
                piece=high_low(piece),
            )
        ),
        window=window,
        turn=turn,
        shift=shift,
        inner_plus=high_low(from_right(np.kron(pair, phases(short, short, CONTRIB, 1)))),
        outer_plus=high_low(from_left(phases(outer, short, blocks, 1))),
        partial=high_low(from_right(phases(short, short, CONTRIB, -1)).T * CONTRIB**-0.5),
        grid_turn=side_by_side(phases(np.arange(FACET_ROWS), short, SUBGRID, -1)).astype(
            np.float32
        ),
        model=high_low(from_right(phases(short, short, CONTRIB, -1)) * SUBGRID**-0.5),
        back=high_low(from_right(phases(short, short, CONTRIB, 1)) * SUBGRID**-0.5),
    )


def split(values):
    high = values.astype(BF16)
    return high, (values - high.astype(F32)).astype(BF16)


def dot(left, right, dims=((1,), (0,))):
    return lax.dot_general(left, right, (dims, ((), ())), preferred_element_type=F32)


def times_table(values, table, dims=((1,), (0,))):
    high, low = split(values)
    return dot(high, table[0], dims) + dot(low, table[0], dims) + dot(high, table[1], dims)


def table_times(table, values, dims=((1,), (0,))):
    high, low = split(values)
    return dot(table[0], high, dims) + dot(table[0], low, dims) + dot(table[1], high, dims)


def iota(shape, dimension):
    return lax.broadcasted_iota(jnp.int32, shape, dimension)


def over(values, size):
    return lax.shift_right_logical(values, jnp.full_like(values, size.bit_length() - 1))


def within(values, size):
    return values & (size - 1)


def swap_halves(values):
    return pltpu.roll(values, HALF, 1)


def table_at(ref, place):
    begin, rows, blocks = place
    parts = [ref[begin + i * rows : begin + (i + 1) * rows, :] for i in range(blocks)]
    return parts[0] if blocks == 1 else jnp.concatenate(parts, axis=1)


def offsets_on_lanes(offsets_ref, columns):
    fronts, owners = offsets_ref.shape
    groups = owners // FACET_ROWS
    own = lax.axis_index("group")
    begins = []
    for step in range(groups):
        group = own + step
        begins.append(jnp.where(group >= groups, group - groups, group) * FACET_ROWS)
    spread = iota((1, fronts * owners * columns), 1)
    place_of = over(spread, columns)
    for place in range(fronts * owners):
        t, step, member = place % fronts, place // fronts % groups, place // (fronts * groups)
        spread = jnp.where(place_of == place, offsets_ref[t, begins[step] + member], spread)
    return spread


def shift_rows(residue, table):
    pick = jnp.where(iota((CONTRIB, residue.shape[1]), 0) == residue, 1.0, 0.0).T.astype(BF16)
    rows = dot(pick, table[0]) + dot(pick, table[1])
    return rows[:, :LANES], rows[:, LANES:]


def one_hot(shape, targets):
    return jnp.where(iota(shape, 0) == targets, 1.0, 0.0).astype(BF16)


def turned_eighths(values, rotation):
    sign = jnp.where(iota(values[0].shape, 1) < HALF, -rotation, rotation).astype(F32)

    def quarter_turn(value):
        return swap_halves(value) * sign

    def four(a, b, c, d):
        even_sum, even_diff = a + c, a - c
        odd_sum, odd_diff = b + d, quarter_turn(b - d)
        return even_sum + odd_sum, even_diff + odd_diff, even_sum - odd_sum, even_diff - odd_diff

    even = four(*values[0::2])
    odd = four(*values[1::2])
    root = math.sqrt(0.5)
    turned = (
        odd[0],
        (odd[1] + quarter_turn(odd[1])) * root,
        quarter_turn(odd[2]),
        (quarter_turn(odd[3]) - odd[3]) * root,
    )
    return [e + o for e, o in zip(even, turned)] + [e - o for e, o in zip(even, turned)]


def pack_samples(cells_ref, values_ref, weights_ref, flags_ref, out_ref):
    for t in range(cells_ref.shape[0]):
        rows = [
            cells_ref[t, 0:1, :].astype(F32) * SUBGRID + cells_ref[t, 1:2, :].astype(F32),
            weights_ref[t] * flags_ref[t].astype(F32),
            values_ref[t],
        ]
        out_ref[4 * t : 4 * t + 4, :] = jnp.concatenate(rows, axis=0)


def start_all(sources, targets, semaphores):
    copies = [
        pltpu.make_async_copy(source, target, semaphores.at[i])
        for i, (source, target) in enumerate(zip(sources, targets))
    ]
    for copy in copies:
        copy.start()
    return copies


def predict(spread, copies, strips_ref, plain_ref, paired_ref, held_refs, out_ref, plain, paired):
    columns, length = strips_ref.shape[1:]
    groups = length // LANES
    pairs = columns // 2
    blocks = length // CONTRIB
    width = spread.shape[1]
    first_block, residue = over(spread, CONTRIB), within(spread, CONTRIB)
    base = within(iota(spread.shape, 1), columns) * blocks
    shape = (columns * blocks, width)
    pick_inside = one_hot(shape, base + first_block)
    pick_beyond = one_hot(shape, base + within(first_block + 1, blocks))
    for copy in copies:
        copy.wait()

    def pair_at(name):
        return [table_at(paired_ref, paired[name, i]) for i in range(2)]

    window = table_at(plain_ref, plain["window"])
    turn_real, turn_imag = table_at(plain_ref, plain["real"]), table_at(plain_ref, plain["imag"])
    low_half = iota((groups, LANES), 1) < HALF
    sections = []
    for part, held in enumerate(held_refs):
        for group in range(groups):
            held[group * columns : (group + 1) * columns, :] = strips_ref[
                part, :, group * LANES : (group + 1) * LANES
            ]
        even, odd = [], []
        for pair in range(pairs):
            first = held[pl.ds(2 * pair, groups, stride=columns), :] * window
            second = held[pl.ds(2 * pair + 1, groups, stride=columns), :] * window
            even.append(jnp.where(low_half, first, swap_halves(second)))
            odd.append(jnp.where(low_half, swap_halves(first), second))
        sections += [jnp.concatenate(even, axis=1), jnp.concatenate(odd, axis=1)]
    section = table_times(pair_at("outer"), jnp.concatenate(sections, axis=0))
    turned = []
    for pair in range(pairs):
        lanes = slice(pair * LANES, (pair + 1) * LANES)
        real, imag = section[:CONTRIB, lanes], section[CONTRIB:, lanes]
        turned.append(
            jnp.concatenate(
                [real * turn_real - imag * turn_imag, real * turn_imag + imag * turn_real],
                axis=1,
            )
        )
    inner = times_table(jnp.concatenate(turned, axis=0), pair_at("inner"))
    spectrum = jnp.concatenate(
        [
            jnp.concatenate(
                [
                    inner[pair * CONTRIB : (pair + 1) * CONTRIB, part * LANES : (part + 1) * LANES]
                    for pair in range(pairs)
                ],
                axis=1,
            )
            for part in range(2)
        ],
        axis=0,
    )
    high, low = split(spectrum)
    inside = dot(high, pick_inside) + dot(low, pick_inside)
    beyond = dot(high, pick_beyond) + dot(low, pick_beyond)
    kappa = within(iota((2 * CONTRIB, width), 0), CONTRIB)
    cutout = jnp.where(kappa >= residue, inside, beyond)
    piece = times_table(cutout.T, pair_at("piece"))
    straight, crossed = shift_rows(residue, pair_at("shift"))
    out_ref[...] = (piece * straight + swap_halves(piece) * crossed).astype(BF16)


def in_first_half():
    return 2 * lax.axis_index("group") < lax.axis_size("group")


def early_kernel(
    offsets, cells, values, weights, flags, strips, plain_table, paired_table,
    out_ref, packed_ref, places_ref,
    offsets_ref, cells_ref, values_ref, weights_ref, flags_ref, strips_ref, plain_ref, paired_ref,
    real_ref, imag_ref, small_semaphores, semaphores, *, plain, paired, share,
):
    columns = strips_ref.shape[1]
    small = start_all(
        (offsets, cells, values, weights, flags),
        (offsets_ref, cells_ref, values_ref, weights_ref, flags_ref),
        small_semaphores,
    )

    def large():
        sources, targets = (strips, plain_table, paired_table), (strips_ref, plain_ref, paired_ref)
        return [
            pltpu.make_async_copy(source, target, semaphores.at[i])
            for i, (source, target) in enumerate(zip(sources, targets))
        ]

    @pl.when(in_first_half())
    def _():
        for copy in large():
            copy.start()

    for copy in small:
        copy.wait()
    for t in range(cells_ref.shape[0]):
        rows = [
            cells_ref[t, 0:1, :].astype(F32) * SUBGRID + cells_ref[t, 1:2, :].astype(F32),
            weights_ref[t] * flags_ref[t].astype(F32),
            values_ref[t],
        ]
        packed_ref[4 * t : 4 * t + 4, :] = jnp.concatenate(rows, axis=0)
    places_ref[...] = offsets_on_lanes(offsets_ref, share)

    @pl.when(in_first_half())
    def _():
        spread = offsets_on_lanes(offsets_ref, columns)
        predict(
            spread, large(), strips_ref, plain_ref, paired_ref, (real_ref, imag_ref), out_ref,
            plain, paired,
        )


def late_kernel(
    early_ref, offsets, strips, plain_table, paired_table, out_ref,
    offsets_ref, strips_ref, plain_ref, paired_ref, real_ref, imag_ref, semaphores,
    *, plain, paired,
):
    @pl.when(in_first_half())
    def _():
        out_ref[...] = early_ref[...]

    @pl.when(jnp.logical_not(in_first_half()))
    def _():
        copies = start_all(
            (offsets, strips, plain_table, paired_table),
            (offsets_ref, strips_ref, plain_ref, paired_ref),
            semaphores,
        )
        copies[0].wait()
        spread = offsets_on_lanes(offsets_ref, strips_ref.shape[1])
        predict(
            spread, copies[1:], strips_ref, plain_ref, paired_ref, (real_ref, imag_ref), out_ref,
            plain, paired,
        )


def prepare_kernel(places_ref, shift_ref, *refs, columns, share, blocks):
    samples_refs, outs = refs[:-5], refs[-5:]
    value_ref, weight_ref, put_ref, straight_ref, crossed_ref = outs
    fronts, samples = samples_refs[0].shape[0] // 4, samples_refs[0].shape[1]
    own = lax.axis_index("group")
    depth = FACET_ROWS * columns
    for spot in range(len(samples_refs) * fronts):
        step, t = spot // fronts, spot % fronts
        sample = samples_refs[step][4 * t : 4 * t + 4, :]
        cell = sample[0:1, :].astype(jnp.int32)
        row, col = over(cell, SUBGRID) - own * columns, within(cell, SUBGRID)
        inside = (row >= 0) & (row < columns)
        target = jnp.where(inside, within(col, FACET_ROWS) * columns + row, -1)
        pick = one_hot((depth, samples), target)
        mask = iota((HALF, samples), 0) == over(col, FACET_ROWS)
        factor = sample[1:2, :]
        highs, lows = [], []
        for term in (factor * sample[2:3, :], factor * sample[3:4, :], factor):
            high = term.astype(BF16).astype(F32)
            highs.append(jnp.where(mask, high, 0.0).astype(BF16))
            lows.append(jnp.where(mask, term - high, 0.0).astype(BF16))
        highs, lows = highs + highs[2:], lows + lows[2:]
        grid = dot(pick, jnp.concatenate(highs, axis=0), ((1,), (1,))) + dot(
            pick, jnp.concatenate(lows, axis=0), ((1,), (1,))
        )
        rows = slice(spot * depth, (spot + 1) * depth)
        value_ref[rows, :] = grid[:, :LANES]
        weight_ref[rows, :] = grid[:, LANES:]
    spread = places_ref[...]
    first_block, residue = over(spread, CONTRIB), within(spread, CONTRIB)
    straight_ref[...], crossed_ref[...] = shift_rows(residue, shift_ref)
    base = within(iota(spread.shape, 1), share) * blocks
    targets = jnp.concatenate([base + first_block, base + within(first_block + 1, blocks)], axis=1)
    put_ref[...] = one_hot(put_ref.shape, targets)


def subgrid_kernel(
    pieces_ref, value_ref, weight_ref, turn_ref, model_ref, back_ref, out_ref, held_ref,
    *, columns, bands,
):
    rows = pieces_ref.shape[0] // FACET_ROWS
    spots = range(rows // columns)
    depth = FACET_ROWS * columns
    share = columns // bands
    pieces = pieces_ref[...].astype(F32)
    sky = turned_eighths(
        [pieces[i * rows : (i + 1) * rows, :] for i in range(FACET_ROWS)], -1.0
    )
    sky = [
        value * turn_ref[0, i : i + 1, :] + swap_halves(value) * turn_ref[1, i : i + 1, :]
        for i, value in enumerate(sky)
    ]
    stacked = jnp.concatenate(
        [value[spot * columns : (spot + 1) * columns, :] for spot in spots for value in sky],
        axis=0,
    )
    grid = value_ref[...] - weight_ref[...] * times_table(stacked, model_ref)
    back = times_table(grid, back_ref)
    lines = []
    for i in range(FACET_ROWS):
        value = jnp.concatenate(
            [
                back[spot * depth + i * columns : spot * depth + (i + 1) * columns, :]
                for spot in spots
            ],
            axis=0,
        )
        lines.append(
            value * turn_ref[0, i : i + 1, :] - swap_halves(value) * turn_ref[1, i : i + 1, :]
        )
    lines = turned_eighths(lines, 1.0)
    for i in range(FACET_ROWS):
        for spot in spots:
            for b in range(bands):
                source = spot * columns + b * share
                target = ((b * FACET_ROWS + i) * len(spots) + spot) * share
                held_ref[target : target + share, :] = lines[i][source : source + share, :]
    out_ref[...] = held_ref[...].astype(BF16)


def return_kernel(
    places_ref, pieces_ref, straight_ref, crossed_ref, put_ref, window_ref, turn_ref, partial_ref,
    inner_ref, outer_ref, out_ref, *line_refs, bands,
):
    columns, _, length = out_ref.shape
    blocks = length // CONTRIB
    groups = length // LANES
    pairs = (columns + 1) // 2
    width = pieces_ref.shape[0] // bands
    summed = pieces_ref[0:width, :].astype(F32)
    for b in range(1, bands):
        summed += pieces_ref[b * width : (b + 1) * width, :].astype(F32)
    summed = summed * straight_ref[...] - swap_halves(summed) * crossed_ref[...]
    residues = table_times(partial_ref, summed, ((1,), (1,)))
    kappa = within(iota((2 * CONTRIB, width), 0), CONTRIB)
    inside = kappa >= within(places_ref[...], CONTRIB)
    both = jnp.concatenate(
        [jnp.where(inside, residues, 0.0), jnp.where(inside, 0.0, residues)], axis=1
    )
    put = put_ref[...]
    high, low = split(both)
    spectrum = dot(high, put, ((1,), (1,))) + dot(low, put, ((1,), (1,)))
    inner = times_table(
        jnp.concatenate(
            [
                jnp.concatenate(
                    [
                        spectrum[:CONTRIB, pair * LANES : (pair + 1) * LANES],
                        spectrum[CONTRIB:, pair * LANES : (pair + 1) * LANES],
                    ],
                    axis=1,
                )
                for pair in range(pairs)
            ],
            axis=0,
        ),
        inner_ref,
    )
    reals, imags = [], []
    for pair in range(pairs):
        rows = slice(pair * CONTRIB, (pair + 1) * CONTRIB)
        real, imag = inner[rows, :LANES], inner[rows, LANES:]
        reals.append(real * turn_ref[0] + imag * turn_ref[1])
        imags.append(imag * turn_ref[0] - real * turn_ref[1])
    lines = table_times(
        outer_ref,
        jnp.concatenate(
            [jnp.concatenate(reals, axis=1), jnp.concatenate(imags, axis=1)], axis=0
        ),
    )
    window = window_ref[...]
    low_half = iota((groups, LANES), 1) < HALF
    for part in range(2):
        for pair in range(pairs):
            lanes = slice(pair * LANES, (pair + 1) * LANES)
            begin = part * blocks
            even = lines[begin : begin + groups, lanes]
            odd = lines[begin + groups : begin + blocks, lanes]
            line_refs[2 * pair][pl.ds(part, groups, stride=2), :] = (
                jnp.where(low_half, even, swap_halves(odd)) * window
            )
            if 2 * pair + 1 < columns:
                line_refs[2 * pair + 1][pl.ds(part, groups, stride=2), :] = (
                    jnp.where(low_half, swap_halves(even), odd) * window
                )
    for column in range(columns):
        for group in range(groups):
            out_ref[column, :, group * LANES : (group + 1) * LANES] = line_refs[column][
                2 * group : 2 * group + 2, :
            ]


def kernel_call(kernel, name, out_shape, spaces, scratch, *operands, flops=0):
    return pl.pallas_call(
        kernel,
        out_shape=out_shape,
        in_specs=[pl.BlockSpec(memory_space=space) for space in spaces],
        out_specs=jax.tree.map(lambda _: pl.BlockSpec(memory_space=pltpu.VMEM), out_shape),
        scratch_shapes=scratch,
        compiler_params=pltpu.CompilerParams(vmem_limit_bytes=VMEM_LIMIT),
        cost_estimate=pl.CostEstimate(flops=flops, bytes_accessed=0, transcendentals=0)
        if flops
        else None,
        name=name,
    )(*operands)


def wide(rows):
    return pltpu.VMEM((rows, LANES), F32)


def local(groups, bands, strips, offsets, cells, values, weights, flags):
    columns, length = strips.shape[-2:]
    fronts = offsets.shape[0]
    share = columns // bands
    facets = groups * FACET_ROWS
    rows = facets * fronts * columns
    width = facets * fronts * share
    made = tables(length)
    plain, plain_places = made.pop("plain")
    paired, paired_places = made.pop("paired")
    made = {key: jnp.asarray(value) for key, value in made.items()}
    held = length // LANES * columns
    small = [offsets, cells[0, :, 0], values[0, :, 0], weights[0], flags[0]]
    large = [strips[0, 0], jnp.asarray(plain), jnp.asarray(paired)]

    def landing(arrays):
        return [
            (pltpu.SMEM if array is offsets else pltpu.VMEM)(array.shape, array.dtype)
            for array in arrays
        ]

    def in_hbm(arrays):
        return [pltpu.with_memory_space_constraint(array, pltpu.HBM) for array in arrays]

    def semaphores(count):
        return pltpu.SemaphoreType.DMA((count,))

    early, packed, places = kernel_call(
        functools.partial(early_kernel, plain=plain_places, paired=paired_places, share=share),
        "early",
        [
            jax.ShapeDtypeStruct((rows, LANES), BF16),
            jax.ShapeDtypeStruct((4 * fronts, cells.shape[-1]), F32),
            jax.ShapeDtypeStruct((1, width), jnp.int32),
        ],
        [pltpu.HBM] * 8,
        landing(small + large) + [wide(held)] * 2 + [semaphores(5), semaphores(3)],
        *in_hbm(small + large),
    )
    pieces = kernel_call(
        functools.partial(late_kernel, plain=plain_places, paired=paired_places), "late",
        pltpu.VMEM((rows, LANES), BF16), [pltpu.VMEM] + [pltpu.HBM] * 4,
        landing([offsets] + large) + [wide(held)] * 2 + [semaphores(4)],
        early, *in_hbm([offsets] + large), flops=LATE_FLOPS,
    )
    gathered = [packed]
    for step in range(1, groups):
        moves = [((group + step) % groups, group) for group in range(groups)]
        gathered.append(lax.ppermute(packed, "group", moves))
    arrived = lax.all_to_all(pieces, "member", split_axis=0, concat_axis=0, tiled=True)
    blocks = length // CONTRIB
    value, weight, put, straight, crossed = kernel_call(
        functools.partial(prepare_kernel, columns=columns, share=share, blocks=blocks), "prepare",
        [jax.ShapeDtypeStruct((rows, LANES), F32)] * 2
        + [jax.ShapeDtypeStruct(((share + share % 2) * blocks, 2 * width), BF16)]
        + [jax.ShapeDtypeStruct((width, LANES), F32)] * 2,
        [pltpu.VMEM] * (2 + len(gathered)), [],
        places, made["shift"], *gathered, flops=PREPARE_FLOPS,
    )
    returned = kernel_call(
        functools.partial(subgrid_kernel, columns=columns, bands=bands), "subgrid",
        jax.ShapeDtypeStruct((rows, LANES), BF16), [pltpu.VMEM] * 6, [wide(rows)],
        arrived, value, weight, made["grid_turn"], made["model"], made["back"],
    )
    delivered = lax.all_to_all(
        returned, ("band", "member"), split_axis=0, concat_axis=0, tiled=True
    )
    lines = kernel_call(
        functools.partial(return_kernel, bands=bands), "lines",
        jax.ShapeDtypeStruct((share, 2, length), F32), [pltpu.VMEM] * 10,
        [wide(2 * length // LANES)] * share,
        places, delivered, straight, crossed, put, made["window"], made["turn"],
        made["partial"], made["inner_plus"], made["outer_plus"],
    )
    return lines[None]


def solution(mesh):
    bands = mesh.shape["band"]
    groups = mesh.shape["facet"] // FACET_ROWS
    split_mesh = Mesh(
        mesh.devices.reshape(groups, FACET_ROWS, bands), ("group", "member", "band")
    )
    facet = ("group", "member")
    placed = (
        P("band", facet, None, None, None),
        P(),
        P("band", None, facet, None, None),
        P("band", None, facet, None, None),
        P("band", None, facet, None),
        P("band", None, facet, None),
    )
    return jax.shard_map(
        functools.partial(local, groups, bands),
        mesh=split_mesh,
        in_specs=placed,
        out_specs=P(facet, "band", None, None),
        check_vma=False,
    )
```

```python
import functools
import math

import jax
import jax.numpy as jnp
import ml_dtypes
import numpy as np
from jax import lax
from jax.experimental import pallas as pl
from jax.experimental.pallas import tpu as pltpu
from jax.sharding import Mesh
from jax.sharding import PartitionSpec as P

CONTRIB = 64
FACET_ROWS = 8
SUBGRID = FACET_ROWS * CONTRIB
SEND_ORDER = tuple(reversed(range(FACET_ROWS)))
RETURN_ORDER = tuple(range(FACET_ROWS))
LANES = 128
HALF = LANES // 2
LATE_FLOPS = 10**10
PREPARE_FLOPS = 2 * 10**10
VMEM_LIMIT = 48 * 1024 * 1024
F32 = jnp.float32
BF16 = jnp.bfloat16


def phases(rows, cols, length, rotation):
    product = np.outer(rows, cols) % length
    return np.exp(rotation * 2j * np.pi * product / length)


def from_left(matrix):
    return np.block([[matrix.real, -matrix.imag], [matrix.imag, matrix.real]])


def from_right(matrix):
    return np.block([[matrix.real, matrix.imag], [-matrix.imag, matrix.real]])


def high_low(table):
    high = table.astype(ml_dtypes.bfloat16)
    low = (table - high.astype(np.float64)).astype(ml_dtypes.bfloat16)
    return np.stack([high, low])


def side_by_side(values):
    straight = np.concatenate([values.real, values.real], axis=-1)
    crossed = np.concatenate([-values.imag, values.imag], axis=-1)
    return np.stack([straight, crossed])


def stack_tables(named):
    places, blocks, begin = {}, [], 0
    for name, table in named.items():
        count = table.shape[1] // LANES
        places[name] = (begin, table.shape[0], count)
        blocks += [table[:, i * LANES : (i + 1) * LANES] for i in range(count)]
        begin += table.shape[0] * count
    return np.concatenate(blocks, axis=0), places


def stack_pairs(named):
    return stack_tables(
        {(name, i): table for name, pair in named.items() for i, table in enumerate(pair)}
    )


def tables(length):
    blocks = length // CONTRIB
    short = np.arange(CONTRIB)
    outer = np.concatenate([np.arange(0, blocks, 2), np.arange(1, blocks, 2)])
    window = 1.0 + 0.5 * np.cos(np.arange(length) * (2.0 * math.pi / length))
    window = (window * length**-0.5).reshape(length // LANES, LANES).astype(np.float32)
    turn = np.tile(phases(short, short, length, -1), (1, 2))
    turn = np.stack([turn.real, turn.imag]).astype(np.float32)
    pair = np.eye(2)
    shift = high_low(np.concatenate(side_by_side(phases(short, short, CONTRIB, -1)), axis=1))
    outer_minus = from_left(phases(short, outer, blocks, -1))
    inner_minus = from_right(np.kron(pair, phases(short, short, CONTRIB, -1)))
    piece = from_right(phases(short, short, CONTRIB, 1)) * CONTRIB**-0.5
    return dict(
        plain=stack_tables(dict(window=window, real=turn[0], imag=turn[1])),
        paired=stack_pairs(
            dict(
                shift=shift,
                outer=high_low(outer_minus),
                inner=high_low(inner_minus),
                piece=high_low(piece),
            )
        ),
        window=window,
        turn=turn,
        shift=shift,
        inner_plus=high_low(from_right(np.kron(pair, phases(short, short, CONTRIB, 1)))),
        outer_plus=high_low(from_left(phases(outer, short, blocks, 1))),
        partial=high_low(from_right(phases(short, short, CONTRIB, -1)).T * CONTRIB**-0.5),
        grid_turn=side_by_side(phases(np.arange(FACET_ROWS), short, SUBGRID, -1)).astype(
            np.float32
        ),
        model=high_low(from_right(phases(short, short, CONTRIB, -1)) * SUBGRID**-0.5),
        back=high_low(from_right(phases(short, short, CONTRIB, 1)) * SUBGRID**-0.5),
    )


def split(values):
    high = values.astype(BF16)
    return high, (values - high.astype(F32)).astype(BF16)


def dot(left, right, dims=((1,), (0,))):
    return lax.dot_general(left, right, (dims, ((), ())), preferred_element_type=F32)


def times_table(values, table, dims=((1,), (0,))):
    high, low = split(values)
    return dot(high, table[0], dims) + dot(low, table[0], dims) + dot(high, table[1], dims)


def table_times(table, values, dims=((1,), (0,))):
    high, low = split(values)
    return dot(table[0], high, dims) + dot(table[0], low, dims) + dot(table[1], high, dims)


def iota(shape, dimension):
    return lax.broadcasted_iota(jnp.int32, shape, dimension)


def over(values, size):
    return lax.shift_right_logical(values, jnp.full_like(values, size.bit_length() - 1))


def within(values, size):
    return values & (size - 1)


def swap_halves(values):
    return pltpu.roll(values, HALF, 1)


def table_at(ref, place):
    begin, rows, blocks = place
    parts = [ref[begin + i * rows : begin + (i + 1) * rows, :] for i in range(blocks)]
    return parts[0] if blocks == 1 else jnp.concatenate(parts, axis=1)


def offsets_on_lanes(offsets_ref, columns, order):
    fronts, owners = offsets_ref.shape
    groups = owners // FACET_ROWS
    own = lax.axis_index("group")
    begins = []
    for step in range(groups):
        group = own + step
        begins.append(jnp.where(group >= groups, group - groups, group) * FACET_ROWS)
    spread = iota((1, fronts * owners * columns), 1)
    place_of = over(spread, columns)
    for place in range(fronts * owners):
        t, step, spot = place % fronts, place // fronts % groups, place // (fronts * groups)
        member = order[spot]
        spread = jnp.where(place_of == place, offsets_ref[t, begins[step] + member], spread)
    return spread


def shift_rows(residue, table):
    pick = jnp.where(iota((CONTRIB, residue.shape[1]), 0) == residue, 1.0, 0.0).T.astype(BF16)
    rows = dot(pick, table[0]) + dot(pick, table[1])
    return rows[:, :LANES], rows[:, LANES:]


def one_hot(shape, targets):
    return jnp.where(iota(shape, 0) == targets, 1.0, 0.0).astype(BF16)


def turned_eighths(values, rotation):
    sign = jnp.where(iota(values[0].shape, 1) < HALF, -rotation, rotation).astype(F32)

    def quarter_turn(value):
        return swap_halves(value) * sign

    def four(a, b, c, d):
        even_sum, even_diff = a + c, a - c
        odd_sum, odd_diff = b + d, quarter_turn(b - d)
        return even_sum + odd_sum, even_diff + odd_diff, even_sum - odd_sum, even_diff - odd_diff

    even = four(*values[0::2])
    odd = four(*values[1::2])
    root = math.sqrt(0.5)
    turned = (
        odd[0],
        (odd[1] + quarter_turn(odd[1])) * root,
        quarter_turn(odd[2]),
        (quarter_turn(odd[3]) - odd[3]) * root,
    )
    return [e + o for e, o in zip(even, turned)] + [e - o for e, o in zip(even, turned)]


def pack_samples(cells_ref, values_ref, weights_ref, flags_ref, out_ref):
    for t in range(cells_ref.shape[0]):
        rows = [
            cells_ref[t, 0:1, :].astype(F32) * SUBGRID + cells_ref[t, 1:2, :].astype(F32),
            weights_ref[t] * flags_ref[t].astype(F32),
            values_ref[t],
        ]
        out_ref[4 * t : 4 * t + 4, :] = jnp.concatenate(rows, axis=0)


def start_all(sources, targets, semaphores):
    copies = [
        pltpu.make_async_copy(source, target, semaphores.at[i])
        for i, (source, target) in enumerate(zip(sources, targets))
    ]
    for copy in copies:
        copy.start()
    return copies


def predict(spread, copies, strips_ref, plain_ref, paired_ref, held_refs, out_ref, plain, paired):
    columns, length = strips_ref.shape[1:]
    groups = length // LANES
    pairs = columns // 2
    blocks = length // CONTRIB
    width = spread.shape[1]
    first_block, residue = over(spread, CONTRIB), within(spread, CONTRIB)
    base = within(iota(spread.shape, 1), columns) * blocks
    shape = (columns * blocks, width)
    pick_inside = one_hot(shape, base + first_block)
    pick_beyond = one_hot(shape, base + within(first_block + 1, blocks))
    for copy in copies:
        copy.wait()

    def pair_at(name):
        return [table_at(paired_ref, paired[name, i]) for i in range(2)]

    window = table_at(plain_ref, plain["window"])
    turn_real, turn_imag = table_at(plain_ref, plain["real"]), table_at(plain_ref, plain["imag"])
    low_half = iota((groups, LANES), 1) < HALF
    sections = []
    for part, held in enumerate(held_refs):
        for group in range(groups):
            held[group * columns : (group + 1) * columns, :] = strips_ref[
                part, :, group * LANES : (group + 1) * LANES
            ]
        even, odd = [], []
        for pair in range(pairs):
            first = held[pl.ds(2 * pair, groups, stride=columns), :] * window
            second = held[pl.ds(2 * pair + 1, groups, stride=columns), :] * window
            even.append(jnp.where(low_half, first, swap_halves(second)))
            odd.append(jnp.where(low_half, swap_halves(first), second))
        sections += [jnp.concatenate(even, axis=1), jnp.concatenate(odd, axis=1)]
    section = table_times(pair_at("outer"), jnp.concatenate(sections, axis=0))
    turned = []
    for pair in range(pairs):
        lanes = slice(pair * LANES, (pair + 1) * LANES)
        real, imag = section[:CONTRIB, lanes], section[CONTRIB:, lanes]
        turned.append(
            jnp.concatenate(
                [real * turn_real - imag * turn_imag, real * turn_imag + imag * turn_real],
                axis=1,
            )
        )
    inner = times_table(jnp.concatenate(turned, axis=0), pair_at("inner"))
    spectrum = jnp.concatenate(
        [
            jnp.concatenate(
                [
                    inner[pair * CONTRIB : (pair + 1) * CONTRIB, part * LANES : (part + 1) * LANES]
                    for pair in range(pairs)
                ],
                axis=1,
            )
            for part in range(2)
        ],
        axis=0,
    )
    high, low = split(spectrum)
    inside = dot(high, pick_inside) + dot(low, pick_inside)
    beyond = dot(high, pick_beyond) + dot(low, pick_beyond)
    kappa = within(iota((2 * CONTRIB, width), 0), CONTRIB)
    cutout = jnp.where(kappa >= residue, inside, beyond)
    piece = times_table(cutout.T, pair_at("piece"))
    straight, crossed = shift_rows(residue, pair_at("shift"))
    out_ref[...] = (piece * straight + swap_halves(piece) * crossed).astype(BF16)


def in_first_half():
    return 2 * lax.axis_index("group") < lax.axis_size("group")


def early_kernel(
    offsets, cells, values, weights, flags, strips, plain_table, paired_table,
    out_ref, packed_ref, places_ref,
    offsets_ref, cells_ref, values_ref, weights_ref, flags_ref, strips_ref, plain_ref, paired_ref,
    real_ref, imag_ref, small_semaphores, semaphores, *, plain, paired, share,
):
    columns = strips_ref.shape[1]
    small = start_all(
        (offsets, cells, values, weights, flags),
        (offsets_ref, cells_ref, values_ref, weights_ref, flags_ref),
        small_semaphores,
    )

    def large():
        sources, targets = (strips, plain_table, paired_table), (strips_ref, plain_ref, paired_ref)
        return [
            pltpu.make_async_copy(source, target, semaphores.at[i])
            for i, (source, target) in enumerate(zip(sources, targets))
        ]

    @pl.when(in_first_half())
    def _():
        for copy in large():
            copy.start()

    for copy in small:
        copy.wait()
    for t in range(cells_ref.shape[0]):
        rows = [
            cells_ref[t, 0:1, :].astype(F32) * SUBGRID + cells_ref[t, 1:2, :].astype(F32),
            weights_ref[t] * flags_ref[t].astype(F32),
            values_ref[t],
        ]
        packed_ref[4 * t : 4 * t + 4, :] = jnp.concatenate(rows, axis=0)
    places_ref[...] = offsets_on_lanes(offsets_ref, share, RETURN_ORDER)

    @pl.when(in_first_half())
    def _():
        spread = offsets_on_lanes(offsets_ref, columns, SEND_ORDER)
        predict(
            spread, large(), strips_ref, plain_ref, paired_ref, (real_ref, imag_ref), out_ref,
            plain, paired,
        )


def late_kernel(
    early_ref, offsets, strips, plain_table, paired_table, out_ref,
    offsets_ref, strips_ref, plain_ref, paired_ref, real_ref, imag_ref, semaphores,
    *, plain, paired,
):
    @pl.when(in_first_half())
    def _():
        out_ref[...] = early_ref[...]

    @pl.when(jnp.logical_not(in_first_half()))
    def _():
        copies = start_all(
            (offsets, strips, plain_table, paired_table),
            (offsets_ref, strips_ref, plain_ref, paired_ref),
            semaphores,
        )
        copies[0].wait()
        spread = offsets_on_lanes(offsets_ref, strips_ref.shape[1], SEND_ORDER)
        predict(
            spread, copies[1:], strips_ref, plain_ref, paired_ref, (real_ref, imag_ref), out_ref,
            plain, paired,
        )


def prepare_kernel(places_ref, shift_ref, *refs, columns, share, blocks):
    samples_refs, outs = refs[:-5], refs[-5:]
    value_ref, weight_ref, put_ref, straight_ref, crossed_ref = outs
    fronts, samples = samples_refs[0].shape[0] // 4, samples_refs[0].shape[1]
    own = lax.axis_index("group")
    depth = FACET_ROWS * columns
    for spot in range(len(samples_refs) * fronts):
        step, t = spot // fronts, spot % fronts
        sample = samples_refs[step][4 * t : 4 * t + 4, :]
        cell = sample[0:1, :].astype(jnp.int32)
        row, col = over(cell, SUBGRID) - own * columns, within(cell, SUBGRID)
        inside = (row >= 0) & (row < columns)
        target = jnp.where(inside, within(col, FACET_ROWS) * columns + row, -1)
        pick = one_hot((depth, samples), target)
        mask = iota((HALF, samples), 0) == over(col, FACET_ROWS)
        factor = sample[1:2, :]
        highs, lows = [], []
        for term in (factor * sample[2:3, :], factor * sample[3:4, :], factor):
            high = term.astype(BF16).astype(F32)
            highs.append(jnp.where(mask, high, 0.0).astype(BF16))
            lows.append(jnp.where(mask, term - high, 0.0).astype(BF16))
        highs, lows = highs + highs[2:], lows + lows[2:]
        grid = dot(pick, jnp.concatenate(highs, axis=0), ((1,), (1,))) + dot(
            pick, jnp.concatenate(lows, axis=0), ((1,), (1,))
        )
        rows = slice(spot * depth, (spot + 1) * depth)
        value_ref[rows, :] = grid[:, :LANES]
        weight_ref[rows, :] = grid[:, LANES:]
    spread = places_ref[...]
    first_block, residue = over(spread, CONTRIB), within(spread, CONTRIB)
    straight_ref[...], crossed_ref[...] = shift_rows(residue, shift_ref)
    base = within(iota(spread.shape, 1), share) * blocks
    targets = jnp.concatenate([base + first_block, base + within(first_block + 1, blocks)], axis=1)
    put_ref[...] = one_hot(put_ref.shape, targets)


def subgrid_kernel(
    pieces_ref, value_ref, weight_ref, turn_ref, model_ref, back_ref, out_ref, held_ref,
    *, columns, bands,
):
    rows = pieces_ref.shape[0] // FACET_ROWS
    spots = range(rows // columns)
    depth = FACET_ROWS * columns
    share = columns // bands
    pieces = pieces_ref[...].astype(F32)
    sky = turned_eighths(
        [
            pieces[spot * rows : (spot + 1) * rows, :]
            for spot in (SEND_ORDER.index(i) for i in range(FACET_ROWS))
        ],
        -1.0,
    )
    sky = [
        value * turn_ref[0, i : i + 1, :] + swap_halves(value) * turn_ref[1, i : i + 1, :]
        for i, value in enumerate(sky)
    ]
    stacked = jnp.concatenate(
        [value[spot * columns : (spot + 1) * columns, :] for spot in spots for value in sky],
        axis=0,
    )
    grid = value_ref[...] - weight_ref[...] * times_table(stacked, model_ref)
    back = times_table(grid, back_ref)
    lines = []
    for i in range(FACET_ROWS):
        value = jnp.concatenate(
            [
                back[spot * depth + i * columns : spot * depth + (i + 1) * columns, :]
                for spot in spots
            ],
            axis=0,
        )
        lines.append(
            value * turn_ref[0, i : i + 1, :] - swap_halves(value) * turn_ref[1, i : i + 1, :]
        )
    lines = turned_eighths(lines, 1.0)
    for i in range(FACET_ROWS):
        for spot in spots:
            for b in range(bands):
                source = spot * columns + b * share
                place = b * FACET_ROWS + RETURN_ORDER.index(i)
                target = (place * len(spots) + spot) * share
                held_ref[target : target + share, :] = lines[i][source : source + share, :]
    out_ref[...] = held_ref[...].astype(BF16)


def return_kernel(
    places_ref, pieces_ref, straight_ref, crossed_ref, put_ref, window_ref, turn_ref, partial_ref,
    inner_ref, outer_ref, out_ref, *line_refs, bands,
):
    columns, _, length = out_ref.shape
    blocks = length // CONTRIB
    groups = length // LANES
    pairs = (columns + 1) // 2
    width = pieces_ref.shape[0] // bands
    summed = pieces_ref[0:width, :].astype(F32)
    for b in range(1, bands):
        summed += pieces_ref[b * width : (b + 1) * width, :].astype(F32)
    summed = summed * straight_ref[...] - swap_halves(summed) * crossed_ref[...]
    residues = table_times(partial_ref, summed, ((1,), (1,)))
    kappa = within(iota((2 * CONTRIB, width), 0), CONTRIB)
    inside = kappa >= within(places_ref[...], CONTRIB)
    both = jnp.concatenate(
        [jnp.where(inside, residues, 0.0), jnp.where(inside, 0.0, residues)], axis=1
    )
    put = put_ref[...]
    high, low = split(both)
    spectrum = dot(high, put, ((1,), (1,))) + dot(low, put, ((1,), (1,)))
    inner = times_table(
        jnp.concatenate(
            [
                jnp.concatenate(
                    [
                        spectrum[:CONTRIB, pair * LANES : (pair + 1) * LANES],
                        spectrum[CONTRIB:, pair * LANES : (pair + 1) * LANES],
                    ],
                    axis=1,
                )
                for pair in range(pairs)
            ],
            axis=0,
        ),
        inner_ref,
    )
    reals, imags = [], []
    for pair in range(pairs):
        rows = slice(pair * CONTRIB, (pair + 1) * CONTRIB)
        real, imag = inner[rows, :LANES], inner[rows, LANES:]
        reals.append(real * turn_ref[0] + imag * turn_ref[1])
        imags.append(imag * turn_ref[0] - real * turn_ref[1])
    lines = table_times(
        outer_ref,
        jnp.concatenate(
            [jnp.concatenate(reals, axis=1), jnp.concatenate(imags, axis=1)], axis=0
        ),
    )
    window = window_ref[...]
    low_half = iota((groups, LANES), 1) < HALF
    for part in range(2):
        for pair in range(pairs):
            lanes = slice(pair * LANES, (pair + 1) * LANES)
            begin = part * blocks
            even = lines[begin : begin + groups, lanes]
            odd = lines[begin + groups : begin + blocks, lanes]
            line_refs[2 * pair][pl.ds(part, groups, stride=2), :] = (
                jnp.where(low_half, even, swap_halves(odd)) * window
            )
            if 2 * pair + 1 < columns:
                line_refs[2 * pair + 1][pl.ds(part, groups, stride=2), :] = (
                    jnp.where(low_half, swap_halves(even), odd) * window
                )
    for column in range(columns):
        for group in range(groups):
            out_ref[column, :, group * LANES : (group + 1) * LANES] = line_refs[column][
                2 * group : 2 * group + 2, :
            ]


def kernel_call(kernel, name, out_shape, spaces, scratch, *operands, flops=0):
    return pl.pallas_call(
        kernel,
        out_shape=out_shape,
        in_specs=[pl.BlockSpec(memory_space=space) for space in spaces],
        out_specs=jax.tree.map(lambda _: pl.BlockSpec(memory_space=pltpu.VMEM), out_shape),
        scratch_shapes=scratch,
        compiler_params=pltpu.CompilerParams(vmem_limit_bytes=VMEM_LIMIT),
        cost_estimate=pl.CostEstimate(flops=flops, bytes_accessed=0, transcendentals=0)
        if flops
        else None,
        name=name,
    )(*operands)


def wide(rows):
    return pltpu.VMEM((rows, LANES), F32)


def local(groups, bands, strips, offsets, cells, values, weights, flags):
    columns, length = strips.shape[-2:]
    fronts = offsets.shape[0]
    share = columns // bands
    facets = groups * FACET_ROWS
    rows = facets * fronts * columns
    width = facets * fronts * share
    made = tables(length)
    plain, plain_places = made.pop("plain")
    paired, paired_places = made.pop("paired")
    made = {key: jnp.asarray(value) for key, value in made.items()}
    held = length // LANES * columns
    small = [offsets, cells[0, :, 0], values[0, :, 0], weights[0], flags[0]]
    large = [strips[0, 0], jnp.asarray(plain), jnp.asarray(paired)]

    def landing(arrays):
        return [
            (pltpu.SMEM if array is offsets else pltpu.VMEM)(array.shape, array.dtype)
            for array in arrays
        ]

    def in_hbm(arrays):
        return [pltpu.with_memory_space_constraint(array, pltpu.HBM) for array in arrays]

    def semaphores(count):
        return pltpu.SemaphoreType.DMA((count,))

    early, packed, places = kernel_call(
        functools.partial(early_kernel, plain=plain_places, paired=paired_places, share=share),
        "early",
        [
            jax.ShapeDtypeStruct((rows, LANES), BF16),
            jax.ShapeDtypeStruct((4 * fronts, cells.shape[-1]), F32),
            jax.ShapeDtypeStruct((1, width), jnp.int32),
        ],
        [pltpu.HBM] * 8,
        landing(small + large) + [wide(held)] * 2 + [semaphores(5), semaphores(3)],
        *in_hbm(small + large),
    )
    pieces = kernel_call(
        functools.partial(late_kernel, plain=plain_places, paired=paired_places), "late",
        jax.ShapeDtypeStruct((rows, LANES), BF16), [pltpu.VMEM] + [pltpu.HBM] * 4,
        landing([offsets] + large) + [wide(held)] * 2 + [semaphores(4)],
        early, *in_hbm([offsets] + large), flops=LATE_FLOPS,
    )
    gathered = [packed]
    for step in range(1, groups):
        moves = [((group + step) % groups, group) for group in range(groups)]
        gathered.append(lax.ppermute(packed, "group", moves))
    arrived = lax.all_to_all(
        pieces, "member", split_axis=0, concat_axis=0, tiled=True,
        axis_index_groups=[list(SEND_ORDER)],
    )
    blocks = length // CONTRIB
    value, weight, put, straight, crossed = kernel_call(
        functools.partial(prepare_kernel, columns=columns, share=share, blocks=blocks), "prepare",
        [jax.ShapeDtypeStruct((rows, LANES), F32)] * 2
        + [jax.ShapeDtypeStruct(((share + share % 2) * blocks, 2 * width), BF16)]
        + [jax.ShapeDtypeStruct((width, LANES), F32)] * 2,
        [pltpu.VMEM] * (2 + len(gathered)), [],
        places, made["shift"], *gathered, flops=PREPARE_FLOPS,
    )
    returned = kernel_call(
        functools.partial(subgrid_kernel, columns=columns, bands=bands), "subgrid",
        jax.ShapeDtypeStruct((rows, LANES), BF16), [pltpu.VMEM] * 6, [wide(rows)],
        arrived, value, weight, made["grid_turn"], made["model"], made["back"],
    )
    delivered = lax.all_to_all(
        returned, ("band", "member"), split_axis=0, concat_axis=0, tiled=True,
        axis_index_groups=[
            [b * FACET_ROWS + member for b in range(bands) for member in RETURN_ORDER]
        ],
    )
    lines = kernel_call(
        functools.partial(return_kernel, bands=bands), "lines",
        jax.ShapeDtypeStruct((share, 2, length), F32), [pltpu.VMEM] * 10,
        [wide(2 * length // LANES)] * share,
        places, delivered, straight, crossed, put, made["window"], made["turn"],
        made["partial"], made["inner_plus"], made["outer_plus"],
    )
    return lines[None]


def solution(mesh):
    bands = mesh.shape["band"]
    groups = mesh.shape["facet"] // FACET_ROWS
    split_mesh = Mesh(
        mesh.devices.reshape(groups, FACET_ROWS, bands), ("group", "member", "band")
    )
    facet = ("group", "member")
    placed = (
        P("band", facet, None, None, None),
        P(),
        P("band", None, facet, None, None),
        P("band", None, facet, None, None),
        P("band", None, facet, None),
        P("band", None, facet, None),
    )
    return jax.shard_map(
        functools.partial(local, groups, bands),
        mesh=split_mesh,
        in_specs=placed,
        out_specs=P(facet, "band", None, None),
        check_vma=False,
    )
```

```python
import functools
import math

import jax
import jax.numpy as jnp
import ml_dtypes
import numpy as np
from jax import lax
from jax.experimental import pallas as pl
from jax.experimental.pallas import tpu as pltpu
from jax.sharding import Mesh
from jax.sharding import PartitionSpec as P

CONTRIB = 64
FACET_ROWS = 8
SUBGRID = FACET_ROWS * CONTRIB
SEND_ORDER = tuple(reversed(range(FACET_ROWS)))
RETURN_ORDER = tuple(reversed(range(FACET_ROWS)))
LANES = 128
HALF = LANES // 2
LATE_FLOPS = 10**10
PREPARE_FLOPS = 2 * 10**10
VMEM_LIMIT = 48 * 1024 * 1024
F32 = jnp.float32
BF16 = jnp.bfloat16


def phases(rows, cols, length, rotation):
    product = np.outer(rows, cols) % length
    return np.exp(rotation * 2j * np.pi * product / length)


def from_left(matrix):
    return np.block([[matrix.real, -matrix.imag], [matrix.imag, matrix.real]])


def from_right(matrix):
    return np.block([[matrix.real, matrix.imag], [-matrix.imag, matrix.real]])


def high_low(table):
    high = table.astype(ml_dtypes.bfloat16)
    low = (table - high.astype(np.float64)).astype(ml_dtypes.bfloat16)
    return np.stack([high, low])


def side_by_side(values):
    straight = np.concatenate([values.real, values.real], axis=-1)
    crossed = np.concatenate([-values.imag, values.imag], axis=-1)
    return np.stack([straight, crossed])


def stack_tables(named):
    places, blocks, begin = {}, [], 0
    for name, table in named.items():
        count = table.shape[1] // LANES
        places[name] = (begin, table.shape[0], count)
        blocks += [table[:, i * LANES : (i + 1) * LANES] for i in range(count)]
        begin += table.shape[0] * count
    return np.concatenate(blocks, axis=0), places


def stack_pairs(named):
    return stack_tables(
        {(name, i): table for name, pair in named.items() for i, table in enumerate(pair)}
    )


def tables(length):
    blocks = length // CONTRIB
    short = np.arange(CONTRIB)
    outer = np.concatenate([np.arange(0, blocks, 2), np.arange(1, blocks, 2)])
    window = 1.0 + 0.5 * np.cos(np.arange(length) * (2.0 * math.pi / length))
    window = (window * length**-0.5).reshape(length // LANES, LANES).astype(np.float32)
    turn = np.tile(phases(short, short, length, -1), (1, 2))
    turn = np.stack([turn.real, turn.imag]).astype(np.float32)
    pair = np.eye(2)
    shift = high_low(np.concatenate(side_by_side(phases(short, short, CONTRIB, -1)), axis=1))
    outer_minus = from_left(phases(short, outer, blocks, -1))
    inner_minus = from_right(np.kron(pair, phases(short, short, CONTRIB, -1)))
    piece = from_right(phases(short, short, CONTRIB, 1)) * CONTRIB**-0.5
    return dict(
        plain=stack_tables(dict(window=window, real=turn[0], imag=turn[1])),
        paired=stack_pairs(
            dict(
                shift=shift,
                outer=high_low(outer_minus),
                inner=high_low(inner_minus),
                piece=high_low(piece),
            )
        ),
        window=window,
        turn=turn,
        shift=shift,
        inner_plus=high_low(from_right(np.kron(pair, phases(short, short, CONTRIB, 1)))),
        outer_plus=high_low(from_left(phases(outer, short, blocks, 1))),
        partial=high_low(from_right(phases(short, short, CONTRIB, -1)).T * CONTRIB**-0.5),
        grid_turn=side_by_side(phases(np.arange(FACET_ROWS), short, SUBGRID, -1)).astype(
            np.float32
        ),
        model=high_low(from_right(phases(short, short, CONTRIB, -1)) * SUBGRID**-0.5),
        back=high_low(from_right(phases(short, short, CONTRIB, 1)) * SUBGRID**-0.5),
    )


def split(values):
    high = values.astype(BF16)
    return high, (values - high.astype(F32)).astype(BF16)


def dot(left, right, dims=((1,), (0,))):
    return lax.dot_general(left, right, (dims, ((), ())), preferred_element_type=F32)


def times_table(values, table, dims=((1,), (0,))):
    high, low = split(values)
    return dot(high, table[0], dims) + dot(low, table[0], dims) + dot(high, table[1], dims)


def table_times(table, values, dims=((1,), (0,))):
    high, low = split(values)
    return dot(table[0], high, dims) + dot(table[0], low, dims) + dot(table[1], high, dims)


def iota(shape, dimension):
    return lax.broadcasted_iota(jnp.int32, shape, dimension)


def over(values, size):
    return lax.shift_right_logical(values, jnp.full_like(values, size.bit_length() - 1))


def within(values, size):
    return values & (size - 1)


def swap_halves(values):
    return pltpu.roll(values, HALF, 1)


def table_at(ref, place):
    begin, rows, blocks = place
    parts = [ref[begin + i * rows : begin + (i + 1) * rows, :] for i in range(blocks)]
    return parts[0] if blocks == 1 else jnp.concatenate(parts, axis=1)


def offsets_on_lanes(offsets_ref, columns, order):
    fronts, owners = offsets_ref.shape
    groups = owners // FACET_ROWS
    own = lax.axis_index("group")
    begins = []
    for step in range(groups):
        group = own + step
        begins.append(jnp.where(group >= groups, group - groups, group) * FACET_ROWS)
    spread = iota((1, fronts * owners * columns), 1)
    place_of = over(spread, columns)
    for place in range(fronts * owners):
        t, step, spot = place % fronts, place // fronts % groups, place // (fronts * groups)
        member = order[spot]
        spread = jnp.where(place_of == place, offsets_ref[t, begins[step] + member], spread)
    return spread


def shift_rows(residue, table):
    pick = jnp.where(iota((CONTRIB, residue.shape[1]), 0) == residue, 1.0, 0.0).T.astype(BF16)
    rows = dot(pick, table[0]) + dot(pick, table[1])
    return rows[:, :LANES], rows[:, LANES:]


def one_hot(shape, targets):
    return jnp.where(iota(shape, 0) == targets, 1.0, 0.0).astype(BF16)


def turned_eighths(values, rotation):
    sign = jnp.where(iota(values[0].shape, 1) < HALF, -rotation, rotation).astype(F32)

    def quarter_turn(value):
        return swap_halves(value) * sign

    def four(a, b, c, d):
        even_sum, even_diff = a + c, a - c
        odd_sum, odd_diff = b + d, quarter_turn(b - d)
        return even_sum + odd_sum, even_diff + odd_diff, even_sum - odd_sum, even_diff - odd_diff

    even = four(*values[0::2])
    odd = four(*values[1::2])
    root = math.sqrt(0.5)
    turned = (
        odd[0],
        (odd[1] + quarter_turn(odd[1])) * root,
        quarter_turn(odd[2]),
        (quarter_turn(odd[3]) - odd[3]) * root,
    )
    return [e + o for e, o in zip(even, turned)] + [e - o for e, o in zip(even, turned)]


def pack_samples(cells_ref, values_ref, weights_ref, flags_ref, out_ref):
    for t in range(cells_ref.shape[0]):
        rows = [
            cells_ref[t, 0:1, :].astype(F32) * SUBGRID + cells_ref[t, 1:2, :].astype(F32),
            weights_ref[t] * flags_ref[t].astype(F32),
            values_ref[t],
        ]
        out_ref[4 * t : 4 * t + 4, :] = jnp.concatenate(rows, axis=0)


def start_all(sources, targets, semaphores):
    copies = [
        pltpu.make_async_copy(source, target, semaphores.at[i])
        for i, (source, target) in enumerate(zip(sources, targets))
    ]
    for copy in copies:
        copy.start()
    return copies


def predict(spread, copies, strips_ref, plain_ref, paired_ref, held_refs, out_ref, plain, paired):
    columns, length = strips_ref.shape[1:]
    groups = length // LANES
    pairs = columns // 2
    blocks = length // CONTRIB
    width = spread.shape[1]
    first_block, residue = over(spread, CONTRIB), within(spread, CONTRIB)
    base = within(iota(spread.shape, 1), columns) * blocks
    shape = (columns * blocks, width)
    pick_inside = one_hot(shape, base + first_block)
    pick_beyond = one_hot(shape, base + within(first_block + 1, blocks))
    for copy in copies:
        copy.wait()

    def pair_at(name):
        return [table_at(paired_ref, paired[name, i]) for i in range(2)]

    window = table_at(plain_ref, plain["window"])
    turn_real, turn_imag = table_at(plain_ref, plain["real"]), table_at(plain_ref, plain["imag"])
    low_half = iota((groups, LANES), 1) < HALF
    sections = []
    for part, held in enumerate(held_refs):
        for group in range(groups):
            held[group * columns : (group + 1) * columns, :] = strips_ref[
                part, :, group * LANES : (group + 1) * LANES
            ]
        even, odd = [], []
        for pair in range(pairs):
            first = held[pl.ds(2 * pair, groups, stride=columns), :] * window
            second = held[pl.ds(2 * pair + 1, groups, stride=columns), :] * window
            even.append(jnp.where(low_half, first, swap_halves(second)))
            odd.append(jnp.where(low_half, swap_halves(first), second))
        sections += [jnp.concatenate(even, axis=1), jnp.concatenate(odd, axis=1)]
    section = table_times(pair_at("outer"), jnp.concatenate(sections, axis=0))
    turned = []
    for pair in range(pairs):
        lanes = slice(pair * LANES, (pair + 1) * LANES)
        real, imag = section[:CONTRIB, lanes], section[CONTRIB:, lanes]
        turned.append(
            jnp.concatenate(
                [real * turn_real - imag * turn_imag, real * turn_imag + imag * turn_real],
                axis=1,
            )
        )
    inner = times_table(jnp.concatenate(turned, axis=0), pair_at("inner"))
    spectrum = jnp.concatenate(
        [
            jnp.concatenate(
                [
                    inner[pair * CONTRIB : (pair + 1) * CONTRIB, part * LANES : (part + 1) * LANES]
                    for pair in range(pairs)
                ],
                axis=1,
            )
            for part in range(2)
        ],
        axis=0,
    )
    high, low = split(spectrum)
    inside = dot(high, pick_inside) + dot(low, pick_inside)
    beyond = dot(high, pick_beyond) + dot(low, pick_beyond)
    kappa = within(iota((2 * CONTRIB, width), 0), CONTRIB)
    cutout = jnp.where(kappa >= residue, inside, beyond)
    piece = times_table(cutout.T, pair_at("piece"))
    straight, crossed = shift_rows(residue, pair_at("shift"))
    out_ref[...] = (piece * straight + swap_halves(piece) * crossed).astype(BF16)


def in_first_half():
    return 2 * lax.axis_index("group") < lax.axis_size("group")


def early_kernel(
    offsets, cells, values, weights, flags, strips, plain_table, paired_table,
    out_ref, packed_ref, places_ref,
    offsets_ref, cells_ref, values_ref, weights_ref, flags_ref, strips_ref, plain_ref, paired_ref,
    real_ref, imag_ref, small_semaphores, semaphores, *, plain, paired, share,
):
    columns = strips_ref.shape[1]
    small = start_all(
        (offsets, cells, values, weights, flags),
        (offsets_ref, cells_ref, values_ref, weights_ref, flags_ref),
        small_semaphores,
    )

    def large():
        sources, targets = (strips, plain_table, paired_table), (strips_ref, plain_ref, paired_ref)
        return [
            pltpu.make_async_copy(source, target, semaphores.at[i])
            for i, (source, target) in enumerate(zip(sources, targets))
        ]

    @pl.when(in_first_half())
    def _():
        for copy in large():
            copy.start()

    for copy in small:
        copy.wait()
    for t in range(cells_ref.shape[0]):
        rows = [
            cells_ref[t, 0:1, :].astype(F32) * SUBGRID + cells_ref[t, 1:2, :].astype(F32),
            weights_ref[t] * flags_ref[t].astype(F32),
            values_ref[t],
        ]
        packed_ref[4 * t : 4 * t + 4, :] = jnp.concatenate(rows, axis=0)
    places_ref[...] = offsets_on_lanes(offsets_ref, share, RETURN_ORDER)

    @pl.when(in_first_half())
    def _():
        spread = offsets_on_lanes(offsets_ref, columns, SEND_ORDER)
        predict(
            spread, large(), strips_ref, plain_ref, paired_ref, (real_ref, imag_ref), out_ref,
            plain, paired,
        )


def late_kernel(
    early_ref, offsets, strips, plain_table, paired_table, out_ref,
    offsets_ref, strips_ref, plain_ref, paired_ref, real_ref, imag_ref, semaphores,
    *, plain, paired,
):
    @pl.when(in_first_half())
    def _():
        out_ref[...] = early_ref[...]

    @pl.when(jnp.logical_not(in_first_half()))
    def _():
        copies = start_all(
            (offsets, strips, plain_table, paired_table),
            (offsets_ref, strips_ref, plain_ref, paired_ref),
            semaphores,
        )
        copies[0].wait()
        spread = offsets_on_lanes(offsets_ref, strips_ref.shape[1], SEND_ORDER)
        predict(
            spread, copies[1:], strips_ref, plain_ref, paired_ref, (real_ref, imag_ref), out_ref,
            plain, paired,
        )


def prepare_kernel(places_ref, shift_ref, *refs, columns, share, blocks):
    samples_refs, outs = refs[:-5], refs[-5:]
    value_ref, weight_ref, put_ref, straight_ref, crossed_ref = outs
    fronts, samples = samples_refs[0].shape[0] // 4, samples_refs[0].shape[1]
    own = lax.axis_index("group")
    depth = FACET_ROWS * columns
    for spot in range(len(samples_refs) * fronts):
        step, t = spot // fronts, spot % fronts
        sample = samples_refs[step][4 * t : 4 * t + 4, :]
        cell = sample[0:1, :].astype(jnp.int32)
        row, col = over(cell, SUBGRID) - own * columns, within(cell, SUBGRID)
        inside = (row >= 0) & (row < columns)
        target = jnp.where(inside, within(col, FACET_ROWS) * columns + row, -1)
        pick = one_hot((depth, samples), target)
        mask = iota((HALF, samples), 0) == over(col, FACET_ROWS)
        factor = sample[1:2, :]
        highs, lows = [], []
        for term in (factor * sample[2:3, :], factor * sample[3:4, :], factor):
            high = term.astype(BF16).astype(F32)
            highs.append(jnp.where(mask, high, 0.0).astype(BF16))
            lows.append(jnp.where(mask, term - high, 0.0).astype(BF16))
        highs, lows = highs + highs[2:], lows + lows[2:]
        grid = dot(pick, jnp.concatenate(highs, axis=0), ((1,), (1,))) + dot(
            pick, jnp.concatenate(lows, axis=0), ((1,), (1,))
        )
        rows = slice(spot * depth, (spot + 1) * depth)
        value_ref[rows, :] = grid[:, :LANES]
        weight_ref[rows, :] = grid[:, LANES:]
    spread = places_ref[...]
    first_block, residue = over(spread, CONTRIB), within(spread, CONTRIB)
    straight_ref[...], crossed_ref[...] = shift_rows(residue, shift_ref)
    base = within(iota(spread.shape, 1), share) * blocks
    targets = jnp.concatenate([base + first_block, base + within(first_block + 1, blocks)], axis=1)
    put_ref[...] = one_hot(put_ref.shape, targets)


def subgrid_kernel(
    pieces_ref, value_ref, weight_ref, turn_ref, model_ref, back_ref, out_ref, held_ref,
    *, columns, bands,
):
    rows = pieces_ref.shape[0] // FACET_ROWS
    spots = range(rows // columns)
    depth = FACET_ROWS * columns
    share = columns // bands
    pieces = pieces_ref[...].astype(F32)
    sky = turned_eighths(
        [
            pieces[spot * rows : (spot + 1) * rows, :]
            for spot in (SEND_ORDER.index(i) for i in range(FACET_ROWS))
        ],
        -1.0,
    )
    sky = [
        value * turn_ref[0, i : i + 1, :] + swap_halves(value) * turn_ref[1, i : i + 1, :]
        for i, value in enumerate(sky)
    ]
    stacked = jnp.concatenate(
        [value[spot * columns : (spot + 1) * columns, :] for spot in spots for value in sky],
        axis=0,
    )
    grid = value_ref[...] - weight_ref[...] * times_table(stacked, model_ref)
    back = times_table(grid, back_ref)
    lines = []
    for i in range(FACET_ROWS):
        value = jnp.concatenate(
            [
                back[spot * depth + i * columns : spot * depth + (i + 1) * columns, :]
                for spot in spots
            ],
            axis=0,
        )
        lines.append(
            value * turn_ref[0, i : i + 1, :] - swap_halves(value) * turn_ref[1, i : i + 1, :]
        )
    lines = turned_eighths(lines, 1.0)
    for i in range(FACET_ROWS):
        for spot in spots:
            for b in range(bands):
                source = spot * columns + b * share
                place = (bands - 1 - b) * FACET_ROWS + RETURN_ORDER.index(i)
                target = (place * len(spots) + spot) * share
                held_ref[target : target + share, :] = lines[i][source : source + share, :]
    out_ref[...] = held_ref[...].astype(BF16)


def return_kernel(
    places_ref, pieces_ref, straight_ref, crossed_ref, put_ref, window_ref, turn_ref, partial_ref,
    inner_ref, outer_ref, out_ref, *line_refs, bands,
):
    columns, _, length = out_ref.shape
    blocks = length // CONTRIB
    groups = length // LANES
    pairs = (columns + 1) // 2
    width = pieces_ref.shape[0] // bands
    summed = pieces_ref[0:width, :].astype(F32)
    for b in range(1, bands):
        summed += pieces_ref[b * width : (b + 1) * width, :].astype(F32)
    summed = summed * straight_ref[...] - swap_halves(summed) * crossed_ref[...]
    residues = table_times(partial_ref, summed, ((1,), (1,)))
    kappa = within(iota((2 * CONTRIB, width), 0), CONTRIB)
    inside = kappa >= within(places_ref[...], CONTRIB)
    both = jnp.concatenate(
        [jnp.where(inside, residues, 0.0), jnp.where(inside, 0.0, residues)], axis=1
    )
    put = put_ref[...]
    high, low = split(both)
    spectrum = dot(high, put, ((1,), (1,))) + dot(low, put, ((1,), (1,)))
    inner = times_table(
        jnp.concatenate(
            [
                jnp.concatenate(
                    [
                        spectrum[:CONTRIB, pair * LANES : (pair + 1) * LANES],
                        spectrum[CONTRIB:, pair * LANES : (pair + 1) * LANES],
                    ],
                    axis=1,
                )
                for pair in range(pairs)
            ],
            axis=0,
        ),
        inner_ref,
    )
    reals, imags = [], []
    for pair in range(pairs):
        rows = slice(pair * CONTRIB, (pair + 1) * CONTRIB)
        real, imag = inner[rows, :LANES], inner[rows, LANES:]
        reals.append(real * turn_ref[0] + imag * turn_ref[1])
        imags.append(imag * turn_ref[0] - real * turn_ref[1])
    lines = table_times(
        outer_ref,
        jnp.concatenate(
            [jnp.concatenate(reals, axis=1), jnp.concatenate(imags, axis=1)], axis=0
        ),
    )
    window = window_ref[...]
    low_half = iota((groups, LANES), 1) < HALF
    for part in range(2):
        for pair in range(pairs):
            lanes = slice(pair * LANES, (pair + 1) * LANES)
            begin = part * blocks
            even = lines[begin : begin + groups, lanes]
            odd = lines[begin + groups : begin + blocks, lanes]
            line_refs[2 * pair][pl.ds(part, groups, stride=2), :] = (
                jnp.where(low_half, even, swap_halves(odd)) * window
            )
            if 2 * pair + 1 < columns:
                line_refs[2 * pair + 1][pl.ds(part, groups, stride=2), :] = (
                    jnp.where(low_half, swap_halves(even), odd) * window
                )
    for column in range(columns):
        for group in range(groups):
            out_ref[column, :, group * LANES : (group + 1) * LANES] = line_refs[column][
                2 * group : 2 * group + 2, :
            ]


def kernel_call(kernel, name, out_shape, spaces, scratch, *operands, flops=0):
    return pl.pallas_call(
        kernel,
        out_shape=out_shape,
        in_specs=[pl.BlockSpec(memory_space=space) for space in spaces],
        out_specs=jax.tree.map(lambda _: pl.BlockSpec(memory_space=pltpu.VMEM), out_shape),
        scratch_shapes=scratch,
        compiler_params=pltpu.CompilerParams(vmem_limit_bytes=VMEM_LIMIT),
        cost_estimate=pl.CostEstimate(flops=flops, bytes_accessed=0, transcendentals=0)
        if flops
        else None,
        name=name,
    )(*operands)


def wide(rows):
    return pltpu.VMEM((rows, LANES), F32)


def local(groups, bands, strips, offsets, cells, values, weights, flags):
    columns, length = strips.shape[-2:]
    fronts = offsets.shape[0]
    share = columns // bands
    facets = groups * FACET_ROWS
    rows = facets * fronts * columns
    width = facets * fronts * share
    made = tables(length)
    plain, plain_places = made.pop("plain")
    paired, paired_places = made.pop("paired")
    made = {key: jnp.asarray(value) for key, value in made.items()}
    held = length // LANES * columns
    small = [offsets, cells[0, :, 0], values[0, :, 0], weights[0], flags[0]]
    large = [strips[0, 0], jnp.asarray(plain), jnp.asarray(paired)]

    def landing(arrays):
        return [
            (pltpu.SMEM if array is offsets else pltpu.VMEM)(array.shape, array.dtype)
            for array in arrays
        ]

    def in_hbm(arrays):
        return [pltpu.with_memory_space_constraint(array, pltpu.HBM) for array in arrays]

    def semaphores(count):
        return pltpu.SemaphoreType.DMA((count,))

    early, packed, places = kernel_call(
        functools.partial(early_kernel, plain=plain_places, paired=paired_places, share=share),
        "early",
        [
            jax.ShapeDtypeStruct((rows, LANES), BF16),
            jax.ShapeDtypeStruct((4 * fronts, cells.shape[-1]), F32),
            jax.ShapeDtypeStruct((1, width), jnp.int32),
        ],
        [pltpu.HBM] * 8,
        landing(small + large) + [wide(held)] * 2 + [semaphores(5), semaphores(3)],
        *in_hbm(small + large),
    )
    pieces = kernel_call(
        functools.partial(late_kernel, plain=plain_places, paired=paired_places), "late",
        jax.ShapeDtypeStruct((rows, LANES), BF16), [pltpu.VMEM] + [pltpu.HBM] * 4,
        landing([offsets] + large) + [wide(held)] * 2 + [semaphores(4)],
        early, *in_hbm([offsets] + large), flops=LATE_FLOPS,
    )
    gathered = [packed]
    for step in range(1, groups):
        moves = [((group + step) % groups, group) for group in range(groups)]
        gathered.append(lax.ppermute(packed, "group", moves))
    arrived = lax.all_to_all(
        pieces, "member", split_axis=0, concat_axis=0, tiled=True,
        axis_index_groups=[list(SEND_ORDER)],
    )
    blocks = length // CONTRIB
    value, weight, put, straight, crossed = kernel_call(
        functools.partial(prepare_kernel, columns=columns, share=share, blocks=blocks), "prepare",
        [jax.ShapeDtypeStruct((rows, LANES), F32)] * 2
        + [jax.ShapeDtypeStruct(((share + share % 2) * blocks, 2 * width), BF16)]
        + [jax.ShapeDtypeStruct((width, LANES), F32)] * 2,
        [pltpu.VMEM] * (2 + len(gathered)), [],
        places, made["shift"], *gathered, flops=PREPARE_FLOPS,
    )
    returned = kernel_call(
        functools.partial(subgrid_kernel, columns=columns, bands=bands), "subgrid",
        jax.ShapeDtypeStruct((rows, LANES), BF16), [pltpu.VMEM] * 6, [wide(rows)],
        arrived, value, weight, made["grid_turn"], made["model"], made["back"],
    )
    delivered = lax.all_to_all(
        returned, ("band", "member"), split_axis=0, concat_axis=0, tiled=True,
        axis_index_groups=[
            [b * FACET_ROWS + member for b in reversed(range(bands)) for member in RETURN_ORDER]
        ],
    )
    lines = kernel_call(
        functools.partial(return_kernel, bands=bands), "lines",
        jax.ShapeDtypeStruct((share, 2, length), F32), [pltpu.VMEM] * 10,
        [wide(2 * length // LANES)] * share,
        places, delivered, straight, crossed, put, made["window"], made["turn"],
        made["partial"], made["inner_plus"], made["outer_plus"],
    )
    return lines[None]


def solution(mesh):
    bands = mesh.shape["band"]
    groups = mesh.shape["facet"] // FACET_ROWS
    split_mesh = Mesh(
        mesh.devices.reshape(groups, FACET_ROWS, bands), ("group", "member", "band")
    )
    facet = ("group", "member")
    placed = (
        P("band", facet, None, None, None),
        P(),
        P("band", None, facet, None, None),
        P("band", None, facet, None, None),
        P("band", None, facet, None),
        P("band", None, facet, None),
    )
    return jax.shard_map(
        functools.partial(local, groups, bands),
        mesh=split_mesh,
        in_specs=placed,
        out_specs=P(facet, "band", None, None),
        check_vma=False,
    )
```

```python
import functools
import math

import jax
import jax.numpy as jnp
import ml_dtypes
import numpy as np
from jax import lax
from jax.experimental import pallas as pl
from jax.experimental.pallas import tpu as pltpu
from jax.sharding import Mesh
from jax.sharding import PartitionSpec as P

CONTRIB = 64
FACET_ROWS = 8
SUBGRID = FACET_ROWS * CONTRIB
SEND_ORDER = tuple(reversed(range(FACET_ROWS)))
RETURN_ORDER = tuple(reversed(range(FACET_ROWS)))
LANES = 128
HALF = LANES // 2
LATE_FLOPS = 10**10
PREPARE_FLOPS = 2 * 10**10
VMEM_LIMIT = 48 * 1024 * 1024
F32 = jnp.float32
BF16 = jnp.bfloat16


def phases(rows, cols, length, rotation):
    product = np.outer(rows, cols) % length
    return np.exp(rotation * 2j * np.pi * product / length)


def from_left(matrix):
    return np.block([[matrix.real, -matrix.imag], [matrix.imag, matrix.real]])


def from_right(matrix):
    return np.block([[matrix.real, matrix.imag], [-matrix.imag, matrix.real]])


def high_low(table):
    high = table.astype(ml_dtypes.bfloat16)
    low = (table - high.astype(np.float64)).astype(ml_dtypes.bfloat16)
    return np.stack([high, low])


def side_by_side(values):
    straight = np.concatenate([values.real, values.real], axis=-1)
    crossed = np.concatenate([-values.imag, values.imag], axis=-1)
    return np.stack([straight, crossed])


def stack_tables(named):
    places, blocks, begin = {}, [], 0
    for name, table in named.items():
        count = table.shape[1] // LANES
        places[name] = (begin, table.shape[0], count)
        blocks += [table[:, i * LANES : (i + 1) * LANES] for i in range(count)]
        begin += table.shape[0] * count
    return np.concatenate(blocks, axis=0), places


def stack_pairs(named):
    return stack_tables(
        {(name, i): table for name, pair in named.items() for i, table in enumerate(pair)}
    )


def tables(length):
    blocks = length // CONTRIB
    short = np.arange(CONTRIB)
    outer = np.concatenate([np.arange(0, blocks, 2), np.arange(1, blocks, 2)])
    window = 1.0 + 0.5 * np.cos(np.arange(length) * (2.0 * math.pi / length))
    window = (window * length**-0.5).reshape(length // LANES, LANES).astype(np.float32)
    turn = np.tile(phases(short, short, length, -1), (1, 2))
    turn = np.stack([turn.real, turn.imag]).astype(np.float32)
    pair = np.eye(2)
    shift = high_low(np.concatenate(side_by_side(phases(short, short, CONTRIB, -1)), axis=1))
    outer_minus = from_left(phases(short, outer, blocks, -1))
    inner_minus = from_right(np.kron(pair, phases(short, short, CONTRIB, -1)))
    piece = from_right(phases(short, short, CONTRIB, 1)) * CONTRIB**-0.5
    return dict(
        plain=stack_tables(dict(window=window, real=turn[0], imag=turn[1])),
        paired=stack_pairs(
            dict(
                shift=shift,
                outer=high_low(outer_minus),
                inner=high_low(inner_minus),
                piece=high_low(piece),
            )
        ),
        window=window,
        turn=turn,
        shift=shift,
        inner_plus=high_low(from_right(np.kron(pair, phases(short, short, CONTRIB, 1)))),
        outer_plus=high_low(from_left(phases(outer, short, blocks, 1))),
        partial=high_low(from_right(phases(short, short, CONTRIB, -1)).T * CONTRIB**-0.5),
        grid_turn=side_by_side(phases(np.arange(FACET_ROWS), short, SUBGRID, -1)).astype(
            np.float32
        ),
        model=high_low(from_right(phases(short, short, CONTRIB, -1)) * SUBGRID**-0.5),
        back=high_low(from_right(phases(short, short, CONTRIB, 1)) * SUBGRID**-0.5),
    )


def split(values):
    high = values.astype(BF16)
    return high, (values - high.astype(F32)).astype(BF16)


def dot(left, right, dims=((1,), (0,))):
    return lax.dot_general(left, right, (dims, ((), ())), preferred_element_type=F32)


def dot_split(values, right):
    rows = values.shape[0]
    both = dot(jnp.concatenate(split(values), axis=0), right)
    return both[:rows] + both[rows:]


def times_table(values, table):
    return dot_split(values, table[0]) + dot(values.astype(BF16), table[1])


def table_times(table, values, dims=((1,), (0,))):
    high, low = split(values)
    rows = table[0].shape[0]
    both = dot(jnp.concatenate([table[0], table[1]], axis=0), high, dims)
    return both[:rows] + both[rows:] + dot(table[0], low, dims)


def iota(shape, dimension):
    return lax.broadcasted_iota(jnp.int32, shape, dimension)


def over(values, size):
    return lax.shift_right_logical(values, jnp.full_like(values, size.bit_length() - 1))


def within(values, size):
    return values & (size - 1)


def swap_halves(values):
    return pltpu.roll(values, HALF, 1)


def table_at(ref, place):
    begin, rows, blocks = place
    parts = [ref[begin + i * rows : begin + (i + 1) * rows, :] for i in range(blocks)]
    return parts[0] if blocks == 1 else jnp.concatenate(parts, axis=1)


def offsets_on_lanes(offsets_ref, columns, order):
    fronts, owners = offsets_ref.shape
    groups = owners // FACET_ROWS
    own = lax.axis_index("group")
    begins = []
    for step in range(groups):
        group = own + step
        begins.append(jnp.where(group >= groups, group - groups, group) * FACET_ROWS)
    spread = iota((1, fronts * owners * columns), 1)
    place_of = over(spread, columns)
    for place in range(fronts * owners):
        t, step, spot = place % fronts, place // fronts % groups, place // (fronts * groups)
        member = order[spot]
        spread = jnp.where(place_of == place, offsets_ref[t, begins[step] + member], spread)
    return spread


def shift_rows(residue, table):
    pick = jnp.where(iota((CONTRIB, residue.shape[1]), 0) == residue, 1.0, 0.0).T.astype(BF16)
    rows = dot(pick, table[0]) + dot(pick, table[1])
    return rows[:, :LANES], rows[:, LANES:]


def one_hot(shape, targets):
    return jnp.where(iota(shape, 0) == targets, 1.0, 0.0).astype(BF16)


def turned_eighths(values, rotation):
    sign = jnp.where(iota(values[0].shape, 1) < HALF, -rotation, rotation).astype(F32)

    def quarter_turn(value):
        return swap_halves(value) * sign

    def four(a, b, c, d):
        even_sum, even_diff = a + c, a - c
        odd_sum, odd_diff = b + d, quarter_turn(b - d)
        return even_sum + odd_sum, even_diff + odd_diff, even_sum - odd_sum, even_diff - odd_diff

    even = four(*values[0::2])
    odd = four(*values[1::2])
    root = math.sqrt(0.5)
    turned = (
        odd[0],
        (odd[1] + quarter_turn(odd[1])) * root,
        quarter_turn(odd[2]),
        (quarter_turn(odd[3]) - odd[3]) * root,
    )
    return [e + o for e, o in zip(even, turned)] + [e - o for e, o in zip(even, turned)]


def pack_samples(cells_ref, values_ref, weights_ref, flags_ref, out_ref):
    for t in range(cells_ref.shape[0]):
        rows = [
            cells_ref[t, 0:1, :].astype(F32) * SUBGRID + cells_ref[t, 1:2, :].astype(F32),
            weights_ref[t] * flags_ref[t].astype(F32),
            values_ref[t],
        ]
        out_ref[4 * t : 4 * t + 4, :] = jnp.concatenate(rows, axis=0)


def start_all(sources, targets, semaphores):
    copies = [
        pltpu.make_async_copy(source, target, semaphores.at[i])
        for i, (source, target) in enumerate(zip(sources, targets))
    ]
    for copy in copies:
        copy.start()
    return copies


def predict(spread, copies, strips_ref, plain_ref, paired_ref, held_refs, out_ref, plain, paired):
    columns, length = strips_ref.shape[1:]
    groups = length // LANES
    pairs = columns // 2
    blocks = length // CONTRIB
    width = spread.shape[1]
    first_block, residue = over(spread, CONTRIB), within(spread, CONTRIB)
    base = within(iota(spread.shape, 1), columns) * blocks
    shape = (columns * blocks, width)
    pick_inside = one_hot(shape, base + first_block)
    pick_beyond = one_hot(shape, base + within(first_block + 1, blocks))
    for copy in copies[:2]:
        copy.wait()

    def pair_at(name):
        return [table_at(paired_ref, paired[name, i]) for i in range(2)]

    window = table_at(plain_ref, plain["window"])
    turn_real, turn_imag = table_at(plain_ref, plain["real"]), table_at(plain_ref, plain["imag"])
    low_half = iota((groups, LANES), 1) < HALF
    sections = []
    for part, held in enumerate(held_refs):
        for group in range(groups):
            held[group * columns : (group + 1) * columns, :] = strips_ref[
                part, :, group * LANES : (group + 1) * LANES
            ]
        even, odd = [], []
        for pair in range(pairs):
            first = held[pl.ds(2 * pair, groups, stride=columns), :] * window
            second = held[pl.ds(2 * pair + 1, groups, stride=columns), :] * window
            even.append(jnp.where(low_half, first, swap_halves(second)))
            odd.append(jnp.where(low_half, swap_halves(first), second))
        sections += [jnp.concatenate(even, axis=1), jnp.concatenate(odd, axis=1)]
    for copy in copies[2:]:
        copy.wait()
    section = table_times(pair_at("outer"), jnp.concatenate(sections, axis=0))
    turned = []
    for pair in range(pairs):
        lanes = slice(pair * LANES, (pair + 1) * LANES)
        real, imag = section[:CONTRIB, lanes], section[CONTRIB:, lanes]
        turned.append(
            jnp.concatenate(
                [real * turn_real - imag * turn_imag, real * turn_imag + imag * turn_real],
                axis=1,
            )
        )
    inner = times_table(jnp.concatenate(turned, axis=0), pair_at("inner"))
    spectrum = jnp.concatenate(
        [
            jnp.concatenate(
                [
                    inner[pair * CONTRIB : (pair + 1) * CONTRIB, part * LANES : (part + 1) * LANES]
                    for pair in range(pairs)
                ],
                axis=1,
            )
            for part in range(2)
        ],
        axis=0,
    )
    inside = dot_split(spectrum, pick_inside)
    beyond = dot_split(spectrum, pick_beyond)
    kappa = within(iota((2 * CONTRIB, width), 0), CONTRIB)
    cutout = jnp.where(kappa >= residue, inside, beyond)
    piece = times_table(cutout.T, pair_at("piece"))
    straight, crossed = shift_rows(residue, pair_at("shift"))
    out_ref[...] = (piece * straight + swap_halves(piece) * crossed).astype(BF16)


def in_first_half():
    return 2 * lax.axis_index("group") < lax.axis_size("group")


def early_kernel(
    offsets, cells, values, weights, flags, strips, plain_table, paired_table,
    out_ref, packed_ref, places_ref, spread_ref, strips_ref, plain_ref, paired_ref,
    offsets_ref, cells_ref, values_ref, weights_ref, flags_ref, real_ref, imag_ref,
    small_semaphores, semaphores, *, plain, paired, share,
):
    small = start_all(
        (offsets, cells, values, weights, flags),
        (offsets_ref, cells_ref, values_ref, weights_ref, flags_ref),
        small_semaphores,
    )
    large = start_all(
        (strips, plain_table, paired_table), (strips_ref, plain_ref, paired_ref), semaphores
    )
    for copy in small:
        copy.wait()
    for t in range(cells_ref.shape[0]):
        rows = [
            cells_ref[t, 0:1, :].astype(F32) * SUBGRID + cells_ref[t, 1:2, :].astype(F32),
            weights_ref[t] * flags_ref[t].astype(F32),
            values_ref[t],
        ]
        packed_ref[4 * t : 4 * t + 4, :] = jnp.concatenate(rows, axis=0)
    places_ref[...] = offsets_on_lanes(offsets_ref, share, RETURN_ORDER)
    spread_ref[...] = offsets_on_lanes(offsets_ref, strips_ref.shape[1], SEND_ORDER)

    @pl.when(in_first_half())
    def _():
        predict(
            spread_ref[...], large, strips_ref, plain_ref, paired_ref, (real_ref, imag_ref),
            out_ref, plain, paired,
        )

    @pl.when(jnp.logical_not(in_first_half()))
    def _():
        for copy in large:
            copy.wait()


def late_kernel(
    early_ref, spread_ref, strips_ref, plain_ref, paired_ref, out_ref, real_ref, imag_ref,
    *, plain, paired,
):
    @pl.when(in_first_half())
    def _():
        out_ref[...] = early_ref[...]

    @pl.when(jnp.logical_not(in_first_half()))
    def _():
        predict(
            spread_ref[...], (), strips_ref, plain_ref, paired_ref, (real_ref, imag_ref), out_ref,
            plain, paired,
        )


def prepare_kernel(places_ref, shift_ref, *refs, columns, share, blocks):
    samples_refs, outs = refs[:-5], refs[-5:]
    value_ref, weight_ref, put_ref, straight_ref, crossed_ref = outs
    fronts, samples = samples_refs[0].shape[0] // 4, samples_refs[0].shape[1]
    own = lax.axis_index("group")
    depth = FACET_ROWS * columns
    for spot in range(len(samples_refs) * fronts):
        step, t = spot // fronts, spot % fronts
        sample = samples_refs[step][4 * t : 4 * t + 4, :]
        cell = sample[0:1, :].astype(jnp.int32)
        row, col = over(cell, SUBGRID) - own * columns, within(cell, SUBGRID)
        inside = (row >= 0) & (row < columns)
        target = jnp.where(inside, within(col, FACET_ROWS) * columns + row, -1)
        pick = one_hot((depth, samples), target)
        mask = iota((HALF, samples), 0) == over(col, FACET_ROWS)
        factor = sample[1:2, :]
        highs, lows = [], []
        for term in (factor * sample[2:3, :], factor * sample[3:4, :], factor):
            high = term.astype(BF16).astype(F32)
            highs.append(jnp.where(mask, high, 0.0).astype(BF16))
            lows.append(jnp.where(mask, term - high, 0.0).astype(BF16))
        highs, lows = highs + highs[2:], lows + lows[2:]
        grid = dot(pick, jnp.concatenate(highs, axis=0), ((1,), (1,))) + dot(
            pick, jnp.concatenate(lows, axis=0), ((1,), (1,))
        )
        rows = slice(spot * depth, (spot + 1) * depth)
        value_ref[rows, :] = grid[:, :LANES]
        weight_ref[rows, :] = grid[:, LANES:]
    spread = places_ref[...]
    first_block, residue = over(spread, CONTRIB), within(spread, CONTRIB)
    straight_ref[...], crossed_ref[...] = shift_rows(residue, shift_ref)
    base = within(iota(spread.shape, 1), share) * blocks
    targets = jnp.concatenate([base + first_block, base + within(first_block + 1, blocks)], axis=1)
    put_ref[...] = one_hot(put_ref.shape, targets)


def subgrid_kernel(
    pieces_ref, value_ref, weight_ref, turn_ref, model_ref, back_ref, out_ref, held_ref,
    *, columns, bands,
):
    rows = pieces_ref.shape[0] // FACET_ROWS
    spots = range(rows // columns)
    depth = FACET_ROWS * columns
    share = columns // bands
    pieces = pieces_ref[...].astype(F32)
    sky = turned_eighths(
        [
            pieces[spot * rows : (spot + 1) * rows, :]
            for spot in (SEND_ORDER.index(i) for i in range(FACET_ROWS))
        ],
        -1.0,
    )
    sky = [
        value * turn_ref[0, i : i + 1, :] + swap_halves(value) * turn_ref[1, i : i + 1, :]
        for i, value in enumerate(sky)
    ]
    stacked = jnp.concatenate(
        [value[spot * columns : (spot + 1) * columns, :] for spot in spots for value in sky],
        axis=0,
    )
    grid = value_ref[...] - weight_ref[...] * times_table(stacked, model_ref)
    back = times_table(grid, back_ref)
    lines = []
    for i in range(FACET_ROWS):
        value = jnp.concatenate(
            [
                back[spot * depth + i * columns : spot * depth + (i + 1) * columns, :]
                for spot in spots
            ],
            axis=0,
        )
        lines.append(
            value * turn_ref[0, i : i + 1, :] - swap_halves(value) * turn_ref[1, i : i + 1, :]
        )
    lines = turned_eighths(lines, 1.0)
    for i in range(FACET_ROWS):
        for spot in spots:
            for b in range(bands):
                source = spot * columns + b * share
                place = (bands - 1 - b) * FACET_ROWS + RETURN_ORDER.index(i)
                target = (place * len(spots) + spot) * share
                held_ref[target : target + share, :] = lines[i][source : source + share, :]
    out_ref[...] = held_ref[...].astype(BF16)


def return_kernel(
    places_ref, pieces_ref, straight_ref, crossed_ref, put_ref, window_ref, turn_ref, partial_ref,
    inner_ref, outer_ref, out_ref, *line_refs, bands,
):
    columns, _, length = out_ref.shape
    blocks = length // CONTRIB
    groups = length // LANES
    pairs = (columns + 1) // 2
    width = pieces_ref.shape[0] // bands
    summed = pieces_ref[0:width, :].astype(F32)
    for b in range(1, bands):
        summed += pieces_ref[b * width : (b + 1) * width, :].astype(F32)
    summed = summed * straight_ref[...] - swap_halves(summed) * crossed_ref[...]
    residues = table_times(partial_ref, summed, ((1,), (1,)))
    kappa = within(iota((2 * CONTRIB, width), 0), CONTRIB)
    inside = kappa >= within(places_ref[...], CONTRIB)
    both = jnp.concatenate(
        [jnp.where(inside, residues, 0.0), jnp.where(inside, 0.0, residues)], axis=1
    )
    put = put_ref[...]
    high, low = split(both)
    spectrum = dot(high, put, ((1,), (1,))) + dot(low, put, ((1,), (1,)))
    inner = times_table(
        jnp.concatenate(
            [
                jnp.concatenate(
                    [
                        spectrum[:CONTRIB, pair * LANES : (pair + 1) * LANES],
                        spectrum[CONTRIB:, pair * LANES : (pair + 1) * LANES],
                    ],
                    axis=1,
                )
                for pair in range(pairs)
            ],
            axis=0,
        ),
        inner_ref,
    )
    reals, imags = [], []
    for pair in range(pairs):
        rows = slice(pair * CONTRIB, (pair + 1) * CONTRIB)
        real, imag = inner[rows, :LANES], inner[rows, LANES:]
        reals.append(real * turn_ref[0] + imag * turn_ref[1])
        imags.append(imag * turn_ref[0] - real * turn_ref[1])
    lines = table_times(
        outer_ref,
        jnp.concatenate(
            [jnp.concatenate(reals, axis=1), jnp.concatenate(imags, axis=1)], axis=0
        ),
    )
    window = window_ref[...]
    low_half = iota((groups, LANES), 1) < HALF
    for part in range(2):
        for pair in range(pairs):
            lanes = slice(pair * LANES, (pair + 1) * LANES)
            begin = part * blocks
            even = lines[begin : begin + groups, lanes]
            odd = lines[begin + groups : begin + blocks, lanes]
            line_refs[2 * pair][pl.ds(part, groups, stride=2), :] = (
                jnp.where(low_half, even, swap_halves(odd)) * window
            )
            if 2 * pair + 1 < columns:
                line_refs[2 * pair + 1][pl.ds(part, groups, stride=2), :] = (
                    jnp.where(low_half, swap_halves(even), odd) * window
                )
    for column in range(columns):
        for group in range(groups):
            out_ref[column, :, group * LANES : (group + 1) * LANES] = line_refs[column][
                2 * group : 2 * group + 2, :
            ]


def kernel_call(kernel, name, out_shape, spaces, scratch, *operands, flops=0):
    return pl.pallas_call(
        kernel,
        out_shape=out_shape,
        in_specs=[pl.BlockSpec(memory_space=space) for space in spaces],
        out_specs=jax.tree.map(lambda _: pl.BlockSpec(memory_space=pltpu.VMEM), out_shape),
        scratch_shapes=scratch,
        compiler_params=pltpu.CompilerParams(vmem_limit_bytes=VMEM_LIMIT),
        cost_estimate=pl.CostEstimate(flops=flops, bytes_accessed=0, transcendentals=0)
        if flops
        else None,
        name=name,
    )(*operands)


def wide(rows):
    return pltpu.VMEM((rows, LANES), F32)


def local(groups, bands, strips, offsets, cells, values, weights, flags):
    columns, length = strips.shape[-2:]
    fronts = offsets.shape[0]
    share = columns // bands
    facets = groups * FACET_ROWS
    rows = facets * fronts * columns
    width = facets * fronts * share
    made = tables(length)
    plain, plain_places = made.pop("plain")
    paired, paired_places = made.pop("paired")
    made = {key: jnp.asarray(value) for key, value in made.items()}
    held = length // LANES * columns
    small = [offsets, cells[0, :, 0], values[0, :, 0], weights[0], flags[0]]
    large = [strips[0, 0], jnp.asarray(plain), jnp.asarray(paired)]

    def landing(arrays):
        return [
            (pltpu.SMEM if array is offsets else pltpu.VMEM)(array.shape, array.dtype)
            for array in arrays
        ]

    def in_hbm(arrays):
        return [pltpu.with_memory_space_constraint(array, pltpu.HBM) for array in arrays]

    def semaphores(count):
        return pltpu.SemaphoreType.DMA((count,))

    early, packed, places, *fetched = kernel_call(
        functools.partial(early_kernel, plain=plain_places, paired=paired_places, share=share),
        "early",
        [
            jax.ShapeDtypeStruct((rows, LANES), BF16),
            jax.ShapeDtypeStruct((4 * fronts, cells.shape[-1]), F32),
            jax.ShapeDtypeStruct((1, width), jnp.int32),
            jax.ShapeDtypeStruct((1, rows), jnp.int32),
        ]
        + [jax.ShapeDtypeStruct(array.shape, array.dtype) for array in large],
        [pltpu.HBM] * 8,
        landing(small) + [wide(held)] * 2 + [semaphores(5), semaphores(3)],
        *in_hbm(small + large),
    )
    pieces = kernel_call(
        functools.partial(late_kernel, plain=plain_places, paired=paired_places), "late",
        jax.ShapeDtypeStruct((rows, LANES), BF16), [pltpu.VMEM] * 5, [wide(held)] * 2,
        early, *fetched, flops=LATE_FLOPS,
    )
    gathered = [packed]
    for step in range(1, groups):
        moves = [((group + step) % groups, group) for group in range(groups)]
        gathered.append(lax.ppermute(packed, "group", moves))
    arrived = lax.all_to_all(
        pieces, "member", split_axis=0, concat_axis=0, tiled=True,
        axis_index_groups=[list(SEND_ORDER)],
    )
    blocks = length // CONTRIB
    value, weight, put, straight, crossed = kernel_call(
        functools.partial(prepare_kernel, columns=columns, share=share, blocks=blocks), "prepare",
        [jax.ShapeDtypeStruct((rows, LANES), F32)] * 2
        + [jax.ShapeDtypeStruct(((share + share % 2) * blocks, 2 * width), BF16)]
        + [jax.ShapeDtypeStruct((width, LANES), F32)] * 2,
        [pltpu.VMEM] * (2 + len(gathered)), [],
        places, made["shift"], *gathered, flops=PREPARE_FLOPS,
    )
    returned = kernel_call(
        functools.partial(subgrid_kernel, columns=columns, bands=bands), "subgrid",
        jax.ShapeDtypeStruct((rows, LANES), BF16), [pltpu.VMEM] * 6, [wide(rows)],
        arrived, value, weight, made["grid_turn"], made["model"], made["back"],
    )
    delivered = lax.all_to_all(
        returned, ("band", "member"), split_axis=0, concat_axis=0, tiled=True,
        axis_index_groups=[
            [b * FACET_ROWS + member for b in reversed(range(bands)) for member in RETURN_ORDER]
        ],
    )
    lines = kernel_call(
        functools.partial(return_kernel, bands=bands), "lines",
        jax.ShapeDtypeStruct((share, 2, length), F32), [pltpu.VMEM] * 10,
        [wide(2 * length // LANES)] * share,
        places, delivered, straight, crossed, put, made["window"], made["turn"],
        made["partial"], made["inner_plus"], made["outer_plus"],
    )
    return lines[None]


def solution(mesh):
    bands = mesh.shape["band"]
    groups = mesh.shape["facet"] // FACET_ROWS
    split_mesh = Mesh(
        mesh.devices.reshape(groups, FACET_ROWS, bands), ("group", "member", "band")
    )
    facet = ("group", "member")
    placed = (
        P("band", facet, None, None, None),
        P(),
        P("band", None, facet, None, None),
        P("band", None, facet, None, None),
        P("band", None, facet, None),
        P("band", None, facet, None),
    )
    return jax.shard_map(
        functools.partial(local, groups, bands),
        mesh=split_mesh,
        in_specs=placed,
        out_specs=P(facet, "band", None, None),
        check_vma=False,
    )
```

```python
import functools
import math

import jax
import jax.numpy as jnp
import ml_dtypes
import numpy as np
from jax import lax
from jax.experimental import pallas as pl
from jax.experimental.pallas import tpu as pltpu
from jax.sharding import Mesh
from jax.sharding import PartitionSpec as P

CONTRIB = 64
FACET_ROWS = 8
SUBGRID = FACET_ROWS * CONTRIB
SEND_ORDER = tuple(reversed(range(FACET_ROWS)))
RETURN_ORDER = tuple(reversed(range(FACET_ROWS)))
LANES = 128
HALF = LANES // 2
EARLY_FLOPS = 10**10
LATE_FLOPS = 10**10
PREPARE_FLOPS = 2 * 10**10
VMEM_LIMIT = 48 * 1024 * 1024
F32 = jnp.float32
BF16 = jnp.bfloat16


def phases(rows, cols, length, rotation):
    product = np.outer(rows, cols) % length
    return np.exp(rotation * 2j * np.pi * product / length)


def from_left(matrix):
    return np.block([[matrix.real, -matrix.imag], [matrix.imag, matrix.real]])


def from_right(matrix):
    return np.block([[matrix.real, matrix.imag], [-matrix.imag, matrix.real]])


def high_low(table):
    high = table.astype(ml_dtypes.bfloat16)
    low = (table - high.astype(np.float64)).astype(ml_dtypes.bfloat16)
    return np.stack([high, low])


def side_by_side(values):
    straight = np.concatenate([values.real, values.real], axis=-1)
    crossed = np.concatenate([-values.imag, values.imag], axis=-1)
    return np.stack([straight, crossed])


def stack_tables(named):
    places, blocks, begin = {}, [], 0
    for name, table in named.items():
        count = table.shape[1] // LANES
        places[name] = (begin, table.shape[0], count)
        blocks += [table[:, i * LANES : (i + 1) * LANES] for i in range(count)]
        begin += table.shape[0] * count
    return np.concatenate(blocks, axis=0), places


def stack_pairs(named):
    return stack_tables(
        {(name, i): table for name, pair in named.items() for i, table in enumerate(pair)}
    )


def tables(length):
    blocks = length // CONTRIB
    short = np.arange(CONTRIB)
    outer = np.concatenate([np.arange(0, blocks, 2), np.arange(1, blocks, 2)])
    window = 1.0 + 0.5 * np.cos(np.arange(length) * (2.0 * math.pi / length))
    window = (window * length**-0.5).reshape(length // LANES, LANES).astype(np.float32)
    turn = np.tile(phases(short, short, length, -1), (1, 2))
    turn = np.stack([turn.real, turn.imag]).astype(np.float32)
    pair = np.eye(2)
    shift = high_low(np.concatenate(side_by_side(phases(short, short, CONTRIB, -1)), axis=1))
    outer_minus = from_left(phases(short, outer, blocks, -1))
    inner_minus = from_right(np.kron(pair, phases(short, short, CONTRIB, -1)))
    piece = from_right(phases(short, short, CONTRIB, 1)) * CONTRIB**-0.5
    return dict(
        plain=stack_tables(dict(window=window, real=turn[0], imag=turn[1])),
        paired=stack_pairs(
            dict(
                shift=shift,
                outer=high_low(outer_minus),
                inner=high_low(inner_minus),
                piece=high_low(piece),
            )
        ),
        window=window,
        turn=turn,
        shift=shift,
        inner_plus=high_low(from_right(np.kron(pair, phases(short, short, CONTRIB, 1)))),
        outer_plus=high_low(from_left(phases(outer, short, blocks, 1))),
        partial=high_low(from_right(phases(short, short, CONTRIB, -1)).T * CONTRIB**-0.5),
        grid_turn=side_by_side(phases(np.arange(FACET_ROWS), short, SUBGRID, -1)).astype(
            np.float32
        ),
        model=high_low(from_right(phases(short, short, CONTRIB, -1)) * SUBGRID**-0.5),
        back=high_low(from_right(phases(short, short, CONTRIB, 1)) * SUBGRID**-0.5),
    )


def split(values):
    high = values.astype(BF16)
    return high, (values - high.astype(F32)).astype(BF16)


def dot(left, right, dims=((1,), (0,))):
    return lax.dot_general(left, right, (dims, ((), ())), preferred_element_type=F32)


def dot_split(values, right):
    rows = values.shape[0]
    both = dot(jnp.concatenate(split(values), axis=0), right)
    return both[:rows] + both[rows:]


def times_table(values, table):
    return dot_split(values, table[0]) + dot(values.astype(BF16), table[1])


def table_times(table, values, dims=((1,), (0,))):
    high, low = split(values)
    rows = table[0].shape[0]
    both = dot(jnp.concatenate([table[0], table[1]], axis=0), high, dims)
    return both[:rows] + both[rows:] + dot(table[0], low, dims)


def iota(shape, dimension):
    return lax.broadcasted_iota(jnp.int32, shape, dimension)


def over(values, size):
    return lax.shift_right_logical(values, jnp.full_like(values, size.bit_length() - 1))


def within(values, size):
    return values & (size - 1)


def swap_halves(values):
    return pltpu.roll(values, HALF, 1)


def table_at(ref, place):
    begin, rows, blocks = place
    parts = [ref[begin + i * rows : begin + (i + 1) * rows, :] for i in range(blocks)]
    return parts[0] if blocks == 1 else jnp.concatenate(parts, axis=1)


def offsets_on_lanes(offsets_ref, columns, order):
    fronts, owners = offsets_ref.shape
    groups = owners // FACET_ROWS
    own = lax.axis_index("group")
    begins = []
    for step in range(groups):
        group = own + step
        begins.append(jnp.where(group >= groups, group - groups, group) * FACET_ROWS)
    spread = iota((1, fronts * owners * columns), 1)
    place_of = over(spread, columns)
    for place in range(fronts * owners):
        t, step, spot = place % fronts, place // fronts % groups, place // (fronts * groups)
        member = order[spot]
        spread = jnp.where(place_of == place, offsets_ref[t, begins[step] + member], spread)
    return spread


def shift_rows(residue, table):
    pick = jnp.where(iota((CONTRIB, residue.shape[1]), 0) == residue, 1.0, 0.0).T.astype(BF16)
    rows = dot(pick, table[0]) + dot(pick, table[1])
    return rows[:, :LANES], rows[:, LANES:]


def one_hot(shape, targets):
    return jnp.where(iota(shape, 0) == targets, 1.0, 0.0).astype(BF16)


def turned_eighths(values, rotation):
    sign = jnp.where(iota(values[0].shape, 1) < HALF, -rotation, rotation).astype(F32)

    def quarter_turn(value):
        return swap_halves(value) * sign

    def four(a, b, c, d):
        even_sum, even_diff = a + c, a - c
        odd_sum, odd_diff = b + d, quarter_turn(b - d)
        return even_sum + odd_sum, even_diff + odd_diff, even_sum - odd_sum, even_diff - odd_diff

    even = four(*values[0::2])
    odd = four(*values[1::2])
    root = math.sqrt(0.5)
    turned = (
        odd[0],
        (odd[1] + quarter_turn(odd[1])) * root,
        quarter_turn(odd[2]),
        (quarter_turn(odd[3]) - odd[3]) * root,
    )
    return [e + o for e, o in zip(even, turned)] + [e - o for e, o in zip(even, turned)]


def pack_samples(cells_ref, values_ref, weights_ref, flags_ref, out_ref):
    for t in range(cells_ref.shape[0]):
        rows = [
            cells_ref[t, 0:1, :].astype(F32) * SUBGRID + cells_ref[t, 1:2, :].astype(F32),
            weights_ref[t] * flags_ref[t].astype(F32),
            values_ref[t],
        ]
        out_ref[4 * t : 4 * t + 4, :] = jnp.concatenate(rows, axis=0)


def start_all(sources, targets, semaphores):
    copies = [
        pltpu.make_async_copy(source, target, semaphores.at[i])
        for i, (source, target) in enumerate(zip(sources, targets))
    ]
    for copy in copies:
        copy.start()
    return copies


def predict(spread, copies, strips_ref, plain_ref, paired_ref, held_refs, out_ref, plain, paired):
    columns, length = strips_ref.shape[1:]
    groups = length // LANES
    pairs = columns // 2
    blocks = length // CONTRIB
    width = spread.shape[1]
    first_block, residue = over(spread, CONTRIB), within(spread, CONTRIB)
    base = within(iota(spread.shape, 1), columns) * blocks
    shape = (columns * blocks, width)
    pick_inside = one_hot(shape, base + first_block)
    pick_beyond = one_hot(shape, base + within(first_block + 1, blocks))
    for copy in copies[:2]:
        copy.wait()

    def pair_at(name):
        return [table_at(paired_ref, paired[name, i]) for i in range(2)]

    window = table_at(plain_ref, plain["window"])
    turn_real, turn_imag = table_at(plain_ref, plain["real"]), table_at(plain_ref, plain["imag"])
    low_half = iota((groups, LANES), 1) < HALF
    sections = []
    for part, held in enumerate(held_refs):
        for group in range(groups):
            held[group * columns : (group + 1) * columns, :] = strips_ref[
                part, :, group * LANES : (group + 1) * LANES
            ]
        even, odd = [], []
        for pair in range(pairs):
            first = held[pl.ds(2 * pair, groups, stride=columns), :] * window
            second = held[pl.ds(2 * pair + 1, groups, stride=columns), :] * window
            even.append(jnp.where(low_half, first, swap_halves(second)))
            odd.append(jnp.where(low_half, swap_halves(first), second))
        sections += [jnp.concatenate(even, axis=1), jnp.concatenate(odd, axis=1)]
    for copy in copies[2:]:
        copy.wait()
    section = table_times(pair_at("outer"), jnp.concatenate(sections, axis=0))
    turned = []
    for pair in range(pairs):
        lanes = slice(pair * LANES, (pair + 1) * LANES)
        real, imag = section[:CONTRIB, lanes], section[CONTRIB:, lanes]
        turned.append(
            jnp.concatenate(
                [real * turn_real - imag * turn_imag, real * turn_imag + imag * turn_real],
                axis=1,
            )
        )
    inner = times_table(jnp.concatenate(turned, axis=0), pair_at("inner"))
    spectrum = jnp.concatenate(
        [
            jnp.concatenate(
                [
                    inner[pair * CONTRIB : (pair + 1) * CONTRIB, part * LANES : (part + 1) * LANES]
                    for pair in range(pairs)
                ],
                axis=1,
            )
            for part in range(2)
        ],
        axis=0,
    )
    inside = dot_split(spectrum, pick_inside)
    beyond = dot_split(spectrum, pick_beyond)
    kappa = within(iota((2 * CONTRIB, width), 0), CONTRIB)
    cutout = jnp.where(kappa >= residue, inside, beyond)
    piece = times_table(cutout.T, pair_at("piece"))
    straight, crossed = shift_rows(residue, pair_at("shift"))
    out_ref[...] = (piece * straight + swap_halves(piece) * crossed).astype(BF16)


def in_first_half():
    return 2 * lax.axis_index("group") < lax.axis_size("group")


def early_kernel(
    offsets, cells, values, weights, flags, strips, plain_table, paired_table,
    out_ref, packed_ref, places_ref, spread_ref,
    offsets_ref, cells_ref, values_ref, weights_ref, flags_ref, strips_ref, plain_ref, paired_ref,
    real_ref, imag_ref, small_semaphores, semaphores, *, plain, paired, share,
):
    small = start_all(
        (offsets, cells, values, weights, flags),
        (offsets_ref, cells_ref, values_ref, weights_ref, flags_ref),
        small_semaphores,
    )

    def large():
        sources, targets = (strips, plain_table, paired_table), (strips_ref, plain_ref, paired_ref)
        return [
            pltpu.make_async_copy(source, target, semaphores.at[i])
            for i, (source, target) in enumerate(zip(sources, targets))
        ]

    @pl.when(in_first_half())
    def _():
        for copy in large():
            copy.start()

    for copy in small:
        copy.wait()
    for t in range(cells_ref.shape[0]):
        rows = [
            cells_ref[t, 0:1, :].astype(F32) * SUBGRID + cells_ref[t, 1:2, :].astype(F32),
            weights_ref[t] * flags_ref[t].astype(F32),
            values_ref[t],
        ]
        packed_ref[4 * t : 4 * t + 4, :] = jnp.concatenate(rows, axis=0)
    places_ref[...] = offsets_on_lanes(offsets_ref, share, RETURN_ORDER)
    spread_ref[...] = offsets_on_lanes(offsets_ref, strips_ref.shape[1], SEND_ORDER)

    @pl.when(in_first_half())
    def _():
        predict(
            spread_ref[...], large(), strips_ref, plain_ref, paired_ref, (real_ref, imag_ref),
            out_ref, plain, paired,
        )


def late_kernel(
    early_ref, spread_ref, strips_ref, plain_ref, paired_ref, out_ref, real_ref, imag_ref,
    *, plain, paired,
):
    @pl.when(in_first_half())
    def _():
        out_ref[...] = early_ref[...]

    @pl.when(jnp.logical_not(in_first_half()))
    def _():
        predict(
            spread_ref[...], (), strips_ref, plain_ref, paired_ref, (real_ref, imag_ref), out_ref,
            plain, paired,
        )


def prepare_kernel(places_ref, shift_ref, *refs, columns, share, blocks):
    samples_refs, outs = refs[:-5], refs[-5:]
    value_ref, weight_ref, put_ref, straight_ref, crossed_ref = outs
    fronts, samples = samples_refs[0].shape[0] // 4, samples_refs[0].shape[1]
    own = lax.axis_index("group")
    depth = FACET_ROWS * columns
    for spot in range(len(samples_refs) * fronts):
        step, t = spot // fronts, spot % fronts
        sample = samples_refs[step][4 * t : 4 * t + 4, :]
        cell = sample[0:1, :].astype(jnp.int32)
        row, col = over(cell, SUBGRID) - own * columns, within(cell, SUBGRID)
        inside = (row >= 0) & (row < columns)
        target = jnp.where(inside, within(col, FACET_ROWS) * columns + row, -1)
        pick = one_hot((depth, samples), target)
        mask = iota((HALF, samples), 0) == over(col, FACET_ROWS)
        factor = sample[1:2, :]
        highs, lows = [], []
        for term in (factor * sample[2:3, :], factor * sample[3:4, :], factor):
            high = term.astype(BF16).astype(F32)
            highs.append(jnp.where(mask, high, 0.0).astype(BF16))
            lows.append(jnp.where(mask, term - high, 0.0).astype(BF16))
        highs, lows = highs + highs[2:], lows + lows[2:]
        grid = dot(pick, jnp.concatenate(highs, axis=0), ((1,), (1,))) + dot(
            pick, jnp.concatenate(lows, axis=0), ((1,), (1,))
        )
        rows = slice(spot * depth, (spot + 1) * depth)
        value_ref[rows, :] = grid[:, :LANES]
        weight_ref[rows, :] = grid[:, LANES:]
    spread = places_ref[...]
    first_block, residue = over(spread, CONTRIB), within(spread, CONTRIB)
    straight_ref[...], crossed_ref[...] = shift_rows(residue, shift_ref)
    base = within(iota(spread.shape, 1), share) * blocks
    targets = jnp.concatenate([base + first_block, base + within(first_block + 1, blocks)], axis=1)
    put_ref[...] = one_hot(put_ref.shape, targets)


def subgrid_kernel(
    pieces_ref, value_ref, weight_ref, turn_ref, model_ref, back_ref, out_ref, held_ref,
    *, columns, bands,
):
    rows = pieces_ref.shape[0] // FACET_ROWS
    spots = range(rows // columns)
    depth = FACET_ROWS * columns
    share = columns // bands
    pieces = pieces_ref[...].astype(F32)
    sky = turned_eighths(
        [
            pieces[spot * rows : (spot + 1) * rows, :]
            for spot in (SEND_ORDER.index(i) for i in range(FACET_ROWS))
        ],
        -1.0,
    )
    sky = [
        value * turn_ref[0, i : i + 1, :] + swap_halves(value) * turn_ref[1, i : i + 1, :]
        for i, value in enumerate(sky)
    ]
    stacked = jnp.concatenate(
        [value[spot * columns : (spot + 1) * columns, :] for spot in spots for value in sky],
        axis=0,
    )
    grid = value_ref[...] - weight_ref[...] * times_table(stacked, model_ref)
    back = times_table(grid, back_ref)
    lines = []
    for i in range(FACET_ROWS):
        value = jnp.concatenate(
            [
                back[spot * depth + i * columns : spot * depth + (i + 1) * columns, :]
                for spot in spots
            ],
            axis=0,
        )
        lines.append(
            value * turn_ref[0, i : i + 1, :] - swap_halves(value) * turn_ref[1, i : i + 1, :]
        )
    lines = turned_eighths(lines, 1.0)
    for i in range(FACET_ROWS):
        for spot in spots:
            for b in range(bands):
                source = spot * columns + b * share
                place = (bands - 1 - b) * FACET_ROWS + RETURN_ORDER.index(i)
                target = (place * len(spots) + spot) * share
                held_ref[target : target + share, :] = lines[i][source : source + share, :]
    out_ref[...] = held_ref[...].astype(BF16)


def return_kernel(
    places_ref, pieces_ref, straight_ref, crossed_ref, put_ref, window_ref, turn_ref, partial_ref,
    inner_ref, outer_ref, out_ref, *line_refs, bands,
):
    columns, _, length = out_ref.shape
    blocks = length // CONTRIB
    groups = length // LANES
    pairs = (columns + 1) // 2
    width = pieces_ref.shape[0] // bands
    summed = pieces_ref[0:width, :].astype(F32)
    for b in range(1, bands):
        summed += pieces_ref[b * width : (b + 1) * width, :].astype(F32)
    summed = summed * straight_ref[...] - swap_halves(summed) * crossed_ref[...]
    residues = table_times(partial_ref, summed, ((1,), (1,)))
    kappa = within(iota((2 * CONTRIB, width), 0), CONTRIB)
    inside = kappa >= within(places_ref[...], CONTRIB)
    both = jnp.concatenate(
        [jnp.where(inside, residues, 0.0), jnp.where(inside, 0.0, residues)], axis=1
    )
    put = put_ref[...]
    high, low = split(both)
    spectrum = dot(high, put, ((1,), (1,))) + dot(low, put, ((1,), (1,)))
    inner = times_table(
        jnp.concatenate(
            [
                jnp.concatenate(
                    [
                        spectrum[:CONTRIB, pair * LANES : (pair + 1) * LANES],
                        spectrum[CONTRIB:, pair * LANES : (pair + 1) * LANES],
                    ],
                    axis=1,
                )
                for pair in range(pairs)
            ],
            axis=0,
        ),
        inner_ref,
    )
    reals, imags = [], []
    for pair in range(pairs):
        rows = slice(pair * CONTRIB, (pair + 1) * CONTRIB)
        real, imag = inner[rows, :LANES], inner[rows, LANES:]
        reals.append(real * turn_ref[0] + imag * turn_ref[1])
        imags.append(imag * turn_ref[0] - real * turn_ref[1])
    lines = table_times(
        outer_ref,
        jnp.concatenate(
            [jnp.concatenate(reals, axis=1), jnp.concatenate(imags, axis=1)], axis=0
        ),
    )
    window = window_ref[...]
    low_half = iota((groups, LANES), 1) < HALF
    for part in range(2):
        for pair in range(pairs):
            lanes = slice(pair * LANES, (pair + 1) * LANES)
            begin = part * blocks
            even = lines[begin : begin + groups, lanes]
            odd = lines[begin + groups : begin + blocks, lanes]
            line_refs[2 * pair][pl.ds(part, groups, stride=2), :] = (
                jnp.where(low_half, even, swap_halves(odd)) * window
            )
            if 2 * pair + 1 < columns:
                line_refs[2 * pair + 1][pl.ds(part, groups, stride=2), :] = (
                    jnp.where(low_half, swap_halves(even), odd) * window
                )
    for column in range(columns):
        for group in range(groups):
            out_ref[column, :, group * LANES : (group + 1) * LANES] = line_refs[column][
                2 * group : 2 * group + 2, :
            ]


def kernel_call(kernel, name, out_shape, spaces, scratch, *operands, flops=0):
    return pl.pallas_call(
        kernel,
        out_shape=out_shape,
        in_specs=[pl.BlockSpec(memory_space=space) for space in spaces],
        out_specs=jax.tree.map(lambda _: pl.BlockSpec(memory_space=pltpu.VMEM), out_shape),
        scratch_shapes=scratch,
        compiler_params=pltpu.CompilerParams(vmem_limit_bytes=VMEM_LIMIT),
        cost_estimate=pl.CostEstimate(flops=flops, bytes_accessed=0, transcendentals=0)
        if flops
        else None,
        name=name,
    )(*operands)


def wide(rows):
    return pltpu.VMEM((rows, LANES), F32)


def local(groups, bands, strips, offsets, cells, values, weights, flags):
    columns, length = strips.shape[-2:]
    fronts = offsets.shape[0]
    share = columns // bands
    facets = groups * FACET_ROWS
    rows = facets * fronts * columns
    width = facets * fronts * share
    made = tables(length)
    plain, plain_places = made.pop("plain")
    paired, paired_places = made.pop("paired")
    made = {key: jnp.asarray(value) for key, value in made.items()}
    held = length // LANES * columns
    small = [offsets, cells[0, :, 0], values[0, :, 0], weights[0], flags[0]]
    large = [strips[0, 0], jnp.asarray(plain), jnp.asarray(paired)]

    def landing(arrays):
        return [
            (pltpu.SMEM if array is offsets else pltpu.VMEM)(array.shape, array.dtype)
            for array in arrays
        ]

    def in_hbm(arrays):
        return [pltpu.with_memory_space_constraint(array, pltpu.HBM) for array in arrays]

    def semaphores(count):
        return pltpu.SemaphoreType.DMA((count,))

    early, packed, places, spread = kernel_call(
        functools.partial(early_kernel, plain=plain_places, paired=paired_places, share=share),
        "early",
        [
            jax.ShapeDtypeStruct((rows, LANES), BF16),
            jax.ShapeDtypeStruct((4 * fronts, cells.shape[-1]), F32),
            jax.ShapeDtypeStruct((1, width), jnp.int32),
            jax.ShapeDtypeStruct((1, rows), jnp.int32),
        ],
        [pltpu.HBM] * 8,
        landing(small + large) + [wide(held)] * 2 + [semaphores(5), semaphores(3)],
        *in_hbm(small + large), flops=EARLY_FLOPS,
    )
    pieces = kernel_call(
        functools.partial(late_kernel, plain=plain_places, paired=paired_places), "late",
        jax.ShapeDtypeStruct((rows, LANES), BF16), [pltpu.VMEM] * 5, [wide(held)] * 2,
        early, spread, *large, flops=LATE_FLOPS,
    )
    gathered = [packed]
    for step in range(1, groups):
        moves = [((group + step) % groups, group) for group in range(groups)]
        gathered.append(lax.ppermute(packed, "group", moves))
    arrived = lax.all_to_all(
        pieces, "member", split_axis=0, concat_axis=0, tiled=True,
        axis_index_groups=[list(SEND_ORDER)],
    )
    blocks = length // CONTRIB
    value, weight, put, straight, crossed = kernel_call(
        functools.partial(prepare_kernel, columns=columns, share=share, blocks=blocks), "prepare",
        [jax.ShapeDtypeStruct((rows, LANES), F32)] * 2
        + [jax.ShapeDtypeStruct(((share + share % 2) * blocks, 2 * width), BF16)]
        + [jax.ShapeDtypeStruct((width, LANES), F32)] * 2,
        [pltpu.VMEM] * (2 + len(gathered)), [],
        places, made["shift"], *gathered, flops=PREPARE_FLOPS,
    )
    returned = kernel_call(
        functools.partial(subgrid_kernel, columns=columns, bands=bands), "subgrid",
        jax.ShapeDtypeStruct((rows, LANES), BF16), [pltpu.VMEM] * 6, [wide(rows)],
        arrived, value, weight, made["grid_turn"], made["model"], made["back"],
    )
    delivered = lax.all_to_all(
        returned, ("band", "member"), split_axis=0, concat_axis=0, tiled=True,
        axis_index_groups=[
            [b * FACET_ROWS + member for b in reversed(range(bands)) for member in RETURN_ORDER]
        ],
    )
    lines = kernel_call(
        functools.partial(return_kernel, bands=bands), "lines",
        jax.ShapeDtypeStruct((share, 2, length), F32), [pltpu.VMEM] * 10,
        [wide(2 * length // LANES)] * share,
        places, delivered, straight, crossed, put, made["window"], made["turn"],
        made["partial"], made["inner_plus"], made["outer_plus"],
    )
    return lines[None]


def solution(mesh):
    bands = mesh.shape["band"]
    groups = mesh.shape["facet"] // FACET_ROWS
    split_mesh = Mesh(
        mesh.devices.reshape(groups, FACET_ROWS, bands), ("group", "member", "band")
    )
    facet = ("group", "member")
    placed = (
        P("band", facet, None, None, None),
        P(),
        P("band", None, facet, None, None),
        P("band", None, facet, None, None),
        P("band", None, facet, None),
        P("band", None, facet, None),
    )
    return jax.shard_map(
        functools.partial(local, groups, bands),
        mesh=split_mesh,
        in_specs=placed,
        out_specs=P(facet, "band", None, None),
        check_vma=False,
    )
```

```python
import functools
import math

import jax
import jax.numpy as jnp
import ml_dtypes
import numpy as np
from jax import lax
from jax.experimental import pallas as pl
from jax.experimental.pallas import tpu as pltpu
from jax.sharding import Mesh
from jax.sharding import PartitionSpec as P

CONTRIB = 64
FACET_ROWS = 8
SUBGRID = FACET_ROWS * CONTRIB
SEND_ORDER = (FACET_ROWS - 1, *range(FACET_ROWS - 1))
PLACE_ORDER = tuple(range(FACET_ROWS))
LANES = 128
HALF = LANES // 2
EARLY_FLOPS = 10**10
LATE_FLOPS = 10**10
PREPARE_FLOPS = 2 * 10**10
VMEM_LIMIT = 48 * 1024 * 1024
F32 = jnp.float32
BF16 = jnp.bfloat16


def phases(rows, cols, length, rotation):
    product = np.outer(rows, cols) % length
    return np.exp(rotation * 2j * np.pi * product / length)


def from_left(matrix):
    return np.block([[matrix.real, -matrix.imag], [matrix.imag, matrix.real]])


def from_right(matrix):
    return np.block([[matrix.real, matrix.imag], [-matrix.imag, matrix.real]])


def high_low(table):
    high = table.astype(ml_dtypes.bfloat16)
    low = (table - high.astype(np.float64)).astype(ml_dtypes.bfloat16)
    return np.stack([high, low])


def side_by_side(values):
    straight = np.concatenate([values.real, values.real], axis=-1)
    crossed = np.concatenate([-values.imag, values.imag], axis=-1)
    return np.stack([straight, crossed])


def stack_tables(named):
    places, blocks, begin = {}, [], 0
    for name, table in named.items():
        count = table.shape[1] // LANES
        places[name] = (begin, table.shape[0], count)
        blocks += [table[:, i * LANES : (i + 1) * LANES] for i in range(count)]
        begin += table.shape[0] * count
    return np.concatenate(blocks, axis=0), places


def stack_pairs(named):
    return stack_tables(
        {(name, i): table for name, pair in named.items() for i, table in enumerate(pair)}
    )


def tables(length):
    blocks = length // CONTRIB
    short = np.arange(CONTRIB)
    outer = np.concatenate([np.arange(0, blocks, 2), np.arange(1, blocks, 2)])
    window = 1.0 + 0.5 * np.cos(np.arange(length) * (2.0 * math.pi / length))
    window = (window * length**-0.5).reshape(length // LANES, LANES).astype(np.float32)
    turn = np.tile(phases(short, short, length, -1), (1, 2))
    turn = np.stack([turn.real, turn.imag]).astype(np.float32)
    pair = np.eye(2)
    shift = high_low(np.concatenate(side_by_side(phases(short, short, CONTRIB, -1)), axis=1))
    outer_minus = from_left(phases(short, outer, blocks, -1))
    inner_minus = from_right(np.kron(pair, phases(short, short, CONTRIB, -1)))
    piece = from_right(phases(short, short, CONTRIB, 1)) * CONTRIB**-0.5
    return dict(
        plain=stack_tables(dict(window=window, real=turn[0], imag=turn[1])),
        paired=stack_pairs(
            dict(
                shift=shift,
                outer=high_low(outer_minus),
                inner=high_low(inner_minus),
                piece=high_low(piece),
            )
        ),
        window=window,
        turn=turn,
        shift=shift,
        inner_plus=high_low(from_right(np.kron(pair, phases(short, short, CONTRIB, 1)))),
        outer_plus=high_low(from_left(phases(outer, short, blocks, 1))),
        partial=high_low(from_right(phases(short, short, CONTRIB, -1)).T * CONTRIB**-0.5),
        grid_turn=side_by_side(phases(np.arange(FACET_ROWS), short, SUBGRID, -1)).astype(
            np.float32
        ),
        model=high_low(from_right(phases(short, short, CONTRIB, -1)) * SUBGRID**-0.5),
        back=high_low(from_right(phases(short, short, CONTRIB, 1)) * SUBGRID**-0.5),
    )


def return_order(bands):
    order = [(b, member) for b in range(bands) for member in PLACE_ORDER]
    return order[-1:] + order[:-1]


def split(values):
    high = values.astype(BF16)
    return high, (values - high.astype(F32)).astype(BF16)


def dot(left, right, dims=((1,), (0,))):
    return lax.dot_general(left, right, (dims, ((), ())), preferred_element_type=F32)


def dot_split(values, right):
    rows = values.shape[0]
    both = dot(jnp.concatenate(split(values), axis=0), right)
    return both[:rows] + both[rows:]


def times_table(values, table):
    return dot_split(values, table[0]) + dot(values.astype(BF16), table[1])


def table_times(table, values, dims=((1,), (0,))):
    high, low = split(values)
    rows = table[0].shape[0]
    both = dot(jnp.concatenate([table[0], table[1]], axis=0), high, dims)
    return both[:rows] + both[rows:] + dot(table[0], low, dims)


def iota(shape, dimension):
    return lax.broadcasted_iota(jnp.int32, shape, dimension)


def over(values, size):
    return lax.shift_right_logical(values, jnp.full_like(values, size.bit_length() - 1))


def within(values, size):
    return values & (size - 1)


def swap_halves(values):
    return pltpu.roll(values, HALF, 1)


def table_at(ref, place):
    begin, rows, blocks = place
    parts = [ref[begin + i * rows : begin + (i + 1) * rows, :] for i in range(blocks)]
    return parts[0] if blocks == 1 else jnp.concatenate(parts, axis=1)


def offsets_on_lanes(offsets_ref, columns, order):
    fronts, owners = offsets_ref.shape
    groups = owners // FACET_ROWS
    own = lax.axis_index("group")
    begins = []
    for step in range(groups):
        group = own + step
        begins.append(jnp.where(group >= groups, group - groups, group) * FACET_ROWS)
    spread = iota((1, fronts * owners * columns), 1)
    place_of = over(spread, columns)
    for place in range(fronts * owners):
        t, step, spot = place % fronts, place // fronts % groups, place // (fronts * groups)
        member = order[spot]
        spread = jnp.where(place_of == place, offsets_ref[t, begins[step] + member], spread)
    return spread


def shift_rows(residue, table):
    pick = jnp.where(iota((CONTRIB, residue.shape[1]), 0) == residue, 1.0, 0.0).T.astype(BF16)
    rows = dot(pick, table[0]) + dot(pick, table[1])
    return rows[:, :LANES], rows[:, LANES:]


def one_hot(shape, targets):
    return jnp.where(iota(shape, 0) == targets, 1.0, 0.0).astype(BF16)


def turned_eighths(values, rotation):
    sign = jnp.where(iota(values[0].shape, 1) < HALF, -rotation, rotation).astype(F32)

    def quarter_turn(value):
        return swap_halves(value) * sign

    def four(a, b, c, d):
        even_sum, even_diff = a + c, a - c
        odd_sum, odd_diff = b + d, quarter_turn(b - d)
        return even_sum + odd_sum, even_diff + odd_diff, even_sum - odd_sum, even_diff - odd_diff

    even = four(*values[0::2])
    odd = four(*values[1::2])
    root = math.sqrt(0.5)
    turned = (
        odd[0],
        (odd[1] + quarter_turn(odd[1])) * root,
        quarter_turn(odd[2]),
        (quarter_turn(odd[3]) - odd[3]) * root,
    )
    return [e + o for e, o in zip(even, turned)] + [e - o for e, o in zip(even, turned)]


def pack_samples(cells_ref, values_ref, weights_ref, flags_ref, out_ref):
    for t in range(cells_ref.shape[0]):
        rows = [
            cells_ref[t, 0:1, :].astype(F32) * SUBGRID + cells_ref[t, 1:2, :].astype(F32),
            weights_ref[t] * flags_ref[t].astype(F32),
            values_ref[t],
        ]
        out_ref[4 * t : 4 * t + 4, :] = jnp.concatenate(rows, axis=0)


def start_all(sources, targets, semaphores):
    copies = [
        pltpu.make_async_copy(source, target, semaphores.at[i])
        for i, (source, target) in enumerate(zip(sources, targets))
    ]
    for copy in copies:
        copy.start()
    return copies


def predict(spread, copies, strips_ref, plain_ref, paired_ref, held_refs, out_ref, plain, paired):
    columns, length = strips_ref.shape[1:]
    groups = length // LANES
    pairs = columns // 2
    blocks = length // CONTRIB
    width = spread.shape[1]
    first_block, residue = over(spread, CONTRIB), within(spread, CONTRIB)
    base = within(iota(spread.shape, 1), columns) * blocks
    shape = (columns * blocks, width)
    pick_inside = one_hot(shape, base + first_block)
    pick_beyond = one_hot(shape, base + within(first_block + 1, blocks))
    for copy in copies[:2]:
        copy.wait()

    def pair_at(name):
        return [table_at(paired_ref, paired[name, i]) for i in range(2)]

    window = table_at(plain_ref, plain["window"])
    turn_real, turn_imag = table_at(plain_ref, plain["real"]), table_at(plain_ref, plain["imag"])
    low_half = iota((groups, LANES), 1) < HALF
    sections = []
    for part, held in enumerate(held_refs):
        for group in range(groups):
            held[group * columns : (group + 1) * columns, :] = strips_ref[
                part, :, group * LANES : (group + 1) * LANES
            ]
        even, odd = [], []
        for pair in range(pairs):
            first = held[pl.ds(2 * pair, groups, stride=columns), :] * window
            second = held[pl.ds(2 * pair + 1, groups, stride=columns), :] * window
            even.append(jnp.where(low_half, first, swap_halves(second)))
            odd.append(jnp.where(low_half, swap_halves(first), second))
        sections += [jnp.concatenate(even, axis=1), jnp.concatenate(odd, axis=1)]
    for copy in copies[2:]:
        copy.wait()
    section = table_times(pair_at("outer"), jnp.concatenate(sections, axis=0))
    turned = []
    for pair in range(pairs):
        lanes = slice(pair * LANES, (pair + 1) * LANES)
        real, imag = section[:CONTRIB, lanes], section[CONTRIB:, lanes]
        turned.append(
            jnp.concatenate(
                [real * turn_real - imag * turn_imag, real * turn_imag + imag * turn_real],
                axis=1,
            )
        )
    inner = times_table(jnp.concatenate(turned, axis=0), pair_at("inner"))
    spectrum = jnp.concatenate(
        [
            jnp.concatenate(
                [
                    inner[pair * CONTRIB : (pair + 1) * CONTRIB, part * LANES : (part + 1) * LANES]
                    for pair in range(pairs)
                ],
                axis=1,
            )
            for part in range(2)
        ],
        axis=0,
    )
    inside = dot_split(spectrum, pick_inside)
    beyond = dot_split(spectrum, pick_beyond)
    kappa = within(iota((2 * CONTRIB, width), 0), CONTRIB)
    cutout = jnp.where(kappa >= residue, inside, beyond)
    piece = times_table(cutout.T, pair_at("piece"))
    straight, crossed = shift_rows(residue, pair_at("shift"))
    out_ref[...] = (piece * straight + swap_halves(piece) * crossed).astype(BF16)


def in_first_half():
    return 2 * lax.axis_index("group") < lax.axis_size("group")


def early_kernel(
    offsets, cells, values, weights, flags, strips, plain_table, paired_table,
    out_ref, packed_ref, places_ref, spread_ref,
    offsets_ref, cells_ref, values_ref, weights_ref, flags_ref, strips_ref, plain_ref, paired_ref,
    real_ref, imag_ref, small_semaphores, semaphores, *, plain, paired, share,
):
    small = start_all(
        (offsets, cells, values, weights, flags),
        (offsets_ref, cells_ref, values_ref, weights_ref, flags_ref),
        small_semaphores,
    )

    def large():
        sources, targets = (strips, plain_table, paired_table), (strips_ref, plain_ref, paired_ref)
        return [
            pltpu.make_async_copy(source, target, semaphores.at[i])
            for i, (source, target) in enumerate(zip(sources, targets))
        ]

    @pl.when(in_first_half())
    def _():
        for copy in large():
            copy.start()

    for copy in small:
        copy.wait()
    for t in range(cells_ref.shape[0]):
        rows = [
            cells_ref[t, 0:1, :].astype(F32) * SUBGRID + cells_ref[t, 1:2, :].astype(F32),
            weights_ref[t] * flags_ref[t].astype(F32),
            values_ref[t],
        ]
        packed_ref[4 * t : 4 * t + 4, :] = jnp.concatenate(rows, axis=0)
    places_ref[...] = offsets_on_lanes(offsets_ref, share, PLACE_ORDER)
    spread_ref[...] = offsets_on_lanes(offsets_ref, strips_ref.shape[1], SEND_ORDER)

    @pl.when(in_first_half())
    def _():
        predict(
            spread_ref[...], large(), strips_ref, plain_ref, paired_ref, (real_ref, imag_ref),
            out_ref, plain, paired,
        )


def late_kernel(
    early_ref, spread_ref, strips_ref, plain_ref, paired_ref, out_ref, real_ref, imag_ref,
    *, plain, paired,
):
    @pl.when(in_first_half())
    def _():
        out_ref[...] = early_ref[...]

    @pl.when(jnp.logical_not(in_first_half()))
    def _():
        predict(
            spread_ref[...], (), strips_ref, plain_ref, paired_ref, (real_ref, imag_ref), out_ref,
            plain, paired,
        )


def prepare_kernel(places_ref, shift_ref, *refs, columns, share, blocks):
    samples_refs, outs = refs[:-5], refs[-5:]
    value_ref, weight_ref, put_ref, straight_ref, crossed_ref = outs
    fronts, samples = samples_refs[0].shape[0] // 4, samples_refs[0].shape[1]
    own = lax.axis_index("group")
    depth = FACET_ROWS * columns
    for spot in range(len(samples_refs) * fronts):
        step, t = spot // fronts, spot % fronts
        sample = samples_refs[step][4 * t : 4 * t + 4, :]
        cell = sample[0:1, :].astype(jnp.int32)
        row, col = over(cell, SUBGRID) - own * columns, within(cell, SUBGRID)
        inside = (row >= 0) & (row < columns)
        target = jnp.where(inside, within(col, FACET_ROWS) * columns + row, -1)
        pick = one_hot((depth, samples), target)
        mask = iota((HALF, samples), 0) == over(col, FACET_ROWS)
        factor = sample[1:2, :]
        highs, lows = [], []
        for term in (factor * sample[2:3, :], factor * sample[3:4, :], factor):
            high = term.astype(BF16).astype(F32)
            highs.append(jnp.where(mask, high, 0.0).astype(BF16))
            lows.append(jnp.where(mask, term - high, 0.0).astype(BF16))
        highs, lows = highs + highs[2:], lows + lows[2:]
        grid = dot(pick, jnp.concatenate(highs, axis=0), ((1,), (1,))) + dot(
            pick, jnp.concatenate(lows, axis=0), ((1,), (1,))
        )
        rows = slice(spot * depth, (spot + 1) * depth)
        value_ref[rows, :] = grid[:, :LANES]
        weight_ref[rows, :] = grid[:, LANES:]
    spread = places_ref[...]
    first_block, residue = over(spread, CONTRIB), within(spread, CONTRIB)
    straight_ref[...], crossed_ref[...] = shift_rows(residue, shift_ref)
    base = within(iota(spread.shape, 1), share) * blocks
    targets = jnp.concatenate([base + first_block, base + within(first_block + 1, blocks)], axis=1)
    put_ref[...] = one_hot(put_ref.shape, targets)


def subgrid_kernel(
    pieces_ref, value_ref, weight_ref, turn_ref, model_ref, back_ref, out_ref, held_ref,
    *, columns, bands,
):
    rows = pieces_ref.shape[0] // FACET_ROWS
    spots = range(rows // columns)
    depth = FACET_ROWS * columns
    share = columns // bands
    pieces = pieces_ref[...].astype(F32)
    sky = turned_eighths(
        [
            pieces[spot * rows : (spot + 1) * rows, :]
            for spot in (SEND_ORDER.index(i) for i in range(FACET_ROWS))
        ],
        -1.0,
    )
    sky = [
        value * turn_ref[0, i : i + 1, :] + swap_halves(value) * turn_ref[1, i : i + 1, :]
        for i, value in enumerate(sky)
    ]
    stacked = jnp.concatenate(
        [value[spot * columns : (spot + 1) * columns, :] for spot in spots for value in sky],
        axis=0,
    )
    grid = value_ref[...] - weight_ref[...] * times_table(stacked, model_ref)
    back = times_table(grid, back_ref)
    lines = []
    for i in range(FACET_ROWS):
        value = jnp.concatenate(
            [
                back[spot * depth + i * columns : spot * depth + (i + 1) * columns, :]
                for spot in spots
            ],
            axis=0,
        )
        lines.append(
            value * turn_ref[0, i : i + 1, :] - swap_halves(value) * turn_ref[1, i : i + 1, :]
        )
    lines = turned_eighths(lines, 1.0)
    for i in range(FACET_ROWS):
        for spot in spots:
            for b in range(bands):
                source = spot * columns + b * share
                place = return_order(bands).index((b, i))
                target = (place * len(spots) + spot) * share
                held_ref[target : target + share, :] = lines[i][source : source + share, :]
    out_ref[...] = held_ref[...].astype(BF16)


def return_kernel(
    places_ref, pieces_ref, straight_ref, crossed_ref, put_ref, window_ref, turn_ref, partial_ref,
    inner_ref, outer_ref, out_ref, *line_refs, bands,
):
    columns, _, length = out_ref.shape
    blocks = length // CONTRIB
    groups = length // LANES
    pairs = (columns + 1) // 2
    width = pieces_ref.shape[0] // bands
    pieces = pieces_ref[...].astype(F32)
    order, rows = return_order(bands), width // FACET_ROWS

    def of_band(b):
        begins = [order.index((b, member)) * rows for member in PLACE_ORDER]
        return jnp.concatenate([pieces[begin : begin + rows, :] for begin in begins], axis=0)

    summed = of_band(0)
    for b in range(1, bands):
        summed += of_band(b)
    summed = summed * straight_ref[...] - swap_halves(summed) * crossed_ref[...]
    residues = table_times(partial_ref, summed, ((1,), (1,)))
    kappa = within(iota((2 * CONTRIB, width), 0), CONTRIB)
    inside = kappa >= within(places_ref[...], CONTRIB)
    both = jnp.concatenate(
        [jnp.where(inside, residues, 0.0), jnp.where(inside, 0.0, residues)], axis=1
    )
    put = put_ref[...]
    high, low = split(both)
    spectrum = dot(high, put, ((1,), (1,))) + dot(low, put, ((1,), (1,)))
    inner = times_table(
        jnp.concatenate(
            [
                jnp.concatenate(
                    [
                        spectrum[:CONTRIB, pair * LANES : (pair + 1) * LANES],
                        spectrum[CONTRIB:, pair * LANES : (pair + 1) * LANES],
                    ],
                    axis=1,
                )
                for pair in range(pairs)
            ],
            axis=0,
        ),
        inner_ref,
    )
    reals, imags = [], []
    for pair in range(pairs):
        rows = slice(pair * CONTRIB, (pair + 1) * CONTRIB)
        real, imag = inner[rows, :LANES], inner[rows, LANES:]
        reals.append(real * turn_ref[0] + imag * turn_ref[1])
        imags.append(imag * turn_ref[0] - real * turn_ref[1])
    lines = table_times(
        outer_ref,
        jnp.concatenate(
            [jnp.concatenate(reals, axis=1), jnp.concatenate(imags, axis=1)], axis=0
        ),
    )
    window = window_ref[...]
    low_half = iota((groups, LANES), 1) < HALF
    for part in range(2):
        for pair in range(pairs):
            lanes = slice(pair * LANES, (pair + 1) * LANES)
            begin = part * blocks
            even = lines[begin : begin + groups, lanes]
            odd = lines[begin + groups : begin + blocks, lanes]
            line_refs[2 * pair][pl.ds(part, groups, stride=2), :] = (
                jnp.where(low_half, even, swap_halves(odd)) * window
            )
            if 2 * pair + 1 < columns:
                line_refs[2 * pair + 1][pl.ds(part, groups, stride=2), :] = (
                    jnp.where(low_half, swap_halves(even), odd) * window
                )
    for column in range(columns):
        for group in range(groups):
            out_ref[column, :, group * LANES : (group + 1) * LANES] = line_refs[column][
                2 * group : 2 * group + 2, :
            ]


def kernel_call(kernel, name, out_shape, spaces, scratch, *operands, flops=0):
    return pl.pallas_call(
        kernel,
        out_shape=out_shape,
        in_specs=[pl.BlockSpec(memory_space=space) for space in spaces],
        out_specs=jax.tree.map(lambda _: pl.BlockSpec(memory_space=pltpu.VMEM), out_shape),
        scratch_shapes=scratch,
        compiler_params=pltpu.CompilerParams(vmem_limit_bytes=VMEM_LIMIT),
        cost_estimate=pl.CostEstimate(flops=flops, bytes_accessed=0, transcendentals=0)
        if flops
        else None,
        name=name,
    )(*operands)


def wide(rows):
    return pltpu.VMEM((rows, LANES), F32)


def local(groups, bands, strips, offsets, cells, values, weights, flags):
    columns, length = strips.shape[-2:]
    fronts = offsets.shape[0]
    share = columns // bands
    facets = groups * FACET_ROWS
    rows = facets * fronts * columns
    width = facets * fronts * share
    made = tables(length)
    plain, plain_places = made.pop("plain")
    paired, paired_places = made.pop("paired")
    made = {key: jnp.asarray(value) for key, value in made.items()}
    held = length // LANES * columns
    small = [offsets, cells[0, :, 0], values[0, :, 0], weights[0], flags[0]]
    large = [strips[0, 0], jnp.asarray(plain), jnp.asarray(paired)]

    def landing(arrays):
        return [
            (pltpu.SMEM if array is offsets else pltpu.VMEM)(array.shape, array.dtype)
            for array in arrays
        ]

    def in_hbm(arrays):
        return [pltpu.with_memory_space_constraint(array, pltpu.HBM) for array in arrays]

    def semaphores(count):
        return pltpu.SemaphoreType.DMA((count,))

    early, packed, places, spread = kernel_call(
        functools.partial(early_kernel, plain=plain_places, paired=paired_places, share=share),
        "early",
        [
            jax.ShapeDtypeStruct((rows, LANES), BF16),
            jax.ShapeDtypeStruct((4 * fronts, cells.shape[-1]), F32),
            jax.ShapeDtypeStruct((1, width), jnp.int32),
            jax.ShapeDtypeStruct((1, rows), jnp.int32),
        ],
        [pltpu.HBM] * 8,
        landing(small + large) + [wide(held)] * 2 + [semaphores(5), semaphores(3)],
        *in_hbm(small + large), flops=EARLY_FLOPS,
    )
    pieces = kernel_call(
        functools.partial(late_kernel, plain=plain_places, paired=paired_places), "late",
        jax.ShapeDtypeStruct((rows, LANES), BF16), [pltpu.VMEM] * 5, [wide(held)] * 2,
        early, spread, *large, flops=LATE_FLOPS,
    )
    gathered = [packed]
    for step in range(1, groups):
        moves = [((group + step) % groups, group) for group in range(groups)]
        gathered.append(lax.ppermute(packed, "group", moves))
    arrived = lax.all_to_all(
        pieces, "member", split_axis=0, concat_axis=0, tiled=True,
        axis_index_groups=[list(SEND_ORDER)],
    )
    blocks = length // CONTRIB
    value, weight, put, straight, crossed = kernel_call(
        functools.partial(prepare_kernel, columns=columns, share=share, blocks=blocks), "prepare",
        [jax.ShapeDtypeStruct((rows, LANES), F32)] * 2
        + [jax.ShapeDtypeStruct(((share + share % 2) * blocks, 2 * width), BF16)]
        + [jax.ShapeDtypeStruct((width, LANES), F32)] * 2,
        [pltpu.VMEM] * (2 + len(gathered)), [],
        places, made["shift"], *gathered, flops=PREPARE_FLOPS,
    )
    returned = kernel_call(
        functools.partial(subgrid_kernel, columns=columns, bands=bands), "subgrid",
        jax.ShapeDtypeStruct((rows, LANES), BF16), [pltpu.VMEM] * 6, [wide(rows)],
        arrived, value, weight, made["grid_turn"], made["model"], made["back"],
    )
    delivered = lax.all_to_all(
        returned, ("band", "member"), split_axis=0, concat_axis=0, tiled=True,
        axis_index_groups=[
            [b * FACET_ROWS + member for b, member in return_order(bands)]
        ],
    )
    lines = kernel_call(
        functools.partial(return_kernel, bands=bands), "lines",
        jax.ShapeDtypeStruct((share, 2, length), F32), [pltpu.VMEM] * 10,
        [wide(2 * length // LANES)] * share,
        places, delivered, straight, crossed, put, made["window"], made["turn"],
        made["partial"], made["inner_plus"], made["outer_plus"],
    )
    return lines[None]


def solution(mesh):
    bands = mesh.shape["band"]
    groups = mesh.shape["facet"] // FACET_ROWS
    split_mesh = Mesh(
        mesh.devices.reshape(groups, FACET_ROWS, bands), ("group", "member", "band")
    )
    facet = ("group", "member")
    placed = (
        P("band", facet, None, None, None),
        P(),
        P("band", None, facet, None, None),
        P("band", None, facet, None, None),
        P("band", None, facet, None),
        P("band", None, facet, None),
    )
    return jax.shard_map(
        functools.partial(local, groups, bands),
        mesh=split_mesh,
        in_specs=placed,
        out_specs=P(facet, "band", None, None),
        check_vma=False,
    )
```

```python
import functools
import math

import jax
import jax.numpy as jnp
import ml_dtypes
import numpy as np
from jax import lax
from jax.experimental import pallas as pl
from jax.experimental.pallas import tpu as pltpu
from jax.sharding import Mesh
from jax.sharding import PartitionSpec as P

CONTRIB = 64
FACET_ROWS = 8
SUBGRID = FACET_ROWS * CONTRIB
SEND_ORDER = tuple(FACET_ROWS - 1 - (i ^ (i >> 1)) for i in range(FACET_ROWS))
PLACE_ORDER = tuple(range(FACET_ROWS))
LANES = 128
HALF = LANES // 2
EARLY_FLOPS = 10**10
LATE_FLOPS = 10**10
PREPARE_FLOPS = 2 * 10**10
VMEM_LIMIT = 48 * 1024 * 1024
F32 = jnp.float32
BF16 = jnp.bfloat16


def phases(rows, cols, length, rotation):
    product = np.outer(rows, cols) % length
    return np.exp(rotation * 2j * np.pi * product / length)


def from_left(matrix):
    return np.block([[matrix.real, -matrix.imag], [matrix.imag, matrix.real]])


def from_right(matrix):
    return np.block([[matrix.real, matrix.imag], [-matrix.imag, matrix.real]])


def high_low(table):
    high = table.astype(ml_dtypes.bfloat16)
    low = (table - high.astype(np.float64)).astype(ml_dtypes.bfloat16)
    return np.stack([high, low])


def side_by_side(values):
    straight = np.concatenate([values.real, values.real], axis=-1)
    crossed = np.concatenate([-values.imag, values.imag], axis=-1)
    return np.stack([straight, crossed])


def stack_tables(named):
    places, blocks, begin = {}, [], 0
    for name, table in named.items():
        count = table.shape[1] // LANES
        places[name] = (begin, table.shape[0], count)
        blocks += [table[:, i * LANES : (i + 1) * LANES] for i in range(count)]
        begin += table.shape[0] * count
    return np.concatenate(blocks, axis=0), places


def stack_pairs(named):
    return stack_tables(
        {(name, i): table for name, pair in named.items() for i, table in enumerate(pair)}
    )


def tables(length):
    blocks = length // CONTRIB
    short = np.arange(CONTRIB)
    outer = np.concatenate([np.arange(0, blocks, 2), np.arange(1, blocks, 2)])
    window = 1.0 + 0.5 * np.cos(np.arange(length) * (2.0 * math.pi / length))
    window = (window * length**-0.5).reshape(length // LANES, LANES).astype(np.float32)
    turn = np.tile(phases(short, short, length, -1), (1, 2))
    turn = np.stack([turn.real, turn.imag]).astype(np.float32)
    pair = np.eye(2)
    shift = high_low(np.concatenate(side_by_side(phases(short, short, CONTRIB, -1)), axis=1))
    outer_minus = from_left(phases(short, outer, blocks, -1))
    inner_minus = from_right(np.kron(pair, phases(short, short, CONTRIB, -1)))
    piece = from_right(phases(short, short, CONTRIB, 1)) * CONTRIB**-0.5
    return dict(
        plain=stack_tables(dict(window=window, real=turn[0], imag=turn[1])),
        paired=stack_pairs(
            dict(
                shift=shift,
                outer=high_low(outer_minus),
                inner=high_low(inner_minus),
                piece=high_low(piece),
            )
        ),
        window=window,
        turn=turn,
        shift=shift,
        inner_plus=high_low(from_right(np.kron(pair, phases(short, short, CONTRIB, 1)))),
        outer_plus=high_low(from_left(phases(outer, short, blocks, 1))),
        partial=high_low(from_right(phases(short, short, CONTRIB, -1)).T * CONTRIB**-0.5),
        grid_turn=side_by_side(phases(np.arange(FACET_ROWS), short, SUBGRID, -1)).astype(
            np.float32
        ),
        model=high_low(from_right(phases(short, short, CONTRIB, -1)) * SUBGRID**-0.5),
        back=high_low(from_right(phases(short, short, CONTRIB, 1)) * SUBGRID**-0.5),
    )


def return_order(bands):
    last = bands * FACET_ROWS - 1
    return [divmod(last - (i ^ (i >> 1)), FACET_ROWS) for i in range(last + 1)]


def split(values):
    high = values.astype(BF16)
    return high, (values - high.astype(F32)).astype(BF16)


def dot(left, right, dims=((1,), (0,))):
    return lax.dot_general(left, right, (dims, ((), ())), preferred_element_type=F32)


def dot_split(values, right):
    rows = values.shape[0]
    both = dot(jnp.concatenate(split(values), axis=0), right)
    return both[:rows] + both[rows:]


def times_table(values, table):
    return dot_split(values, table[0]) + dot(values.astype(BF16), table[1])


def table_times(table, values, dims=((1,), (0,))):
    high, low = split(values)
    rows = table[0].shape[0]
    both = dot(jnp.concatenate([table[0], table[1]], axis=0), high, dims)
    return both[:rows] + both[rows:] + dot(table[0], low, dims)


def iota(shape, dimension):
    return lax.broadcasted_iota(jnp.int32, shape, dimension)


def over(values, size):
    return lax.shift_right_logical(values, jnp.full_like(values, size.bit_length() - 1))


def within(values, size):
    return values & (size - 1)


def swap_halves(values):
    return pltpu.roll(values, HALF, 1)


def table_at(ref, place):
    begin, rows, blocks = place
    parts = [ref[begin + i * rows : begin + (i + 1) * rows, :] for i in range(blocks)]
    return parts[0] if blocks == 1 else jnp.concatenate(parts, axis=1)


def offsets_on_lanes(offsets_ref, columns, order):
    fronts, owners = offsets_ref.shape
    groups = owners // FACET_ROWS
    own = lax.axis_index("group")
    begins = []
    for step in range(groups):
        group = own + step
        begins.append(jnp.where(group >= groups, group - groups, group) * FACET_ROWS)
    spread = iota((1, fronts * owners * columns), 1)
    place_of = over(spread, columns)
    for place in range(fronts * owners):
        t, step, spot = place % fronts, place // fronts % groups, place // (fronts * groups)
        member = order[spot]
        spread = jnp.where(place_of == place, offsets_ref[t, begins[step] + member], spread)
    return spread


def shift_rows(residue, table):
    pick = jnp.where(iota((CONTRIB, residue.shape[1]), 0) == residue, 1.0, 0.0).T.astype(BF16)
    rows = dot(pick, table[0]) + dot(pick, table[1])
    return rows[:, :LANES], rows[:, LANES:]


def one_hot(shape, targets):
    return jnp.where(iota(shape, 0) == targets, 1.0, 0.0).astype(BF16)


def turned_eighths(values, rotation):
    sign = jnp.where(iota(values[0].shape, 1) < HALF, -rotation, rotation).astype(F32)

    def quarter_turn(value):
        return swap_halves(value) * sign

    def four(a, b, c, d):
        even_sum, even_diff = a + c, a - c
        odd_sum, odd_diff = b + d, quarter_turn(b - d)
        return even_sum + odd_sum, even_diff + odd_diff, even_sum - odd_sum, even_diff - odd_diff

    even = four(*values[0::2])
    odd = four(*values[1::2])
    root = math.sqrt(0.5)
    turned = (
        odd[0],
        (odd[1] + quarter_turn(odd[1])) * root,
        quarter_turn(odd[2]),
        (quarter_turn(odd[3]) - odd[3]) * root,
    )
    return [e + o for e, o in zip(even, turned)] + [e - o for e, o in zip(even, turned)]


def pack_samples(cells_ref, values_ref, weights_ref, flags_ref, out_ref):
    for t in range(cells_ref.shape[0]):
        rows = [
            cells_ref[t, 0:1, :].astype(F32) * SUBGRID + cells_ref[t, 1:2, :].astype(F32),
            weights_ref[t] * flags_ref[t].astype(F32),
            values_ref[t],
        ]
        out_ref[4 * t : 4 * t + 4, :] = jnp.concatenate(rows, axis=0)


def start_all(sources, targets, semaphores):
    copies = [
        pltpu.make_async_copy(source, target, semaphores.at[i])
        for i, (source, target) in enumerate(zip(sources, targets))
    ]
    for copy in copies:
        copy.start()
    return copies


def predict(spread, copies, strips_ref, plain_ref, paired_ref, held_refs, out_ref, plain, paired):
    columns, length = strips_ref.shape[1:]
    groups = length // LANES
    pairs = columns // 2
    blocks = length // CONTRIB
    width = spread.shape[1]
    first_block, residue = over(spread, CONTRIB), within(spread, CONTRIB)
    base = within(iota(spread.shape, 1), columns) * blocks
    shape = (columns * blocks, width)
    pick_inside = one_hot(shape, base + first_block)
    pick_beyond = one_hot(shape, base + within(first_block + 1, blocks))
    for copy in copies[:2]:
        copy.wait()

    def pair_at(name):
        return [table_at(paired_ref, paired[name, i]) for i in range(2)]

    window = table_at(plain_ref, plain["window"])
    turn_real, turn_imag = table_at(plain_ref, plain["real"]), table_at(plain_ref, plain["imag"])
    low_half = iota((groups, LANES), 1) < HALF
    sections = []
    for part, held in enumerate(held_refs):
        for group in range(groups):
            held[group * columns : (group + 1) * columns, :] = strips_ref[
                part, :, group * LANES : (group + 1) * LANES
            ]
        even, odd = [], []
        for pair in range(pairs):
            first = held[pl.ds(2 * pair, groups, stride=columns), :] * window
            second = held[pl.ds(2 * pair + 1, groups, stride=columns), :] * window
            even.append(jnp.where(low_half, first, swap_halves(second)))
            odd.append(jnp.where(low_half, swap_halves(first), second))
        sections += [jnp.concatenate(even, axis=1), jnp.concatenate(odd, axis=1)]
    for copy in copies[2:]:
        copy.wait()
    section = table_times(pair_at("outer"), jnp.concatenate(sections, axis=0))
    turned = []
    for pair in range(pairs):
        lanes = slice(pair * LANES, (pair + 1) * LANES)
        real, imag = section[:CONTRIB, lanes], section[CONTRIB:, lanes]
        turned.append(
            jnp.concatenate(
                [real * turn_real - imag * turn_imag, real * turn_imag + imag * turn_real],
                axis=1,
            )
        )
    inner = times_table(jnp.concatenate(turned, axis=0), pair_at("inner"))
    spectrum = jnp.concatenate(
        [
            jnp.concatenate(
                [
                    inner[pair * CONTRIB : (pair + 1) * CONTRIB, part * LANES : (part + 1) * LANES]
                    for pair in range(pairs)
                ],
                axis=1,
            )
            for part in range(2)
        ],
        axis=0,
    )
    inside = dot_split(spectrum, pick_inside)
    beyond = dot_split(spectrum, pick_beyond)
    kappa = within(iota((2 * CONTRIB, width), 0), CONTRIB)
    cutout = jnp.where(kappa >= residue, inside, beyond)
    piece = times_table(cutout.T, pair_at("piece"))
    straight, crossed = shift_rows(residue, pair_at("shift"))
    out_ref[...] = (piece * straight + swap_halves(piece) * crossed).astype(BF16)


def in_first_half():
    return 2 * lax.axis_index("group") < lax.axis_size("group")


def early_kernel(
    offsets, cells, values, weights, flags, strips, plain_table, paired_table,
    out_ref, packed_ref, places_ref, spread_ref,
    offsets_ref, cells_ref, values_ref, weights_ref, flags_ref, strips_ref, plain_ref, paired_ref,
    real_ref, imag_ref, small_semaphores, semaphores, *, plain, paired, share,
):
    def large():
        sources, targets = (strips, plain_table, paired_table), (strips_ref, plain_ref, paired_ref)
        return [
            pltpu.make_async_copy(source, target, semaphores.at[i])
            for i, (source, target) in enumerate(zip(sources, targets))
        ]

    @pl.when(in_first_half())
    def _():
        for copy in large():
            copy.start()

    small = start_all(
        (offsets, cells, values, weights, flags),
        (offsets_ref, cells_ref, values_ref, weights_ref, flags_ref),
        small_semaphores,
    )
    for copy in small:
        copy.wait()
    for t in range(cells_ref.shape[0]):
        rows = [
            cells_ref[t, 0:1, :].astype(F32) * SUBGRID + cells_ref[t, 1:2, :].astype(F32),
            weights_ref[t] * flags_ref[t].astype(F32),
            values_ref[t],
        ]
        packed_ref[4 * t : 4 * t + 4, :] = jnp.concatenate(rows, axis=0)
    places_ref[...] = offsets_on_lanes(offsets_ref, share, PLACE_ORDER)
    spread_ref[...] = offsets_on_lanes(offsets_ref, strips_ref.shape[1], SEND_ORDER)

    @pl.when(in_first_half())
    def _():
        predict(
            spread_ref[...], large(), strips_ref, plain_ref, paired_ref, (real_ref, imag_ref),
            out_ref, plain, paired,
        )


def late_kernel(
    early_ref, spread_ref, strips_ref, plain_ref, paired_ref, out_ref, real_ref, imag_ref,
    *, plain, paired,
):
    @pl.when(in_first_half())
    def _():
        out_ref[...] = early_ref[...]

    @pl.when(jnp.logical_not(in_first_half()))
    def _():
        predict(
            spread_ref[...], (), strips_ref, plain_ref, paired_ref, (real_ref, imag_ref), out_ref,
            plain, paired,
        )


def prepare_kernel(places_ref, shift_ref, *refs, columns, share, blocks):
    samples_refs, outs = refs[:-5], refs[-5:]
    value_ref, weight_ref, put_ref, straight_ref, crossed_ref = outs
    fronts, samples = samples_refs[0].shape[0] // 4, samples_refs[0].shape[1]
    own = lax.axis_index("group")
    depth = FACET_ROWS * columns
    for spot in range(len(samples_refs) * fronts):
        step, t = spot // fronts, spot % fronts
        sample = samples_refs[step][4 * t : 4 * t + 4, :]
        cell = sample[0:1, :].astype(jnp.int32)
        row, col = over(cell, SUBGRID) - own * columns, within(cell, SUBGRID)
        inside = (row >= 0) & (row < columns)
        target = jnp.where(inside, within(col, FACET_ROWS) * columns + row, -1)
        pick = one_hot((depth, samples), target)
        mask = iota((HALF, samples), 0) == over(col, FACET_ROWS)
        factor = sample[1:2, :]
        highs, lows = [], []
        for term in (factor * sample[2:3, :], factor * sample[3:4, :], factor):
            high = term.astype(BF16).astype(F32)
            highs.append(jnp.where(mask, high, 0.0).astype(BF16))
            lows.append(jnp.where(mask, term - high, 0.0).astype(BF16))
        highs, lows = highs + highs[2:], lows + lows[2:]
        grid = dot(pick, jnp.concatenate(highs, axis=0), ((1,), (1,))) + dot(
            pick, jnp.concatenate(lows, axis=0), ((1,), (1,))
        )
        rows = slice(spot * depth, (spot + 1) * depth)
        value_ref[rows, :] = grid[:, :LANES]
        weight_ref[rows, :] = grid[:, LANES:]
    spread = places_ref[...]
    first_block, residue = over(spread, CONTRIB), within(spread, CONTRIB)
    straight_ref[...], crossed_ref[...] = shift_rows(residue, shift_ref)
    base = within(iota(spread.shape, 1), share) * blocks
    targets = jnp.concatenate([base + first_block, base + within(first_block + 1, blocks)], axis=1)
    put_ref[...] = one_hot(put_ref.shape, targets)


def subgrid_kernel(
    pieces_ref, value_ref, weight_ref, turn_ref, model_ref, back_ref, out_ref, held_ref,
    *, columns, bands,
):
    rows = pieces_ref.shape[0] // FACET_ROWS
    spots = range(rows // columns)
    depth = FACET_ROWS * columns
    share = columns // bands
    pieces = pieces_ref[...].astype(F32)
    sky = turned_eighths(
        [
            pieces[spot * rows : (spot + 1) * rows, :]
            for spot in (SEND_ORDER.index(i) for i in range(FACET_ROWS))
        ],
        -1.0,
    )
    sky = [
        value * turn_ref[0, i : i + 1, :] + swap_halves(value) * turn_ref[1, i : i + 1, :]
        for i, value in enumerate(sky)
    ]
    stacked = jnp.concatenate(
        [value[spot * columns : (spot + 1) * columns, :] for spot in spots for value in sky],
        axis=0,
    )
    grid = value_ref[...] - weight_ref[...] * times_table(stacked, model_ref)
    back = times_table(grid, back_ref)
    lines = []
    for i in range(FACET_ROWS):
        value = jnp.concatenate(
            [
                back[spot * depth + i * columns : spot * depth + (i + 1) * columns, :]
                for spot in spots
            ],
            axis=0,
        )
        lines.append(
            value * turn_ref[0, i : i + 1, :] - swap_halves(value) * turn_ref[1, i : i + 1, :]
        )
    lines = turned_eighths(lines, 1.0)
    for i in range(FACET_ROWS):
        for spot in spots:
            for b in range(bands):
                source = spot * columns + b * share
                place = return_order(bands).index((b, i))
                target = (place * len(spots) + spot) * share
                held_ref[target : target + share, :] = lines[i][source : source + share, :]
    out_ref[...] = held_ref[...].astype(BF16)


def return_kernel(
    places_ref, pieces_ref, straight_ref, crossed_ref, put_ref, window_ref, turn_ref, partial_ref,
    inner_ref, outer_ref, result, out_ref, semaphores, *line_refs, bands,
):
    columns, _, length = out_ref.shape
    blocks = length // CONTRIB
    groups = length // LANES
    pairs = (columns + 1) // 2
    width = pieces_ref.shape[0] // bands
    pieces = pieces_ref[...].astype(F32)
    order, rows = return_order(bands), width // FACET_ROWS

    def of_band(b):
        begins = [order.index((b, member)) * rows for member in PLACE_ORDER]
        return jnp.concatenate([pieces[begin : begin + rows, :] for begin in begins], axis=0)

    summed = of_band(0)
    for b in range(1, bands):
        summed += of_band(b)
    summed = summed * straight_ref[...] - swap_halves(summed) * crossed_ref[...]
    residues = table_times(partial_ref, summed, ((1,), (1,)))
    kappa = within(iota((2 * CONTRIB, width), 0), CONTRIB)
    inside = kappa >= within(places_ref[...], CONTRIB)
    both = jnp.concatenate(
        [jnp.where(inside, residues, 0.0), jnp.where(inside, 0.0, residues)], axis=1
    )
    put = put_ref[...]
    high, low = split(both)
    spectrum = dot(high, put, ((1,), (1,))) + dot(low, put, ((1,), (1,)))
    inner = times_table(
        jnp.concatenate(
            [
                jnp.concatenate(
                    [
                        spectrum[:CONTRIB, pair * LANES : (pair + 1) * LANES],
                        spectrum[CONTRIB:, pair * LANES : (pair + 1) * LANES],
                    ],
                    axis=1,
                )
                for pair in range(pairs)
            ],
            axis=0,
        ),
        inner_ref,
    )
    reals, imags = [], []
    for pair in range(pairs):
        rows = slice(pair * CONTRIB, (pair + 1) * CONTRIB)
        real, imag = inner[rows, :LANES], inner[rows, LANES:]
        reals.append(real * turn_ref[0] + imag * turn_ref[1])
        imags.append(imag * turn_ref[0] - real * turn_ref[1])
    lines = table_times(
        outer_ref,
        jnp.concatenate(
            [jnp.concatenate(reals, axis=1), jnp.concatenate(imags, axis=1)], axis=0
        ),
    )
    window = window_ref[...]
    low_half = iota((groups, LANES), 1) < HALF
    copies = []
    for pair in range(pairs):
        lanes = slice(pair * LANES, (pair + 1) * LANES)
        held = [column for column in (2 * pair, 2 * pair + 1) if column < columns]
        for part in range(2):
            begin = part * blocks
            even = lines[begin : begin + groups, lanes]
            odd = lines[begin + groups : begin + blocks, lanes]
            both = (
                jnp.where(low_half, even, swap_halves(odd)),
                jnp.where(low_half, swap_halves(even), odd),
            )
            for column, line in zip(held, both):
                line_refs[column][pl.ds(part, groups, stride=2), :] = line * window
        for column in held:
            for group in range(groups):
                out_ref[column, :, group * LANES : (group + 1) * LANES] = line_refs[column][
                    2 * group : 2 * group + 2, :
                ]
            copies.append(
                pltpu.make_async_copy(
                    out_ref.at[column], result.at[column], semaphores.at[column]
                )
            )
            copies[-1].start()
    for copy in copies:
        copy.wait()


def kernel_call(
    kernel, name, out_shape, spaces, scratch, *operands, flops=0, out_space=pltpu.VMEM
):
    return pl.pallas_call(
        kernel,
        out_shape=out_shape,
        in_specs=[pl.BlockSpec(memory_space=space) for space in spaces],
        out_specs=jax.tree.map(lambda _: pl.BlockSpec(memory_space=out_space), out_shape),
        scratch_shapes=scratch,
        compiler_params=pltpu.CompilerParams(vmem_limit_bytes=VMEM_LIMIT),
        cost_estimate=pl.CostEstimate(flops=flops, bytes_accessed=0, transcendentals=0)
        if flops
        else None,
        name=name,
    )(*operands)


def wide(rows):
    return pltpu.VMEM((rows, LANES), F32)


def local(groups, bands, strips, offsets, cells, values, weights, flags):
    columns, length = strips.shape[-2:]
    fronts = offsets.shape[0]
    share = columns // bands
    facets = groups * FACET_ROWS
    rows = facets * fronts * columns
    width = facets * fronts * share
    made = tables(length)
    plain, plain_places = made.pop("plain")
    paired, paired_places = made.pop("paired")
    made = {key: jnp.asarray(value) for key, value in made.items()}
    held = length // LANES * columns
    small = [offsets, cells[0, :, 0], values[0, :, 0], weights[0], flags[0]]
    large = [strips[0, 0], jnp.asarray(plain), jnp.asarray(paired)]

    def landing(arrays):
        return [
            (pltpu.SMEM if array is offsets else pltpu.VMEM)(array.shape, array.dtype)
            for array in arrays
        ]

    def in_hbm(arrays):
        return [pltpu.with_memory_space_constraint(array, pltpu.HBM) for array in arrays]

    def semaphores(count):
        return pltpu.SemaphoreType.DMA((count,))

    early, packed, places, spread = kernel_call(
        functools.partial(early_kernel, plain=plain_places, paired=paired_places, share=share),
        "early",
        [
            jax.ShapeDtypeStruct((rows, LANES), BF16),
            jax.ShapeDtypeStruct((4 * fronts, cells.shape[-1]), F32),
            jax.ShapeDtypeStruct((1, width), jnp.int32),
            jax.ShapeDtypeStruct((1, rows), jnp.int32),
        ],
        [pltpu.HBM] * 8,
        landing(small + large) + [wide(held)] * 2 + [semaphores(5), semaphores(3)],
        *in_hbm(small + large), flops=EARLY_FLOPS,
    )
    pieces = kernel_call(
        functools.partial(late_kernel, plain=plain_places, paired=paired_places), "late",
        jax.ShapeDtypeStruct((rows, LANES), BF16), [pltpu.VMEM] * 5, [wide(held)] * 2,
        early, spread, *large, flops=LATE_FLOPS,
    )
    gathered = [packed]
    for step in range(1, groups):
        moves = [((group + step) % groups, group) for group in range(groups)]
        gathered.append(lax.ppermute(packed, "group", moves))
    arrived = lax.all_to_all(
        pieces, "member", split_axis=0, concat_axis=0, tiled=True,
        axis_index_groups=[list(SEND_ORDER)],
    )
    blocks = length // CONTRIB
    value, weight, put, straight, crossed = kernel_call(
        functools.partial(prepare_kernel, columns=columns, share=share, blocks=blocks), "prepare",
        [jax.ShapeDtypeStruct((rows, LANES), F32)] * 2
        + [jax.ShapeDtypeStruct(((share + share % 2) * blocks, 2 * width), BF16)]
        + [jax.ShapeDtypeStruct((width, LANES), F32)] * 2,
        [pltpu.VMEM] * (2 + len(gathered)), [],
        places, made["shift"], *gathered, flops=PREPARE_FLOPS,
    )
    returned = kernel_call(
        functools.partial(subgrid_kernel, columns=columns, bands=bands), "subgrid",
        jax.ShapeDtypeStruct((rows, LANES), BF16), [pltpu.VMEM] * 6, [wide(rows)],
        arrived, value, weight, made["grid_turn"], made["model"], made["back"],
    )
    delivered = lax.all_to_all(
        returned, ("band", "member"), split_axis=0, concat_axis=0, tiled=True,
        axis_index_groups=[
            [b * FACET_ROWS + member for b, member in return_order(bands)]
        ],
    )
    lines = kernel_call(
        functools.partial(return_kernel, bands=bands), "lines",
        jax.ShapeDtypeStruct((share, 2, length), F32), [pltpu.VMEM] * 10,
        [pltpu.VMEM((share, 2, length), F32), semaphores(share)]
        + [wide(2 * length // LANES)] * share,
        places, delivered, straight, crossed, put, made["window"], made["turn"],
        made["partial"], made["inner_plus"], made["outer_plus"], out_space=pltpu.HBM,
    )
    return lines[None]


def solution(mesh):
    bands = mesh.shape["band"]
    groups = mesh.shape["facet"] // FACET_ROWS
    split_mesh = Mesh(
        mesh.devices.reshape(groups, FACET_ROWS, bands), ("group", "member", "band")
    )
    facet = ("group", "member")
    placed = (
        P("band", facet, None, None, None),
        P(),
        P("band", None, facet, None, None),
        P("band", None, facet, None, None),
        P("band", None, facet, None),
        P("band", None, facet, None),
    )
    return jax.shard_map(
        functools.partial(local, groups, bands),
        mesh=split_mesh,
        in_specs=placed,
        out_specs=P(facet, "band", None, None),
        check_vma=False,
    )
```

```python
import functools
import math

import jax
import jax.numpy as jnp
import ml_dtypes
import numpy as np
from jax import lax
from jax.experimental import pallas as pl
from jax.experimental.pallas import tpu as pltpu
from jax.sharding import Mesh
from jax.sharding import PartitionSpec as P

CONTRIB = 64
FACET_ROWS = 8
SUBGRID = FACET_ROWS * CONTRIB
SEND_ORDER = (FACET_ROWS - 1, *range(FACET_ROWS - 1))
PLACE_ORDER = tuple(range(FACET_ROWS))
LANES = 128
HALF = LANES // 2
EARLY_FLOPS = 10**10
LATE_FLOPS = 10**10
PREPARE_FLOPS = 2 * 10**10
VMEM_LIMIT = 48 * 1024 * 1024
F32 = jnp.float32
BF16 = jnp.bfloat16


def phases(rows, cols, length, rotation):
    product = np.outer(rows, cols) % length
    return np.exp(rotation * 2j * np.pi * product / length)


def from_left(matrix):
    return np.block([[matrix.real, -matrix.imag], [matrix.imag, matrix.real]])


def from_right(matrix):
    return np.block([[matrix.real, matrix.imag], [-matrix.imag, matrix.real]])


def high_low(table):
    high = table.astype(ml_dtypes.bfloat16)
    low = (table - high.astype(np.float64)).astype(ml_dtypes.bfloat16)
    return np.stack([high, low])


def side_by_side(values):
    straight = np.concatenate([values.real, values.real], axis=-1)
    crossed = np.concatenate([-values.imag, values.imag], axis=-1)
    return np.stack([straight, crossed])


def stack_tables(named):
    places, blocks, begin = {}, [], 0
    for name, table in named.items():
        count = table.shape[1] // LANES
        places[name] = (begin, table.shape[0], count)
        blocks += [table[:, i * LANES : (i + 1) * LANES] for i in range(count)]
        begin += table.shape[0] * count
    return np.concatenate(blocks, axis=0), places


def stack_pairs(named):
    return stack_tables(
        {(name, i): table for name, pair in named.items() for i, table in enumerate(pair)}
    )


def tables(length):
    blocks = length // CONTRIB
    short = np.arange(CONTRIB)
    outer = np.concatenate([np.arange(0, blocks, 2), np.arange(1, blocks, 2)])
    window = 1.0 + 0.5 * np.cos(np.arange(length) * (2.0 * math.pi / length))
    window = (window * length**-0.5).reshape(length // LANES, LANES).astype(np.float32)
    turn = np.tile(phases(short, short, length, -1), (1, 2))
    turn = np.stack([turn.real, turn.imag]).astype(np.float32)
    pair = np.eye(2)
    shift = high_low(np.concatenate(side_by_side(phases(short, short, CONTRIB, -1)), axis=1))
    outer_minus = from_left(phases(short, outer, blocks, -1))
    inner_minus = from_right(np.kron(pair, phases(short, short, CONTRIB, -1)))
    piece = from_right(phases(short, short, CONTRIB, 1)) * CONTRIB**-0.5
    return dict(
        plain=stack_tables(dict(window=window, real=turn[0], imag=turn[1])),
        paired=stack_pairs(
            dict(
                shift=shift,
                outer=high_low(outer_minus),
                inner=high_low(inner_minus),
                piece=high_low(piece),
            )
        ),
        window=window,
        turn=turn,
        shift=shift,
        inner_plus=high_low(from_right(np.kron(pair, phases(short, short, CONTRIB, 1)))),
        outer_plus=high_low(from_left(phases(outer, short, blocks, 1))),
        partial=high_low(from_right(phases(short, short, CONTRIB, -1)).T * CONTRIB**-0.5),
        grid_turn=side_by_side(phases(np.arange(FACET_ROWS), short, SUBGRID, -1)).astype(
            np.float32
        ),
        model=high_low(from_right(phases(short, short, CONTRIB, -1)) * SUBGRID**-0.5),
        back=high_low(from_right(phases(short, short, CONTRIB, 1)) * SUBGRID**-0.5),
    )


def return_order(bands):
    order = [(b, member) for b in range(bands) for member in PLACE_ORDER]
    return order[-1:] + order[:-1]


def split(values):
    high = values.astype(BF16)
    return high, (values - high.astype(F32)).astype(BF16)


def dot(left, right, dims=((1,), (0,))):
    return lax.dot_general(left, right, (dims, ((), ())), preferred_element_type=F32)


def dot_split(values, right):
    rows = values.shape[0]
    both = dot(jnp.concatenate(split(values), axis=0), right)
    return both[:rows] + both[rows:]


def times_table(values, table):
    return dot_split(values, table[0]) + dot(values.astype(BF16), table[1])


def table_times(table, values, dims=((1,), (0,))):
    high, low = split(values)
    rows = table[0].shape[0]
    both = dot(jnp.concatenate([table[0], table[1]], axis=0), high, dims)
    return both[:rows] + both[rows:] + dot(table[0], low, dims)


def iota(shape, dimension):
    return lax.broadcasted_iota(jnp.int32, shape, dimension)


def over(values, size):
    return lax.shift_right_logical(values, jnp.full_like(values, size.bit_length() - 1))


def within(values, size):
    return values & (size - 1)


def swap_halves(values):
    return pltpu.roll(values, HALF, 1)


def table_at(ref, place):
    begin, rows, blocks = place
    parts = [ref[begin + i * rows : begin + (i + 1) * rows, :] for i in range(blocks)]
    return parts[0] if blocks == 1 else jnp.concatenate(parts, axis=1)


def offsets_on_lanes(offsets_ref, columns, order):
    fronts, owners = offsets_ref.shape
    groups = owners // FACET_ROWS
    place = over(iota((1, fronts * owners * columns), 1), columns)
    front = within(place, fronts)
    group = within(over(place, fronts) + lax.axis_index("group"), groups)
    spot = over(place, fronts * groups)
    member = jnp.zeros_like(spot)
    for i, value in enumerate(order):
        member = jnp.where(spot == i, value, member)
    owner = group * FACET_ROWS + member
    pick = one_hot((owners, place.shape[1]), owner)
    offsets = offsets_ref[...]
    blocks = dot(over(offsets, CONTRIB).astype(F32).astype(BF16), pick)
    residues = dot(within(offsets, CONTRIB).astype(F32).astype(BF16), pick)
    spread = jnp.zeros_like(place, dtype=F32)
    for t in range(fronts):
        here = blocks[t : t + 1, :] * CONTRIB + residues[t : t + 1, :]
        spread = jnp.where(front == t, here, spread)
    return spread.astype(jnp.int32)


def shift_rows(residue, table):
    pick = jnp.where(iota((CONTRIB, residue.shape[1]), 0) == residue, 1.0, 0.0).T.astype(BF16)
    rows = dot(pick, table[0]) + dot(pick, table[1])
    return rows[:, :LANES], rows[:, LANES:]


def one_hot(shape, targets):
    return jnp.where(iota(shape, 0) == targets, 1.0, 0.0).astype(BF16)


def turned_eighths(values, rotation):
    sign = jnp.where(iota(values[0].shape, 1) < HALF, -rotation, rotation).astype(F32)

    def quarter_turn(value):
        return swap_halves(value) * sign

    def four(a, b, c, d):
        even_sum, even_diff = a + c, a - c
        odd_sum, odd_diff = b + d, quarter_turn(b - d)
        return even_sum + odd_sum, even_diff + odd_diff, even_sum - odd_sum, even_diff - odd_diff

    even = four(*values[0::2])
    odd = four(*values[1::2])
    root = math.sqrt(0.5)
    turned = (
        odd[0],
        (odd[1] + quarter_turn(odd[1])) * root,
        quarter_turn(odd[2]),
        (quarter_turn(odd[3]) - odd[3]) * root,
    )
    return [e + o for e, o in zip(even, turned)] + [e - o for e, o in zip(even, turned)]


def pack_samples(cells_ref, values_ref, weights_ref, flags_ref, out_ref):
    for t in range(cells_ref.shape[0]):
        rows = [
            cells_ref[t, 0:1, :].astype(F32) * SUBGRID + cells_ref[t, 1:2, :].astype(F32),
            weights_ref[t] * flags_ref[t].astype(F32),
            values_ref[t],
        ]
        out_ref[4 * t : 4 * t + 4, :] = jnp.concatenate(rows, axis=0)


def start_all(sources, targets, semaphores):
    copies = [
        pltpu.make_async_copy(source, target, semaphores.at[i])
        for i, (source, target) in enumerate(zip(sources, targets))
    ]
    for copy in copies:
        copy.start()
    return copies


def predict(spread, copies, strips_ref, plain_ref, paired_ref, held_refs, out_ref, plain, paired):
    columns, length = strips_ref.shape[1:]
    groups = length // LANES
    pairs = columns // 2
    blocks = length // CONTRIB
    width = spread.shape[1]
    first_block, residue = over(spread, CONTRIB), within(spread, CONTRIB)
    column = within(iota(spread.shape, 1), columns)
    kappa = iota((CONTRIB, width), 0)
    block = within(first_block + jnp.where(kappa < residue, 1, 0), blocks)
    source = within(column, 2) * blocks + block
    pair_of = over(column, 2)
    for copy in copies[:2]:
        copy.wait()

    def pair_at(name):
        return [table_at(paired_ref, paired[name, i]) for i in range(2)]

    window = table_at(plain_ref, plain["window"])
    turn_real, turn_imag = table_at(plain_ref, plain["real"]), table_at(plain_ref, plain["imag"])
    low_half = iota((groups, LANES), 1) < HALF
    sections = []
    for part, held in enumerate(held_refs):
        for group in range(groups):
            held[group * columns : (group + 1) * columns, :] = strips_ref[
                part, :, group * LANES : (group + 1) * LANES
            ]
        even, odd = [], []
        for pair in range(pairs):
            first = held[pl.ds(2 * pair, groups, stride=columns), :] * window
            second = held[pl.ds(2 * pair + 1, groups, stride=columns), :] * window
            even.append(jnp.where(low_half, first, swap_halves(second)))
            odd.append(jnp.where(low_half, swap_halves(first), second))
        sections += [jnp.concatenate(even, axis=1), jnp.concatenate(odd, axis=1)]
    for copy in copies[2:]:
        copy.wait()
    section = table_times(pair_at("outer"), jnp.concatenate(sections, axis=0))
    turned = []
    for pair in range(pairs):
        lanes = slice(pair * LANES, (pair + 1) * LANES)
        real, imag = section[:CONTRIB, lanes], section[CONTRIB:, lanes]
        turned.append(
            jnp.concatenate(
                [real * turn_real - imag * turn_imag, real * turn_imag + imag * turn_real],
                axis=1,
            )
        )
    inner = times_table(jnp.concatenate(turned, axis=0), pair_at("inner"))
    cutouts = []
    for part in range(2):
        tiles = []
        for tile in range(width // LANES):
            lanes = slice(tile * LANES, (tile + 1) * LANES)
            chosen = None
            for pair in range(pairs):
                rows = inner[pair * CONTRIB : (pair + 1) * CONTRIB, part * LANES : (part + 1) * LANES]
                found = jnp.take_along_axis(
                    rows, source[:, lanes], axis=1, mode="promise_in_bounds"
                )
                here = pair_of[:, lanes] == pair
                chosen = found if chosen is None else jnp.where(here, found, chosen)
            tiles.append(chosen)
        cutouts.append(jnp.concatenate(tiles, axis=1))
    cutout = jnp.concatenate(cutouts, axis=0)
    piece = times_table(cutout.T, pair_at("piece"))
    straight, crossed = shift_rows(residue, pair_at("shift"))
    out_ref[...] = (piece * straight + swap_halves(piece) * crossed).astype(BF16)


def in_first_half():
    return 2 * lax.axis_index("group") < lax.axis_size("group")


def early_kernel(
    cells, values, weights, flags, offsets, strips, plain_table, paired_table, out_ref, packed_ref,
    cells_ref, values_ref, weights_ref, flags_ref, offsets_ref, strips_ref, plain_ref, paired_ref,
    real_ref, imag_ref, small_semaphores, semaphores, *, plain, paired,
):
    small = start_all(
        (cells, values, weights, flags),
        (cells_ref, values_ref, weights_ref, flags_ref),
        small_semaphores,
    )

    def large():
        sources = (offsets, strips, plain_table, paired_table)
        targets = (offsets_ref, strips_ref, plain_ref, paired_ref)
        return [
            pltpu.make_async_copy(source, target, semaphores.at[i])
            for i, (source, target) in enumerate(zip(sources, targets))
        ]

    @pl.when(in_first_half())
    def _():
        for copy in large():
            copy.start()

    for copy in small:
        copy.wait()
    for t in range(cells_ref.shape[0]):
        rows = [
            cells_ref[t, 0:1, :].astype(F32) * SUBGRID + cells_ref[t, 1:2, :].astype(F32),
            weights_ref[t] * flags_ref[t].astype(F32),
            values_ref[t],
        ]
        packed_ref[4 * t : 4 * t + 4, :] = jnp.concatenate(rows, axis=0)

    @pl.when(in_first_half())
    def _():
        copies = large()
        copies[0].wait()
        predict(
            offsets_on_lanes(offsets_ref, strips_ref.shape[1], SEND_ORDER), copies[1:],
            strips_ref, plain_ref, paired_ref, (real_ref, imag_ref), out_ref, plain, paired,
        )


def late_kernel(
    early_ref, offsets_ref, strips_ref, plain_ref, paired_ref, out_ref, real_ref, imag_ref,
    *, plain, paired,
):
    @pl.when(in_first_half())
    def _():
        out_ref[...] = early_ref[...]

    @pl.when(jnp.logical_not(in_first_half()))
    def _():
        predict(
            offsets_on_lanes(offsets_ref, strips_ref.shape[1], SEND_ORDER), (),
            strips_ref, plain_ref, paired_ref, (real_ref, imag_ref), out_ref, plain, paired,
        )


def prepare_kernel(offsets_ref, shift_ref, *refs, columns, share, blocks):
    samples_refs, outs = refs[:-6], refs[-6:]
    value_ref, weight_ref, put_ref, straight_ref, crossed_ref, places_ref = outs
    fronts, samples = samples_refs[0].shape[0] // 4, samples_refs[0].shape[1]
    own = lax.axis_index("group")
    depth = FACET_ROWS * columns
    for spot in range(len(samples_refs) * fronts):
        step, t = spot // fronts, spot % fronts
        sample = samples_refs[step][4 * t : 4 * t + 4, :]
        cell = sample[0:1, :].astype(jnp.int32)
        row, col = over(cell, SUBGRID) - own * columns, within(cell, SUBGRID)
        inside = (row >= 0) & (row < columns)
        target = jnp.where(inside, within(col, FACET_ROWS) * columns + row, -1)
        pick = one_hot((depth, samples), target)
        mask = iota((HALF, samples), 0) == over(col, FACET_ROWS)
        factor = sample[1:2, :]
        highs, lows = [], []
        for term in (factor * sample[2:3, :], factor * sample[3:4, :], factor):
            high = term.astype(BF16).astype(F32)
            highs.append(jnp.where(mask, high, 0.0).astype(BF16))
            lows.append(jnp.where(mask, term - high, 0.0).astype(BF16))
        highs, lows = highs + highs[2:], lows + lows[2:]
        grid = dot(pick, jnp.concatenate(highs, axis=0), ((1,), (1,))) + dot(
            pick, jnp.concatenate(lows, axis=0), ((1,), (1,))
        )
        rows = slice(spot * depth, (spot + 1) * depth)
        value_ref[rows, :] = grid[:, :LANES]
        weight_ref[rows, :] = grid[:, LANES:]
    spread = offsets_on_lanes(offsets_ref, share, PLACE_ORDER)
    places_ref[...] = spread
    first_block, residue = over(spread, CONTRIB), within(spread, CONTRIB)
    straight_ref[...], crossed_ref[...] = shift_rows(residue, shift_ref)
    base = within(iota(spread.shape, 1), share) * blocks
    targets = jnp.concatenate([base + first_block, base + within(first_block + 1, blocks)], axis=1)
    put_ref[...] = one_hot(put_ref.shape, targets)


def subgrid_kernel(
    pieces_ref, value_ref, weight_ref, turn_ref, model_ref, back_ref, out_ref, held_ref,
    *, columns, bands,
):
    rows = pieces_ref.shape[0] // FACET_ROWS
    spots = range(rows // columns)
    depth = FACET_ROWS * columns
    share = columns // bands
    pieces = pieces_ref[...].astype(F32)
    sky = turned_eighths(
        [
            pieces[spot * rows : (spot + 1) * rows, :]
            for spot in (SEND_ORDER.index(i) for i in range(FACET_ROWS))
        ],
        -1.0,
    )
    sky = [
        value * turn_ref[0, i : i + 1, :] + swap_halves(value) * turn_ref[1, i : i + 1, :]
        for i, value in enumerate(sky)
    ]
    stacked = jnp.concatenate(
        [value[spot * columns : (spot + 1) * columns, :] for spot in spots for value in sky],
        axis=0,
    )
    grid = value_ref[...] - weight_ref[...] * times_table(stacked, model_ref)
    back = times_table(grid, back_ref)
    lines = []
    for i in range(FACET_ROWS):
        value = jnp.concatenate(
            [
                back[spot * depth + i * columns : spot * depth + (i + 1) * columns, :]
                for spot in spots
            ],
            axis=0,
        )
        lines.append(
            value * turn_ref[0, i : i + 1, :] - swap_halves(value) * turn_ref[1, i : i + 1, :]
        )
    lines = turned_eighths(lines, 1.0)
    for i in range(FACET_ROWS):
        for spot in spots:
            for b in range(bands):
                source = spot * columns + b * share
                place = return_order(bands).index((b, i))
                target = (place * len(spots) + spot) * share
                held_ref[target : target + share, :] = lines[i][source : source + share, :]
    out_ref[...] = held_ref[...].astype(BF16)


def return_kernel(
    places_ref, pieces_ref, straight_ref, crossed_ref, put_ref, window_ref, turn_ref, partial_ref,
    inner_ref, outer_ref, out_ref, *line_refs, bands,
):
    columns, _, length = out_ref.shape
    blocks = length // CONTRIB
    groups = length // LANES
    pairs = (columns + 1) // 2
    width = pieces_ref.shape[0] // bands
    pieces = pieces_ref[...].astype(F32)
    order, rows = return_order(bands), width // FACET_ROWS

    def of_band(b):
        begins = [order.index((b, member)) * rows for member in PLACE_ORDER]
        return jnp.concatenate([pieces[begin : begin + rows, :] for begin in begins], axis=0)

    summed = of_band(0)
    for b in range(1, bands):
        summed += of_band(b)
    summed = summed * straight_ref[...] - swap_halves(summed) * crossed_ref[...]
    residues = table_times(partial_ref, summed, ((1,), (1,)))
    kappa = within(iota((2 * CONTRIB, width), 0), CONTRIB)
    inside = kappa >= within(places_ref[...], CONTRIB)
    both = jnp.concatenate(
        [jnp.where(inside, residues, 0.0), jnp.where(inside, 0.0, residues)], axis=1
    )
    put = put_ref[...]
    high, low = split(both)
    spectrum = dot(high, put, ((1,), (1,))) + dot(low, put, ((1,), (1,)))
    inner = times_table(
        jnp.concatenate(
            [
                jnp.concatenate(
                    [
                        spectrum[:CONTRIB, pair * LANES : (pair + 1) * LANES],
                        spectrum[CONTRIB:, pair * LANES : (pair + 1) * LANES],
                    ],
                    axis=1,
                )
                for pair in range(pairs)
            ],
            axis=0,
        ),
        inner_ref,
    )
    reals, imags = [], []
    for pair in range(pairs):
        rows = slice(pair * CONTRIB, (pair + 1) * CONTRIB)
        real, imag = inner[rows, :LANES], inner[rows, LANES:]
        reals.append(real * turn_ref[0] + imag * turn_ref[1])
        imags.append(imag * turn_ref[0] - real * turn_ref[1])
    lines = table_times(
        outer_ref,
        jnp.concatenate(
            [jnp.concatenate(reals, axis=1), jnp.concatenate(imags, axis=1)], axis=0
        ),
    )
    window = window_ref[...]
    low_half = iota((groups, LANES), 1) < HALF
    for part in range(2):
        for pair in range(pairs):
            lanes = slice(pair * LANES, (pair + 1) * LANES)
            begin = part * blocks
            even = lines[begin : begin + groups, lanes]
            odd = lines[begin + groups : begin + blocks, lanes]
            line_refs[2 * pair][pl.ds(part, groups, stride=2), :] = (
                jnp.where(low_half, even, swap_halves(odd)) * window
            )
            if 2 * pair + 1 < columns:
                line_refs[2 * pair + 1][pl.ds(part, groups, stride=2), :] = (
                    jnp.where(low_half, swap_halves(even), odd) * window
                )
    for column in range(columns):
        for group in range(groups):
            out_ref[column, :, group * LANES : (group + 1) * LANES] = line_refs[column][
                2 * group : 2 * group + 2, :
            ]


def kernel_call(kernel, name, out_shape, spaces, scratch, *operands, flops=0):
    return pl.pallas_call(
        kernel,
        out_shape=out_shape,
        in_specs=[pl.BlockSpec(memory_space=space) for space in spaces],
        out_specs=jax.tree.map(lambda _: pl.BlockSpec(memory_space=pltpu.VMEM), out_shape),
        scratch_shapes=scratch,
        compiler_params=pltpu.CompilerParams(vmem_limit_bytes=VMEM_LIMIT),
        cost_estimate=pl.CostEstimate(flops=flops, bytes_accessed=0, transcendentals=0)
        if flops
        else None,
        name=name,
    )(*operands)


def wide(rows):
    return pltpu.VMEM((rows, LANES), F32)


def local(groups, bands, strips, offsets, cells, values, weights, flags):
    columns, length = strips.shape[-2:]
    fronts = offsets.shape[0]
    share = columns // bands
    facets = groups * FACET_ROWS
    rows = facets * fronts * columns
    width = facets * fronts * share
    made = tables(length)
    plain, plain_places = made.pop("plain")
    paired, paired_places = made.pop("paired")
    made = {key: jnp.asarray(value) for key, value in made.items()}
    held = length // LANES * columns
    small = [cells[0, :, 0], values[0, :, 0], weights[0], flags[0]]
    large = [strips[0, 0], jnp.asarray(plain), jnp.asarray(paired)]

    def landing(arrays):
        return [pltpu.VMEM(array.shape, array.dtype) for array in arrays]

    def in_hbm(arrays):
        return [pltpu.with_memory_space_constraint(array, pltpu.HBM) for array in arrays]

    def semaphores(count):
        return pltpu.SemaphoreType.DMA((count,))

    early, packed = kernel_call(
        functools.partial(early_kernel, plain=plain_places, paired=paired_places), "early",
        [
            jax.ShapeDtypeStruct((rows, LANES), BF16),
            jax.ShapeDtypeStruct((4 * fronts, cells.shape[-1]), F32),
        ],
        [pltpu.HBM] * 8,
        landing(small + [offsets] + large) + [wide(held)] * 2 + [semaphores(4), semaphores(4)],
        *in_hbm(small + [offsets] + large), flops=EARLY_FLOPS,
    )
    pieces = kernel_call(
        functools.partial(late_kernel, plain=plain_places, paired=paired_places), "late",
        jax.ShapeDtypeStruct((rows, LANES), BF16), [pltpu.VMEM] * 5, [wide(held)] * 2,
        early, offsets, *large, flops=LATE_FLOPS,
    )
    gathered = [packed]
    for step in range(1, groups):
        moves = [((group + step) % groups, group) for group in range(groups)]
        gathered.append(lax.ppermute(packed, "group", moves))
    arrived = lax.all_to_all(
        pieces, "member", split_axis=0, concat_axis=0, tiled=True,
        axis_index_groups=[list(SEND_ORDER)],
    )
    blocks = length // CONTRIB
    value, weight, put, straight, crossed, places = kernel_call(
        functools.partial(prepare_kernel, columns=columns, share=share, blocks=blocks), "prepare",
        [jax.ShapeDtypeStruct((rows, LANES), F32)] * 2
        + [jax.ShapeDtypeStruct(((share + share % 2) * blocks, 2 * width), BF16)]
        + [jax.ShapeDtypeStruct((width, LANES), F32)] * 2
        + [jax.ShapeDtypeStruct((1, width), jnp.int32)],
        [pltpu.VMEM] * (2 + len(gathered)), [],
        offsets, made["shift"], *gathered, flops=PREPARE_FLOPS,
    )
    returned = kernel_call(
        functools.partial(subgrid_kernel, columns=columns, bands=bands), "subgrid",
        jax.ShapeDtypeStruct((rows, LANES), BF16), [pltpu.VMEM] * 6, [wide(rows)],
        arrived, value, weight, made["grid_turn"], made["model"], made["back"],
    )
    delivered = lax.all_to_all(
        returned, ("band", "member"), split_axis=0, concat_axis=0, tiled=True,
        axis_index_groups=[
            [b * FACET_ROWS + member for b, member in return_order(bands)]
        ],
    )
    lines = kernel_call(
        functools.partial(return_kernel, bands=bands), "lines",
        jax.ShapeDtypeStruct((share, 2, length), F32), [pltpu.VMEM] * 10,
        [wide(2 * length // LANES)] * share,
        places, delivered, straight, crossed, put, made["window"], made["turn"],
        made["partial"], made["inner_plus"], made["outer_plus"],
    )
    return lines[None]


def solution(mesh):
    bands = mesh.shape["band"]
    groups = mesh.shape["facet"] // FACET_ROWS
    split_mesh = Mesh(
        mesh.devices.reshape(groups, FACET_ROWS, bands), ("group", "member", "band")
    )
    facet = ("group", "member")
    placed = (
        P("band", facet, None, None, None),
        P(),
        P("band", None, facet, None, None),
        P("band", None, facet, None, None),
        P("band", None, facet, None),
        P("band", None, facet, None),
    )
    return jax.shard_map(
        functools.partial(local, groups, bands),
        mesh=split_mesh,
        in_specs=placed,
        out_specs=P(facet, "band", None, None),
        check_vma=False,
    )
```

```python
import functools
import math

import jax
import jax.numpy as jnp
import ml_dtypes
import numpy as np
from jax import lax
from jax.experimental import pallas as pl
from jax.experimental.pallas import tpu as pltpu
from jax.sharding import Mesh
from jax.sharding import PartitionSpec as P

CONTRIB = 64
FACET_ROWS = 8
SUBGRID = FACET_ROWS * CONTRIB
SEND_ORDER = (FACET_ROWS - 1, *range(FACET_ROWS - 1))
PLACE_ORDER = tuple(range(FACET_ROWS))
LANES = 128
HALF = LANES // 2
PADDED_ROWS = 64
EARLY_FLOPS = 10**10
LATE_FLOPS = 10**10
PREPARE_FLOPS = 2 * 10**10
VMEM_LIMIT = 48 * 1024 * 1024
F32 = jnp.float32
BF16 = jnp.bfloat16


def phases(rows, cols, length, rotation):
    product = np.outer(rows, cols) % length
    return np.exp(rotation * 2j * np.pi * product / length)


def from_left(matrix):
    return np.block([[matrix.real, -matrix.imag], [matrix.imag, matrix.real]])


def from_right(matrix):
    return np.block([[matrix.real, matrix.imag], [-matrix.imag, matrix.real]])


def high_low(table):
    high = table.astype(ml_dtypes.bfloat16)
    low = (table - high.astype(np.float64)).astype(ml_dtypes.bfloat16)
    return np.stack([high, low])


def side_by_side(values):
    straight = np.concatenate([values.real, values.real], axis=-1)
    crossed = np.concatenate([-values.imag, values.imag], axis=-1)
    return np.stack([straight, crossed])


def stack_tables(named):
    places, blocks, begin = {}, [], 0
    for name, table in named.items():
        count = table.shape[1] // LANES
        places[name] = (begin, table.shape[0], count)
        blocks += [table[:, i * LANES : (i + 1) * LANES] for i in range(count)]
        begin += table.shape[0] * count
    return np.concatenate(blocks, axis=0), places


def stack_pairs(named):
    return stack_tables(
        {(name, i): table for name, pair in named.items() for i, table in enumerate(pair)}
    )


def tables(length):
    blocks = length // CONTRIB
    short = np.arange(CONTRIB)
    outer = np.concatenate([np.arange(0, blocks, 2), np.arange(1, blocks, 2)])
    window = 1.0 + 0.5 * np.cos(np.arange(length) * (2.0 * math.pi / length))
    window = (window * length**-0.5).reshape(length // LANES, LANES).astype(np.float32)
    turn = np.tile(phases(short, short, length, -1), (1, 2))
    turn = np.stack([turn.real, turn.imag]).astype(np.float32)
    pair = np.eye(2)
    shift = high_low(np.concatenate(side_by_side(phases(short, short, CONTRIB, -1)), axis=1))
    outer_minus = from_left(phases(short, outer, blocks, -1))
    inner_minus = from_right(np.kron(pair, phases(short, short, CONTRIB, -1)))
    piece = from_right(phases(short, short, CONTRIB, 1)) * CONTRIB**-0.5
    return dict(
        plain=stack_tables(dict(window=window, real=turn[0], imag=turn[1])),
        paired=stack_pairs(
            dict(
                shift=shift,
                outer=high_low(outer_minus),
                inner=high_low(inner_minus),
                piece=high_low(piece),
            )
        ),
        window=window,
        turn=turn,
        shift=shift,
        inner_plus=high_low(from_right(np.kron(pair, phases(short, short, CONTRIB, 1)))),
        outer_plus=high_low(from_left(phases(outer, short, blocks, 1))),
        partial=high_low(from_right(phases(short, short, CONTRIB, -1)).T * CONTRIB**-0.5),
        grid_turn=side_by_side(phases(np.arange(FACET_ROWS), short, SUBGRID, -1)).astype(
            np.float32
        ),
        model=high_low(from_right(phases(short, short, CONTRIB, -1)) * SUBGRID**-0.5),
        back=high_low(from_right(phases(short, short, CONTRIB, 1)) * SUBGRID**-0.5),
    )


def return_order(bands):
    order = [(b, member) for b in range(bands) for member in PLACE_ORDER]
    return order[-1:] + order[:-1]


def split(values):
    high = values.astype(BF16)
    return high, (values - high.astype(F32)).astype(BF16)


def dot(left, right, dims=((1,), (0,))):
    return lax.dot_general(left, right, (dims, ((), ())), preferred_element_type=F32)


def dot_split(values, right):
    rows = values.shape[0]
    both = dot(jnp.concatenate(split(values), axis=0), right)
    return both[:rows] + both[rows:]


def times_table(values, table):
    return dot_split(values, table[0]) + dot(values.astype(BF16), table[1])


def table_times(table, values, dims=((1,), (0,))):
    high, low = split(values)
    rows = table[0].shape[0]
    both = dot(jnp.concatenate([table[0], table[1]], axis=0), high, dims)
    return both[:rows] + both[rows:] + dot(table[0], low, dims)


def iota(shape, dimension):
    return lax.broadcasted_iota(jnp.int32, shape, dimension)


def over(values, size):
    return lax.shift_right_logical(values, jnp.full_like(values, size.bit_length() - 1))


def within(values, size):
    return values & (size - 1)


def swap_halves(values):
    return pltpu.roll(values, HALF, 1)


def table_at(ref, place):
    begin, rows, blocks = place
    parts = [ref[begin + i * rows : begin + (i + 1) * rows, :] for i in range(blocks)]
    return parts[0] if blocks == 1 else jnp.concatenate(parts, axis=1)


def offsets_on_lanes(offsets_ref, columns, order):
    fronts, owners = offsets_ref.shape
    groups = owners // FACET_ROWS
    place = over(iota((1, fronts * owners * columns), 1), columns)
    front = within(place, fronts)
    group = within(over(place, fronts) + lax.axis_index("group"), groups)
    spot = over(place, fronts * groups)
    member = jnp.zeros_like(spot)
    for i, value in enumerate(order):
        member = jnp.where(spot == i, value, member)
    owner = group * FACET_ROWS + member
    pick = one_hot((owners, place.shape[1]), owner)
    offsets = offsets_ref[...]
    blocks = dot(over(offsets, CONTRIB).astype(F32).astype(BF16), pick)
    residues = dot(within(offsets, CONTRIB).astype(F32).astype(BF16), pick)
    spread = jnp.zeros_like(place, dtype=F32)
    for t in range(fronts):
        here = blocks[t : t + 1, :] * CONTRIB + residues[t : t + 1, :]
        spread = jnp.where(front == t, here, spread)
    return spread.astype(jnp.int32)


def shift_rows(residue, table):
    pick = jnp.where(iota((CONTRIB, residue.shape[1]), 0) == residue, 1.0, 0.0).T.astype(BF16)
    rows = dot(pick, table[0]) + dot(pick, table[1])
    return rows[:, :LANES], rows[:, LANES:]


def one_hot(shape, targets):
    return jnp.where(iota(shape, 0) == targets, 1.0, 0.0).astype(BF16)


def turned_eighths(values, rotation):
    sign = jnp.where(iota(values[0].shape, 1) < HALF, -rotation, rotation).astype(F32)

    def quarter_turn(value):
        return swap_halves(value) * sign

    def four(a, b, c, d):
        even_sum, even_diff = a + c, a - c
        odd_sum, odd_diff = b + d, quarter_turn(b - d)
        return even_sum + odd_sum, even_diff + odd_diff, even_sum - odd_sum, even_diff - odd_diff

    even = four(*values[0::2])
    odd = four(*values[1::2])
    root = math.sqrt(0.5)
    turned = (
        odd[0],
        (odd[1] + quarter_turn(odd[1])) * root,
        quarter_turn(odd[2]),
        (quarter_turn(odd[3]) - odd[3]) * root,
    )
    return [e + o for e, o in zip(even, turned)] + [e - o for e, o in zip(even, turned)]


def pack_samples(cells_ref, values_ref, weights_ref, flags_ref, out_ref):
    for t in range(cells_ref.shape[0]):
        rows = [
            cells_ref[t, 0:1, :].astype(F32) * SUBGRID + cells_ref[t, 1:2, :].astype(F32),
            weights_ref[t] * flags_ref[t].astype(F32),
            values_ref[t],
        ]
        out_ref[4 * t : 4 * t + 4, :] = jnp.concatenate(rows, axis=0)


def start_all(sources, targets, semaphores):
    copies = [
        pltpu.make_async_copy(source, target, semaphores.at[i])
        for i, (source, target) in enumerate(zip(sources, targets))
    ]
    for copy in copies:
        copy.start()
    return copies


def predict(spread, copies, strips_ref, plain_ref, paired_ref, held_refs, out_ref, plain, paired):
    columns, length = strips_ref.shape[1:]
    groups = length // LANES
    pairs = columns // 2
    blocks = length // CONTRIB
    width = spread.shape[1]
    first_block, residue = over(spread, CONTRIB), within(spread, CONTRIB)
    column = within(iota(spread.shape, 1), columns)
    kappa = iota((CONTRIB, width), 0)
    block = within(first_block + jnp.where(kappa < residue, 1, 0), blocks)
    source = within(column, 2) * blocks + block
    pair_of = over(column, 2)
    for copy in copies[:2]:
        copy.wait()

    def pair_at(name):
        return [table_at(paired_ref, paired[name, i]) for i in range(2)]

    window = table_at(plain_ref, plain["window"])
    turn_real, turn_imag = table_at(plain_ref, plain["real"]), table_at(plain_ref, plain["imag"])
    low_half = iota((groups, LANES), 1) < HALF
    sections = []
    for part, held in enumerate(held_refs):
        for group in range(groups):
            held[group * columns : (group + 1) * columns, :] = strips_ref[
                part, :, group * LANES : (group + 1) * LANES
            ]
        even, odd = [], []
        for pair in range(pairs):
            first = held[pl.ds(2 * pair, groups, stride=columns), :] * window
            second = held[pl.ds(2 * pair + 1, groups, stride=columns), :] * window
            even.append(jnp.where(low_half, first, swap_halves(second)))
            odd.append(jnp.where(low_half, swap_halves(first), second))
        sections += [jnp.concatenate(even, axis=1), jnp.concatenate(odd, axis=1)]
    for copy in copies[2:]:
        copy.wait()
    section = table_times(pair_at("outer"), jnp.concatenate(sections, axis=0))
    turned = []
    for pair in range(pairs):
        lanes = slice(pair * LANES, (pair + 1) * LANES)
        real, imag = section[:CONTRIB, lanes], section[CONTRIB:, lanes]
        turned.append(
            jnp.concatenate(
                [real * turn_real - imag * turn_imag, real * turn_imag + imag * turn_real],
                axis=1,
            )
        )
    inner = times_table(jnp.concatenate(turned, axis=0), pair_at("inner"))
    cutouts = []
    for part in range(2):
        tiles = []
        for tile in range(width // LANES):
            lanes = slice(tile * LANES, (tile + 1) * LANES)
            chosen = None
            for pair in range(pairs):
                rows = inner[pair * CONTRIB : (pair + 1) * CONTRIB, part * LANES : (part + 1) * LANES]
                found = jnp.take_along_axis(
                    rows, source[:, lanes], axis=1, mode="promise_in_bounds"
                )
                here = pair_of[:, lanes] == pair
                chosen = found if chosen is None else jnp.where(here, found, chosen)
            tiles.append(chosen)
        cutouts.append(jnp.concatenate(tiles, axis=1))
    cutout = jnp.concatenate(cutouts, axis=0)
    piece = times_table(cutout.T, pair_at("piece"))
    straight, crossed = shift_rows(residue, pair_at("shift"))
    out_ref[...] = (piece * straight + swap_halves(piece) * crossed).astype(BF16)


def in_first_half():
    return 2 * lax.axis_index("group") < lax.axis_size("group")


def early_kernel(
    cells, values, weights, flags, offsets, strips, plain_table, paired_table, out_ref, packed_ref,
    cells_ref, values_ref, weights_ref, flags_ref, offsets_ref, strips_ref, plain_ref, paired_ref,
    real_ref, imag_ref, small_semaphores, semaphores, *, plain, paired,
):
    small = start_all(
        (cells, values, weights, flags),
        (cells_ref, values_ref, weights_ref, flags_ref),
        small_semaphores,
    )

    def large():
        sources = (offsets, strips, plain_table, paired_table)
        targets = (offsets_ref, strips_ref, plain_ref, paired_ref)
        return [
            pltpu.make_async_copy(source, target, semaphores.at[i])
            for i, (source, target) in enumerate(zip(sources, targets))
        ]

    @pl.when(in_first_half())
    def _():
        for copy in large():
            copy.start()

    for copy in small:
        copy.wait()
    for t in range(cells_ref.shape[0]):
        rows = [
            cells_ref[t, 0:1, :].astype(F32) * SUBGRID + cells_ref[t, 1:2, :].astype(F32),
            weights_ref[t] * flags_ref[t].astype(F32),
            values_ref[t],
        ]
        packed_ref[4 * t : 4 * t + 4, :] = jnp.concatenate(rows, axis=0)

    @pl.when(in_first_half())
    def _():
        copies = large()
        copies[0].wait()
        predict(
            offsets_on_lanes(offsets_ref, strips_ref.shape[1], SEND_ORDER), copies[1:],
            strips_ref, plain_ref, paired_ref, (real_ref, imag_ref), out_ref, plain, paired,
        )


def late_kernel(
    early_ref, offsets_ref, strips_ref, plain_ref, paired_ref, out_ref, real_ref, imag_ref,
    *, plain, paired,
):
    @pl.when(in_first_half())
    def _():
        out_ref[...] = early_ref[...]

    @pl.when(jnp.logical_not(in_first_half()))
    def _():
        predict(
            offsets_on_lanes(offsets_ref, strips_ref.shape[1], SEND_ORDER), (),
            strips_ref, plain_ref, paired_ref, (real_ref, imag_ref), out_ref, plain, paired,
        )


def prepare_kernel(offsets_ref, shift_ref, *refs, columns, share, blocks):
    samples_refs, outs = refs[:-6], refs[-6:]
    value_ref, weight_ref, put_ref, straight_ref, crossed_ref, places_ref = outs
    fronts, samples = offsets_ref.shape[0], samples_refs[0].shape[1]
    own = lax.axis_index("group")
    depth = FACET_ROWS * columns
    for spot in range(len(samples_refs) * fronts):
        step, t = spot // fronts, spot % fronts
        sample = samples_refs[step][4 * t : 4 * t + 4, :]
        cell = sample[0:1, :].astype(jnp.int32)
        row, col = over(cell, SUBGRID) - own * columns, within(cell, SUBGRID)
        inside = (row >= 0) & (row < columns)
        target = jnp.where(inside, within(col, FACET_ROWS) * columns + row, -1)
        pick = one_hot((depth, samples), target)
        mask = iota((HALF, samples), 0) == over(col, FACET_ROWS)
        factor = sample[1:2, :]
        highs, lows = [], []
        for term in (factor * sample[2:3, :], factor * sample[3:4, :], factor):
            high = term.astype(BF16).astype(F32)
            highs.append(jnp.where(mask, high, 0.0).astype(BF16))
            lows.append(jnp.where(mask, term - high, 0.0).astype(BF16))
        highs, lows = highs + highs[2:], lows + lows[2:]
        grid = dot(pick, jnp.concatenate(highs, axis=0), ((1,), (1,))) + dot(
            pick, jnp.concatenate(lows, axis=0), ((1,), (1,))
        )
        rows = slice(spot * depth, (spot + 1) * depth)
        value_ref[rows, :] = grid[:, :LANES]
        weight_ref[rows, :] = grid[:, LANES:]
    spread = offsets_on_lanes(offsets_ref, share, PLACE_ORDER)
    places_ref[...] = spread
    first_block, residue = over(spread, CONTRIB), within(spread, CONTRIB)
    straight_ref[...], crossed_ref[...] = shift_rows(residue, shift_ref)
    base = within(iota(spread.shape, 1), share) * blocks
    targets = jnp.concatenate([base + first_block, base + within(first_block + 1, blocks)], axis=1)
    put_ref[...] = one_hot(put_ref.shape, targets)


def subgrid_kernel(
    pieces_ref, value_ref, weight_ref, turn_ref, model_ref, back_ref, out_ref, held_ref,
    *, columns, bands,
):
    rows = pieces_ref.shape[0] // FACET_ROWS
    spots = range(rows // columns)
    depth = FACET_ROWS * columns
    share = columns // bands
    pieces = pieces_ref[...].astype(F32)
    sky = turned_eighths(
        [
            pieces[spot * rows : (spot + 1) * rows, :]
            for spot in (SEND_ORDER.index(i) for i in range(FACET_ROWS))
        ],
        -1.0,
    )
    sky = [
        value * turn_ref[0, i : i + 1, :] + swap_halves(value) * turn_ref[1, i : i + 1, :]
        for i, value in enumerate(sky)
    ]
    stacked = jnp.concatenate(
        [value[spot * columns : (spot + 1) * columns, :] for spot in spots for value in sky],
        axis=0,
    )
    grid = value_ref[...] - weight_ref[...] * times_table(stacked, model_ref)
    back = times_table(grid, back_ref)
    lines = []
    for i in range(FACET_ROWS):
        value = jnp.concatenate(
            [
                back[spot * depth + i * columns : spot * depth + (i + 1) * columns, :]
                for spot in spots
            ],
            axis=0,
        )
        lines.append(
            value * turn_ref[0, i : i + 1, :] - swap_halves(value) * turn_ref[1, i : i + 1, :]
        )
    lines = turned_eighths(lines, 1.0)
    for i in range(FACET_ROWS):
        for spot in spots:
            for b in range(bands):
                source = spot * columns + b * share
                place = return_order(bands).index((b, i))
                target = (place * len(spots) + spot) * share
                held_ref[target : target + share, :] = lines[i][source : source + share, :]
    out_ref[...] = held_ref[...].astype(BF16)


def return_kernel(
    places_ref, pieces_ref, straight_ref, crossed_ref, put_ref, window_ref, turn_ref, partial_ref,
    inner_ref, outer_ref, out_ref, *line_refs, bands,
):
    columns, _, length = out_ref.shape
    blocks = length // CONTRIB
    groups = length // LANES
    pairs = (columns + 1) // 2
    width = pieces_ref.shape[0] // bands
    pieces = pieces_ref[...].astype(F32)
    order, rows = return_order(bands), width // FACET_ROWS

    def of_band(b):
        begins = [order.index((b, member)) * rows for member in PLACE_ORDER]
        return jnp.concatenate([pieces[begin : begin + rows, :] for begin in begins], axis=0)

    summed = of_band(0)
    for b in range(1, bands):
        summed += of_band(b)
    summed = summed * straight_ref[...] - swap_halves(summed) * crossed_ref[...]
    residues = table_times(partial_ref, summed, ((1,), (1,)))
    kappa = within(iota((2 * CONTRIB, width), 0), CONTRIB)
    inside = kappa >= within(places_ref[...], CONTRIB)
    both = jnp.concatenate(
        [jnp.where(inside, residues, 0.0), jnp.where(inside, 0.0, residues)], axis=1
    )
    put = put_ref[...]
    high, low = split(both)
    spectrum = dot(high, put, ((1,), (1,))) + dot(low, put, ((1,), (1,)))
    inner = times_table(
        jnp.concatenate(
            [
                jnp.concatenate(
                    [
                        spectrum[:CONTRIB, pair * LANES : (pair + 1) * LANES],
                        spectrum[CONTRIB:, pair * LANES : (pair + 1) * LANES],
                    ],
                    axis=1,
                )
                for pair in range(pairs)
            ],
            axis=0,
        ),
        inner_ref,
    )
    reals, imags = [], []
    for pair in range(pairs):
        rows = slice(pair * CONTRIB, (pair + 1) * CONTRIB)
        real, imag = inner[rows, :LANES], inner[rows, LANES:]
        reals.append(real * turn_ref[0] + imag * turn_ref[1])
        imags.append(imag * turn_ref[0] - real * turn_ref[1])
    lines = table_times(
        outer_ref,
        jnp.concatenate(
            [jnp.concatenate(reals, axis=1), jnp.concatenate(imags, axis=1)], axis=0
        ),
    )
    window = window_ref[...]
    low_half = iota((groups, LANES), 1) < HALF
    for part in range(2):
        for pair in range(pairs):
            lanes = slice(pair * LANES, (pair + 1) * LANES)
            begin = part * blocks
            even = lines[begin : begin + groups, lanes]
            odd = lines[begin + groups : begin + blocks, lanes]
            line_refs[2 * pair][pl.ds(part, groups, stride=2), :] = (
                jnp.where(low_half, even, swap_halves(odd)) * window
            )
            if 2 * pair + 1 < columns:
                line_refs[2 * pair + 1][pl.ds(part, groups, stride=2), :] = (
                    jnp.where(low_half, swap_halves(even), odd) * window
                )
    for column in range(columns):
        for group in range(groups):
            out_ref[column, :, group * LANES : (group + 1) * LANES] = line_refs[column][
                2 * group : 2 * group + 2, :
            ]


def kernel_call(kernel, name, out_shape, spaces, scratch, *operands, flops=0):
    return pl.pallas_call(
        kernel,
        out_shape=out_shape,
        in_specs=[pl.BlockSpec(memory_space=space) for space in spaces],
        out_specs=jax.tree.map(lambda _: pl.BlockSpec(memory_space=pltpu.VMEM), out_shape),
        scratch_shapes=scratch,
        compiler_params=pltpu.CompilerParams(vmem_limit_bytes=VMEM_LIMIT),
        cost_estimate=pl.CostEstimate(flops=flops, bytes_accessed=0, transcendentals=0)
        if flops
        else None,
        name=name,
    )(*operands)


def wide(rows):
    return pltpu.VMEM((rows, LANES), F32)


def local(groups, bands, strips, offsets, cells, values, weights, flags):
    columns, length = strips.shape[-2:]
    fronts = offsets.shape[0]
    share = columns // bands
    facets = groups * FACET_ROWS
    rows = facets * fronts * columns
    width = facets * fronts * share
    made = tables(length)
    plain, plain_places = made.pop("plain")
    paired, paired_places = made.pop("paired")
    made = {key: jnp.asarray(value) for key, value in made.items()}
    held = length // LANES * columns
    small = [cells[0, :, 0], values[0, :, 0], weights[0], flags[0]]
    large = [strips[0, 0], jnp.asarray(plain), jnp.asarray(paired)]

    def landing(arrays):
        return [pltpu.VMEM(array.shape, array.dtype) for array in arrays]

    def in_hbm(arrays):
        return [pltpu.with_memory_space_constraint(array, pltpu.HBM) for array in arrays]

    def semaphores(count):
        return pltpu.SemaphoreType.DMA((count,))

    early, packed = kernel_call(
        functools.partial(early_kernel, plain=plain_places, paired=paired_places), "early",
        [
            jax.ShapeDtypeStruct((rows, LANES), BF16),
            jax.ShapeDtypeStruct((PADDED_ROWS, cells.shape[-1]), F32),
        ],
        [pltpu.HBM] * 8,
        landing(small + [offsets] + large) + [wide(held)] * 2 + [semaphores(4), semaphores(4)],
        *in_hbm(small + [offsets] + large), flops=EARLY_FLOPS,
    )
    pieces = kernel_call(
        functools.partial(late_kernel, plain=plain_places, paired=paired_places), "late",
        jax.ShapeDtypeStruct((rows, LANES), BF16), [pltpu.VMEM] * 5, [wide(held)] * 2,
        early, offsets, *large, flops=LATE_FLOPS,
    )
    gathered = [packed]
    for step in range(1, groups):
        moves = [((group + step) % groups, group) for group in range(groups)]
        gathered.append(lax.ppermute(packed, "group", moves))
    arrived = lax.all_to_all(
        pieces, "member", split_axis=0, concat_axis=0, tiled=True,
        axis_index_groups=[list(SEND_ORDER)],
    )
    gathered, arrived = lax.optimization_barrier((gathered, arrived))
    blocks = length // CONTRIB
    value, weight, put, straight, crossed, places = kernel_call(
        functools.partial(prepare_kernel, columns=columns, share=share, blocks=blocks), "prepare",
        [jax.ShapeDtypeStruct((rows, LANES), F32)] * 2
        + [jax.ShapeDtypeStruct(((share + share % 2) * blocks, 2 * width), BF16)]
        + [jax.ShapeDtypeStruct((width, LANES), F32)] * 2
        + [jax.ShapeDtypeStruct((1, width), jnp.int32)],
        [pltpu.VMEM] * (2 + len(gathered)), [],
        offsets, made["shift"], *gathered, flops=PREPARE_FLOPS,
    )
    returned = kernel_call(
        functools.partial(subgrid_kernel, columns=columns, bands=bands), "subgrid",
        jax.ShapeDtypeStruct((rows, LANES), BF16), [pltpu.VMEM] * 6, [wide(rows)],
        arrived, value, weight, made["grid_turn"], made["model"], made["back"],
    )
    delivered = lax.all_to_all(
        returned, ("band", "member"), split_axis=0, concat_axis=0, tiled=True,
        axis_index_groups=[
            [b * FACET_ROWS + member for b, member in return_order(bands)]
        ],
    )
    lines = kernel_call(
        functools.partial(return_kernel, bands=bands), "lines",
        jax.ShapeDtypeStruct((share, 2, length), F32), [pltpu.VMEM] * 10,
        [wide(2 * length // LANES)] * share,
        places, delivered, straight, crossed, put, made["window"], made["turn"],
        made["partial"], made["inner_plus"], made["outer_plus"],
    )
    return lines[None]


def solution(mesh):
    bands = mesh.shape["band"]
    groups = mesh.shape["facet"] // FACET_ROWS
    split_mesh = Mesh(
        mesh.devices.reshape(groups, FACET_ROWS, bands), ("group", "member", "band")
    )
    facet = ("group", "member")
    placed = (
        P("band", facet, None, None, None),
        P(),
        P("band", None, facet, None, None),
        P("band", None, facet, None, None),
        P("band", None, facet, None),
        P("band", None, facet, None),
    )
    return jax.shard_map(
        functools.partial(local, groups, bands),
        mesh=split_mesh,
        in_specs=placed,
        out_specs=P(facet, "band", None, None),
        check_vma=False,
    )
```

```python
import functools
import math

import jax
import jax.numpy as jnp
import ml_dtypes
import numpy as np
from jax import lax
from jax.experimental import pallas as pl
from jax.experimental.pallas import tpu as pltpu
from jax.sharding import Mesh
from jax.sharding import PartitionSpec as P

CONTRIB = 64
FACET_ROWS = 8
SUBGRID = FACET_ROWS * CONTRIB
SEND_ORDER = (FACET_ROWS - 1, *range(FACET_ROWS - 1))
PLACE_ORDER = tuple(range(FACET_ROWS))
LANES = 128
HALF = LANES // 2
PADDED_ROWS = 8
EARLY_FLOPS = 10**10
LATE_FLOPS = 10**10
PREPARE_FLOPS = 2 * 10**10
VMEM_LIMIT = 48 * 1024 * 1024
F32 = jnp.float32
BF16 = jnp.bfloat16


def phases(rows, cols, length, rotation):
    product = np.outer(rows, cols) % length
    return np.exp(rotation * 2j * np.pi * product / length)


def from_left(matrix):
    return np.block([[matrix.real, -matrix.imag], [matrix.imag, matrix.real]])


def from_right(matrix):
    return np.block([[matrix.real, matrix.imag], [-matrix.imag, matrix.real]])


def high_low(table):
    high = table.astype(ml_dtypes.bfloat16)
    low = (table - high.astype(np.float64)).astype(ml_dtypes.bfloat16)
    return np.stack([high, low])


def side_by_side(values):
    straight = np.concatenate([values.real, values.real], axis=-1)
    crossed = np.concatenate([-values.imag, values.imag], axis=-1)
    return np.stack([straight, crossed])


def stack_tables(named):
    places, blocks, begin = {}, [], 0
    for name, table in named.items():
        count = table.shape[1] // LANES
        places[name] = (begin, table.shape[0], count)
        blocks += [table[:, i * LANES : (i + 1) * LANES] for i in range(count)]
        begin += table.shape[0] * count
    return np.concatenate(blocks, axis=0), places


def stack_pairs(named):
    return stack_tables(
        {(name, i): table for name, pair in named.items() for i, table in enumerate(pair)}
    )


def tables(length):
    blocks = length // CONTRIB
    short = np.arange(CONTRIB)
    outer = np.concatenate([np.arange(0, blocks, 2), np.arange(1, blocks, 2)])
    window = 1.0 + 0.5 * np.cos(np.arange(length) * (2.0 * math.pi / length))
    window = (window * length**-0.5).reshape(length // LANES, LANES).astype(np.float32)
    turn = np.tile(phases(short, short, length, -1), (1, 2))
    turn = np.stack([turn.real, turn.imag]).astype(np.float32)
    pair = np.eye(2)
    shift = high_low(np.concatenate(side_by_side(phases(short, short, CONTRIB, -1)), axis=1))
    outer_minus = from_left(phases(short, outer, blocks, -1))
    inner_minus = from_right(np.kron(pair, phases(short, short, CONTRIB, -1)))
    piece = from_right(phases(short, short, CONTRIB, 1)) * CONTRIB**-0.5
    return dict(
        plain=stack_tables(dict(window=window, real=turn[0], imag=turn[1])),
        paired=stack_pairs(
            dict(
                shift=shift,
                outer=high_low(outer_minus),
                inner=high_low(inner_minus),
                piece=high_low(piece),
            )
        ),
        window=window,
        turn=turn,
        shift=shift,
        inner_plus=high_low(from_right(np.kron(pair, phases(short, short, CONTRIB, 1)))),
        outer_plus=high_low(from_left(phases(outer, short, blocks, 1))),
        partial=high_low(from_right(phases(short, short, CONTRIB, -1)).T * CONTRIB**-0.5),
        grid_turn=side_by_side(phases(np.arange(FACET_ROWS), short, SUBGRID, -1)).astype(
            np.float32
        ),
        model=high_low(from_right(phases(short, short, CONTRIB, -1)) * SUBGRID**-0.5),
        back=high_low(from_right(phases(short, short, CONTRIB, 1)) * SUBGRID**-0.5),
    )


def return_order(bands):
    order = [(b, member) for b in range(bands) for member in PLACE_ORDER]
    return order[-1:] + order[:-1]


def split(values):
    high = values.astype(BF16)
    return high, (values - high.astype(F32)).astype(BF16)


def dot(left, right, dims=((1,), (0,))):
    return lax.dot_general(left, right, (dims, ((), ())), preferred_element_type=F32)


def dot_split(values, right):
    rows = values.shape[0]
    both = dot(jnp.concatenate(split(values), axis=0), right)
    return both[:rows] + both[rows:]


def times_table(values, table):
    return dot_split(values, table[0]) + dot(values.astype(BF16), table[1])


def table_times(table, values, dims=((1,), (0,))):
    high, low = split(values)
    rows = table[0].shape[0]
    both = dot(jnp.concatenate([table[0], table[1]], axis=0), high, dims)
    return both[:rows] + both[rows:] + dot(table[0], low, dims)


def iota(shape, dimension):
    return lax.broadcasted_iota(jnp.int32, shape, dimension)


def over(values, size):
    return lax.shift_right_logical(values, jnp.full_like(values, size.bit_length() - 1))


def within(values, size):
    return values & (size - 1)


def swap_halves(values):
    return pltpu.roll(values, HALF, 1)


def table_at(ref, place):
    begin, rows, blocks = place
    parts = [ref[begin + i * rows : begin + (i + 1) * rows, :] for i in range(blocks)]
    return parts[0] if blocks == 1 else jnp.concatenate(parts, axis=1)


def offsets_on_lanes(offsets_ref, columns, order):
    fronts, owners = offsets_ref.shape
    groups = owners // FACET_ROWS
    place = over(iota((1, fronts * owners * columns), 1), columns)
    front = within(place, fronts)
    group = within(over(place, fronts) + lax.axis_index("group"), groups)
    spot = over(place, fronts * groups)
    member = jnp.zeros_like(spot)
    for i, value in enumerate(order):
        member = jnp.where(spot == i, value, member)
    owner = group * FACET_ROWS + member
    pick = one_hot((owners, place.shape[1]), owner)
    offsets = offsets_ref[...]
    blocks = dot(over(offsets, CONTRIB).astype(F32).astype(BF16), pick)
    residues = dot(within(offsets, CONTRIB).astype(F32).astype(BF16), pick)
    spread = jnp.zeros_like(place, dtype=F32)
    for t in range(fronts):
        here = blocks[t : t + 1, :] * CONTRIB + residues[t : t + 1, :]
        spread = jnp.where(front == t, here, spread)
    return spread.astype(jnp.int32)


def shift_rows(residue, table):
    pick = jnp.where(iota((CONTRIB, residue.shape[1]), 0) == residue, 1.0, 0.0).T.astype(BF16)
    rows = dot(pick, table[0]) + dot(pick, table[1])
    return rows[:, :LANES], rows[:, LANES:]


def one_hot(shape, targets):
    return jnp.where(iota(shape, 0) == targets, 1.0, 0.0).astype(BF16)


def turned_eighths(values, rotation):
    sign = jnp.where(iota(values[0].shape, 1) < HALF, -rotation, rotation).astype(F32)

    def quarter_turn(value):
        return swap_halves(value) * sign

    def four(a, b, c, d):
        even_sum, even_diff = a + c, a - c
        odd_sum, odd_diff = b + d, quarter_turn(b - d)
        return even_sum + odd_sum, even_diff + odd_diff, even_sum - odd_sum, even_diff - odd_diff

    even = four(*values[0::2])
    odd = four(*values[1::2])
    root = math.sqrt(0.5)
    turned = (
        odd[0],
        (odd[1] + quarter_turn(odd[1])) * root,
        quarter_turn(odd[2]),
        (quarter_turn(odd[3]) - odd[3]) * root,
    )
    return [e + o for e, o in zip(even, turned)] + [e - o for e, o in zip(even, turned)]


def pack_samples(cells_ref, values_ref, weights_ref, flags_ref, out_ref):
    for t in range(cells_ref.shape[0]):
        rows = [
            cells_ref[t, 0:1, :].astype(F32) * SUBGRID + cells_ref[t, 1:2, :].astype(F32),
            weights_ref[t] * flags_ref[t].astype(F32),
            values_ref[t],
        ]
        out_ref[4 * t : 4 * t + 4, :] = jnp.concatenate(rows, axis=0)


def start_all(sources, targets, semaphores):
    copies = [
        pltpu.make_async_copy(source, target, semaphores.at[i])
        for i, (source, target) in enumerate(zip(sources, targets))
    ]
    for copy in copies:
        copy.start()
    return copies


def predict(spread, copies, strips_ref, plain_ref, paired_ref, held_refs, out_ref, plain, paired):
    columns, length = strips_ref.shape[1:]
    groups = length // LANES
    pairs = columns // 2
    blocks = length // CONTRIB
    width = spread.shape[1]
    first_block, residue = over(spread, CONTRIB), within(spread, CONTRIB)
    column = within(iota(spread.shape, 1), columns)
    kappa = iota((CONTRIB, width), 0)
    block = within(first_block + jnp.where(kappa < residue, 1, 0), blocks)
    source = within(column, 2) * blocks + block
    pair_of = over(column, 2)
    for copy in copies[:2]:
        copy.wait()

    def pair_at(name):
        return [table_at(paired_ref, paired[name, i]) for i in range(2)]

    window = table_at(plain_ref, plain["window"])
    turn_real, turn_imag = table_at(plain_ref, plain["real"]), table_at(plain_ref, plain["imag"])
    low_half = iota((groups, LANES), 1) < HALF
    sections = []
    for part, held in enumerate(held_refs):
        for group in range(groups):
            held[group * columns : (group + 1) * columns, :] = strips_ref[
                part, :, group * LANES : (group + 1) * LANES
            ]
        even, odd = [], []
        for pair in range(pairs):
            first = held[pl.ds(2 * pair, groups, stride=columns), :] * window
            second = held[pl.ds(2 * pair + 1, groups, stride=columns), :] * window
            even.append(jnp.where(low_half, first, swap_halves(second)))
            odd.append(jnp.where(low_half, swap_halves(first), second))
        sections += [jnp.concatenate(even, axis=1), jnp.concatenate(odd, axis=1)]
    for copy in copies[2:]:
        copy.wait()
    section = table_times(pair_at("outer"), jnp.concatenate(sections, axis=0))
    turned = []
    for pair in range(pairs):
        lanes = slice(pair * LANES, (pair + 1) * LANES)
        real, imag = section[:CONTRIB, lanes], section[CONTRIB:, lanes]
        turned.append(
            jnp.concatenate(
                [real * turn_real - imag * turn_imag, real * turn_imag + imag * turn_real],
                axis=1,
            )
        )
    inner = times_table(jnp.concatenate(turned, axis=0), pair_at("inner"))
    cutouts = []
    for part in range(2):
        tiles = []
        for tile in range(width // LANES):
            lanes = slice(tile * LANES, (tile + 1) * LANES)
            chosen = None
            for pair in range(pairs):
                rows = inner[pair * CONTRIB : (pair + 1) * CONTRIB, part * LANES : (part + 1) * LANES]
                found = jnp.take_along_axis(
                    rows, source[:, lanes], axis=1, mode="promise_in_bounds"
                )
                here = pair_of[:, lanes] == pair
                chosen = found if chosen is None else jnp.where(here, found, chosen)
            tiles.append(chosen)
        cutouts.append(jnp.concatenate(tiles, axis=1))
    cutout = jnp.concatenate(cutouts, axis=0)
    piece = times_table(cutout.T, pair_at("piece"))
    straight, crossed = shift_rows(residue, pair_at("shift"))
    out_ref[...] = (piece * straight + swap_halves(piece) * crossed).astype(BF16)


def in_first_half():
    return 2 * lax.axis_index("group") < lax.axis_size("group")


def early_kernel(
    cells, values, weights, flags, offsets, strips, plain_table, paired_table, out_ref, packed_ref,
    cells_ref, values_ref, weights_ref, flags_ref, offsets_ref, strips_ref, plain_ref, paired_ref,
    real_ref, imag_ref, small_semaphores, semaphores, *, plain, paired,
):
    small = start_all(
        (cells, values, weights, flags),
        (cells_ref, values_ref, weights_ref, flags_ref),
        small_semaphores,
    )

    def large():
        sources = (offsets, strips, plain_table, paired_table)
        targets = (offsets_ref, strips_ref, plain_ref, paired_ref)
        return [
            pltpu.make_async_copy(source, target, semaphores.at[i])
            for i, (source, target) in enumerate(zip(sources, targets))
        ]

    @pl.when(in_first_half())
    def _():
        for copy in large():
            copy.start()

    for copy in small:
        copy.wait()
    for t in range(cells_ref.shape[0]):
        rows = [
            cells_ref[t, 0:1, :].astype(F32) * SUBGRID + cells_ref[t, 1:2, :].astype(F32),
            weights_ref[t] * flags_ref[t].astype(F32),
            values_ref[t],
        ]
        packed_ref[4 * t : 4 * t + 4, :] = jnp.concatenate(rows, axis=0)

    @pl.when(in_first_half())
    def _():
        copies = large()
        copies[0].wait()
        predict(
            offsets_on_lanes(offsets_ref, strips_ref.shape[1], SEND_ORDER), copies[1:],
            strips_ref, plain_ref, paired_ref, (real_ref, imag_ref), out_ref, plain, paired,
        )


def late_kernel(
    early_ref, offsets_ref, strips_ref, plain_ref, paired_ref, out_ref, real_ref, imag_ref,
    *, plain, paired,
):
    @pl.when(in_first_half())
    def _():
        out_ref[...] = early_ref[...]

    @pl.when(jnp.logical_not(in_first_half()))
    def _():
        predict(
            offsets_on_lanes(offsets_ref, strips_ref.shape[1], SEND_ORDER), (),
            strips_ref, plain_ref, paired_ref, (real_ref, imag_ref), out_ref, plain, paired,
        )


def prepare_kernel(offsets_ref, shift_ref, *refs, columns, share, blocks):
    samples_refs, outs = refs[:-6], refs[-6:]
    value_ref, weight_ref, put_ref, straight_ref, crossed_ref, places_ref = outs
    fronts, samples = offsets_ref.shape[0], samples_refs[0].shape[1]
    own = lax.axis_index("group")
    depth = FACET_ROWS * columns
    for spot in range(len(samples_refs) * fronts):
        step, t = spot // fronts, spot % fronts
        sample = samples_refs[step][4 * t : 4 * t + 4, :]
        cell = sample[0:1, :].astype(jnp.int32)
        row, col = over(cell, SUBGRID) - own * columns, within(cell, SUBGRID)
        inside = (row >= 0) & (row < columns)
        target = jnp.where(inside, within(col, FACET_ROWS) * columns + row, -1)
        pick = one_hot((depth, samples), target)
        mask = iota((HALF, samples), 0) == over(col, FACET_ROWS)
        factor = sample[1:2, :]
        highs, lows = [], []
        for term in (factor * sample[2:3, :], factor * sample[3:4, :], factor):
            high = term.astype(BF16).astype(F32)
            highs.append(jnp.where(mask, high, 0.0).astype(BF16))
            lows.append(jnp.where(mask, term - high, 0.0).astype(BF16))
        highs, lows = highs + highs[2:], lows + lows[2:]
        grid = dot(pick, jnp.concatenate(highs, axis=0), ((1,), (1,))) + dot(
            pick, jnp.concatenate(lows, axis=0), ((1,), (1,))
        )
        rows = slice(spot * depth, (spot + 1) * depth)
        value_ref[rows, :] = grid[:, :LANES]
        weight_ref[rows, :] = grid[:, LANES:]
    spread = offsets_on_lanes(offsets_ref, share, PLACE_ORDER)
    places_ref[...] = spread
    first_block, residue = over(spread, CONTRIB), within(spread, CONTRIB)
    straight_ref[...], crossed_ref[...] = shift_rows(residue, shift_ref)
    base = within(iota(spread.shape, 1), share) * blocks
    targets = jnp.concatenate([base + first_block, base + within(first_block + 1, blocks)], axis=1)
    put_ref[...] = one_hot(put_ref.shape, targets)


def subgrid_kernel(
    pieces_ref, value_ref, weight_ref, turn_ref, model_ref, back_ref, out_ref, held_ref,
    *, columns, bands,
):
    rows = pieces_ref.shape[0] // FACET_ROWS
    spots = range(rows // columns)
    depth = FACET_ROWS * columns
    share = columns // bands
    pieces = pieces_ref[...].astype(F32)
    sky = turned_eighths(
        [
            pieces[spot * rows : (spot + 1) * rows, :]
            for spot in (SEND_ORDER.index(i) for i in range(FACET_ROWS))
        ],
        -1.0,
    )
    sky = [
        value * turn_ref[0, i : i + 1, :] + swap_halves(value) * turn_ref[1, i : i + 1, :]
        for i, value in enumerate(sky)
    ]
    stacked = jnp.concatenate(
        [value[spot * columns : (spot + 1) * columns, :] for spot in spots for value in sky],
        axis=0,
    )
    grid = value_ref[...] - weight_ref[...] * times_table(stacked, model_ref)
    back = times_table(grid, back_ref)
    lines = []
    for i in range(FACET_ROWS):
        value = jnp.concatenate(
            [
                back[spot * depth + i * columns : spot * depth + (i + 1) * columns, :]
                for spot in spots
            ],
            axis=0,
        )
        lines.append(
            value * turn_ref[0, i : i + 1, :] - swap_halves(value) * turn_ref[1, i : i + 1, :]
        )
    lines = turned_eighths(lines, 1.0)
    for i in range(FACET_ROWS):
        for spot in spots:
            for b in range(bands):
                source = spot * columns + b * share
                place = return_order(bands).index((b, i))
                target = (place * len(spots) + spot) * share
                held_ref[target : target + share, :] = lines[i][source : source + share, :]
    out_ref[...] = held_ref[...].astype(BF16)


def return_kernel(
    places_ref, pieces_ref, straight_ref, crossed_ref, put_ref, window_ref, turn_ref, partial_ref,
    inner_ref, outer_ref, out_ref, *line_refs, bands,
):
    columns, _, length = out_ref.shape
    blocks = length // CONTRIB
    groups = length // LANES
    pairs = (columns + 1) // 2
    width = pieces_ref.shape[0] // bands
    pieces = pieces_ref[...].astype(F32)
    order, rows = return_order(bands), width // FACET_ROWS

    def of_band(b):
        begins = [order.index((b, member)) * rows for member in PLACE_ORDER]
        return jnp.concatenate([pieces[begin : begin + rows, :] for begin in begins], axis=0)

    summed = of_band(0)
    for b in range(1, bands):
        summed += of_band(b)
    summed = summed * straight_ref[...] - swap_halves(summed) * crossed_ref[...]
    residues = table_times(partial_ref, summed, ((1,), (1,)))
    kappa = within(iota((2 * CONTRIB, width), 0), CONTRIB)
    inside = kappa >= within(places_ref[...], CONTRIB)
    both = jnp.concatenate(
        [jnp.where(inside, residues, 0.0), jnp.where(inside, 0.0, residues)], axis=1
    )
    put = put_ref[...]
    high, low = split(both)
    spectrum = dot(high, put, ((1,), (1,))) + dot(low, put, ((1,), (1,)))
    inner = times_table(
        jnp.concatenate(
            [
                jnp.concatenate(
                    [
                        spectrum[:CONTRIB, pair * LANES : (pair + 1) * LANES],
                        spectrum[CONTRIB:, pair * LANES : (pair + 1) * LANES],
                    ],
                    axis=1,
                )
                for pair in range(pairs)
            ],
            axis=0,
        ),
        inner_ref,
    )
    reals, imags = [], []
    for pair in range(pairs):
        rows = slice(pair * CONTRIB, (pair + 1) * CONTRIB)
        real, imag = inner[rows, :LANES], inner[rows, LANES:]
        reals.append(real * turn_ref[0] + imag * turn_ref[1])
        imags.append(imag * turn_ref[0] - real * turn_ref[1])
    lines = table_times(
        outer_ref,
        jnp.concatenate(
            [jnp.concatenate(reals, axis=1), jnp.concatenate(imags, axis=1)], axis=0
        ),
    )
    window = window_ref[...]
    low_half = iota((groups, LANES), 1) < HALF
    for part in range(2):
        for pair in range(pairs):
            lanes = slice(pair * LANES, (pair + 1) * LANES)
            begin = part * blocks
            even = lines[begin : begin + groups, lanes]
            odd = lines[begin + groups : begin + blocks, lanes]
            line_refs[2 * pair][pl.ds(part, groups, stride=2), :] = (
                jnp.where(low_half, even, swap_halves(odd)) * window
            )
            if 2 * pair + 1 < columns:
                line_refs[2 * pair + 1][pl.ds(part, groups, stride=2), :] = (
                    jnp.where(low_half, swap_halves(even), odd) * window
                )
    for column in range(columns):
        for group in range(groups):
            out_ref[column, :, group * LANES : (group + 1) * LANES] = line_refs[column][
                2 * group : 2 * group + 2, :
            ]


def kernel_call(kernel, name, out_shape, spaces, scratch, *operands, flops=0):
    return pl.pallas_call(
        kernel,
        out_shape=out_shape,
        in_specs=[pl.BlockSpec(memory_space=space) for space in spaces],
        out_specs=jax.tree.map(lambda _: pl.BlockSpec(memory_space=pltpu.VMEM), out_shape),
        scratch_shapes=scratch,
        compiler_params=pltpu.CompilerParams(vmem_limit_bytes=VMEM_LIMIT),
        cost_estimate=pl.CostEstimate(flops=flops, bytes_accessed=0, transcendentals=0)
        if flops
        else None,
        name=name,
    )(*operands)


def wide(rows):
    return pltpu.VMEM((rows, LANES), F32)


def local(groups, bands, strips, offsets, cells, values, weights, flags):
    columns, length = strips.shape[-2:]
    fronts = offsets.shape[0]
    share = columns // bands
    facets = groups * FACET_ROWS
    rows = facets * fronts * columns
    width = facets * fronts * share
    made = tables(length)
    plain, plain_places = made.pop("plain")
    paired, paired_places = made.pop("paired")
    made = {key: jnp.asarray(value) for key, value in made.items()}
    held = length // LANES * columns
    small = [cells[0, :, 0], values[0, :, 0], weights[0], flags[0]]
    large = [strips[0, 0], jnp.asarray(plain), jnp.asarray(paired)]

    def landing(arrays):
        return [pltpu.VMEM(array.shape, array.dtype) for array in arrays]

    def in_hbm(arrays):
        return [pltpu.with_memory_space_constraint(array, pltpu.HBM) for array in arrays]

    def semaphores(count):
        return pltpu.SemaphoreType.DMA((count,))

    early, packed = kernel_call(
        functools.partial(early_kernel, plain=plain_places, paired=paired_places), "early",
        [
            jax.ShapeDtypeStruct((rows, LANES), BF16),
            jax.ShapeDtypeStruct((PADDED_ROWS, cells.shape[-1]), F32),
        ],
        [pltpu.HBM] * 8,
        landing(small + [offsets] + large) + [wide(held)] * 2 + [semaphores(4), semaphores(4)],
        *in_hbm(small + [offsets] + large), flops=EARLY_FLOPS,
    )
    pieces = kernel_call(
        functools.partial(late_kernel, plain=plain_places, paired=paired_places), "late",
        jax.ShapeDtypeStruct((rows, LANES), BF16), [pltpu.VMEM] * 5, [wide(held)] * 2,
        early, offsets, *large, flops=LATE_FLOPS,
    )
    gathered = [packed]
    for step in range(1, groups):
        moves = [((group + step) % groups, group) for group in range(groups)]
        gathered.append(lax.ppermute(packed, "group", moves))
    arrived = lax.all_to_all(
        pieces, "member", split_axis=0, concat_axis=0, tiled=True,
        axis_index_groups=[list(SEND_ORDER)],
    )
    gathered, arrived = lax.optimization_barrier((gathered, arrived))
    blocks = length // CONTRIB
    value, weight, put, straight, crossed, places = kernel_call(
        functools.partial(prepare_kernel, columns=columns, share=share, blocks=blocks), "prepare",
        [jax.ShapeDtypeStruct((rows, LANES), F32)] * 2
        + [jax.ShapeDtypeStruct(((share + share % 2) * blocks, 2 * width), BF16)]
        + [jax.ShapeDtypeStruct((width, LANES), F32)] * 2
        + [jax.ShapeDtypeStruct((1, width), jnp.int32)],
        [pltpu.VMEM] * (2 + len(gathered)), [],
        offsets, made["shift"], *gathered, flops=PREPARE_FLOPS,
    )
    returned = kernel_call(
        functools.partial(subgrid_kernel, columns=columns, bands=bands), "subgrid",
        jax.ShapeDtypeStruct((rows, LANES), BF16), [pltpu.VMEM] * 6, [wide(rows)],
        arrived, value, weight, made["grid_turn"], made["model"], made["back"],
    )
    delivered = lax.all_to_all(
        returned, ("band", "member"), split_axis=0, concat_axis=0, tiled=True,
        axis_index_groups=[
            [b * FACET_ROWS + member for b, member in return_order(bands)]
        ],
    )
    lines = kernel_call(
        functools.partial(return_kernel, bands=bands), "lines",
        jax.ShapeDtypeStruct((share, 2, length), F32), [pltpu.VMEM] * 10,
        [wide(2 * length // LANES)] * share,
        places, delivered, straight, crossed, put, made["window"], made["turn"],
        made["partial"], made["inner_plus"], made["outer_plus"],
    )
    return lines[None]


def solution(mesh):
    bands = mesh.shape["band"]
    groups = mesh.shape["facet"] // FACET_ROWS
    split_mesh = Mesh(
        mesh.devices.reshape(groups, FACET_ROWS, bands), ("group", "member", "band")
    )
    facet = ("group", "member")
    placed = (
        P("band", facet, None, None, None),
        P(),
        P("band", None, facet, None, None),
        P("band", None, facet, None, None),
        P("band", None, facet, None),
        P("band", None, facet, None),
    )
    return jax.shard_map(
        functools.partial(local, groups, bands),
        mesh=split_mesh,
        in_specs=placed,
        out_specs=P(facet, "band", None, None),
        check_vma=False,
    )
```

```python
import functools
import math

import jax
import jax.numpy as jnp
import ml_dtypes
import numpy as np
from jax import lax
from jax.experimental import pallas as pl
from jax.experimental.pallas import tpu as pltpu
from jax.sharding import Mesh
from jax.sharding import PartitionSpec as P

CONTRIB = 64
FACET_ROWS = 8
SUBGRID = FACET_ROWS * CONTRIB
SEND_ORDER = (FACET_ROWS - 1, *range(FACET_ROWS - 1))
PLACE_ORDER = tuple(range(FACET_ROWS))
LANES = 128
HALF = LANES // 2
PADDED_ROWS = 32
EARLY_FLOPS = 10**10
LATE_FLOPS = 10**10
PREPARE_FLOPS = 2 * 10**10
VMEM_LIMIT = 48 * 1024 * 1024
F32 = jnp.float32
BF16 = jnp.bfloat16


def phases(rows, cols, length, rotation):
    product = np.outer(rows, cols) % length
    return np.exp(rotation * 2j * np.pi * product / length)


def from_left(matrix):
    return np.block([[matrix.real, -matrix.imag], [matrix.imag, matrix.real]])


def from_right(matrix):
    return np.block([[matrix.real, matrix.imag], [-matrix.imag, matrix.real]])


def high_low(table):
    high = table.astype(ml_dtypes.bfloat16)
    low = (table - high.astype(np.float64)).astype(ml_dtypes.bfloat16)
    return np.stack([high, low])


def side_by_side(values):
    straight = np.concatenate([values.real, values.real], axis=-1)
    crossed = np.concatenate([-values.imag, values.imag], axis=-1)
    return np.stack([straight, crossed])


def stack_tables(named):
    places, blocks, begin = {}, [], 0
    for name, table in named.items():
        count = table.shape[1] // LANES
        places[name] = (begin, table.shape[0], count)
        blocks += [table[:, i * LANES : (i + 1) * LANES] for i in range(count)]
        begin += table.shape[0] * count
    return np.concatenate(blocks, axis=0), places


def stack_pairs(named):
    return stack_tables(
        {(name, i): table for name, pair in named.items() for i, table in enumerate(pair)}
    )


def tables(length):
    blocks = length // CONTRIB
    short = np.arange(CONTRIB)
    outer = np.concatenate([np.arange(0, blocks, 2), np.arange(1, blocks, 2)])
    window = 1.0 + 0.5 * np.cos(np.arange(length) * (2.0 * math.pi / length))
    window = (window * length**-0.5).reshape(length // LANES, LANES).astype(np.float32)
    turn = np.tile(phases(short, short, length, -1), (1, 2))
    turn = np.stack([turn.real, turn.imag]).astype(np.float32)
    pair = np.eye(2)
    shift = high_low(np.concatenate(side_by_side(phases(short, short, CONTRIB, -1)), axis=1))
    outer_minus = from_left(phases(short, outer, blocks, -1))
    inner_minus = from_right(np.kron(pair, phases(short, short, CONTRIB, -1)))
    piece = from_right(phases(short, short, CONTRIB, 1)) * CONTRIB**-0.5
    return dict(
        plain=stack_tables(dict(window=window, real=turn[0], imag=turn[1])),
        paired=stack_pairs(
            dict(
                shift=shift,
                outer=high_low(outer_minus),
                inner=high_low(inner_minus),
                piece=high_low(piece),
            )
        ),
        window=window,
        turn=turn,
        shift=shift,
        inner_plus=high_low(from_right(np.kron(pair, phases(short, short, CONTRIB, 1)))),
        outer_plus=high_low(from_left(phases(outer, short, blocks, 1))),
        partial=high_low(from_right(phases(short, short, CONTRIB, -1)).T * CONTRIB**-0.5),
        grid_turn=side_by_side(phases(np.arange(FACET_ROWS), short, SUBGRID, -1)).astype(
            np.float32
        ),
        model=high_low(from_right(phases(short, short, CONTRIB, -1)) * SUBGRID**-0.5),
        back=high_low(from_right(phases(short, short, CONTRIB, 1)) * SUBGRID**-0.5),
    )


def return_order(bands):
    order = [(b, member) for b in range(bands) for member in PLACE_ORDER]
    return order[-1:] + order[:-1]


def split(values):
    high = values.astype(BF16)
    return high, (values - high.astype(F32)).astype(BF16)


def dot(left, right, dims=((1,), (0,))):
    return lax.dot_general(left, right, (dims, ((), ())), preferred_element_type=F32)


def dot_split(values, right):
    rows = values.shape[0]
    both = dot(jnp.concatenate(split(values), axis=0), right)
    return both[:rows] + both[rows:]


def times_table(values, table):
    return dot_split(values, table[0]) + dot(values.astype(BF16), table[1])


def table_times(table, values, dims=((1,), (0,))):
    high, low = split(values)
    rows = table[0].shape[0]
    both = dot(jnp.concatenate([table[0], table[1]], axis=0), high, dims)
    return both[:rows] + both[rows:] + dot(table[0], low, dims)


def iota(shape, dimension):
    return lax.broadcasted_iota(jnp.int32, shape, dimension)


def over(values, size):
    return lax.shift_right_logical(values, jnp.full_like(values, size.bit_length() - 1))


def within(values, size):
    return values & (size - 1)


def swap_halves(values):
    return pltpu.roll(values, HALF, 1)


def table_at(ref, place):
    begin, rows, blocks = place
    parts = [ref[begin + i * rows : begin + (i + 1) * rows, :] for i in range(blocks)]
    return parts[0] if blocks == 1 else jnp.concatenate(parts, axis=1)


def offsets_on_lanes(offsets_ref, columns, order):
    fronts, owners = offsets_ref.shape
    groups = owners // FACET_ROWS
    place = over(iota((1, fronts * owners * columns), 1), columns)
    front = within(place, fronts)
    group = within(over(place, fronts) + lax.axis_index("group"), groups)
    spot = over(place, fronts * groups)
    member = jnp.zeros_like(spot)
    for i, value in enumerate(order):
        member = jnp.where(spot == i, value, member)
    owner = group * FACET_ROWS + member
    pick = one_hot((owners, place.shape[1]), owner)
    offsets = offsets_ref[...]
    blocks = dot(over(offsets, CONTRIB).astype(F32).astype(BF16), pick)
    residues = dot(within(offsets, CONTRIB).astype(F32).astype(BF16), pick)
    spread = jnp.zeros_like(place, dtype=F32)
    for t in range(fronts):
        here = blocks[t : t + 1, :] * CONTRIB + residues[t : t + 1, :]
        spread = jnp.where(front == t, here, spread)
    return spread.astype(jnp.int32)


def shift_rows(residue, table):
    pick = jnp.where(iota((CONTRIB, residue.shape[1]), 0) == residue, 1.0, 0.0).T.astype(BF16)
    rows = dot(pick, table[0]) + dot(pick, table[1])
    return rows[:, :LANES], rows[:, LANES:]


def one_hot(shape, targets):
    return jnp.where(iota(shape, 0) == targets, 1.0, 0.0).astype(BF16)


def turned_eighths(values, rotation):
    sign = jnp.where(iota(values[0].shape, 1) < HALF, -rotation, rotation).astype(F32)

    def quarter_turn(value):
        return swap_halves(value) * sign

    def four(a, b, c, d):
        even_sum, even_diff = a + c, a - c
        odd_sum, odd_diff = b + d, quarter_turn(b - d)
        return even_sum + odd_sum, even_diff + odd_diff, even_sum - odd_sum, even_diff - odd_diff

    even = four(*values[0::2])
    odd = four(*values[1::2])
    root = math.sqrt(0.5)
    turned = (
        odd[0],
        (odd[1] + quarter_turn(odd[1])) * root,
        quarter_turn(odd[2]),
        (quarter_turn(odd[3]) - odd[3]) * root,
    )
    return [e + o for e, o in zip(even, turned)] + [e - o for e, o in zip(even, turned)]


def pack_samples(cells_ref, values_ref, weights_ref, flags_ref, out_ref):
    for t in range(cells_ref.shape[0]):
        rows = [
            cells_ref[t, 0:1, :].astype(F32) * SUBGRID + cells_ref[t, 1:2, :].astype(F32),
            weights_ref[t] * flags_ref[t].astype(F32),
            values_ref[t],
        ]
        out_ref[4 * t : 4 * t + 4, :] = jnp.concatenate(rows, axis=0)


def start_all(sources, targets, semaphores):
    copies = [
        pltpu.make_async_copy(source, target, semaphores.at[i])
        for i, (source, target) in enumerate(zip(sources, targets))
    ]
    for copy in copies:
        copy.start()
    return copies


def predict(spread, copies, strips_ref, plain_ref, paired_ref, held_refs, out_ref, plain, paired):
    columns, length = strips_ref.shape[1:]
    groups = length // LANES
    pairs = columns // 2
    blocks = length // CONTRIB
    width = spread.shape[1]
    first_block, residue = over(spread, CONTRIB), within(spread, CONTRIB)
    column = within(iota(spread.shape, 1), columns)
    kappa = iota((CONTRIB, width), 0)
    block = within(first_block + jnp.where(kappa < residue, 1, 0), blocks)
    source = within(column, 2) * blocks + block
    pair_of = over(column, 2)
    for copy in copies[:2]:
        copy.wait()

    def pair_at(name):
        return [table_at(paired_ref, paired[name, i]) for i in range(2)]

    window = table_at(plain_ref, plain["window"])
    turn_real, turn_imag = table_at(plain_ref, plain["real"]), table_at(plain_ref, plain["imag"])
    low_half = iota((groups, LANES), 1) < HALF
    sections = []
    for part, held in enumerate(held_refs):
        for group in range(groups):
            held[group * columns : (group + 1) * columns, :] = strips_ref[
                part, :, group * LANES : (group + 1) * LANES
            ]
        even, odd = [], []
        for pair in range(pairs):
            first = held[pl.ds(2 * pair, groups, stride=columns), :] * window
            second = held[pl.ds(2 * pair + 1, groups, stride=columns), :] * window
            even.append(jnp.where(low_half, first, swap_halves(second)))
            odd.append(jnp.where(low_half, swap_halves(first), second))
        sections += [jnp.concatenate(even, axis=1), jnp.concatenate(odd, axis=1)]
    for copy in copies[2:]:
        copy.wait()
    section = table_times(pair_at("outer"), jnp.concatenate(sections, axis=0))
    turned = []
    for pair in range(pairs):
        lanes = slice(pair * LANES, (pair + 1) * LANES)
        real, imag = section[:CONTRIB, lanes], section[CONTRIB:, lanes]
        turned.append(
            jnp.concatenate(
                [real * turn_real - imag * turn_imag, real * turn_imag + imag * turn_real],
                axis=1,
            )
        )
    inner = times_table(jnp.concatenate(turned, axis=0), pair_at("inner"))
    cutouts = []
    for part in range(2):
        tiles = []
        for tile in range(width // LANES):
            lanes = slice(tile * LANES, (tile + 1) * LANES)
            chosen = None
            for pair in range(pairs):
                rows = inner[pair * CONTRIB : (pair + 1) * CONTRIB, part * LANES : (part + 1) * LANES]
                found = jnp.take_along_axis(
                    rows, source[:, lanes], axis=1, mode="promise_in_bounds"
                )
                here = pair_of[:, lanes] == pair
                chosen = found if chosen is None else jnp.where(here, found, chosen)
            tiles.append(chosen)
        cutouts.append(jnp.concatenate(tiles, axis=1))
    cutout = jnp.concatenate(cutouts, axis=0)
    piece = times_table(cutout.T, pair_at("piece"))
    straight, crossed = shift_rows(residue, pair_at("shift"))
    out_ref[...] = (piece * straight + swap_halves(piece) * crossed).astype(BF16)


def in_first_half():
    return 2 * lax.axis_index("group") < lax.axis_size("group")


def early_kernel(
    cells, values, weights, flags, offsets, strips, plain_table, paired_table, out_ref, packed_ref,
    cells_ref, values_ref, weights_ref, flags_ref, offsets_ref, strips_ref, plain_ref, paired_ref,
    real_ref, imag_ref, small_semaphores, semaphores, *, plain, paired,
):
    small = start_all(
        (cells, values, weights, flags),
        (cells_ref, values_ref, weights_ref, flags_ref),
        small_semaphores,
    )

    def large():
        sources = (offsets, strips, plain_table, paired_table)
        targets = (offsets_ref, strips_ref, plain_ref, paired_ref)
        return [
            pltpu.make_async_copy(source, target, semaphores.at[i])
            for i, (source, target) in enumerate(zip(sources, targets))
        ]

    @pl.when(in_first_half())
    def _():
        for copy in large():
            copy.start()

    for copy in small:
        copy.wait()
    for t in range(cells_ref.shape[0]):
        rows = [
            cells_ref[t, 0:1, :].astype(F32) * SUBGRID + cells_ref[t, 1:2, :].astype(F32),
            weights_ref[t] * flags_ref[t].astype(F32),
            values_ref[t],
        ]
        packed_ref[4 * t : 4 * t + 4, :] = jnp.concatenate(rows, axis=0)

    @pl.when(in_first_half())
    def _():
        copies = large()
        copies[0].wait()
        predict(
            offsets_on_lanes(offsets_ref, strips_ref.shape[1], SEND_ORDER), copies[1:],
            strips_ref, plain_ref, paired_ref, (real_ref, imag_ref), out_ref, plain, paired,
        )


def late_kernel(
    early_ref, offsets_ref, strips_ref, plain_ref, paired_ref, out_ref, real_ref, imag_ref,
    *, plain, paired,
):
    @pl.when(in_first_half())
    def _():
        out_ref[...] = early_ref[...]

    @pl.when(jnp.logical_not(in_first_half()))
    def _():
        predict(
            offsets_on_lanes(offsets_ref, strips_ref.shape[1], SEND_ORDER), (),
            strips_ref, plain_ref, paired_ref, (real_ref, imag_ref), out_ref, plain, paired,
        )


def prepare_kernel(offsets_ref, shift_ref, *refs, columns, share, blocks):
    samples_refs, outs = refs[:-6], refs[-6:]
    value_ref, weight_ref, put_ref, straight_ref, crossed_ref, places_ref = outs
    fronts, samples = offsets_ref.shape[0], samples_refs[0].shape[1]
    own = lax.axis_index("group")
    depth = FACET_ROWS * columns
    for spot in range(len(samples_refs) * fronts):
        step, t = spot // fronts, spot % fronts
        sample = samples_refs[step][4 * t : 4 * t + 4, :]
        cell = sample[0:1, :].astype(jnp.int32)
        row, col = over(cell, SUBGRID) - own * columns, within(cell, SUBGRID)
        inside = (row >= 0) & (row < columns)
        target = jnp.where(inside, within(col, FACET_ROWS) * columns + row, -1)
        pick = one_hot((depth, samples), target)
        mask = iota((HALF, samples), 0) == over(col, FACET_ROWS)
        factor = sample[1:2, :]
        highs, lows = [], []
        for term in (factor * sample[2:3, :], factor * sample[3:4, :], factor):
            high = term.astype(BF16).astype(F32)
            highs.append(jnp.where(mask, high, 0.0).astype(BF16))
            lows.append(jnp.where(mask, term - high, 0.0).astype(BF16))
        highs, lows = highs + highs[2:], lows + lows[2:]
        grid = dot(pick, jnp.concatenate(highs, axis=0), ((1,), (1,))) + dot(
            pick, jnp.concatenate(lows, axis=0), ((1,), (1,))
        )
        rows = slice(spot * depth, (spot + 1) * depth)
        value_ref[rows, :] = grid[:, :LANES]
        weight_ref[rows, :] = grid[:, LANES:]
    spread = offsets_on_lanes(offsets_ref, share, PLACE_ORDER)
    places_ref[...] = spread
    first_block, residue = over(spread, CONTRIB), within(spread, CONTRIB)
    straight_ref[...], crossed_ref[...] = shift_rows(residue, shift_ref)
    base = within(iota(spread.shape, 1), share) * blocks
    targets = jnp.concatenate([base + first_block, base + within(first_block + 1, blocks)], axis=1)
    put_ref[...] = one_hot(put_ref.shape, targets)


def subgrid_kernel(
    pieces_ref, value_ref, weight_ref, turn_ref, model_ref, back_ref, out_ref, held_ref,
    *, columns, bands,
):
    rows = pieces_ref.shape[0] // FACET_ROWS
    spots = range(rows // columns)
    depth = FACET_ROWS * columns
    share = columns // bands
    pieces = pieces_ref[...].astype(F32)
    sky = turned_eighths(
        [
            pieces[spot * rows : (spot + 1) * rows, :]
            for spot in (SEND_ORDER.index(i) for i in range(FACET_ROWS))
        ],
        -1.0,
    )
    sky = [
        value * turn_ref[0, i : i + 1, :] + swap_halves(value) * turn_ref[1, i : i + 1, :]
        for i, value in enumerate(sky)
    ]
    stacked = jnp.concatenate(
        [value[spot * columns : (spot + 1) * columns, :] for spot in spots for value in sky],
        axis=0,
    )
    grid = value_ref[...] - weight_ref[...] * times_table(stacked, model_ref)
    back = times_table(grid, back_ref)
    lines = []
    for i in range(FACET_ROWS):
        value = jnp.concatenate(
            [
                back[spot * depth + i * columns : spot * depth + (i + 1) * columns, :]
                for spot in spots
            ],
            axis=0,
        )
        lines.append(
            value * turn_ref[0, i : i + 1, :] - swap_halves(value) * turn_ref[1, i : i + 1, :]
        )
    lines = turned_eighths(lines, 1.0)
    for i in range(FACET_ROWS):
        for spot in spots:
            for b in range(bands):
                source = spot * columns + b * share
                place = return_order(bands).index((b, i))
                target = (place * len(spots) + spot) * share
                held_ref[target : target + share, :] = lines[i][source : source + share, :]
    out_ref[...] = held_ref[...].astype(BF16)


def return_kernel(
    places_ref, pieces_ref, straight_ref, crossed_ref, put_ref, window_ref, turn_ref, partial_ref,
    inner_ref, outer_ref, out_ref, *line_refs, bands,
):
    columns, _, length = out_ref.shape
    blocks = length // CONTRIB
    groups = length // LANES
    pairs = (columns + 1) // 2
    width = pieces_ref.shape[0] // bands
    pieces = pieces_ref[...].astype(F32)
    order, rows = return_order(bands), width // FACET_ROWS

    def of_band(b):
        begins = [order.index((b, member)) * rows for member in PLACE_ORDER]
        return jnp.concatenate([pieces[begin : begin + rows, :] for begin in begins], axis=0)

    summed = of_band(0)
    for b in range(1, bands):
        summed += of_band(b)
    summed = summed * straight_ref[...] - swap_halves(summed) * crossed_ref[...]
    residues = table_times(partial_ref, summed, ((1,), (1,)))
    kappa = within(iota((2 * CONTRIB, width), 0), CONTRIB)
    inside = kappa >= within(places_ref[...], CONTRIB)
    both = jnp.concatenate(
        [jnp.where(inside, residues, 0.0), jnp.where(inside, 0.0, residues)], axis=1
    )
    put = put_ref[...]
    high, low = split(both)
    spectrum = dot(high, put, ((1,), (1,))) + dot(low, put, ((1,), (1,)))
    inner = times_table(
        jnp.concatenate(
            [
                jnp.concatenate(
                    [
                        spectrum[:CONTRIB, pair * LANES : (pair + 1) * LANES],
                        spectrum[CONTRIB:, pair * LANES : (pair + 1) * LANES],
                    ],
                    axis=1,
                )
                for pair in range(pairs)
            ],
            axis=0,
        ),
        inner_ref,
    )
    reals, imags = [], []
    for pair in range(pairs):
        rows = slice(pair * CONTRIB, (pair + 1) * CONTRIB)
        real, imag = inner[rows, :LANES], inner[rows, LANES:]
        reals.append(real * turn_ref[0] + imag * turn_ref[1])
        imags.append(imag * turn_ref[0] - real * turn_ref[1])
    lines = table_times(
        outer_ref,
        jnp.concatenate(
            [jnp.concatenate(reals, axis=1), jnp.concatenate(imags, axis=1)], axis=0
        ),
    )
    window = window_ref[...]
    low_half = iota((groups, LANES), 1) < HALF
    for part in range(2):
        for pair in range(pairs):
            lanes = slice(pair * LANES, (pair + 1) * LANES)
            begin = part * blocks
            even = lines[begin : begin + groups, lanes]
            odd = lines[begin + groups : begin + blocks, lanes]
            line_refs[2 * pair][pl.ds(part, groups, stride=2), :] = (
                jnp.where(low_half, even, swap_halves(odd)) * window
            )
            if 2 * pair + 1 < columns:
                line_refs[2 * pair + 1][pl.ds(part, groups, stride=2), :] = (
                    jnp.where(low_half, swap_halves(even), odd) * window
                )
    for column in range(columns):
        for group in range(groups):
            out_ref[column, :, group * LANES : (group + 1) * LANES] = line_refs[column][
                2 * group : 2 * group + 2, :
            ]


def kernel_call(kernel, name, out_shape, spaces, scratch, *operands, flops=0):
    return pl.pallas_call(
        kernel,
        out_shape=out_shape,
        in_specs=[pl.BlockSpec(memory_space=space) for space in spaces],
        out_specs=jax.tree.map(lambda _: pl.BlockSpec(memory_space=pltpu.VMEM), out_shape),
        scratch_shapes=scratch,
        compiler_params=pltpu.CompilerParams(vmem_limit_bytes=VMEM_LIMIT),
        cost_estimate=pl.CostEstimate(flops=flops, bytes_accessed=0, transcendentals=0)
        if flops
        else None,
        name=name,
    )(*operands)


def wide(rows):
    return pltpu.VMEM((rows, LANES), F32)


def local(groups, bands, strips, offsets, cells, values, weights, flags):
    columns, length = strips.shape[-2:]
    fronts = offsets.shape[0]
    share = columns // bands
    facets = groups * FACET_ROWS
    rows = facets * fronts * columns
    width = facets * fronts * share
    made = tables(length)
    plain, plain_places = made.pop("plain")
    paired, paired_places = made.pop("paired")
    made = {key: jnp.asarray(value) for key, value in made.items()}
    held = length // LANES * columns
    small = [cells[0, :, 0], values[0, :, 0], weights[0], flags[0]]
    large = [strips[0, 0], jnp.asarray(plain), jnp.asarray(paired)]

    def landing(arrays):
        return [pltpu.VMEM(array.shape, array.dtype) for array in arrays]

    def in_hbm(arrays):
        return [pltpu.with_memory_space_constraint(array, pltpu.HBM) for array in arrays]

    def semaphores(count):
        return pltpu.SemaphoreType.DMA((count,))

    early, packed = kernel_call(
        functools.partial(early_kernel, plain=plain_places, paired=paired_places), "early",
        [
            jax.ShapeDtypeStruct((rows, LANES), BF16),
            jax.ShapeDtypeStruct((PADDED_ROWS, cells.shape[-1]), F32),
        ],
        [pltpu.HBM] * 8,
        landing(small + [offsets] + large) + [wide(held)] * 2 + [semaphores(4), semaphores(4)],
        *in_hbm(small + [offsets] + large), flops=EARLY_FLOPS,
    )
    pieces = kernel_call(
        functools.partial(late_kernel, plain=plain_places, paired=paired_places), "late",
        jax.ShapeDtypeStruct((rows, LANES), BF16), [pltpu.VMEM] * 5, [wide(held)] * 2,
        early, offsets, *large, flops=LATE_FLOPS,
    )
    gathered = [packed]
    for step in range(1, groups):
        moves = [((group + step) % groups, group) for group in range(groups)]
        gathered.append(lax.ppermute(packed, "group", moves))
    arrived = lax.all_to_all(
        pieces, "member", split_axis=0, concat_axis=0, tiled=True,
        axis_index_groups=[list(SEND_ORDER)],
    )
    gathered, arrived = lax.optimization_barrier((gathered, arrived))
    blocks = length // CONTRIB
    value, weight, put, straight, crossed, places = kernel_call(
        functools.partial(prepare_kernel, columns=columns, share=share, blocks=blocks), "prepare",
        [jax.ShapeDtypeStruct((rows, LANES), F32)] * 2
        + [jax.ShapeDtypeStruct(((share + share % 2) * blocks, 2 * width), BF16)]
        + [jax.ShapeDtypeStruct((width, LANES), F32)] * 2
        + [jax.ShapeDtypeStruct((1, width), jnp.int32)],
        [pltpu.VMEM] * (2 + len(gathered)), [],
        offsets, made["shift"], *gathered, flops=PREPARE_FLOPS,
    )
    returned = kernel_call(
        functools.partial(subgrid_kernel, columns=columns, bands=bands), "subgrid",
        jax.ShapeDtypeStruct((rows, LANES), BF16), [pltpu.VMEM] * 6, [wide(rows)],
        arrived, value, weight, made["grid_turn"], made["model"], made["back"],
    )
    delivered = lax.all_to_all(
        returned, ("band", "member"), split_axis=0, concat_axis=0, tiled=True,
        axis_index_groups=[
            [b * FACET_ROWS + member for b, member in return_order(bands)]
        ],
    )
    lines = kernel_call(
        functools.partial(return_kernel, bands=bands), "lines",
        jax.ShapeDtypeStruct((share, 2, length), F32), [pltpu.VMEM] * 10,
        [wide(2 * length // LANES)] * share,
        places, delivered, straight, crossed, put, made["window"], made["turn"],
        made["partial"], made["inner_plus"], made["outer_plus"],
    )
    return lines[None]


def solution(mesh):
    bands = mesh.shape["band"]
    groups = mesh.shape["facet"] // FACET_ROWS
    split_mesh = Mesh(
        mesh.devices.reshape(groups, FACET_ROWS, bands), ("group", "member", "band")
    )
    facet = ("group", "member")
    placed = (
        P("band", facet, None, None, None),
        P(),
        P("band", None, facet, None, None),
        P("band", None, facet, None, None),
        P("band", None, facet, None),
        P("band", None, facet, None),
    )
    return jax.shard_map(
        functools.partial(local, groups, bands),
        mesh=split_mesh,
        in_specs=placed,
        out_specs=P(facet, "band", None, None),
        check_vma=False,
    )
```

```python
import functools
import math

import jax
import jax.numpy as jnp
import ml_dtypes
import numpy as np
from jax import lax
from jax.experimental import pallas as pl
from jax.experimental.pallas import tpu as pltpu
from jax.sharding import Mesh
from jax.sharding import PartitionSpec as P

CONTRIB = 64
FACET_ROWS = 8
SUBGRID = FACET_ROWS * CONTRIB
SEND_ORDER = (FACET_ROWS - 1, *range(FACET_ROWS - 1))
PLACE_ORDER = tuple(range(FACET_ROWS))
LANES = 128
HALF = LANES // 2
PADDED_ROWS = 40
EARLY_FLOPS = 10**10
LATE_FLOPS = 10**10
PREPARE_FLOPS = 2 * 10**10
VMEM_LIMIT = 48 * 1024 * 1024
F32 = jnp.float32
BF16 = jnp.bfloat16


def phases(rows, cols, length, rotation):
    product = np.outer(rows, cols) % length
    return np.exp(rotation * 2j * np.pi * product / length)


def from_left(matrix):
    return np.block([[matrix.real, -matrix.imag], [matrix.imag, matrix.real]])


def from_right(matrix):
    return np.block([[matrix.real, matrix.imag], [-matrix.imag, matrix.real]])


def high_low(table):
    high = table.astype(ml_dtypes.bfloat16)
    low = (table - high.astype(np.float64)).astype(ml_dtypes.bfloat16)
    return np.stack([high, low])


def side_by_side(values):
    straight = np.concatenate([values.real, values.real], axis=-1)
    crossed = np.concatenate([-values.imag, values.imag], axis=-1)
    return np.stack([straight, crossed])


def stack_tables(named):
    places, blocks, begin = {}, [], 0
    for name, table in named.items():
        count = table.shape[1] // LANES
        places[name] = (begin, table.shape[0], count)
        blocks += [table[:, i * LANES : (i + 1) * LANES] for i in range(count)]
        begin += table.shape[0] * count
    return np.concatenate(blocks, axis=0), places


def stack_pairs(named):
    return stack_tables(
        {(name, i): table for name, pair in named.items() for i, table in enumerate(pair)}
    )


def tables(length):
    blocks = length // CONTRIB
    short = np.arange(CONTRIB)
    outer = np.concatenate([np.arange(0, blocks, 2), np.arange(1, blocks, 2)])
    window = 1.0 + 0.5 * np.cos(np.arange(length) * (2.0 * math.pi / length))
    window = (window * length**-0.5).reshape(length // LANES, LANES).astype(np.float32)
    turn = np.tile(phases(short, short, length, -1), (1, 2))
    turn = np.stack([turn.real, turn.imag]).astype(np.float32)
    pair = np.eye(2)
    shift = high_low(np.concatenate(side_by_side(phases(short, short, CONTRIB, -1)), axis=1))
    outer_minus = from_left(phases(short, outer, blocks, -1))
    inner_minus = from_right(np.kron(pair, phases(short, short, CONTRIB, -1)))
    piece = from_right(phases(short, short, CONTRIB, 1)) * CONTRIB**-0.5
    return dict(
        plain=stack_tables(dict(window=window, real=turn[0], imag=turn[1])),
        paired=stack_pairs(
            dict(
                shift=shift,
                outer=high_low(outer_minus),
                inner=high_low(inner_minus),
                piece=high_low(piece),
            )
        ),
        window=window,
        turn=turn,
        shift=shift,
        inner_plus=high_low(from_right(np.kron(pair, phases(short, short, CONTRIB, 1)))),
        outer_plus=high_low(from_left(phases(outer, short, blocks, 1))),
        partial=high_low(from_right(phases(short, short, CONTRIB, -1)).T * CONTRIB**-0.5),
        grid_turn=side_by_side(phases(np.arange(FACET_ROWS), short, SUBGRID, -1)).astype(
            np.float32
        ),
        model=high_low(from_right(phases(short, short, CONTRIB, -1)) * SUBGRID**-0.5),
        back=high_low(from_right(phases(short, short, CONTRIB, 1)) * SUBGRID**-0.5),
    )


def return_order(bands):
    order = [(b, member) for b in range(bands) for member in PLACE_ORDER]
    return order[-1:] + order[:-1]


def split(values):
    high = values.astype(BF16)
    return high, (values - high.astype(F32)).astype(BF16)


def dot(left, right, dims=((1,), (0,))):
    return lax.dot_general(left, right, (dims, ((), ())), preferred_element_type=F32)


def dot_split(values, right):
    rows = values.shape[0]
    both = dot(jnp.concatenate(split(values), axis=0), right)
    return both[:rows] + both[rows:]


def times_table(values, table):
    return dot_split(values, table[0]) + dot(values.astype(BF16), table[1])


def table_times(table, values, dims=((1,), (0,))):
    high, low = split(values)
    rows = table[0].shape[0]
    both = dot(jnp.concatenate([table[0], table[1]], axis=0), high, dims)
    return both[:rows] + both[rows:] + dot(table[0], low, dims)


def iota(shape, dimension):
    return lax.broadcasted_iota(jnp.int32, shape, dimension)


def over(values, size):
    return lax.shift_right_logical(values, jnp.full_like(values, size.bit_length() - 1))


def within(values, size):
    return values & (size - 1)


def swap_halves(values):
    return pltpu.roll(values, HALF, 1)


def table_at(ref, place):
    begin, rows, blocks = place
    parts = [ref[begin + i * rows : begin + (i + 1) * rows, :] for i in range(blocks)]
    return parts[0] if blocks == 1 else jnp.concatenate(parts, axis=1)


def offsets_on_lanes(offsets_ref, columns, order):
    fronts, owners = offsets_ref.shape
    groups = owners // FACET_ROWS
    place = over(iota((1, fronts * owners * columns), 1), columns)
    front = within(place, fronts)
    group = within(over(place, fronts) + lax.axis_index("group"), groups)
    spot = over(place, fronts * groups)
    member = jnp.zeros_like(spot)
    for i, value in enumerate(order):
        member = jnp.where(spot == i, value, member)
    owner = group * FACET_ROWS + member
    pick = one_hot((owners, place.shape[1]), owner)
    offsets = offsets_ref[...]
    blocks = dot(over(offsets, CONTRIB).astype(F32).astype(BF16), pick)
    residues = dot(within(offsets, CONTRIB).astype(F32).astype(BF16), pick)
    spread = jnp.zeros_like(place, dtype=F32)
    for t in range(fronts):
        here = blocks[t : t + 1, :] * CONTRIB + residues[t : t + 1, :]
        spread = jnp.where(front == t, here, spread)
    return spread.astype(jnp.int32)


def shift_rows(residue, table):
    pick = jnp.where(iota((CONTRIB, residue.shape[1]), 0) == residue, 1.0, 0.0).T.astype(BF16)
    rows = dot(pick, table[0]) + dot(pick, table[1])
    return rows[:, :LANES], rows[:, LANES:]


def one_hot(shape, targets):
    return jnp.where(iota(shape, 0) == targets, 1.0, 0.0).astype(BF16)


def turned_eighths(values, rotation):
    sign = jnp.where(iota(values[0].shape, 1) < HALF, -rotation, rotation).astype(F32)

    def quarter_turn(value):
        return swap_halves(value) * sign

    def four(a, b, c, d):
        even_sum, even_diff = a + c, a - c
        odd_sum, odd_diff = b + d, quarter_turn(b - d)
        return even_sum + odd_sum, even_diff + odd_diff, even_sum - odd_sum, even_diff - odd_diff

    even = four(*values[0::2])
    odd = four(*values[1::2])
    root = math.sqrt(0.5)
    turned = (
        odd[0],
        (odd[1] + quarter_turn(odd[1])) * root,
        quarter_turn(odd[2]),
        (quarter_turn(odd[3]) - odd[3]) * root,
    )
    return [e + o for e, o in zip(even, turned)] + [e - o for e, o in zip(even, turned)]


def pack_samples(cells_ref, values_ref, weights_ref, flags_ref, out_ref):
    for t in range(cells_ref.shape[0]):
        rows = [
            cells_ref[t, 0:1, :].astype(F32) * SUBGRID + cells_ref[t, 1:2, :].astype(F32),
            weights_ref[t] * flags_ref[t].astype(F32),
            values_ref[t],
        ]
        out_ref[4 * t : 4 * t + 4, :] = jnp.concatenate(rows, axis=0)


def start_all(sources, targets, semaphores):
    copies = [
        pltpu.make_async_copy(source, target, semaphores.at[i])
        for i, (source, target) in enumerate(zip(sources, targets))
    ]
    for copy in copies:
        copy.start()
    return copies


def predict(spread, copies, strips_ref, plain_ref, paired_ref, held_refs, out_ref, plain, paired):
    columns, length = strips_ref.shape[1:]
    groups = length // LANES
    pairs = columns // 2
    blocks = length // CONTRIB
    width = spread.shape[1]
    first_block, residue = over(spread, CONTRIB), within(spread, CONTRIB)
    column = within(iota(spread.shape, 1), columns)
    kappa = iota((CONTRIB, width), 0)
    block = within(first_block + jnp.where(kappa < residue, 1, 0), blocks)
    source = within(column, 2) * blocks + block
    pair_of = over(column, 2)
    for copy in copies[:2]:
        copy.wait()

    def pair_at(name):
        return [table_at(paired_ref, paired[name, i]) for i in range(2)]

    window = table_at(plain_ref, plain["window"])
    turn_real, turn_imag = table_at(plain_ref, plain["real"]), table_at(plain_ref, plain["imag"])
    low_half = iota((groups, LANES), 1) < HALF
    sections = []
    for part, held in enumerate(held_refs):
        for group in range(groups):
            held[group * columns : (group + 1) * columns, :] = strips_ref[
                part, :, group * LANES : (group + 1) * LANES
            ]
        even, odd = [], []
        for pair in range(pairs):
            first = held[pl.ds(2 * pair, groups, stride=columns), :] * window
            second = held[pl.ds(2 * pair + 1, groups, stride=columns), :] * window
            even.append(jnp.where(low_half, first, swap_halves(second)))
            odd.append(jnp.where(low_half, swap_halves(first), second))
        sections += [jnp.concatenate(even, axis=1), jnp.concatenate(odd, axis=1)]
    for copy in copies[2:]:
        copy.wait()
    section = table_times(pair_at("outer"), jnp.concatenate(sections, axis=0))
    turned = []
    for pair in range(pairs):
        lanes = slice(pair * LANES, (pair + 1) * LANES)
        real, imag = section[:CONTRIB, lanes], section[CONTRIB:, lanes]
        turned.append(
            jnp.concatenate(
                [real * turn_real - imag * turn_imag, real * turn_imag + imag * turn_real],
                axis=1,
            )
        )
    inner = times_table(jnp.concatenate(turned, axis=0), pair_at("inner"))
    cutouts = []
    for part in range(2):
        tiles = []
        for tile in range(width // LANES):
            lanes = slice(tile * LANES, (tile + 1) * LANES)
            chosen = None
            for pair in range(pairs):
                rows = inner[pair * CONTRIB : (pair + 1) * CONTRIB, part * LANES : (part + 1) * LANES]
                found = jnp.take_along_axis(
                    rows, source[:, lanes], axis=1, mode="promise_in_bounds"
                )
                here = pair_of[:, lanes] == pair
                chosen = found if chosen is None else jnp.where(here, found, chosen)
            tiles.append(chosen)
        cutouts.append(jnp.concatenate(tiles, axis=1))
    cutout = jnp.concatenate(cutouts, axis=0)
    piece = times_table(cutout.T, pair_at("piece"))
    straight, crossed = shift_rows(residue, pair_at("shift"))
    out_ref[...] = (piece * straight + swap_halves(piece) * crossed).astype(BF16)


def in_first_half():
    return 2 * lax.axis_index("group") < lax.axis_size("group")


def early_kernel(
    cells, values, weights, flags, offsets, strips, plain_table, paired_table, out_ref, packed_ref,
    cells_ref, values_ref, weights_ref, flags_ref, offsets_ref, strips_ref, plain_ref, paired_ref,
    real_ref, imag_ref, small_semaphores, semaphores, *, plain, paired,
):
    small = start_all(
        (cells, values, weights, flags),
        (cells_ref, values_ref, weights_ref, flags_ref),
        small_semaphores,
    )

    def large():
        sources = (offsets, strips, plain_table, paired_table)
        targets = (offsets_ref, strips_ref, plain_ref, paired_ref)
        return [
            pltpu.make_async_copy(source, target, semaphores.at[i])
            for i, (source, target) in enumerate(zip(sources, targets))
        ]

    @pl.when(in_first_half())
    def _():
        for copy in large():
            copy.start()

    for copy in small:
        copy.wait()
    for t in range(cells_ref.shape[0]):
        rows = [
            cells_ref[t, 0:1, :].astype(F32) * SUBGRID + cells_ref[t, 1:2, :].astype(F32),
            weights_ref[t] * flags_ref[t].astype(F32),
            values_ref[t],
        ]
        packed_ref[4 * t : 4 * t + 4, :] = jnp.concatenate(rows, axis=0)

    @pl.when(in_first_half())
    def _():
        copies = large()
        copies[0].wait()
        predict(
            offsets_on_lanes(offsets_ref, strips_ref.shape[1], SEND_ORDER), copies[1:],
            strips_ref, plain_ref, paired_ref, (real_ref, imag_ref), out_ref, plain, paired,
        )


def late_kernel(
    early_ref, offsets_ref, strips_ref, plain_ref, paired_ref, out_ref, real_ref, imag_ref,
    *, plain, paired,
):
    @pl.when(in_first_half())
    def _():
        out_ref[...] = early_ref[...]

    @pl.when(jnp.logical_not(in_first_half()))
    def _():
        predict(
            offsets_on_lanes(offsets_ref, strips_ref.shape[1], SEND_ORDER), (),
            strips_ref, plain_ref, paired_ref, (real_ref, imag_ref), out_ref, plain, paired,
        )


def prepare_kernel(offsets_ref, shift_ref, *refs, columns, share, blocks):
    samples_refs, outs = refs[:-6], refs[-6:]
    value_ref, weight_ref, put_ref, straight_ref, crossed_ref, places_ref = outs
    fronts, samples = offsets_ref.shape[0], samples_refs[0].shape[1]
    own = lax.axis_index("group")
    depth = FACET_ROWS * columns
    for spot in range(len(samples_refs) * fronts):
        step, t = spot // fronts, spot % fronts
        sample = samples_refs[step][4 * t : 4 * t + 4, :]
        cell = sample[0:1, :].astype(jnp.int32)
        row, col = over(cell, SUBGRID) - own * columns, within(cell, SUBGRID)
        inside = (row >= 0) & (row < columns)
        target = jnp.where(inside, within(col, FACET_ROWS) * columns + row, -1)
        pick = one_hot((depth, samples), target)
        mask = iota((HALF, samples), 0) == over(col, FACET_ROWS)
        factor = sample[1:2, :]
        highs, lows = [], []
        for term in (factor * sample[2:3, :], factor * sample[3:4, :], factor):
            high = term.astype(BF16).astype(F32)
            highs.append(jnp.where(mask, high, 0.0).astype(BF16))
            lows.append(jnp.where(mask, term - high, 0.0).astype(BF16))
        highs, lows = highs + highs[2:], lows + lows[2:]
        grid = dot(pick, jnp.concatenate(highs, axis=0), ((1,), (1,))) + dot(
            pick, jnp.concatenate(lows, axis=0), ((1,), (1,))
        )
        rows = slice(spot * depth, (spot + 1) * depth)
        value_ref[rows, :] = grid[:, :LANES]
        weight_ref[rows, :] = grid[:, LANES:]
    spread = offsets_on_lanes(offsets_ref, share, PLACE_ORDER)
    places_ref[...] = spread
    first_block, residue = over(spread, CONTRIB), within(spread, CONTRIB)
    straight_ref[...], crossed_ref[...] = shift_rows(residue, shift_ref)
    base = within(iota(spread.shape, 1), share) * blocks
    targets = jnp.concatenate([base + first_block, base + within(first_block + 1, blocks)], axis=1)
    put_ref[...] = one_hot(put_ref.shape, targets)


def subgrid_kernel(
    pieces_ref, value_ref, weight_ref, turn_ref, model_ref, back_ref, out_ref, held_ref,
    *, columns, bands,
):
    rows = pieces_ref.shape[0] // FACET_ROWS
    spots = range(rows // columns)
    depth = FACET_ROWS * columns
    share = columns // bands
    pieces = pieces_ref[...].astype(F32)
    sky = turned_eighths(
        [
            pieces[spot * rows : (spot + 1) * rows, :]
            for spot in (SEND_ORDER.index(i) for i in range(FACET_ROWS))
        ],
        -1.0,
    )
    sky = [
        value * turn_ref[0, i : i + 1, :] + swap_halves(value) * turn_ref[1, i : i + 1, :]
        for i, value in enumerate(sky)
    ]
    stacked = jnp.concatenate(
        [value[spot * columns : (spot + 1) * columns, :] for spot in spots for value in sky],
        axis=0,
    )
    grid = value_ref[...] - weight_ref[...] * times_table(stacked, model_ref)
    back = times_table(grid, back_ref)
    lines = []
    for i in range(FACET_ROWS):
        value = jnp.concatenate(
            [
                back[spot * depth + i * columns : spot * depth + (i + 1) * columns, :]
                for spot in spots
            ],
            axis=0,
        )
        lines.append(
            value * turn_ref[0, i : i + 1, :] - swap_halves(value) * turn_ref[1, i : i + 1, :]
        )
    lines = turned_eighths(lines, 1.0)
    for i in range(FACET_ROWS):
        for spot in spots:
            for b in range(bands):
                source = spot * columns + b * share
                place = return_order(bands).index((b, i))
                target = (place * len(spots) + spot) * share
                held_ref[target : target + share, :] = lines[i][source : source + share, :]
    out_ref[...] = held_ref[...].astype(BF16)


def return_kernel(
    places_ref, pieces_ref, straight_ref, crossed_ref, put_ref, window_ref, turn_ref, partial_ref,
    inner_ref, outer_ref, out_ref, *line_refs, bands,
):
    columns, _, length = out_ref.shape
    blocks = length // CONTRIB
    groups = length // LANES
    pairs = (columns + 1) // 2
    width = pieces_ref.shape[0] // bands
    pieces = pieces_ref[...].astype(F32)
    order, rows = return_order(bands), width // FACET_ROWS

    def of_band(b):
        begins = [order.index((b, member)) * rows for member in PLACE_ORDER]
        return jnp.concatenate([pieces[begin : begin + rows, :] for begin in begins], axis=0)

    summed = of_band(0)
    for b in range(1, bands):
        summed += of_band(b)
    summed = summed * straight_ref[...] - swap_halves(summed) * crossed_ref[...]
    residues = table_times(partial_ref, summed, ((1,), (1,)))
    kappa = within(iota((2 * CONTRIB, width), 0), CONTRIB)
    inside = kappa >= within(places_ref[...], CONTRIB)
    both = jnp.concatenate(
        [jnp.where(inside, residues, 0.0), jnp.where(inside, 0.0, residues)], axis=1
    )
    put = put_ref[...]
    high, low = split(both)
    spectrum = dot(high, put, ((1,), (1,))) + dot(low, put, ((1,), (1,)))
    inner = times_table(
        jnp.concatenate(
            [
                jnp.concatenate(
                    [
                        spectrum[:CONTRIB, pair * LANES : (pair + 1) * LANES],
                        spectrum[CONTRIB:, pair * LANES : (pair + 1) * LANES],
                    ],
                    axis=1,
                )
                for pair in range(pairs)
            ],
            axis=0,
        ),
        inner_ref,
    )
    reals, imags = [], []
    for pair in range(pairs):
        rows = slice(pair * CONTRIB, (pair + 1) * CONTRIB)
        real, imag = inner[rows, :LANES], inner[rows, LANES:]
        reals.append(real * turn_ref[0] + imag * turn_ref[1])
        imags.append(imag * turn_ref[0] - real * turn_ref[1])
    lines = table_times(
        outer_ref,
        jnp.concatenate(
            [jnp.concatenate(reals, axis=1), jnp.concatenate(imags, axis=1)], axis=0
        ),
    )
    window = window_ref[...]
    low_half = iota((groups, LANES), 1) < HALF
    for part in range(2):
        for pair in range(pairs):
            lanes = slice(pair * LANES, (pair + 1) * LANES)
            begin = part * blocks
            even = lines[begin : begin + groups, lanes]
            odd = lines[begin + groups : begin + blocks, lanes]
            line_refs[2 * pair][pl.ds(part, groups, stride=2), :] = (
                jnp.where(low_half, even, swap_halves(odd)) * window
            )
            if 2 * pair + 1 < columns:
                line_refs[2 * pair + 1][pl.ds(part, groups, stride=2), :] = (
                    jnp.where(low_half, swap_halves(even), odd) * window
                )
    for column in range(columns):
        for group in range(groups):
            out_ref[column, :, group * LANES : (group + 1) * LANES] = line_refs[column][
                2 * group : 2 * group + 2, :
            ]


def kernel_call(kernel, name, out_shape, spaces, scratch, *operands, flops=0):
    return pl.pallas_call(
        kernel,
        out_shape=out_shape,
        in_specs=[pl.BlockSpec(memory_space=space) for space in spaces],
        out_specs=jax.tree.map(lambda _: pl.BlockSpec(memory_space=pltpu.VMEM), out_shape),
        scratch_shapes=scratch,
        compiler_params=pltpu.CompilerParams(vmem_limit_bytes=VMEM_LIMIT),
        cost_estimate=pl.CostEstimate(flops=flops, bytes_accessed=0, transcendentals=0)
        if flops
        else None,
        name=name,
    )(*operands)


def wide(rows):
    return pltpu.VMEM((rows, LANES), F32)


def local(groups, bands, strips, offsets, cells, values, weights, flags):
    columns, length = strips.shape[-2:]
    fronts = offsets.shape[0]
    share = columns // bands
    facets = groups * FACET_ROWS
    rows = facets * fronts * columns
    width = facets * fronts * share
    made = tables(length)
    plain, plain_places = made.pop("plain")
    paired, paired_places = made.pop("paired")
    made = {key: jnp.asarray(value) for key, value in made.items()}
    held = length // LANES * columns
    small = [cells[0, :, 0], values[0, :, 0], weights[0], flags[0]]
    large = [strips[0, 0], jnp.asarray(plain), jnp.asarray(paired)]

    def landing(arrays):
        return [pltpu.VMEM(array.shape, array.dtype) for array in arrays]

    def in_hbm(arrays):
        return [pltpu.with_memory_space_constraint(array, pltpu.HBM) for array in arrays]

    def semaphores(count):
        return pltpu.SemaphoreType.DMA((count,))

    early, packed = kernel_call(
        functools.partial(early_kernel, plain=plain_places, paired=paired_places), "early",
        [
            jax.ShapeDtypeStruct((rows, LANES), BF16),
            jax.ShapeDtypeStruct((PADDED_ROWS, cells.shape[-1]), F32),
        ],
        [pltpu.HBM] * 8,
        landing(small + [offsets] + large) + [wide(held)] * 2 + [semaphores(4), semaphores(4)],
        *in_hbm(small + [offsets] + large), flops=EARLY_FLOPS,
    )
    pieces = kernel_call(
        functools.partial(late_kernel, plain=plain_places, paired=paired_places), "late",
        jax.ShapeDtypeStruct((rows, LANES), BF16), [pltpu.VMEM] * 5, [wide(held)] * 2,
        early, offsets, *large, flops=LATE_FLOPS,
    )
    gathered = [packed]
    for step in range(1, groups):
        moves = [((group + step) % groups, group) for group in range(groups)]
        gathered.append(lax.ppermute(packed, "group", moves))
    arrived = lax.all_to_all(
        pieces, "member", split_axis=0, concat_axis=0, tiled=True,
        axis_index_groups=[list(SEND_ORDER)],
    )
    gathered, arrived = lax.optimization_barrier((gathered, arrived))
    blocks = length // CONTRIB
    value, weight, put, straight, crossed, places = kernel_call(
        functools.partial(prepare_kernel, columns=columns, share=share, blocks=blocks), "prepare",
        [jax.ShapeDtypeStruct((rows, LANES), F32)] * 2
        + [jax.ShapeDtypeStruct(((share + share % 2) * blocks, 2 * width), BF16)]
        + [jax.ShapeDtypeStruct((width, LANES), F32)] * 2
        + [jax.ShapeDtypeStruct((1, width), jnp.int32)],
        [pltpu.VMEM] * (2 + len(gathered)), [],
        offsets, made["shift"], *gathered, flops=PREPARE_FLOPS,
    )
    returned = kernel_call(
        functools.partial(subgrid_kernel, columns=columns, bands=bands), "subgrid",
        jax.ShapeDtypeStruct((rows, LANES), BF16), [pltpu.VMEM] * 6, [wide(rows)],
        arrived, value, weight, made["grid_turn"], made["model"], made["back"],
    )
    delivered = lax.all_to_all(
        returned, ("band", "member"), split_axis=0, concat_axis=0, tiled=True,
        axis_index_groups=[
            [b * FACET_ROWS + member for b, member in return_order(bands)]
        ],
    )
    lines = kernel_call(
        functools.partial(return_kernel, bands=bands), "lines",
        jax.ShapeDtypeStruct((share, 2, length), F32), [pltpu.VMEM] * 10,
        [wide(2 * length // LANES)] * share,
        places, delivered, straight, crossed, put, made["window"], made["turn"],
        made["partial"], made["inner_plus"], made["outer_plus"],
    )
    return lines[None]


def solution(mesh):
    bands = mesh.shape["band"]
    groups = mesh.shape["facet"] // FACET_ROWS
    split_mesh = Mesh(
        mesh.devices.reshape(groups, FACET_ROWS, bands), ("group", "member", "band")
    )
    facet = ("group", "member")
    placed = (
        P("band", facet, None, None, None),
        P(),
        P("band", None, facet, None, None),
        P("band", None, facet, None, None),
        P("band", None, facet, None),
        P("band", None, facet, None),
    )
    return jax.shard_map(
        functools.partial(local, groups, bands),
        mesh=split_mesh,
        in_specs=placed,
        out_specs=P(facet, "band", None, None),
        check_vma=False,
    )
```

```python
import functools
import math

import jax
import jax.numpy as jnp
import ml_dtypes
import numpy as np
from jax import lax
from jax.experimental import pallas as pl
from jax.experimental.pallas import tpu as pltpu
from jax.sharding import Mesh
from jax.sharding import PartitionSpec as P

CONTRIB = 64
FACET_ROWS = 8
SUBGRID = FACET_ROWS * CONTRIB
SEND_ORDER = (FACET_ROWS - 2, *range(FACET_ROWS - 2), FACET_ROWS - 1)
PLACE_ORDER = tuple(range(FACET_ROWS))
LANES = 128
HALF = LANES // 2
EARLY_FLOPS = 10**10
LATE_FLOPS = 10**10
PREPARE_FLOPS = 2 * 10**10
VMEM_LIMIT = 48 * 1024 * 1024
F32 = jnp.float32
BF16 = jnp.bfloat16


def phases(rows, cols, length, rotation):
    product = np.outer(rows, cols) % length
    return np.exp(rotation * 2j * np.pi * product / length)


def from_left(matrix):
    return np.block([[matrix.real, -matrix.imag], [matrix.imag, matrix.real]])


def from_right(matrix):
    return np.block([[matrix.real, matrix.imag], [-matrix.imag, matrix.real]])


def high_low(table):
    high = table.astype(ml_dtypes.bfloat16)
    low = (table - high.astype(np.float64)).astype(ml_dtypes.bfloat16)
    return np.stack([high, low])


def side_by_side(values):
    straight = np.concatenate([values.real, values.real], axis=-1)
    crossed = np.concatenate([-values.imag, values.imag], axis=-1)
    return np.stack([straight, crossed])


def stack_tables(named):
    places, blocks, begin = {}, [], 0
    for name, table in named.items():
        count = table.shape[1] // LANES
        places[name] = (begin, table.shape[0], count)
        blocks += [table[:, i * LANES : (i + 1) * LANES] for i in range(count)]
        begin += table.shape[0] * count
    return np.concatenate(blocks, axis=0), places


def stack_pairs(named):
    return stack_tables(
        {(name, i): table for name, pair in named.items() for i, table in enumerate(pair)}
    )


def tables(length):
    blocks = length // CONTRIB
    short = np.arange(CONTRIB)
    outer = np.concatenate([np.arange(0, blocks, 2), np.arange(1, blocks, 2)])
    window = 1.0 + 0.5 * np.cos(np.arange(length) * (2.0 * math.pi / length))
    window = (window * length**-0.5).reshape(length // LANES, LANES).astype(np.float32)
    turn = np.tile(phases(short, short, length, -1), (1, 2))
    turn = np.stack([turn.real, turn.imag]).astype(np.float32)
    pair = np.eye(2)
    shift = high_low(np.concatenate(side_by_side(phases(short, short, CONTRIB, -1)), axis=1))
    outer_minus = from_left(phases(short, outer, blocks, -1))
    inner_minus = from_right(np.kron(pair, phases(short, short, CONTRIB, -1)))
    piece = from_right(phases(short, short, CONTRIB, 1)) * CONTRIB**-0.5
    return dict(
        plain=stack_tables(dict(window=window, real=turn[0], imag=turn[1])),
        paired=stack_pairs(
            dict(
                shift=shift,
                outer=high_low(outer_minus),
                inner=high_low(inner_minus),
                piece=high_low(piece),
            )
        ),
        window=window,
        turn=turn,
        shift=shift,
        inner_plus=high_low(from_right(np.kron(pair, phases(short, short, CONTRIB, 1)))),
        outer_plus=high_low(from_left(phases(outer, short, blocks, 1))),
        partial=high_low(from_right(phases(short, short, CONTRIB, -1)).T * CONTRIB**-0.5),
        grid_turn=side_by_side(phases(np.arange(FACET_ROWS), short, SUBGRID, -1)).astype(
            np.float32
        ),
        model=high_low(from_right(phases(short, short, CONTRIB, -1)) * SUBGRID**-0.5),
        back=high_low(from_right(phases(short, short, CONTRIB, 1)) * SUBGRID**-0.5),
    )


def return_order(bands):
    order = [(b, member) for b in range(bands) for member in PLACE_ORDER]
    return order[-2:-1] + order[:-2] + order[-1:]


def split(values):
    high = values.astype(BF16)
    return high, (values - high.astype(F32)).astype(BF16)


def dot(left, right, dims=((1,), (0,))):
    return lax.dot_general(left, right, (dims, ((), ())), preferred_element_type=F32)


def dot_split(values, right):
    rows = values.shape[0]
    both = dot(jnp.concatenate(split(values), axis=0), right)
    return both[:rows] + both[rows:]


def times_table(values, table):
    return dot_split(values, table[0]) + dot(values.astype(BF16), table[1])


def table_times(table, values, dims=((1,), (0,))):
    high, low = split(values)
    rows = table[0].shape[0]
    both = dot(jnp.concatenate([table[0], table[1]], axis=0), high, dims)
    return both[:rows] + both[rows:] + dot(table[0], low, dims)


def iota(shape, dimension):
    return lax.broadcasted_iota(jnp.int32, shape, dimension)


def over(values, size):
    return lax.shift_right_logical(values, jnp.full_like(values, size.bit_length() - 1))


def within(values, size):
    return values & (size - 1)


def swap_halves(values):
    return pltpu.roll(values, HALF, 1)


def table_at(ref, place):
    begin, rows, blocks = place
    parts = [ref[begin + i * rows : begin + (i + 1) * rows, :] for i in range(blocks)]
    return parts[0] if blocks == 1 else jnp.concatenate(parts, axis=1)


def offsets_on_lanes(offsets_ref, columns, order):
    fronts, owners = offsets_ref.shape
    groups = owners // FACET_ROWS
    place = over(iota((1, fronts * owners * columns), 1), columns)
    front = within(place, fronts)
    group = within(over(place, fronts) + lax.axis_index("group"), groups)
    spot = over(place, fronts * groups)
    member = jnp.zeros_like(spot)
    for i, value in enumerate(order):
        member = jnp.where(spot == i, value, member)
    owner = group * FACET_ROWS + member
    pick = one_hot((owners, place.shape[1]), owner)
    offsets = offsets_ref[...]
    blocks = dot(over(offsets, CONTRIB).astype(F32).astype(BF16), pick)
    residues = dot(within(offsets, CONTRIB).astype(F32).astype(BF16), pick)
    spread = jnp.zeros_like(place, dtype=F32)
    for t in range(fronts):
        here = blocks[t : t + 1, :] * CONTRIB + residues[t : t + 1, :]
        spread = jnp.where(front == t, here, spread)
    return spread.astype(jnp.int32)


def shift_rows(residue, table):
    pick = jnp.where(iota((CONTRIB, residue.shape[1]), 0) == residue, 1.0, 0.0).T.astype(BF16)
    rows = dot(pick, table[0]) + dot(pick, table[1])
    return rows[:, :LANES], rows[:, LANES:]


def one_hot(shape, targets):
    return jnp.where(iota(shape, 0) == targets, 1.0, 0.0).astype(BF16)


def turned_eighths(values, rotation):
    sign = jnp.where(iota(values[0].shape, 1) < HALF, -rotation, rotation).astype(F32)

    def quarter_turn(value):
        return swap_halves(value) * sign

    def four(a, b, c, d):
        even_sum, even_diff = a + c, a - c
        odd_sum, odd_diff = b + d, quarter_turn(b - d)
        return even_sum + odd_sum, even_diff + odd_diff, even_sum - odd_sum, even_diff - odd_diff

    even = four(*values[0::2])
    odd = four(*values[1::2])
    root = math.sqrt(0.5)
    turned = (
        odd[0],
        (odd[1] + quarter_turn(odd[1])) * root,
        quarter_turn(odd[2]),
        (quarter_turn(odd[3]) - odd[3]) * root,
    )
    return [e + o for e, o in zip(even, turned)] + [e - o for e, o in zip(even, turned)]


def pack_samples(cells_ref, values_ref, weights_ref, flags_ref, out_ref):
    for t in range(cells_ref.shape[0]):
        rows = [
            cells_ref[t, 0:1, :].astype(F32) * SUBGRID + cells_ref[t, 1:2, :].astype(F32),
            weights_ref[t] * flags_ref[t].astype(F32),
            values_ref[t],
        ]
        out_ref[4 * t : 4 * t + 4, :] = jnp.concatenate(rows, axis=0)


def start_all(sources, targets, semaphores):
    copies = [
        pltpu.make_async_copy(source, target, semaphores.at[i])
        for i, (source, target) in enumerate(zip(sources, targets))
    ]
    for copy in copies:
        copy.start()
    return copies


def predict(spread, copies, strips_ref, plain_ref, paired_ref, held_refs, out_ref, plain, paired):
    columns, length = strips_ref.shape[1:]
    groups = length // LANES
    pairs = columns // 2
    blocks = length // CONTRIB
    width = spread.shape[1]
    first_block, residue = over(spread, CONTRIB), within(spread, CONTRIB)
    column = within(iota(spread.shape, 1), columns)
    kappa = iota((CONTRIB, width), 0)
    block = within(first_block + jnp.where(kappa < residue, 1, 0), blocks)
    source = within(column, 2) * blocks + block
    pair_of = over(column, 2)
    for copy in copies[:2]:
        copy.wait()

    def pair_at(name):
        return [table_at(paired_ref, paired[name, i]) for i in range(2)]

    window = table_at(plain_ref, plain["window"])
    turn_real, turn_imag = table_at(plain_ref, plain["real"]), table_at(plain_ref, plain["imag"])
    low_half = iota((groups, LANES), 1) < HALF
    sections = []
    for part, held in enumerate(held_refs):
        for group in range(groups):
            held[group * columns : (group + 1) * columns, :] = strips_ref[
                part, :, group * LANES : (group + 1) * LANES
            ]
        even, odd = [], []
        for pair in range(pairs):
            first = held[pl.ds(2 * pair, groups, stride=columns), :] * window
            second = held[pl.ds(2 * pair + 1, groups, stride=columns), :] * window
            even.append(jnp.where(low_half, first, swap_halves(second)))
            odd.append(jnp.where(low_half, swap_halves(first), second))
        sections += [jnp.concatenate(even, axis=1), jnp.concatenate(odd, axis=1)]
    for copy in copies[2:]:
        copy.wait()
    section = table_times(pair_at("outer"), jnp.concatenate(sections, axis=0))
    turned = []
    for pair in range(pairs):
        lanes = slice(pair * LANES, (pair + 1) * LANES)
        real, imag = section[:CONTRIB, lanes], section[CONTRIB:, lanes]
        turned.append(
            jnp.concatenate(
                [real * turn_real - imag * turn_imag, real * turn_imag + imag * turn_real],
                axis=1,
            )
        )
    inner = times_table(jnp.concatenate(turned, axis=0), pair_at("inner"))
    cutouts = []
    for part in range(2):
        tiles = []
        for tile in range(width // LANES):
            lanes = slice(tile * LANES, (tile + 1) * LANES)
            chosen = None
            for pair in range(pairs):
                rows = inner[pair * CONTRIB : (pair + 1) * CONTRIB, part * LANES : (part + 1) * LANES]
                found = jnp.take_along_axis(
                    rows, source[:, lanes], axis=1, mode="promise_in_bounds"
                )
                here = pair_of[:, lanes] == pair
                chosen = found if chosen is None else jnp.where(here, found, chosen)
            tiles.append(chosen)
        cutouts.append(jnp.concatenate(tiles, axis=1))
    cutout = jnp.concatenate(cutouts, axis=0)
    piece = times_table(cutout.T, pair_at("piece"))
    straight, crossed = shift_rows(residue, pair_at("shift"))
    out_ref[...] = (piece * straight + swap_halves(piece) * crossed).astype(BF16)


def in_first_half():
    return 2 * lax.axis_index("group") < lax.axis_size("group")


def early_kernel(
    cells, values, weights, flags, offsets, strips, plain_table, paired_table, out_ref, packed_ref,
    cells_ref, values_ref, weights_ref, flags_ref, offsets_ref, strips_ref, plain_ref, paired_ref,
    real_ref, imag_ref, small_semaphores, semaphores, *, plain, paired,
):
    small = start_all(
        (cells, values, weights, flags),
        (cells_ref, values_ref, weights_ref, flags_ref),
        small_semaphores,
    )

    def large():
        sources = (offsets, strips, plain_table, paired_table)
        targets = (offsets_ref, strips_ref, plain_ref, paired_ref)
        return [
            pltpu.make_async_copy(source, target, semaphores.at[i])
            for i, (source, target) in enumerate(zip(sources, targets))
        ]

    @pl.when(in_first_half())
    def _():
        for copy in large():
            copy.start()

    for copy in small:
        copy.wait()
    for t in range(cells_ref.shape[0]):
        rows = [
            cells_ref[t, 0:1, :].astype(F32) * SUBGRID + cells_ref[t, 1:2, :].astype(F32),
            weights_ref[t] * flags_ref[t].astype(F32),
            values_ref[t],
        ]
        packed_ref[4 * t : 4 * t + 4, :] = jnp.concatenate(rows, axis=0)

    @pl.when(in_first_half())
    def _():
        copies = large()
        copies[0].wait()
        predict(
            offsets_on_lanes(offsets_ref, strips_ref.shape[1], SEND_ORDER), copies[1:],
            strips_ref, plain_ref, paired_ref, (real_ref, imag_ref), out_ref, plain, paired,
        )


def late_kernel(
    early_ref, offsets_ref, strips_ref, plain_ref, paired_ref, out_ref, pieces_ref, real_ref,
    imag_ref, semaphore, *, plain, paired,
):
    @pl.when(jnp.logical_not(in_first_half()))
    def _():
        predict(
            offsets_on_lanes(offsets_ref, strips_ref.shape[1], SEND_ORDER), (),
            strips_ref, plain_ref, paired_ref, (real_ref, imag_ref), pieces_ref, plain, paired,
        )
        copy = pltpu.make_async_copy(pieces_ref, out_ref, semaphore)
        copy.start()
        copy.wait()


def prepare_kernel(offsets_ref, shift_ref, *refs, columns, share, blocks):
    samples_refs, outs = refs[:-6], refs[-6:]
    value_ref, weight_ref, put_ref, straight_ref, crossed_ref, places_ref = outs
    fronts, samples = samples_refs[0].shape[0] // 4, samples_refs[0].shape[1]
    own = lax.axis_index("group")
    depth = FACET_ROWS * columns
    for spot in range(len(samples_refs) * fronts):
        step, t = spot // fronts, spot % fronts
        sample = samples_refs[step][4 * t : 4 * t + 4, :]
        cell = sample[0:1, :].astype(jnp.int32)
        row, col = over(cell, SUBGRID) - own * columns, within(cell, SUBGRID)
        inside = (row >= 0) & (row < columns)
        target = jnp.where(inside, within(col, FACET_ROWS) * columns + row, -1)
        pick = one_hot((depth, samples), target)
        mask = iota((HALF, samples), 0) == over(col, FACET_ROWS)
        factor = sample[1:2, :]
        highs, lows = [], []
        for term in (factor * sample[2:3, :], factor * sample[3:4, :], factor):
            high = term.astype(BF16).astype(F32)
            highs.append(jnp.where(mask, high, 0.0).astype(BF16))
            lows.append(jnp.where(mask, term - high, 0.0).astype(BF16))
        highs, lows = highs + highs[2:], lows + lows[2:]
        grid = dot(pick, jnp.concatenate(highs, axis=0), ((1,), (1,))) + dot(
            pick, jnp.concatenate(lows, axis=0), ((1,), (1,))
        )
        rows = slice(spot * depth, (spot + 1) * depth)
        value_ref[rows, :] = grid[:, :LANES]
        weight_ref[rows, :] = grid[:, LANES:]
    spread = offsets_on_lanes(offsets_ref, share, PLACE_ORDER)
    places_ref[...] = spread
    first_block, residue = over(spread, CONTRIB), within(spread, CONTRIB)
    straight_ref[...], crossed_ref[...] = shift_rows(residue, shift_ref)
    base = within(iota(spread.shape, 1), share) * blocks
    targets = jnp.concatenate([base + first_block, base + within(first_block + 1, blocks)], axis=1)
    put_ref[...] = one_hot(put_ref.shape, targets)


def subgrid_kernel(
    pieces_ref, value_ref, weight_ref, turn_ref, model_ref, back_ref, out_ref, held_ref,
    *, columns, bands,
):
    rows = pieces_ref.shape[0] // FACET_ROWS
    spots = range(rows // columns)
    depth = FACET_ROWS * columns
    share = columns // bands
    pieces = pieces_ref[...].astype(F32)
    sky = turned_eighths(
        [
            pieces[spot * rows : (spot + 1) * rows, :]
            for spot in (SEND_ORDER.index(i) for i in range(FACET_ROWS))
        ],
        -1.0,
    )
    sky = [
        value * turn_ref[0, i : i + 1, :] + swap_halves(value) * turn_ref[1, i : i + 1, :]
        for i, value in enumerate(sky)
    ]
    stacked = jnp.concatenate(
        [value[spot * columns : (spot + 1) * columns, :] for spot in spots for value in sky],
        axis=0,
    )
    grid = value_ref[...] - weight_ref[...] * times_table(stacked, model_ref)
    back = times_table(grid, back_ref)
    lines = []
    for i in range(FACET_ROWS):
        value = jnp.concatenate(
            [
                back[spot * depth + i * columns : spot * depth + (i + 1) * columns, :]
                for spot in spots
            ],
            axis=0,
        )
        lines.append(
            value * turn_ref[0, i : i + 1, :] - swap_halves(value) * turn_ref[1, i : i + 1, :]
        )
    lines = turned_eighths(lines, 1.0)
    for i in range(FACET_ROWS):
        for spot in spots:
            for b in range(bands):
                source = spot * columns + b * share
                place = return_order(bands).index((b, i))
                target = (place * len(spots) + spot) * share
                held_ref[target : target + share, :] = lines[i][source : source + share, :]
    out_ref[...] = held_ref[...].astype(BF16)


def return_kernel(
    places_ref, pieces_ref, straight_ref, crossed_ref, put_ref, window_ref, turn_ref, partial_ref,
    inner_ref, outer_ref, out_ref, *line_refs, bands,
):
    columns, _, length = out_ref.shape
    blocks = length // CONTRIB
    groups = length // LANES
    pairs = (columns + 1) // 2
    width = pieces_ref.shape[0] // bands
    pieces = pieces_ref[...].astype(F32)
    order, rows = return_order(bands), width // FACET_ROWS

    def of_band(b):
        begins = [order.index((b, member)) * rows for member in PLACE_ORDER]
        return jnp.concatenate([pieces[begin : begin + rows, :] for begin in begins], axis=0)

    summed = of_band(0)
    for b in range(1, bands):
        summed += of_band(b)
    summed = summed * straight_ref[...] - swap_halves(summed) * crossed_ref[...]
    residues = table_times(partial_ref, summed, ((1,), (1,)))
    kappa = within(iota((2 * CONTRIB, width), 0), CONTRIB)
    inside = kappa >= within(places_ref[...], CONTRIB)
    both = jnp.concatenate(
        [jnp.where(inside, residues, 0.0), jnp.where(inside, 0.0, residues)], axis=1
    )
    put = put_ref[...]
    high, low = split(both)
    spectrum = dot(high, put, ((1,), (1,))) + dot(low, put, ((1,), (1,)))
    inner = times_table(
        jnp.concatenate(
            [
                jnp.concatenate(
                    [
                        spectrum[:CONTRIB, pair * LANES : (pair + 1) * LANES],
                        spectrum[CONTRIB:, pair * LANES : (pair + 1) * LANES],
                    ],
                    axis=1,
                )
                for pair in range(pairs)
            ],
            axis=0,
        ),
        inner_ref,
    )
    reals, imags = [], []
    for pair in range(pairs):
        rows = slice(pair * CONTRIB, (pair + 1) * CONTRIB)
        real, imag = inner[rows, :LANES], inner[rows, LANES:]
        reals.append(real * turn_ref[0] + imag * turn_ref[1])
        imags.append(imag * turn_ref[0] - real * turn_ref[1])
    lines = table_times(
        outer_ref,
        jnp.concatenate(
            [jnp.concatenate(reals, axis=1), jnp.concatenate(imags, axis=1)], axis=0
        ),
    )
    window = window_ref[...]
    low_half = iota((groups, LANES), 1) < HALF
    for part in range(2):
        for pair in range(pairs):
            lanes = slice(pair * LANES, (pair + 1) * LANES)
            begin = part * blocks
            even = lines[begin : begin + groups, lanes]
            odd = lines[begin + groups : begin + blocks, lanes]
            line_refs[2 * pair][pl.ds(part, groups, stride=2), :] = (
                jnp.where(low_half, even, swap_halves(odd)) * window
            )
            if 2 * pair + 1 < columns:
                line_refs[2 * pair + 1][pl.ds(part, groups, stride=2), :] = (
                    jnp.where(low_half, swap_halves(even), odd) * window
                )
    for column in range(columns):
        for group in range(groups):
            out_ref[column, :, group * LANES : (group + 1) * LANES] = line_refs[column][
                2 * group : 2 * group + 2, :
            ]


def kernel_call(
    kernel, name, out_shape, spaces, scratch, *operands, flops=0, out_space=pltpu.VMEM, aliases={}
):
    return pl.pallas_call(
        kernel,
        out_shape=out_shape,
        in_specs=[pl.BlockSpec(memory_space=space) for space in spaces],
        out_specs=jax.tree.map(lambda _: pl.BlockSpec(memory_space=out_space), out_shape),
        input_output_aliases=aliases,
        scratch_shapes=scratch,
        compiler_params=pltpu.CompilerParams(vmem_limit_bytes=VMEM_LIMIT),
        cost_estimate=pl.CostEstimate(flops=flops, bytes_accessed=0, transcendentals=0)
        if flops
        else None,
        name=name,
    )(*operands)


def wide(rows):
    return pltpu.VMEM((rows, LANES), F32)


def local(groups, bands, strips, offsets, cells, values, weights, flags):
    columns, length = strips.shape[-2:]
    fronts = offsets.shape[0]
    share = columns // bands
    facets = groups * FACET_ROWS
    rows = facets * fronts * columns
    width = facets * fronts * share
    made = tables(length)
    plain, plain_places = made.pop("plain")
    paired, paired_places = made.pop("paired")
    made = {key: jnp.asarray(value) for key, value in made.items()}
    held = length // LANES * columns
    small = [cells[0, :, 0], values[0, :, 0], weights[0], flags[0]]
    large = [strips[0, 0], jnp.asarray(plain), jnp.asarray(paired)]

    def landing(arrays):
        return [pltpu.VMEM(array.shape, array.dtype) for array in arrays]

    def in_hbm(arrays):
        return [pltpu.with_memory_space_constraint(array, pltpu.HBM) for array in arrays]

    def semaphores(count):
        return pltpu.SemaphoreType.DMA((count,))

    early, packed = kernel_call(
        functools.partial(early_kernel, plain=plain_places, paired=paired_places), "early",
        [
            jax.ShapeDtypeStruct((rows, LANES), BF16),
            jax.ShapeDtypeStruct((4 * fronts, cells.shape[-1]), F32),
        ],
        [pltpu.HBM] * 8,
        landing(small + [offsets] + large) + [wide(held)] * 2 + [semaphores(4), semaphores(4)],
        *in_hbm(small + [offsets] + large), flops=EARLY_FLOPS,
    )
    pieces = kernel_call(
        functools.partial(late_kernel, plain=plain_places, paired=paired_places), "late",
        jax.ShapeDtypeStruct((rows, LANES), BF16), [pltpu.HBM] + [pltpu.VMEM] * 4,
        [pltpu.VMEM((rows, LANES), BF16)] + [wide(held)] * 2 + [pltpu.SemaphoreType.DMA],
        early, offsets, *large, flops=LATE_FLOPS, out_space=pltpu.HBM, aliases={0: 0},
    )
    gathered = [packed]
    for step in range(1, groups):
        moves = [((group + step) % groups, group) for group in range(groups)]
        gathered.append(lax.ppermute(packed, "group", moves))
    arrived = lax.all_to_all(
        pieces, "member", split_axis=0, concat_axis=0, tiled=True,
        axis_index_groups=[list(SEND_ORDER)],
    )
    blocks = length // CONTRIB
    value, weight, put, straight, crossed, places = kernel_call(
        functools.partial(prepare_kernel, columns=columns, share=share, blocks=blocks), "prepare",
        [jax.ShapeDtypeStruct((rows, LANES), F32)] * 2
        + [jax.ShapeDtypeStruct(((share + share % 2) * blocks, 2 * width), BF16)]
        + [jax.ShapeDtypeStruct((width, LANES), F32)] * 2
        + [jax.ShapeDtypeStruct((1, width), jnp.int32)],
        [pltpu.VMEM] * (2 + len(gathered)), [],
        offsets, made["shift"], *gathered, flops=PREPARE_FLOPS,
    )
    returned = kernel_call(
        functools.partial(subgrid_kernel, columns=columns, bands=bands), "subgrid",
        jax.ShapeDtypeStruct((rows, LANES), BF16), [pltpu.VMEM] * 6, [wide(rows)],
        arrived, value, weight, made["grid_turn"], made["model"], made["back"],
    )
    delivered = lax.all_to_all(
        returned, ("band", "member"), split_axis=0, concat_axis=0, tiled=True,
        axis_index_groups=[
            [b * FACET_ROWS + member for b, member in return_order(bands)]
        ],
    )
    lines = kernel_call(
        functools.partial(return_kernel, bands=bands), "lines",
        jax.ShapeDtypeStruct((share, 2, length), F32), [pltpu.VMEM] * 10,
        [wide(2 * length // LANES)] * share,
        places, delivered, straight, crossed, put, made["window"], made["turn"],
        made["partial"], made["inner_plus"], made["outer_plus"],
    )
    return lines[None]


def solution(mesh):
    bands = mesh.shape["band"]
    groups = mesh.shape["facet"] // FACET_ROWS
    split_mesh = Mesh(
        mesh.devices.reshape(groups, FACET_ROWS, bands), ("group", "member", "band")
    )
    facet = ("group", "member")
    placed = (
        P("band", facet, None, None, None),
        P(),
        P("band", None, facet, None, None),
        P("band", None, facet, None, None),
        P("band", None, facet, None),
        P("band", None, facet, None),
    )
    return jax.shard_map(
        functools.partial(local, groups, bands),
        mesh=split_mesh,
        in_specs=placed,
        out_specs=P(facet, "band", None, None),
        check_vma=False,
    )
```

```python
import functools
import math

import jax
import jax.numpy as jnp
import ml_dtypes
import numpy as np
from jax import lax
from jax.experimental import pallas as pl
from jax.experimental.pallas import tpu as pltpu
from jax.sharding import Mesh
from jax.sharding import PartitionSpec as P

CONTRIB = 64
FACET_ROWS = 8
SUBGRID = FACET_ROWS * CONTRIB
SEND_ORDER = (FACET_ROWS - 1, *range(FACET_ROWS - 1))
PLACE_ORDER = tuple(range(FACET_ROWS))
LANES = 128
HALF = LANES // 2
EARLY_FLOPS = 10**10
LATE_FLOPS = 10**10
PREPARE_FLOPS = 2 * 10**10
VMEM_LIMIT = 48 * 1024 * 1024
F32 = jnp.float32
BF16 = jnp.bfloat16


def phases(rows, cols, length, rotation):
    product = np.outer(rows, cols) % length
    return np.exp(rotation * 2j * np.pi * product / length)


def from_left(matrix):
    return np.block([[matrix.real, -matrix.imag], [matrix.imag, matrix.real]])


def from_right(matrix):
    return np.block([[matrix.real, matrix.imag], [-matrix.imag, matrix.real]])


def high_low(table):
    high = table.astype(ml_dtypes.bfloat16)
    low = (table - high.astype(np.float64)).astype(ml_dtypes.bfloat16)
    return np.stack([high, low])


def side_by_side(values):
    straight = np.concatenate([values.real, values.real], axis=-1)
    crossed = np.concatenate([-values.imag, values.imag], axis=-1)
    return np.stack([straight, crossed])


def stack_tables(named):
    places, blocks, begin = {}, [], 0
    for name, table in named.items():
        count = table.shape[1] // LANES
        places[name] = (begin, table.shape[0], count)
        blocks += [table[:, i * LANES : (i + 1) * LANES] for i in range(count)]
        begin += table.shape[0] * count
    return np.concatenate(blocks, axis=0), places


def stack_pairs(named):
    return stack_tables(
        {(name, i): table for name, pair in named.items() for i, table in enumerate(pair)}
    )


def tables(length):
    blocks = length // CONTRIB
    short = np.arange(CONTRIB)
    outer = np.concatenate([np.arange(0, blocks, 2), np.arange(1, blocks, 2)])
    window = 1.0 + 0.5 * np.cos(np.arange(length) * (2.0 * math.pi / length))
    window = (window * length**-0.5).reshape(length // LANES, LANES).astype(np.float32)
    turn = np.tile(phases(short, short, length, -1), (1, 2))
    turn = np.stack([turn.real, turn.imag]).astype(np.float32)
    pair = np.eye(2)
    shift = high_low(np.concatenate(side_by_side(phases(short, short, CONTRIB, -1)), axis=1))
    outer_minus = from_left(phases(short, outer, blocks, -1))
    inner_minus = from_right(np.kron(pair, phases(short, short, CONTRIB, -1)))
    piece = from_right(phases(short, short, CONTRIB, 1)) * CONTRIB**-0.5
    return dict(
        plain=stack_tables(dict(window=window, real=turn[0], imag=turn[1])),
        paired=stack_pairs(
            dict(
                shift=shift,
                outer=high_low(outer_minus),
                inner=high_low(inner_minus),
                piece=high_low(piece),
            )
        ),
        window=window,
        turn=turn,
        shift=shift,
        inner_plus=high_low(from_right(np.kron(pair, phases(short, short, CONTRIB, 1)))),
        outer_plus=high_low(from_left(phases(outer, short, blocks, 1))),
        partial=high_low(from_right(phases(short, short, CONTRIB, -1)).T * CONTRIB**-0.5),
        grid_turn=side_by_side(phases(np.arange(FACET_ROWS), short, SUBGRID, -1)).astype(
            np.float32
        ),
        model=high_low(from_right(phases(short, short, CONTRIB, -1)) * SUBGRID**-0.5),
        back=high_low(from_right(phases(short, short, CONTRIB, 1)) * SUBGRID**-0.5),
    )


def return_order(bands):
    order = [(b, member) for b in range(bands) for member in PLACE_ORDER]
    last_band, last_member = order[-1]

    def nearness(entry):
        return -((entry[0] ^ last_band).bit_count() + ((entry[1] ^ last_member) >> 1).bit_count())

    return order[-1:] + sorted(order[:-1], key=nearness)


def split(values):
    high = values.astype(BF16)
    return high, (values - high.astype(F32)).astype(BF16)


def dot(left, right, dims=((1,), (0,))):
    return lax.dot_general(left, right, (dims, ((), ())), preferred_element_type=F32)


def dot_split(values, right):
    rows = values.shape[0]
    both = dot(jnp.concatenate(split(values), axis=0), right)
    return both[:rows] + both[rows:]


def times_table(values, table):
    return dot_split(values, table[0]) + dot(values.astype(BF16), table[1])


def table_times(table, values, dims=((1,), (0,))):
    high, low = split(values)
    rows = table[0].shape[0]
    both = dot(jnp.concatenate([table[0], table[1]], axis=0), high, dims)
    return both[:rows] + both[rows:] + dot(table[0], low, dims)


def iota(shape, dimension):
    return lax.broadcasted_iota(jnp.int32, shape, dimension)


def over(values, size):
    return lax.shift_right_logical(values, jnp.full_like(values, size.bit_length() - 1))


def within(values, size):
    return values & (size - 1)


def swap_halves(values):
    return pltpu.roll(values, HALF, 1)


def table_at(ref, place):
    begin, rows, blocks = place
    parts = [ref[begin + i * rows : begin + (i + 1) * rows, :] for i in range(blocks)]
    return parts[0] if blocks == 1 else jnp.concatenate(parts, axis=1)


def offsets_on_lanes(offsets_ref, columns, order):
    fronts, owners = offsets_ref.shape
    groups = owners // FACET_ROWS
    own = lax.axis_index("group")
    begins = []
    for step in range(groups):
        group = own + step
        begins.append(jnp.where(group >= groups, group - groups, group) * FACET_ROWS)
    spread = iota((1, fronts * owners * columns), 1)
    place_of = over(spread, columns)
    for place in range(fronts * owners):
        t, step, spot = place % fronts, place // fronts % groups, place // (fronts * groups)
        member = order[spot]
        spread = jnp.where(place_of == place, offsets_ref[t, begins[step] + member], spread)
    return spread


def shift_rows(residue, table):
    pick = jnp.where(iota((CONTRIB, residue.shape[1]), 0) == residue, 1.0, 0.0).T.astype(BF16)
    rows = dot(pick, table[0]) + dot(pick, table[1])
    return rows[:, :LANES], rows[:, LANES:]


def one_hot(shape, targets):
    return jnp.where(iota(shape, 0) == targets, 1.0, 0.0).astype(BF16)


def turned_eighths(values, rotation):
    sign = jnp.where(iota(values[0].shape, 1) < HALF, -rotation, rotation).astype(F32)

    def quarter_turn(value):
        return swap_halves(value) * sign

    def four(a, b, c, d):
        even_sum, even_diff = a + c, a - c
        odd_sum, odd_diff = b + d, quarter_turn(b - d)
        return even_sum + odd_sum, even_diff + odd_diff, even_sum - odd_sum, even_diff - odd_diff

    even = four(*values[0::2])
    odd = four(*values[1::2])
    root = math.sqrt(0.5)
    turned = (
        odd[0],
        (odd[1] + quarter_turn(odd[1])) * root,
        quarter_turn(odd[2]),
        (quarter_turn(odd[3]) - odd[3]) * root,
    )
    return [e + o for e, o in zip(even, turned)] + [e - o for e, o in zip(even, turned)]


def pack_samples(cells_ref, values_ref, weights_ref, flags_ref, out_ref):
    for t in range(cells_ref.shape[0]):
        rows = [
            cells_ref[t, 0:1, :].astype(F32) * SUBGRID + cells_ref[t, 1:2, :].astype(F32),
            weights_ref[t] * flags_ref[t].astype(F32),
            values_ref[t],
        ]
        out_ref[4 * t : 4 * t + 4, :] = jnp.concatenate(rows, axis=0)


def start_all(sources, targets, semaphores):
    copies = [
        pltpu.make_async_copy(source, target, semaphores.at[i])
        for i, (source, target) in enumerate(zip(sources, targets))
    ]
    for copy in copies:
        copy.start()
    return copies


def predict(spread, copies, strips_ref, plain_ref, paired_ref, held_refs, out_ref, plain, paired):
    columns, length = strips_ref.shape[1:]
    groups = length // LANES
    pairs = columns // 2
    blocks = length // CONTRIB
    width = spread.shape[1]
    first_block, residue = over(spread, CONTRIB), within(spread, CONTRIB)
    base = within(iota(spread.shape, 1), columns) * blocks
    shape = (columns * blocks, width)
    pick_inside = one_hot(shape, base + first_block)
    pick_beyond = one_hot(shape, base + within(first_block + 1, blocks))
    for copy in copies[:2]:
        copy.wait()

    def pair_at(name):
        return [table_at(paired_ref, paired[name, i]) for i in range(2)]

    window = table_at(plain_ref, plain["window"])
    turn_real, turn_imag = table_at(plain_ref, plain["real"]), table_at(plain_ref, plain["imag"])
    low_half = iota((groups, LANES), 1) < HALF
    sections = []
    for part, held in enumerate(held_refs):
        for group in range(groups):
            held[group * columns : (group + 1) * columns, :] = strips_ref[
                part, :, group * LANES : (group + 1) * LANES
            ]
        even, odd = [], []
        for pair in range(pairs):
            first = held[pl.ds(2 * pair, groups, stride=columns), :] * window
            second = held[pl.ds(2 * pair + 1, groups, stride=columns), :] * window
            even.append(jnp.where(low_half, first, swap_halves(second)))
            odd.append(jnp.where(low_half, swap_halves(first), second))
        sections += [jnp.concatenate(even, axis=1), jnp.concatenate(odd, axis=1)]
    for copy in copies[2:]:
        copy.wait()
    section = table_times(pair_at("outer"), jnp.concatenate(sections, axis=0))
    turned = []
    for pair in range(pairs):
        lanes = slice(pair * LANES, (pair + 1) * LANES)
        real, imag = section[:CONTRIB, lanes], section[CONTRIB:, lanes]
        turned.append(
            jnp.concatenate(
                [real * turn_real - imag * turn_imag, real * turn_imag + imag * turn_real],
                axis=1,
            )
        )
    inner = times_table(jnp.concatenate(turned, axis=0), pair_at("inner"))
    spectrum = jnp.concatenate(
        [
            jnp.concatenate(
                [
                    inner[pair * CONTRIB : (pair + 1) * CONTRIB, part * LANES : (part + 1) * LANES]
                    for pair in range(pairs)
                ],
                axis=1,
            )
            for part in range(2)
        ],
        axis=0,
    )
    inside = dot_split(spectrum, pick_inside)
    beyond = dot_split(spectrum, pick_beyond)
    kappa = within(iota((2 * CONTRIB, width), 0), CONTRIB)
    cutout = jnp.where(kappa >= residue, inside, beyond)
    piece = times_table(cutout.T, pair_at("piece"))
    straight, crossed = shift_rows(residue, pair_at("shift"))
    out_ref[...] = (piece * straight + swap_halves(piece) * crossed).astype(BF16)


def in_first_half():
    return 2 * lax.axis_index("group") < lax.axis_size("group")


def early_kernel(
    offsets, cells, values, weights, flags, strips, plain_table, paired_table,
    out_ref, packed_ref, places_ref, spread_ref,
    offsets_ref, cells_ref, values_ref, weights_ref, flags_ref, strips_ref, plain_ref, paired_ref,
    real_ref, imag_ref, small_semaphores, semaphores, *, plain, paired, share,
):
    small = start_all(
        (offsets, cells, values, weights, flags),
        (offsets_ref, cells_ref, values_ref, weights_ref, flags_ref),
        small_semaphores,
    )

    def large():
        sources, targets = (strips, plain_table, paired_table), (strips_ref, plain_ref, paired_ref)
        return [
            pltpu.make_async_copy(source, target, semaphores.at[i])
            for i, (source, target) in enumerate(zip(sources, targets))
        ]

    @pl.when(in_first_half())
    def _():
        for copy in large():
            copy.start()

    for copy in small:
        copy.wait()
    for t in range(cells_ref.shape[0]):
        rows = [
            cells_ref[t, 0:1, :].astype(F32) * SUBGRID + cells_ref[t, 1:2, :].astype(F32),
            weights_ref[t] * flags_ref[t].astype(F32),
            values_ref[t],
        ]
        packed_ref[4 * t : 4 * t + 4, :] = jnp.concatenate(rows, axis=0)
    places_ref[...] = offsets_on_lanes(offsets_ref, share, PLACE_ORDER)
    spread_ref[...] = offsets_on_lanes(offsets_ref, strips_ref.shape[1], SEND_ORDER)

    @pl.when(in_first_half())
    def _():
        predict(
            spread_ref[...], large(), strips_ref, plain_ref, paired_ref, (real_ref, imag_ref),
            out_ref, plain, paired,
        )


def late_kernel(
    early_ref, spread_ref, strips_ref, plain_ref, paired_ref, out_ref, real_ref, imag_ref,
    *, plain, paired,
):
    @pl.when(in_first_half())
    def _():
        out_ref[...] = early_ref[...]

    @pl.when(jnp.logical_not(in_first_half()))
    def _():
        predict(
            spread_ref[...], (), strips_ref, plain_ref, paired_ref, (real_ref, imag_ref), out_ref,
            plain, paired,
        )


def prepare_kernel(places_ref, shift_ref, *refs, columns, share, blocks):
    samples_refs, outs = refs[:-5], refs[-5:]
    value_ref, weight_ref, put_ref, straight_ref, crossed_ref = outs
    fronts, samples = samples_refs[0].shape[0] // 4, samples_refs[0].shape[1]
    own = lax.axis_index("group")
    depth = FACET_ROWS * columns
    for spot in range(len(samples_refs) * fronts):
        step, t = spot // fronts, spot % fronts
        sample = samples_refs[step][4 * t : 4 * t + 4, :]
        cell = sample[0:1, :].astype(jnp.int32)
        row, col = over(cell, SUBGRID) - own * columns, within(cell, SUBGRID)
        inside = (row >= 0) & (row < columns)
        target = jnp.where(inside, within(col, FACET_ROWS) * columns + row, -1)
        pick = one_hot((depth, samples), target)
        mask = iota((HALF, samples), 0) == over(col, FACET_ROWS)
        factor = sample[1:2, :]
        highs, lows = [], []
        for term in (factor * sample[2:3, :], factor * sample[3:4, :], factor):
            high = term.astype(BF16).astype(F32)
            highs.append(jnp.where(mask, high, 0.0).astype(BF16))
            lows.append(jnp.where(mask, term - high, 0.0).astype(BF16))
        highs, lows = highs + highs[2:], lows + lows[2:]
        grid = dot(pick, jnp.concatenate(highs, axis=0), ((1,), (1,))) + dot(
            pick, jnp.concatenate(lows, axis=0), ((1,), (1,))
        )
        rows = slice(spot * depth, (spot + 1) * depth)
        value_ref[rows, :] = grid[:, :LANES]
        weight_ref[rows, :] = grid[:, LANES:]
    spread = places_ref[...]
    first_block, residue = over(spread, CONTRIB), within(spread, CONTRIB)
    straight_ref[...], crossed_ref[...] = shift_rows(residue, shift_ref)
    base = within(iota(spread.shape, 1), share) * blocks
    targets = jnp.concatenate([base + first_block, base + within(first_block + 1, blocks)], axis=1)
    put_ref[...] = one_hot(put_ref.shape, targets)


def subgrid_kernel(
    pieces_ref, value_ref, weight_ref, turn_ref, model_ref, back_ref, out_ref, held_ref,
    *, columns, bands,
):
    rows = pieces_ref.shape[0] // FACET_ROWS
    spots = range(rows // columns)
    depth = FACET_ROWS * columns
    share = columns // bands
    pieces = pieces_ref[...].astype(F32)
    sky = turned_eighths(
        [
            pieces[spot * rows : (spot + 1) * rows, :]
            for spot in (SEND_ORDER.index(i) for i in range(FACET_ROWS))
        ],
        -1.0,
    )
    sky = [
        value * turn_ref[0, i : i + 1, :] + swap_halves(value) * turn_ref[1, i : i + 1, :]
        for i, value in enumerate(sky)
    ]
    stacked = jnp.concatenate(
        [value[spot * columns : (spot + 1) * columns, :] for spot in spots for value in sky],
        axis=0,
    )
    grid = value_ref[...] - weight_ref[...] * times_table(stacked, model_ref)
    back = times_table(grid, back_ref)
    lines = []
    for i in range(FACET_ROWS):
        value = jnp.concatenate(
            [
                back[spot * depth + i * columns : spot * depth + (i + 1) * columns, :]
                for spot in spots
            ],
            axis=0,
        )
        lines.append(
            value * turn_ref[0, i : i + 1, :] - swap_halves(value) * turn_ref[1, i : i + 1, :]
        )
    lines = turned_eighths(lines, 1.0)
    for i in range(FACET_ROWS):
        for spot in spots:
            for b in range(bands):
                source = spot * columns + b * share
                place = return_order(bands).index((b, i))
                target = (place * len(spots) + spot) * share
                held_ref[target : target + share, :] = lines[i][source : source + share, :]
    out_ref[...] = held_ref[...].astype(BF16)


def return_kernel(
    places_ref, pieces_ref, straight_ref, crossed_ref, put_ref, window_ref, turn_ref, partial_ref,
    inner_ref, outer_ref, out_ref, *line_refs, bands,
):
    columns, _, length = out_ref.shape
    blocks = length // CONTRIB
    groups = length // LANES
    pairs = (columns + 1) // 2
    width = pieces_ref.shape[0] // bands
    pieces = pieces_ref[...].astype(F32)
    order, rows = return_order(bands), width // FACET_ROWS

    def of_band(b):
        begins = [order.index((b, member)) * rows for member in PLACE_ORDER]
        return jnp.concatenate([pieces[begin : begin + rows, :] for begin in begins], axis=0)

    summed = of_band(0)
    for b in range(1, bands):
        summed += of_band(b)
    summed = summed * straight_ref[...] - swap_halves(summed) * crossed_ref[...]
    residues = table_times(partial_ref, summed, ((1,), (1,)))
    kappa = within(iota((2 * CONTRIB, width), 0), CONTRIB)
    inside = kappa >= within(places_ref[...], CONTRIB)
    both = jnp.concatenate(
        [jnp.where(inside, residues, 0.0), jnp.where(inside, 0.0, residues)], axis=1
    )
    put = put_ref[...]
    high, low = split(both)
    spectrum = dot(high, put, ((1,), (1,))) + dot(low, put, ((1,), (1,)))
    inner = times_table(
        jnp.concatenate(
            [
                jnp.concatenate(
                    [
                        spectrum[:CONTRIB, pair * LANES : (pair + 1) * LANES],
                        spectrum[CONTRIB:, pair * LANES : (pair + 1) * LANES],
                    ],
                    axis=1,
                )
                for pair in range(pairs)
            ],
            axis=0,
        ),
        inner_ref,
    )
    reals, imags = [], []
    for pair in range(pairs):
        rows = slice(pair * CONTRIB, (pair + 1) * CONTRIB)
        real, imag = inner[rows, :LANES], inner[rows, LANES:]
        reals.append(real * turn_ref[0] + imag * turn_ref[1])
        imags.append(imag * turn_ref[0] - real * turn_ref[1])
    lines = table_times(
        outer_ref,
        jnp.concatenate(
            [jnp.concatenate(reals, axis=1), jnp.concatenate(imags, axis=1)], axis=0
        ),
    )
    window = window_ref[...]
    low_half = iota((groups, LANES), 1) < HALF
    for part in range(2):
        for pair in range(pairs):
            lanes = slice(pair * LANES, (pair + 1) * LANES)
            begin = part * blocks
            even = lines[begin : begin + groups, lanes]
            odd = lines[begin + groups : begin + blocks, lanes]
            line_refs[2 * pair][pl.ds(part, groups, stride=2), :] = (
                jnp.where(low_half, even, swap_halves(odd)) * window
            )
            if 2 * pair + 1 < columns:
                line_refs[2 * pair + 1][pl.ds(part, groups, stride=2), :] = (
                    jnp.where(low_half, swap_halves(even), odd) * window
                )
    for column in range(columns):
        for group in range(groups):
            out_ref[column, :, group * LANES : (group + 1) * LANES] = line_refs[column][
                2 * group : 2 * group + 2, :
            ]


def kernel_call(kernel, name, out_shape, spaces, scratch, *operands, flops=0):
    return pl.pallas_call(
        kernel,
        out_shape=out_shape,
        in_specs=[pl.BlockSpec(memory_space=space) for space in spaces],
        out_specs=jax.tree.map(lambda _: pl.BlockSpec(memory_space=pltpu.VMEM), out_shape),
        scratch_shapes=scratch,
        compiler_params=pltpu.CompilerParams(vmem_limit_bytes=VMEM_LIMIT),
        cost_estimate=pl.CostEstimate(flops=flops, bytes_accessed=0, transcendentals=0)
        if flops
        else None,
        name=name,
    )(*operands)


def wide(rows):
    return pltpu.VMEM((rows, LANES), F32)


def local(groups, bands, strips, offsets, cells, values, weights, flags):
    columns, length = strips.shape[-2:]
    fronts = offsets.shape[0]
    share = columns // bands
    facets = groups * FACET_ROWS
    rows = facets * fronts * columns
    width = facets * fronts * share
    made = tables(length)
    plain, plain_places = made.pop("plain")
    paired, paired_places = made.pop("paired")
    made = {key: jnp.asarray(value) for key, value in made.items()}
    held = length // LANES * columns
    small = [offsets, cells[0, :, 0], values[0, :, 0], weights[0], flags[0]]
    large = [strips[0, 0], jnp.asarray(plain), jnp.asarray(paired)]

    def landing(arrays):
        return [
            (pltpu.SMEM if array is offsets else pltpu.VMEM)(array.shape, array.dtype)
            for array in arrays
        ]

    def in_hbm(arrays):
        return [pltpu.with_memory_space_constraint(array, pltpu.HBM) for array in arrays]

    def semaphores(count):
        return pltpu.SemaphoreType.DMA((count,))

    early, packed, places, spread = kernel_call(
        functools.partial(early_kernel, plain=plain_places, paired=paired_places, share=share),
        "early",
        [
            jax.ShapeDtypeStruct((rows, LANES), BF16),
            jax.ShapeDtypeStruct((4 * fronts, cells.shape[-1]), F32),
            jax.ShapeDtypeStruct((1, width), jnp.int32),
            jax.ShapeDtypeStruct((1, rows), jnp.int32),
        ],
        [pltpu.HBM] * 8,
        landing(small + large) + [wide(held)] * 2 + [semaphores(5), semaphores(3)],
        *in_hbm(small + large), flops=EARLY_FLOPS,
    )
    pieces = kernel_call(
        functools.partial(late_kernel, plain=plain_places, paired=paired_places), "late",
        jax.ShapeDtypeStruct((rows, LANES), BF16), [pltpu.VMEM] * 5, [wide(held)] * 2,
        early, spread, *large, flops=LATE_FLOPS,
    )
    gathered = [packed]
    for step in range(1, groups):
        moves = [((group + step) % groups, group) for group in range(groups)]
        gathered.append(lax.ppermute(packed, "group", moves))
    arrived = lax.all_to_all(
        pieces, "member", split_axis=0, concat_axis=0, tiled=True,
        axis_index_groups=[list(SEND_ORDER)],
    )
    blocks = length // CONTRIB
    value, weight, put, straight, crossed = kernel_call(
        functools.partial(prepare_kernel, columns=columns, share=share, blocks=blocks), "prepare",
        [jax.ShapeDtypeStruct((rows, LANES), F32)] * 2
        + [jax.ShapeDtypeStruct(((share + share % 2) * blocks, 2 * width), BF16)]
        + [jax.ShapeDtypeStruct((width, LANES), F32)] * 2,
        [pltpu.VMEM] * (2 + len(gathered)), [],
        places, made["shift"], *gathered, flops=PREPARE_FLOPS,
    )
    returned = kernel_call(
        functools.partial(subgrid_kernel, columns=columns, bands=bands), "subgrid",
        jax.ShapeDtypeStruct((rows, LANES), BF16), [pltpu.VMEM] * 6, [wide(rows)],
        arrived, value, weight, made["grid_turn"], made["model"], made["back"],
    )
    delivered = lax.all_to_all(
        returned, ("band", "member"), split_axis=0, concat_axis=0, tiled=True,
        axis_index_groups=[
            [b * FACET_ROWS + member for b, member in return_order(bands)]
        ],
    )
    lines = kernel_call(
        functools.partial(return_kernel, bands=bands), "lines",
        jax.ShapeDtypeStruct((share, 2, length), F32), [pltpu.VMEM] * 10,
        [wide(2 * length // LANES)] * share,
        places, delivered, straight, crossed, put, made["window"], made["turn"],
        made["partial"], made["inner_plus"], made["outer_plus"],
    )
    return lines[None]


def solution(mesh):
    bands = mesh.shape["band"]
    groups = mesh.shape["facet"] // FACET_ROWS
    split_mesh = Mesh(
        mesh.devices.reshape(groups, FACET_ROWS, bands), ("group", "member", "band")
    )
    facet = ("group", "member")
    placed = (
        P("band", facet, None, None, None),
        P(),
        P("band", None, facet, None, None),
        P("band", None, facet, None, None),
        P("band", None, facet, None),
        P("band", None, facet, None),
    )
    return jax.shard_map(
        functools.partial(local, groups, bands),
        mesh=split_mesh,
        in_specs=placed,
        out_specs=P(facet, "band", None, None),
        check_vma=False,
    )
```

```python
import functools
import math

import jax
import jax.numpy as jnp
import ml_dtypes
import numpy as np
from jax import lax
from jax.experimental import pallas as pl
from jax.experimental.pallas import tpu as pltpu
from jax.sharding import Mesh
from jax.sharding import PartitionSpec as P

CONTRIB = 64
FACET_ROWS = 8
SUBGRID = FACET_ROWS * CONTRIB
SEND_ORDER = (FACET_ROWS - 1, *range(FACET_ROWS - 1))
PLACE_ORDER = tuple(range(FACET_ROWS))
LANES = 128
HALF = LANES // 2
EARLY_FLOPS = 10**10
LATE_FLOPS = 10**10
PREPARE_FLOPS = 2 * 10**10
VMEM_LIMIT = 48 * 1024 * 1024
F32 = jnp.float32
BF16 = jnp.bfloat16


def phases(rows, cols, length, rotation):
    product = np.outer(rows, cols) % length
    return np.exp(rotation * 2j * np.pi * product / length)


def from_left(matrix):
    return np.block([[matrix.real, -matrix.imag], [matrix.imag, matrix.real]])


def from_right(matrix):
    return np.block([[matrix.real, matrix.imag], [-matrix.imag, matrix.real]])


def high_low(table):
    high = table.astype(ml_dtypes.bfloat16)
    low = (table - high.astype(np.float64)).astype(ml_dtypes.bfloat16)
    return np.stack([high, low])


def side_by_side(values):
    straight = np.concatenate([values.real, values.real], axis=-1)
    crossed = np.concatenate([-values.imag, values.imag], axis=-1)
    return np.stack([straight, crossed])


def stack_tables(named):
    places, blocks, begin = {}, [], 0
    for name, table in named.items():
        count = table.shape[1] // LANES
        places[name] = (begin, table.shape[0], count)
        blocks += [table[:, i * LANES : (i + 1) * LANES] for i in range(count)]
        begin += table.shape[0] * count
    return np.concatenate(blocks, axis=0), places


def stack_pairs(named):
    return stack_tables(
        {(name, i): table for name, pair in named.items() for i, table in enumerate(pair)}
    )


def tables(length):
    blocks = length // CONTRIB
    short = np.arange(CONTRIB)
    outer = np.concatenate([np.arange(0, blocks, 2), np.arange(1, blocks, 2)])
    window = 1.0 + 0.5 * np.cos(np.arange(length) * (2.0 * math.pi / length))
    window = (window * length**-0.5).reshape(length // LANES, LANES).astype(np.float32)
    turn = np.tile(phases(short, short, length, -1), (1, 2))
    turn = np.stack([turn.real, turn.imag]).astype(np.float32)
    pair = np.eye(2)
    shift = high_low(np.concatenate(side_by_side(phases(short, short, CONTRIB, -1)), axis=1))
    outer_minus = from_left(phases(short, outer, blocks, -1))
    inner_minus = from_right(np.kron(pair, phases(short, short, CONTRIB, -1)))
    piece = from_right(phases(short, short, CONTRIB, 1)) * CONTRIB**-0.5
    return dict(
        plain=stack_tables(dict(window=window, real=turn[0], imag=turn[1])),
        paired=stack_pairs(
            dict(
                shift=shift,
                outer=high_low(outer_minus),
                inner=high_low(inner_minus),
                piece=high_low(piece),
            )
        ),
        window=np.repeat(window, 2, axis=0),
        turn=turn,
        shift=shift,
        inner_plus=high_low(from_right(np.kron(pair, phases(short, short, CONTRIB, 1)))),
        outer_plus=high_low(
            from_left(phases(outer, short, blocks, 1))
            .reshape(2, blocks, 2 * CONTRIB)
            .transpose(1, 0, 2)
            .reshape(2 * blocks, 2 * CONTRIB)
        ),
        partial=high_low(from_right(phases(short, short, CONTRIB, -1)).T * CONTRIB**-0.5),
        grid_turn=side_by_side(phases(np.arange(FACET_ROWS), short, SUBGRID, -1)).astype(
            np.float32
        ),
        model=high_low(from_right(phases(short, short, CONTRIB, -1)) * SUBGRID**-0.5),
        back=high_low(from_right(phases(short, short, CONTRIB, 1)) * SUBGRID**-0.5),
    )


def return_order(bands):
    order = [(b, member) for b in range(bands) for member in PLACE_ORDER]
    return order[-1:] + order[:-1]


def split(values):
    high = values.astype(BF16)
    return high, (values - high.astype(F32)).astype(BF16)


def dot(left, right, dims=((1,), (0,))):
    return lax.dot_general(left, right, (dims, ((), ())), preferred_element_type=F32)


def dot_split(values, right, dims=((1,), (0,))):
    rows = values.shape[0]
    both = dot(jnp.concatenate(split(values), axis=0), right, dims)
    return both[:rows] + both[rows:]


def times_table(values, table):
    return dot_split(values, table[0]) + dot(values.astype(BF16), table[1])


def table_times(table, values, dims=((1,), (0,))):
    high, low = split(values)
    rows = table[0].shape[0]
    both = dot(jnp.concatenate([table[0], table[1]], axis=0), high, dims)
    return both[:rows] + both[rows:] + dot(table[0], low, dims)


def iota(shape, dimension):
    return lax.broadcasted_iota(jnp.int32, shape, dimension)


def over(values, size):
    return lax.shift_right_logical(values, jnp.full_like(values, size.bit_length() - 1))


def within(values, size):
    return values & (size - 1)


def swap_halves(values):
    return pltpu.roll(values, HALF, 1)


def table_at(ref, place):
    begin, rows, blocks = place
    parts = [ref[begin + i * rows : begin + (i + 1) * rows, :] for i in range(blocks)]
    return parts[0] if blocks == 1 else jnp.concatenate(parts, axis=1)


def offsets_on_lanes(offsets_ref, columns, order):
    fronts, owners = offsets_ref.shape
    groups = owners // FACET_ROWS
    own = lax.axis_index("group")
    begins = []
    for step in range(groups):
        group = own + step
        begins.append(jnp.where(group >= groups, group - groups, group) * FACET_ROWS)
    spread = iota((1, fronts * owners * columns), 1)
    place_of = over(spread, columns)
    for place in range(fronts * owners):
        t, step, spot = place % fronts, place // fronts % groups, place // (fronts * groups)
        member = order[spot]
        spread = jnp.where(place_of == place, offsets_ref[t, begins[step] + member], spread)
    return spread


def shift_rows(residue, table):
    pick = jnp.where(iota((CONTRIB, residue.shape[1]), 0) == residue, 1.0, 0.0).T.astype(BF16)
    rows = dot(pick, table[0]) + dot(pick, table[1])
    return rows[:, :LANES], rows[:, LANES:]


def one_hot(shape, targets):
    return jnp.where(iota(shape, 0) == targets, 1.0, 0.0).astype(BF16)


def turned_eighths(values, rotation):
    sign = jnp.where(iota(values[0].shape, 1) < HALF, -rotation, rotation).astype(F32)

    def quarter_turn(value):
        return swap_halves(value) * sign

    def four(a, b, c, d):
        even_sum, even_diff = a + c, a - c
        odd_sum, odd_diff = b + d, quarter_turn(b - d)
        return even_sum + odd_sum, even_diff + odd_diff, even_sum - odd_sum, even_diff - odd_diff

    even = four(*values[0::2])
    odd = four(*values[1::2])
    root = math.sqrt(0.5)
    turned = (
        odd[0],
        (odd[1] + quarter_turn(odd[1])) * root,
        quarter_turn(odd[2]),
        (quarter_turn(odd[3]) - odd[3]) * root,
    )
    return [e + o for e, o in zip(even, turned)] + [e - o for e, o in zip(even, turned)]


def pack_samples(cells_ref, values_ref, weights_ref, flags_ref, out_ref):
    for t in range(cells_ref.shape[0]):
        rows = [
            cells_ref[t, 0:1, :].astype(F32) * SUBGRID + cells_ref[t, 1:2, :].astype(F32),
            weights_ref[t] * flags_ref[t].astype(F32),
            values_ref[t],
        ]
        out_ref[4 * t : 4 * t + 4, :] = jnp.concatenate(rows, axis=0)


def start_all(sources, targets, semaphores):
    copies = [
        pltpu.make_async_copy(source, target, semaphores.at[i])
        for i, (source, target) in enumerate(zip(sources, targets))
    ]
    for copy in copies:
        copy.start()
    return copies


def predict(spread, copies, strips_ref, plain_ref, paired_ref, held_refs, out_ref, plain, paired):
    columns, length = strips_ref.shape[1:]
    groups = length // LANES
    pairs = columns // 2
    blocks = length // CONTRIB
    width = spread.shape[1]
    first_block, residue = over(spread, CONTRIB), within(spread, CONTRIB)
    base = within(iota(spread.shape, 1), columns) * blocks
    shape = (columns * blocks, width)
    pick_inside = one_hot(shape, base + first_block)
    pick_beyond = one_hot(shape, base + within(first_block + 1, blocks))
    for copy in copies[:2]:
        copy.wait()

    def pair_at(name):
        return [table_at(paired_ref, paired[name, i]) for i in range(2)]

    window = table_at(plain_ref, plain["window"])
    turn_real, turn_imag = table_at(plain_ref, plain["real"]), table_at(plain_ref, plain["imag"])
    low_half = iota((groups, LANES), 1) < HALF
    sections = []
    for part, held in enumerate(held_refs):
        for group in range(groups):
            held[group * columns : (group + 1) * columns, :] = strips_ref[
                part, :, group * LANES : (group + 1) * LANES
            ]
        even, odd = [], []
        for pair in range(pairs):
            first = held[pl.ds(2 * pair, groups, stride=columns), :] * window
            second = held[pl.ds(2 * pair + 1, groups, stride=columns), :] * window
            even.append(jnp.where(low_half, first, swap_halves(second)))
            odd.append(jnp.where(low_half, swap_halves(first), second))
        sections += [jnp.concatenate(even, axis=1), jnp.concatenate(odd, axis=1)]
    for copy in copies[2:]:
        copy.wait()
    section = table_times(pair_at("outer"), jnp.concatenate(sections, axis=0))
    turned = []
    for pair in range(pairs):
        lanes = slice(pair * LANES, (pair + 1) * LANES)
        real, imag = section[:CONTRIB, lanes], section[CONTRIB:, lanes]
        turned.append(
            jnp.concatenate(
                [real * turn_real - imag * turn_imag, real * turn_imag + imag * turn_real],
                axis=1,
            )
        )
    inner = times_table(jnp.concatenate(turned, axis=0), pair_at("inner"))
    spectrum = jnp.concatenate(
        [
            jnp.concatenate(
                [
                    inner[pair * CONTRIB : (pair + 1) * CONTRIB, part * LANES : (part + 1) * LANES]
                    for pair in range(pairs)
                ],
                axis=1,
            )
            for part in range(2)
        ],
        axis=0,
    )
    inside = dot_split(spectrum, pick_inside)
    beyond = dot_split(spectrum, pick_beyond)
    kappa = within(iota((2 * CONTRIB, width), 0), CONTRIB)
    cutout = jnp.where(kappa >= residue, inside, beyond)
    piece = times_table(cutout.T, pair_at("piece"))
    straight, crossed = shift_rows(residue, pair_at("shift"))
    out_ref[...] = (piece * straight + swap_halves(piece) * crossed).astype(BF16)


def in_first_half():
    return 2 * lax.axis_index("group") < lax.axis_size("group")


def early_kernel(
    offsets, cells, values, weights, flags, strips, plain_table, paired_table,
    out_ref, packed_ref, places_ref, spread_ref,
    offsets_ref, cells_ref, values_ref, weights_ref, flags_ref, strips_ref, plain_ref, paired_ref,
    real_ref, imag_ref, small_semaphores, semaphores, *, plain, paired, share,
):
    small = start_all(
        (offsets, cells, values, weights, flags),
        (offsets_ref, cells_ref, values_ref, weights_ref, flags_ref),
        small_semaphores,
    )

    def large():
        sources, targets = (strips, plain_table, paired_table), (strips_ref, plain_ref, paired_ref)
        return [
            pltpu.make_async_copy(source, target, semaphores.at[i])
            for i, (source, target) in enumerate(zip(sources, targets))
        ]

    @pl.when(in_first_half())
    def _():
        for copy in large():
            copy.start()

    for copy in small:
        copy.wait()
    for t in range(cells_ref.shape[0]):
        rows = [
            cells_ref[t, 0:1, :].astype(F32) * SUBGRID + cells_ref[t, 1:2, :].astype(F32),
            weights_ref[t] * flags_ref[t].astype(F32),
            values_ref[t],
        ]
        packed_ref[4 * t : 4 * t + 4, :] = jnp.concatenate(rows, axis=0)
    places_ref[...] = offsets_on_lanes(offsets_ref, share, PLACE_ORDER)
    spread_ref[...] = offsets_on_lanes(offsets_ref, strips_ref.shape[1], SEND_ORDER)

    @pl.when(in_first_half())
    def _():
        predict(
            spread_ref[...], large(), strips_ref, plain_ref, paired_ref, (real_ref, imag_ref),
            out_ref, plain, paired,
        )


def late_kernel(
    early_ref, spread_ref, strips_ref, plain_ref, paired_ref, out_ref, real_ref, imag_ref,
    *, plain, paired,
):
    @pl.when(in_first_half())
    def _():
        out_ref[...] = early_ref[...]

    @pl.when(jnp.logical_not(in_first_half()))
    def _():
        predict(
            spread_ref[...], (), strips_ref, plain_ref, paired_ref, (real_ref, imag_ref), out_ref,
            plain, paired,
        )


def prepare_kernel(places_ref, shift_ref, *refs, columns, share, blocks):
    samples_refs, outs = refs[:-5], refs[-5:]
    value_ref, weight_ref, put_ref, straight_ref, crossed_ref = outs
    fronts, samples = samples_refs[0].shape[0] // 4, samples_refs[0].shape[1]
    own = lax.axis_index("group")
    depth = FACET_ROWS * columns
    for spot in range(len(samples_refs) * fronts):
        step, t = spot // fronts, spot % fronts
        sample = samples_refs[step][4 * t : 4 * t + 4, :]
        cell = sample[0:1, :].astype(jnp.int32)
        row, col = over(cell, SUBGRID) - own * columns, within(cell, SUBGRID)
        inside = (row >= 0) & (row < columns)
        target = jnp.where(inside, within(col, FACET_ROWS) * columns + row, -1)
        pick = one_hot((depth, samples), target)
        mask = iota((HALF, samples), 0) == over(col, FACET_ROWS)
        factor = sample[1:2, :]
        highs, lows = [], []
        for term in (factor * sample[2:3, :], factor * sample[3:4, :], factor):
            high = term.astype(BF16).astype(F32)
            highs.append(jnp.where(mask, high, 0.0).astype(BF16))
            lows.append(jnp.where(mask, term - high, 0.0).astype(BF16))
        highs, lows = highs + highs[2:], lows + lows[2:]
        grid = dot(pick, jnp.concatenate(highs, axis=0), ((1,), (1,))) + dot(
            pick, jnp.concatenate(lows, axis=0), ((1,), (1,))
        )
        rows = slice(spot * depth, (spot + 1) * depth)
        value_ref[rows, :] = grid[:, :LANES]
        weight_ref[rows, :] = grid[:, LANES:]
    spread = places_ref[...]
    first_block, residue = over(spread, CONTRIB), within(spread, CONTRIB)
    straight_ref[...], crossed_ref[...] = shift_rows(residue, shift_ref)
    base = within(iota(spread.shape, 1), share) * blocks
    targets = jnp.concatenate([base + first_block, base + within(first_block + 1, blocks)], axis=1)
    put_ref[...] = one_hot(put_ref.shape, targets)


def subgrid_kernel(
    pieces_ref, value_ref, weight_ref, turn_ref, model_ref, back_ref, out_ref, held_ref,
    *, columns, bands,
):
    rows = pieces_ref.shape[0] // FACET_ROWS
    spots = range(rows // columns)
    depth = FACET_ROWS * columns
    share = columns // bands
    pieces = pieces_ref[...].astype(F32)
    sky = turned_eighths(
        [
            pieces[spot * rows : (spot + 1) * rows, :]
            for spot in (SEND_ORDER.index(i) for i in range(FACET_ROWS))
        ],
        -1.0,
    )
    sky = [
        value * turn_ref[0, i : i + 1, :] + swap_halves(value) * turn_ref[1, i : i + 1, :]
        for i, value in enumerate(sky)
    ]
    stacked = jnp.concatenate(
        [value[spot * columns : (spot + 1) * columns, :] for spot in spots for value in sky],
        axis=0,
    )
    grid = value_ref[...] - weight_ref[...] * times_table(stacked, model_ref)
    back = times_table(grid, back_ref)
    lines = []
    for i in range(FACET_ROWS):
        value = jnp.concatenate(
            [
                back[spot * depth + i * columns : spot * depth + (i + 1) * columns, :]
                for spot in spots
            ],
            axis=0,
        )
        lines.append(
            value * turn_ref[0, i : i + 1, :] - swap_halves(value) * turn_ref[1, i : i + 1, :]
        )
    lines = turned_eighths(lines, 1.0)
    for i in range(FACET_ROWS):
        for spot in spots:
            for b in range(bands):
                source = spot * columns + b * share
                place = return_order(bands).index((b, i))
                target = (place * len(spots) + spot) * share
                held_ref[target : target + share, :] = lines[i][source : source + share, :]
    out_ref[...] = held_ref[...].astype(BF16)


def return_kernel(
    places_ref, pieces_ref, straight_ref, crossed_ref, put_ref, window_ref, turn_ref, partial_ref,
    inner_ref, outer_ref, out_ref, *line_refs, bands,
):
    columns, _, length = out_ref.shape
    blocks = length // CONTRIB
    groups = length // LANES
    pairs = (columns + 1) // 2
    width = pieces_ref.shape[0] // bands
    pieces = pieces_ref[...].astype(F32)
    order, rows = return_order(bands), width // FACET_ROWS

    def of_band(b):
        begins = [order.index((b, member)) * rows for member in PLACE_ORDER]
        return jnp.concatenate([pieces[begin : begin + rows, :] for begin in begins], axis=0)

    summed = of_band(0)
    for b in range(1, bands):
        summed += of_band(b)
    summed = summed * straight_ref[...] - swap_halves(summed) * crossed_ref[...]
    residues = table_times(partial_ref, summed, ((1,), (1,)))
    kappa = within(iota((2 * CONTRIB, width), 0), CONTRIB)
    inside = kappa >= within(places_ref[...], CONTRIB)
    both = jnp.concatenate(
        [jnp.where(inside, residues, 0.0), jnp.where(inside, 0.0, residues)], axis=1
    )
    spectrum = dot_split(both, put_ref[...], ((1,), (1,)))
    inner = times_table(
        jnp.concatenate(
            [
                jnp.concatenate(
                    [
                        spectrum[:CONTRIB, pair * LANES : (pair + 1) * LANES],
                        spectrum[CONTRIB:, pair * LANES : (pair + 1) * LANES],
                    ],
                    axis=1,
                )
                for pair in range(pairs)
            ],
            axis=0,
        ),
        inner_ref,
    )
    reals, imags = [], []
    for pair in range(pairs):
        rows = slice(pair * CONTRIB, (pair + 1) * CONTRIB)
        real, imag = inner[rows, :LANES], inner[rows, LANES:]
        reals.append(real * turn_ref[0] + imag * turn_ref[1])
        imags.append(imag * turn_ref[0] - real * turn_ref[1])
    lines = table_times(
        outer_ref,
        jnp.concatenate(
            [jnp.concatenate(reals, axis=1), jnp.concatenate(imags, axis=1)], axis=0
        ),
    )
    window = window_ref[...]
    low_half = iota((blocks, LANES), 1) < HALF
    for pair in range(pairs):
        lanes = slice(pair * LANES, (pair + 1) * LANES)
        even, odd = lines[:blocks, lanes], lines[blocks:, lanes]
        line_refs[2 * pair][...] = jnp.where(low_half, even, swap_halves(odd)) * window
        if 2 * pair + 1 < columns:
            line_refs[2 * pair + 1][...] = jnp.where(low_half, swap_halves(even), odd) * window
    for column in range(columns):
        for group in range(groups):
            out_ref[column, :, group * LANES : (group + 1) * LANES] = line_refs[column][
                2 * group : 2 * group + 2, :
            ]


def kernel_call(kernel, name, out_shape, spaces, scratch, *operands, flops=0):
    return pl.pallas_call(
        kernel,
        out_shape=out_shape,
        in_specs=[pl.BlockSpec(memory_space=space) for space in spaces],
        out_specs=jax.tree.map(lambda _: pl.BlockSpec(memory_space=pltpu.VMEM), out_shape),
        scratch_shapes=scratch,
        compiler_params=pltpu.CompilerParams(vmem_limit_bytes=VMEM_LIMIT),
        cost_estimate=pl.CostEstimate(flops=flops, bytes_accessed=0, transcendentals=0)
        if flops
        else None,
        name=name,
    )(*operands)


def wide(rows):
    return pltpu.VMEM((rows, LANES), F32)


def local(groups, bands, strips, offsets, cells, values, weights, flags):
    columns, length = strips.shape[-2:]
    fronts = offsets.shape[0]
    share = columns // bands
    facets = groups * FACET_ROWS
    rows = facets * fronts * columns
    width = facets * fronts * share
    made = tables(length)
    plain, plain_places = made.pop("plain")
    paired, paired_places = made.pop("paired")
    made = {key: jnp.asarray(value) for key, value in made.items()}
    held = length // LANES * columns
    small = [offsets, cells[0, :, 0], values[0, :, 0], weights[0], flags[0]]
    large = [strips[0, 0], jnp.asarray(plain), jnp.asarray(paired)]

    def landing(arrays):
        return [
            (pltpu.SMEM if array is offsets else pltpu.VMEM)(array.shape, array.dtype)
            for array in arrays
        ]

    def in_hbm(arrays):
        return [pltpu.with_memory_space_constraint(array, pltpu.HBM) for array in arrays]

    def semaphores(count):
        return pltpu.SemaphoreType.DMA((count,))

    early, packed, places, spread = kernel_call(
        functools.partial(early_kernel, plain=plain_places, paired=paired_places, share=share),
        "early",
        [
            jax.ShapeDtypeStruct((rows, LANES), BF16),
            jax.ShapeDtypeStruct((4 * fronts, cells.shape[-1]), F32),
            jax.ShapeDtypeStruct((1, width), jnp.int32),
            jax.ShapeDtypeStruct((1, rows), jnp.int32),
        ],
        [pltpu.HBM] * 8,
        landing(small + large) + [wide(held)] * 2 + [semaphores(5), semaphores(3)],
        *in_hbm(small + large), flops=EARLY_FLOPS,
    )
    pieces = kernel_call(
        functools.partial(late_kernel, plain=plain_places, paired=paired_places), "late",
        jax.ShapeDtypeStruct((rows, LANES), BF16), [pltpu.VMEM] * 5, [wide(held)] * 2,
        early, spread, *large, flops=LATE_FLOPS,
    )
    gathered = [packed]
    for step in range(1, groups):
        moves = [((group + step) % groups, group) for group in range(groups)]
        gathered.append(lax.ppermute(packed, "group", moves))
    arrived = lax.all_to_all(
        pieces, "member", split_axis=0, concat_axis=0, tiled=True,
        axis_index_groups=[list(SEND_ORDER)],
    )
    blocks = length // CONTRIB
    value, weight, put, straight, crossed = kernel_call(
        functools.partial(prepare_kernel, columns=columns, share=share, blocks=blocks), "prepare",
        [jax.ShapeDtypeStruct((rows, LANES), F32)] * 2
        + [jax.ShapeDtypeStruct(((share + share % 2) * blocks, 2 * width), BF16)]
        + [jax.ShapeDtypeStruct((width, LANES), F32)] * 2,
        [pltpu.VMEM] * (2 + len(gathered)), [],
        places, made["shift"], *gathered, flops=PREPARE_FLOPS,
    )
    returned = kernel_call(
        functools.partial(subgrid_kernel, columns=columns, bands=bands), "subgrid",
        jax.ShapeDtypeStruct((rows, LANES), BF16), [pltpu.VMEM] * 6, [wide(rows)],
        arrived, value, weight, made["grid_turn"], made["model"], made["back"],
    )
    delivered = lax.all_to_all(
        returned, ("band", "member"), split_axis=0, concat_axis=0, tiled=True,
        axis_index_groups=[
            [b * FACET_ROWS + member for b, member in return_order(bands)]
        ],
    )
    lines = kernel_call(
        functools.partial(return_kernel, bands=bands), "lines",
        jax.ShapeDtypeStruct((share, 2, length), F32), [pltpu.VMEM] * 10,
        [wide(2 * length // LANES)] * share,
        places, delivered, straight, crossed, put, made["window"], made["turn"],
        made["partial"], made["inner_plus"], made["outer_plus"],
    )
    return lines[None]


def solution(mesh):
    bands = mesh.shape["band"]
    groups = mesh.shape["facet"] // FACET_ROWS
    split_mesh = Mesh(
        mesh.devices.reshape(groups, FACET_ROWS, bands), ("group", "member", "band")
    )
    facet = ("group", "member")
    placed = (
        P("band", facet, None, None, None),
        P(),
        P("band", None, facet, None, None),
        P("band", None, facet, None, None),
        P("band", None, facet, None),
        P("band", None, facet, None),
    )
    return jax.shard_map(
        functools.partial(local, groups, bands),
        mesh=split_mesh,
        in_specs=placed,
        out_specs=P(facet, "band", None, None),
        check_vma=False,
    )
```

```python
import functools
import math

import jax
import jax.numpy as jnp
import ml_dtypes
import numpy as np
from jax import lax
from jax.experimental import pallas as pl
from jax.experimental.pallas import tpu as pltpu
from jax.sharding import Mesh
from jax.sharding import PartitionSpec as P

CONTRIB = 64
FACET_ROWS = 8
SUBGRID = FACET_ROWS * CONTRIB
SEND_ORDER = (FACET_ROWS - 1, *range(FACET_ROWS - 1))
PLACE_ORDER = tuple(range(FACET_ROWS))
LANES = 128
HALF = LANES // 2
EARLY_FLOPS = 10**10
LATE_FLOPS = 10**10
PREPARE_FLOPS = 2 * 10**10
VMEM_LIMIT = 48 * 1024 * 1024
F32 = jnp.float32
BF16 = jnp.bfloat16


def phases(rows, cols, length, rotation):
    product = np.outer(rows, cols) % length
    return np.exp(rotation * 2j * np.pi * product / length)


def from_left(matrix):
    return np.block([[matrix.real, -matrix.imag], [matrix.imag, matrix.real]])


def from_right(matrix):
    return np.block([[matrix.real, matrix.imag], [-matrix.imag, matrix.real]])


def high_low(table):
    high = table.astype(ml_dtypes.bfloat16)
    low = (table - high.astype(np.float64)).astype(ml_dtypes.bfloat16)
    return np.stack([high, low])


def side_by_side(values):
    straight = np.concatenate([values.real, values.real], axis=-1)
    crossed = np.concatenate([-values.imag, values.imag], axis=-1)
    return np.stack([straight, crossed])


def stack_tables(named):
    places, blocks, begin = {}, [], 0
    for name, table in named.items():
        count = table.shape[1] // LANES
        places[name] = (begin, table.shape[0], count)
        blocks += [table[:, i * LANES : (i + 1) * LANES] for i in range(count)]
        begin += table.shape[0] * count
    return np.concatenate(blocks, axis=0), places


def stack_pairs(named):
    return stack_tables(
        {(name, i): table for name, pair in named.items() for i, table in enumerate(pair)}
    )


def tables(length):
    blocks = length // CONTRIB
    short = np.arange(CONTRIB)
    outer = np.concatenate([np.arange(0, blocks, 2), np.arange(1, blocks, 2)])
    window = 1.0 + 0.5 * np.cos(np.arange(length) * (2.0 * math.pi / length))
    window = (window * length**-0.5).reshape(length // LANES, LANES).astype(np.float32)
    turn = np.tile(phases(short, short, length, -1), (1, 2))
    turn = np.stack([turn.real, turn.imag]).astype(np.float32)
    pair = np.eye(2)
    shift = high_low(np.concatenate(side_by_side(phases(short, short, CONTRIB, -1)), axis=1))
    outer_minus = from_left(phases(short, outer, blocks, -1))
    inner_minus = from_right(np.kron(pair, phases(short, short, CONTRIB, -1)))
    piece = from_right(phases(short, short, CONTRIB, 1)) * CONTRIB**-0.5
    return dict(
        plain=stack_tables(dict(window=window, real=turn[0], imag=turn[1])),
        paired=stack_pairs(
            dict(
                shift=shift,
                outer=high_low(outer_minus),
                inner=high_low(inner_minus),
                piece=high_low(piece),
            )
        ),
        window=np.repeat(window, 2, axis=0),
        turn=turn,
        shift=shift,
        inner_plus=high_low(from_right(np.kron(pair, phases(short, short, CONTRIB, 1)))),
        outer_plus=high_low(
            from_left(phases(outer, short, blocks, 1))
            .reshape(2, blocks, 2 * CONTRIB)
            .transpose(1, 0, 2)
            .reshape(2 * blocks, 2 * CONTRIB)
        ),
        partial=high_low(from_right(phases(short, short, CONTRIB, -1)).T * CONTRIB**-0.5),
        grid_turn=side_by_side(phases(np.arange(FACET_ROWS), short, SUBGRID, -1)).astype(
            np.float32
        ),
        model=high_low(from_right(phases(short, short, CONTRIB, -1)) * SUBGRID**-0.5),
        back=high_low(from_right(phases(short, short, CONTRIB, 1)) * SUBGRID**-0.5),
    )


def return_order(bands):
    order = [(b, member) for b in range(bands) for member in PLACE_ORDER]
    return order[-1:] + order[:-1]


def split(values):
    high = values.astype(BF16)
    return high, (values - high.astype(F32)).astype(BF16)


def dot(left, right, dims=((1,), (0,))):
    return lax.dot_general(left, right, (dims, ((), ())), preferred_element_type=F32)


def dot_split(values, right, dims=((1,), (0,))):
    rows = values.shape[0]
    both = dot(jnp.concatenate(split(values), axis=0), right, dims)
    return both[:rows] + both[rows:]


def times_table(values, table):
    return dot_split(values, table[0]) + dot(values.astype(BF16), table[1])


def table_times(table, values, dims=((1,), (0,))):
    high, low = split(values)
    rows = table[0].shape[0]
    both = dot(jnp.concatenate([table[0], table[1]], axis=0), high, dims)
    return both[:rows] + both[rows:] + dot(table[0], low, dims)


def iota(shape, dimension):
    return lax.broadcasted_iota(jnp.int32, shape, dimension)


def over(values, size):
    return lax.shift_right_logical(values, jnp.full_like(values, size.bit_length() - 1))


def within(values, size):
    return values & (size - 1)


def swap_halves(values):
    return pltpu.roll(values, HALF, 1)


def table_at(ref, place):
    begin, rows, blocks = place
    parts = [ref[begin + i * rows : begin + (i + 1) * rows, :] for i in range(blocks)]
    return parts[0] if blocks == 1 else jnp.concatenate(parts, axis=1)


def offsets_on_lanes(offsets_ref, columns, order):
    fronts, owners = offsets_ref.shape
    groups = owners // FACET_ROWS
    place = over(iota((1, fronts * owners * columns), 1), columns)
    front = within(place, fronts)
    group = within(over(place, fronts) + lax.axis_index("group"), groups)
    spot = over(place, fronts * groups)
    member = jnp.zeros_like(spot)
    for i, value in enumerate(order):
        member = jnp.where(spot == i, value, member)
    owner = group * FACET_ROWS + member
    pick = one_hot((owners, place.shape[1]), owner)
    offsets = offsets_ref[...]
    blocks = dot(over(offsets, CONTRIB).astype(F32).astype(BF16), pick)
    residues = dot(within(offsets, CONTRIB).astype(F32).astype(BF16), pick)
    spread = jnp.zeros_like(place, dtype=F32)
    for t in range(fronts):
        here = blocks[t : t + 1, :] * CONTRIB + residues[t : t + 1, :]
        spread = jnp.where(front == t, here, spread)
    return spread.astype(jnp.int32)


def shift_rows(residue, table):
    pick = jnp.where(iota((CONTRIB, residue.shape[1]), 0) == residue, 1.0, 0.0).T.astype(BF16)
    rows = dot(pick, table[0]) + dot(pick, table[1])
    return rows[:, :LANES], rows[:, LANES:]


def one_hot(shape, targets):
    return jnp.where(iota(shape, 0) == targets, 1.0, 0.0).astype(BF16)


def turned_eighths(values, rotation):
    sign = jnp.where(iota(values[0].shape, 1) < HALF, -rotation, rotation).astype(F32)

    def quarter_turn(value):
        return swap_halves(value) * sign

    def four(a, b, c, d):
        even_sum, even_diff = a + c, a - c
        odd_sum, odd_diff = b + d, quarter_turn(b - d)
        return even_sum + odd_sum, even_diff + odd_diff, even_sum - odd_sum, even_diff - odd_diff

    even = four(*values[0::2])
    odd = four(*values[1::2])
    root = math.sqrt(0.5)
    turned = (
        odd[0],
        (odd[1] + quarter_turn(odd[1])) * root,
        quarter_turn(odd[2]),
        (quarter_turn(odd[3]) - odd[3]) * root,
    )
    return [e + o for e, o in zip(even, turned)] + [e - o for e, o in zip(even, turned)]


def pack_samples(cells_ref, values_ref, weights_ref, flags_ref, out_ref):
    for t in range(cells_ref.shape[0]):
        rows = [
            cells_ref[t, 0:1, :].astype(F32) * SUBGRID + cells_ref[t, 1:2, :].astype(F32),
            weights_ref[t] * flags_ref[t].astype(F32),
            values_ref[t],
        ]
        out_ref[4 * t : 4 * t + 4, :] = jnp.concatenate(rows, axis=0)


def start_all(sources, targets, semaphores):
    copies = [
        pltpu.make_async_copy(source, target, semaphores.at[i])
        for i, (source, target) in enumerate(zip(sources, targets))
    ]
    for copy in copies:
        copy.start()
    return copies


def predict(spread, copies, strips_ref, plain_ref, paired_ref, held_refs, out_ref, plain, paired):
    columns, length = strips_ref.shape[1:]
    groups = length // LANES
    pairs = columns // 2
    blocks = length // CONTRIB
    width = spread.shape[1]
    first_block, residue = over(spread, CONTRIB), within(spread, CONTRIB)
    column = within(iota(spread.shape, 1), columns)
    kappa = iota((CONTRIB, width), 0)
    block = within(first_block + jnp.where(kappa < residue, 1, 0), blocks)
    source = within(column, 2) * blocks + block
    pair_of = over(column, 2)
    for copy in copies[:2]:
        copy.wait()

    def pair_at(name):
        return [table_at(paired_ref, paired[name, i]) for i in range(2)]

    window = table_at(plain_ref, plain["window"])
    turn_real, turn_imag = table_at(plain_ref, plain["real"]), table_at(plain_ref, plain["imag"])
    low_half = iota((groups, LANES), 1) < HALF
    sections = []
    for part, held in enumerate(held_refs):
        for group in range(groups):
            held[group * columns : (group + 1) * columns, :] = strips_ref[
                part, :, group * LANES : (group + 1) * LANES
            ]
        even, odd = [], []
        for pair in range(pairs):
            first = held[pl.ds(2 * pair, groups, stride=columns), :] * window
            second = held[pl.ds(2 * pair + 1, groups, stride=columns), :] * window
            even.append(jnp.where(low_half, first, swap_halves(second)))
            odd.append(jnp.where(low_half, swap_halves(first), second))
        sections += [jnp.concatenate(even, axis=1), jnp.concatenate(odd, axis=1)]
    for copy in copies[2:]:
        copy.wait()
    section = table_times(pair_at("outer"), jnp.concatenate(sections, axis=0))
    turned = []
    for pair in range(pairs):
        lanes = slice(pair * LANES, (pair + 1) * LANES)
        real, imag = section[:CONTRIB, lanes], section[CONTRIB:, lanes]
        turned.append(
            jnp.concatenate(
                [real * turn_real - imag * turn_imag, real * turn_imag + imag * turn_real],
                axis=1,
            )
        )
    inner = times_table(jnp.concatenate(turned, axis=0), pair_at("inner"))
    cutouts = []
    for part in range(2):
        tiles = []
        for tile in range(width // LANES):
            lanes = slice(tile * LANES, (tile + 1) * LANES)
            chosen = None
            for pair in range(pairs):
                rows = inner[pair * CONTRIB : (pair + 1) * CONTRIB, part * LANES : (part + 1) * LANES]
                found = jnp.take_along_axis(
                    rows, source[:, lanes], axis=1, mode="promise_in_bounds"
                )
                here = pair_of[:, lanes] == pair
                chosen = found if chosen is None else jnp.where(here, found, chosen)
            tiles.append(chosen)
        cutouts.append(jnp.concatenate(tiles, axis=1))
    cutout = jnp.concatenate(cutouts, axis=0)
    piece = times_table(cutout.T, pair_at("piece"))
    straight, crossed = shift_rows(residue, pair_at("shift"))
    out_ref[...] = (piece * straight + swap_halves(piece) * crossed).astype(BF16)


def in_first_half():
    return 2 * lax.axis_index("group") < lax.axis_size("group")


def early_kernel(
    cells, values, weights, flags, offsets, strips, plain_table, paired_table, out_ref, packed_ref,
    cells_ref, values_ref, weights_ref, flags_ref, offsets_ref, strips_ref, plain_ref, paired_ref,
    real_ref, imag_ref, small_semaphores, semaphores, *, plain, paired,
):
    small = start_all(
        (cells, values, weights, flags),
        (cells_ref, values_ref, weights_ref, flags_ref),
        small_semaphores,
    )

    def large():
        sources = (offsets, strips, plain_table, paired_table)
        targets = (offsets_ref, strips_ref, plain_ref, paired_ref)
        return [
            pltpu.make_async_copy(source, target, semaphores.at[i])
            for i, (source, target) in enumerate(zip(sources, targets))
        ]

    @pl.when(in_first_half())
    def _():
        for copy in large():
            copy.start()

    for copy in small:
        copy.wait()
    for t in range(cells_ref.shape[0]):
        rows = [
            cells_ref[t, 0:1, :].astype(F32) * SUBGRID + cells_ref[t, 1:2, :].astype(F32),
            weights_ref[t] * flags_ref[t].astype(F32),
            values_ref[t],
        ]
        packed_ref[4 * t : 4 * t + 4, :] = jnp.concatenate(rows, axis=0)

    @pl.when(in_first_half())
    def _():
        copies = large()
        copies[0].wait()
        predict(
            offsets_on_lanes(offsets_ref, strips_ref.shape[1], SEND_ORDER), copies[1:],
            strips_ref, plain_ref, paired_ref, (real_ref, imag_ref), out_ref, plain, paired,
        )


def late_kernel(
    early_ref, offsets_ref, strips_ref, plain_ref, paired_ref, out_ref, real_ref, imag_ref,
    *, plain, paired,
):
    @pl.when(in_first_half())
    def _():
        out_ref[...] = early_ref[...]

    @pl.when(jnp.logical_not(in_first_half()))
    def _():
        predict(
            offsets_on_lanes(offsets_ref, strips_ref.shape[1], SEND_ORDER), (),
            strips_ref, plain_ref, paired_ref, (real_ref, imag_ref), out_ref, plain, paired,
        )


def prepare_kernel(offsets_ref, shift_ref, *refs, columns, share, blocks):
    samples_refs, outs = refs[:-6], refs[-6:]
    value_ref, weight_ref, put_ref, straight_ref, crossed_ref, places_ref = outs
    fronts, samples = samples_refs[0].shape[0] // 4, samples_refs[0].shape[1]
    own = lax.axis_index("group")
    depth = FACET_ROWS * columns
    for spot in range(len(samples_refs) * fronts):
        step, t = spot // fronts, spot % fronts
        sample = samples_refs[step][4 * t : 4 * t + 4, :]
        cell = sample[0:1, :].astype(jnp.int32)
        row, col = over(cell, SUBGRID) - own * columns, within(cell, SUBGRID)
        inside = (row >= 0) & (row < columns)
        target = jnp.where(inside, within(col, FACET_ROWS) * columns + row, -1)
        pick = one_hot((depth, samples), target)
        mask = iota((HALF, samples), 0) == over(col, FACET_ROWS)
        factor = sample[1:2, :]
        highs, lows = [], []
        for term in (factor * sample[2:3, :], factor * sample[3:4, :], factor):
            high = term.astype(BF16).astype(F32)
            highs.append(jnp.where(mask, high, 0.0).astype(BF16))
            lows.append(jnp.where(mask, term - high, 0.0).astype(BF16))
        highs, lows = highs + highs[2:], lows + lows[2:]
        grid = dot(pick, jnp.concatenate(highs, axis=0), ((1,), (1,))) + dot(
            pick, jnp.concatenate(lows, axis=0), ((1,), (1,))
        )
        rows = slice(spot * depth, (spot + 1) * depth)
        value_ref[rows, :] = grid[:, :LANES]
        weight_ref[rows, :] = grid[:, LANES:]
    spread = offsets_on_lanes(offsets_ref, share, PLACE_ORDER)
    places_ref[...] = spread
    first_block, residue = over(spread, CONTRIB), within(spread, CONTRIB)
    straight_ref[...], crossed_ref[...] = shift_rows(residue, shift_ref)
    base = within(iota(spread.shape, 1), share) * blocks
    targets = jnp.concatenate([base + first_block, base + within(first_block + 1, blocks)], axis=1)
    put_ref[...] = one_hot(put_ref.shape, targets)


def subgrid_kernel(
    pieces_ref, value_ref, weight_ref, turn_ref, model_ref, back_ref, out_ref, held_ref,
    *, columns, bands,
):
    rows = pieces_ref.shape[0] // FACET_ROWS
    spots = range(rows // columns)
    depth = FACET_ROWS * columns
    share = columns // bands
    pieces = pieces_ref[...].astype(F32)
    sky = turned_eighths(
        [
            pieces[spot * rows : (spot + 1) * rows, :]
            for spot in (SEND_ORDER.index(i) for i in range(FACET_ROWS))
        ],
        -1.0,
    )
    sky = [
        value * turn_ref[0, i : i + 1, :] + swap_halves(value) * turn_ref[1, i : i + 1, :]
        for i, value in enumerate(sky)
    ]
    stacked = jnp.concatenate(
        [value[spot * columns : (spot + 1) * columns, :] for spot in spots for value in sky],
        axis=0,
    )
    grid = value_ref[...] - weight_ref[...] * times_table(stacked, model_ref)
    back = times_table(grid, back_ref)
    lines = []
    for i in range(FACET_ROWS):
        value = jnp.concatenate(
            [
                back[spot * depth + i * columns : spot * depth + (i + 1) * columns, :]
                for spot in spots
            ],
            axis=0,
        )
        lines.append(
            value * turn_ref[0, i : i + 1, :] - swap_halves(value) * turn_ref[1, i : i + 1, :]
        )
    lines = turned_eighths(lines, 1.0)
    for i in range(FACET_ROWS):
        for spot in spots:
            for b in range(bands):
                source = spot * columns + b * share
                place = return_order(bands).index((b, i))
                target = (place * len(spots) + spot) * share
                held_ref[target : target + share, :] = lines[i][source : source + share, :]
    out_ref[...] = held_ref[...].astype(BF16)


def return_kernel(
    places_ref, pieces_ref, straight_ref, crossed_ref, put_ref, window_ref, turn_ref, partial_ref,
    inner_ref, outer_ref, out_ref, *line_refs, bands,
):
    columns, _, length = out_ref.shape
    blocks = length // CONTRIB
    groups = length // LANES
    pairs = (columns + 1) // 2
    width = pieces_ref.shape[0] // bands
    pieces = pieces_ref[...].astype(F32)
    order, rows = return_order(bands), width // FACET_ROWS

    def of_band(b):
        begins = [order.index((b, member)) * rows for member in PLACE_ORDER]
        return jnp.concatenate([pieces[begin : begin + rows, :] for begin in begins], axis=0)

    summed = of_band(0)
    for b in range(1, bands):
        summed += of_band(b)
    summed = summed * straight_ref[...] - swap_halves(summed) * crossed_ref[...]
    residues = table_times(partial_ref, summed, ((1,), (1,)))
    kappa = within(iota((2 * CONTRIB, width), 0), CONTRIB)
    inside = kappa >= within(places_ref[...], CONTRIB)
    both = jnp.concatenate(
        [jnp.where(inside, residues, 0.0), jnp.where(inside, 0.0, residues)], axis=1
    )
    spectrum = dot_split(both, put_ref[...], ((1,), (1,)))
    inner = times_table(
        jnp.concatenate(
            [
                jnp.concatenate(
                    [
                        spectrum[:CONTRIB, pair * LANES : (pair + 1) * LANES],
                        spectrum[CONTRIB:, pair * LANES : (pair + 1) * LANES],
                    ],
                    axis=1,
                )
                for pair in range(pairs)
            ],
            axis=0,
        ),
        inner_ref,
    )
    reals, imags = [], []
    for pair in range(pairs):
        rows = slice(pair * CONTRIB, (pair + 1) * CONTRIB)
        real, imag = inner[rows, :LANES], inner[rows, LANES:]
        reals.append(real * turn_ref[0] + imag * turn_ref[1])
        imags.append(imag * turn_ref[0] - real * turn_ref[1])
    lines = table_times(
        outer_ref,
        jnp.concatenate(
            [jnp.concatenate(reals, axis=1), jnp.concatenate(imags, axis=1)], axis=0
        ),
    )
    window = window_ref[...]
    low_half = iota((blocks, LANES), 1) < HALF
    for pair in range(pairs):
        lanes = slice(pair * LANES, (pair + 1) * LANES)
        even, odd = lines[:blocks, lanes], lines[blocks:, lanes]
        line_refs[2 * pair][...] = jnp.where(low_half, even, swap_halves(odd)) * window
        if 2 * pair + 1 < columns:
            line_refs[2 * pair + 1][...] = jnp.where(low_half, swap_halves(even), odd) * window
    for column in range(columns):
        for group in range(groups):
            out_ref[column, :, group * LANES : (group + 1) * LANES] = line_refs[column][
                2 * group : 2 * group + 2, :
            ]


def kernel_call(kernel, name, out_shape, spaces, scratch, *operands, flops=0):
    return pl.pallas_call(
        kernel,
        out_shape=out_shape,
        in_specs=[pl.BlockSpec(memory_space=space) for space in spaces],
        out_specs=jax.tree.map(lambda _: pl.BlockSpec(memory_space=pltpu.VMEM), out_shape),
        scratch_shapes=scratch,
        compiler_params=pltpu.CompilerParams(vmem_limit_bytes=VMEM_LIMIT),
        cost_estimate=pl.CostEstimate(flops=flops, bytes_accessed=0, transcendentals=0)
        if flops
        else None,
        name=name,
    )(*operands)


def wide(rows):
    return pltpu.VMEM((rows, LANES), F32)


def local(groups, bands, strips, offsets, cells, values, weights, flags):
    columns, length = strips.shape[-2:]
    fronts = offsets.shape[0]
    share = columns // bands
    facets = groups * FACET_ROWS
    rows = facets * fronts * columns
    width = facets * fronts * share
    made = tables(length)
    plain, plain_places = made.pop("plain")
    paired, paired_places = made.pop("paired")
    made = {key: jnp.asarray(value) for key, value in made.items()}
    held = length // LANES * columns
    small = [cells[0, :, 0], values[0, :, 0], weights[0], flags[0]]
    large = [strips[0, 0], jnp.asarray(plain), jnp.asarray(paired)]

    def landing(arrays):
        return [pltpu.VMEM(array.shape, array.dtype) for array in arrays]

    def in_hbm(arrays):
        return [pltpu.with_memory_space_constraint(array, pltpu.HBM) for array in arrays]

    def semaphores(count):
        return pltpu.SemaphoreType.DMA((count,))

    early, packed = kernel_call(
        functools.partial(early_kernel, plain=plain_places, paired=paired_places), "early",
        [
            jax.ShapeDtypeStruct((rows, LANES), BF16),
            jax.ShapeDtypeStruct((4 * fronts, cells.shape[-1]), F32),
        ],
        [pltpu.HBM] * 8,
        landing(small + [offsets] + large) + [wide(held)] * 2 + [semaphores(4), semaphores(4)],
        *in_hbm(small + [offsets] + large), flops=EARLY_FLOPS,
    )
    early, *later = lax.optimization_barrier((early, offsets, *large))
    pieces = kernel_call(
        functools.partial(late_kernel, plain=plain_places, paired=paired_places), "late",
        jax.ShapeDtypeStruct((rows, LANES), BF16), [pltpu.VMEM] * 5, [wide(held)] * 2,
        early, *later, flops=LATE_FLOPS,
    )
    gathered = [packed]
    for step in range(1, groups):
        moves = [((group + step) % groups, group) for group in range(groups)]
        gathered.append(lax.ppermute(packed, "group", moves))
    arrived = lax.all_to_all(
        pieces, "member", split_axis=0, concat_axis=0, tiled=True,
        axis_index_groups=[list(SEND_ORDER)],
    )
    blocks = length // CONTRIB
    value, weight, put, straight, crossed, places = kernel_call(
        functools.partial(prepare_kernel, columns=columns, share=share, blocks=blocks), "prepare",
        [jax.ShapeDtypeStruct((rows, LANES), F32)] * 2
        + [jax.ShapeDtypeStruct(((share + share % 2) * blocks, 2 * width), BF16)]
        + [jax.ShapeDtypeStruct((width, LANES), F32)] * 2
        + [jax.ShapeDtypeStruct((1, width), jnp.int32)],
        [pltpu.VMEM] * (2 + len(gathered)), [],
        offsets, made["shift"], *gathered, flops=PREPARE_FLOPS,
    )
    returned = kernel_call(
        functools.partial(subgrid_kernel, columns=columns, bands=bands), "subgrid",
        jax.ShapeDtypeStruct((rows, LANES), BF16), [pltpu.VMEM] * 6, [wide(rows)],
        arrived, value, weight, made["grid_turn"], made["model"], made["back"],
    )
    delivered = lax.all_to_all(
        returned, ("band", "member"), split_axis=0, concat_axis=0, tiled=True,
        axis_index_groups=[
            [b * FACET_ROWS + member for b, member in return_order(bands)]
        ],
    )
    lines = kernel_call(
        functools.partial(return_kernel, bands=bands), "lines",
        jax.ShapeDtypeStruct((share, 2, length), F32), [pltpu.VMEM] * 10,
        [wide(2 * length // LANES)] * share,
        places, delivered, straight, crossed, put, made["window"], made["turn"],
        made["partial"], made["inner_plus"], made["outer_plus"],
    )
    return lines[None]


def solution(mesh):
    bands = mesh.shape["band"]
    groups = mesh.shape["facet"] // FACET_ROWS
    split_mesh = Mesh(
        mesh.devices.reshape(groups, FACET_ROWS, bands), ("group", "member", "band")
    )
    facet = ("group", "member")
    placed = (
        P("band", facet, None, None, None),
        P(),
        P("band", None, facet, None, None),
        P("band", None, facet, None, None),
        P("band", None, facet, None),
        P("band", None, facet, None),
    )
    return jax.shard_map(
        functools.partial(local, groups, bands),
        mesh=split_mesh,
        in_specs=placed,
        out_specs=P(facet, "band", None, None),
        check_vma=False,
    )
```

```python
import functools
import math

import jax
import jax.numpy as jnp
import ml_dtypes
import numpy as np
from jax import lax
from jax.experimental import pallas as pl
from jax.experimental.pallas import tpu as pltpu
from jax.sharding import Mesh
from jax.sharding import PartitionSpec as P

CONTRIB = 64
FACET_ROWS = 8
SUBGRID = FACET_ROWS * CONTRIB
SEND_ORDER = (FACET_ROWS - 1, *range(FACET_ROWS - 1))
PLACE_ORDER = tuple(range(FACET_ROWS))
LANES = 128
HALF = LANES // 2
EARLY_FLOPS = 10**10
LATE_FLOPS = 10**10
PREPARE_FLOPS = 2 * 10**10
VMEM_LIMIT = 48 * 1024 * 1024
F32 = jnp.float32
BF16 = jnp.bfloat16


def phases(rows, cols, length, rotation):
    product = np.outer(rows, cols) % length
    return np.exp(rotation * 2j * np.pi * product / length)


def from_left(matrix):
    return np.block([[matrix.real, -matrix.imag], [matrix.imag, matrix.real]])


def from_right(matrix):
    return np.block([[matrix.real, matrix.imag], [-matrix.imag, matrix.real]])


def high_low(table):
    high = table.astype(ml_dtypes.bfloat16)
    low = (table - high.astype(np.float64)).astype(ml_dtypes.bfloat16)
    return np.stack([high, low])


def side_by_side(values):
    straight = np.concatenate([values.real, values.real], axis=-1)
    crossed = np.concatenate([-values.imag, values.imag], axis=-1)
    return np.stack([straight, crossed])


def stack_tables(named):
    places, blocks, begin = {}, [], 0
    for name, table in named.items():
        count = table.shape[1] // LANES
        places[name] = (begin, table.shape[0], count)
        blocks += [table[:, i * LANES : (i + 1) * LANES] for i in range(count)]
        begin += table.shape[0] * count
    return np.concatenate(blocks, axis=0), places


def stack_pairs(named):
    return stack_tables(
        {(name, i): table for name, pair in named.items() for i, table in enumerate(pair)}
    )


def tables(length):
    blocks = length // CONTRIB
    short = np.arange(CONTRIB)
    outer = np.concatenate([np.arange(0, blocks, 2), np.arange(1, blocks, 2)])
    window = 1.0 + 0.5 * np.cos(np.arange(length) * (2.0 * math.pi / length))
    window = (window * length**-0.5).reshape(length // LANES, LANES).astype(np.float32)
    turn = np.tile(phases(short, short, length, -1), (1, 2))
    turn = np.stack([turn.real, turn.imag]).astype(np.float32)
    pair = np.eye(2)
    shift = high_low(np.concatenate(side_by_side(phases(short, short, CONTRIB, -1)), axis=1))
    outer_minus = from_left(phases(short, outer, blocks, -1))
    inner_minus = from_right(np.kron(pair, phases(short, short, CONTRIB, -1)))
    piece = from_right(phases(short, short, CONTRIB, 1)) * CONTRIB**-0.5
    return dict(
        plain=stack_tables(dict(window=window, real=turn[0], imag=turn[1])),
        paired=stack_pairs(
            dict(
                shift=shift,
                outer=high_low(outer_minus),
                inner=high_low(inner_minus),
                piece=high_low(piece),
            )
        ),
        window=np.repeat(window, 2, axis=0),
        turn=turn,
        shift=shift,
        inner_plus=high_low(from_right(np.kron(pair, phases(short, short, CONTRIB, 1)))),
        outer_plus=high_low(
            from_left(phases(outer, short, blocks, 1))
            .reshape(2, blocks, 2 * CONTRIB)
            .transpose(1, 0, 2)
            .reshape(2 * blocks, 2 * CONTRIB)
        ),
        partial=high_low(from_right(phases(short, short, CONTRIB, -1)).T * CONTRIB**-0.5),
        grid_turn=side_by_side(phases(np.arange(FACET_ROWS), short, SUBGRID, -1)).astype(
            np.float32
        ),
        model=high_low(from_right(phases(short, short, CONTRIB, -1)) * SUBGRID**-0.5),
        back=high_low(from_right(phases(short, short, CONTRIB, 1)) * SUBGRID**-0.5),
    )


def return_order(bands):
    order = [(b, member) for b in range(bands) for member in PLACE_ORDER]
    lead = FACET_ROWS - 1
    return order[lead : lead + 1] + order[:lead] + order[lead + 1 :]


def split(values):
    high = values.astype(BF16)
    return high, (values - high.astype(F32)).astype(BF16)


def dot(left, right, dims=((1,), (0,))):
    return lax.dot_general(left, right, (dims, ((), ())), preferred_element_type=F32)


def dot_split(values, right, dims=((1,), (0,))):
    rows = values.shape[0]
    both = dot(jnp.concatenate(split(values), axis=0), right, dims)
    return both[:rows] + both[rows:]


def times_table(values, table):
    return dot_split(values, table[0]) + dot(values.astype(BF16), table[1])


def table_times(table, values, dims=((1,), (0,))):
    high, low = split(values)
    rows = table[0].shape[0]
    both = dot(jnp.concatenate([table[0], table[1]], axis=0), high, dims)
    return both[:rows] + both[rows:] + dot(table[0], low, dims)


def iota(shape, dimension):
    return lax.broadcasted_iota(jnp.int32, shape, dimension)


def over(values, size):
    return lax.shift_right_logical(values, jnp.full_like(values, size.bit_length() - 1))


def within(values, size):
    return values & (size - 1)


def swap_halves(values):
    return pltpu.roll(values, HALF, 1)


def table_at(ref, place):
    begin, rows, blocks = place
    parts = [ref[begin + i * rows : begin + (i + 1) * rows, :] for i in range(blocks)]
    return parts[0] if blocks == 1 else jnp.concatenate(parts, axis=1)


def offsets_on_lanes(offsets_ref, columns, order):
    fronts, owners = offsets_ref.shape
    groups = owners // FACET_ROWS
    own = lax.axis_index("group")
    begins = []
    for step in range(groups):
        group = own + step
        begins.append(jnp.where(group >= groups, group - groups, group) * FACET_ROWS)
    spread = iota((1, fronts * owners * columns), 1)
    place_of = over(spread, columns)
    for place in range(fronts * owners):
        t, step, spot = place % fronts, place // fronts % groups, place // (fronts * groups)
        member = order[spot]
        spread = jnp.where(place_of == place, offsets_ref[t, begins[step] + member], spread)
    return spread


def shift_rows(residue, table):
    pick = jnp.where(iota((CONTRIB, residue.shape[1]), 0) == residue, 1.0, 0.0).T.astype(BF16)
    rows = dot(pick, table[0]) + dot(pick, table[1])
    return rows[:, :LANES], rows[:, LANES:]


def one_hot(shape, targets):
    return jnp.where(iota(shape, 0) == targets, 1.0, 0.0).astype(BF16)


def turned_eighths(values, rotation):
    sign = jnp.where(iota(values[0].shape, 1) < HALF, -rotation, rotation).astype(F32)

    def quarter_turn(value):
        return swap_halves(value) * sign

    def four(a, b, c, d):
        even_sum, even_diff = a + c, a - c
        odd_sum, odd_diff = b + d, quarter_turn(b - d)
        return even_sum + odd_sum, even_diff + odd_diff, even_sum - odd_sum, even_diff - odd_diff

    even = four(*values[0::2])
    odd = four(*values[1::2])
    root = math.sqrt(0.5)
    turned = (
        odd[0],
        (odd[1] + quarter_turn(odd[1])) * root,
        quarter_turn(odd[2]),
        (quarter_turn(odd[3]) - odd[3]) * root,
    )
    return [e + o for e, o in zip(even, turned)] + [e - o for e, o in zip(even, turned)]


def pack_samples(cells_ref, values_ref, weights_ref, flags_ref, out_ref):
    for t in range(cells_ref.shape[0]):
        rows = [
            cells_ref[t, 0:1, :].astype(F32) * SUBGRID + cells_ref[t, 1:2, :].astype(F32),
            weights_ref[t] * flags_ref[t].astype(F32),
            values_ref[t],
        ]
        out_ref[4 * t : 4 * t + 4, :] = jnp.concatenate(rows, axis=0)


def start_all(sources, targets, semaphores):
    copies = [
        pltpu.make_async_copy(source, target, semaphores.at[i])
        for i, (source, target) in enumerate(zip(sources, targets))
    ]
    for copy in copies:
        copy.start()
    return copies


def predict(spread, copies, strips_ref, plain_ref, paired_ref, held_refs, out_ref, plain, paired):
    columns, length = strips_ref.shape[1:]
    groups = length // LANES
    pairs = columns // 2
    blocks = length // CONTRIB
    width = spread.shape[1]
    first_block, residue = over(spread, CONTRIB), within(spread, CONTRIB)
    base = within(iota(spread.shape, 1), columns) * blocks
    shape = (columns * blocks, width)
    pick_inside = one_hot(shape, base + first_block)
    pick_beyond = one_hot(shape, base + within(first_block + 1, blocks))
    for copy in copies[:2]:
        copy.wait()

    def pair_at(name):
        return [table_at(paired_ref, paired[name, i]) for i in range(2)]

    window = table_at(plain_ref, plain["window"])
    turn_real, turn_imag = table_at(plain_ref, plain["real"]), table_at(plain_ref, plain["imag"])
    low_half = iota((groups, LANES), 1) < HALF
    sections = []
    for part, held in enumerate(held_refs):
        for group in range(groups):
            held[group * columns : (group + 1) * columns, :] = strips_ref[
                part, :, group * LANES : (group + 1) * LANES
            ]
        even, odd = [], []
        for pair in range(pairs):
            first = held[pl.ds(2 * pair, groups, stride=columns), :] * window
            second = held[pl.ds(2 * pair + 1, groups, stride=columns), :] * window
            even.append(jnp.where(low_half, first, swap_halves(second)))
            odd.append(jnp.where(low_half, swap_halves(first), second))
        sections += [jnp.concatenate(even, axis=1), jnp.concatenate(odd, axis=1)]
    for copy in copies[2:]:
        copy.wait()
    section = table_times(pair_at("outer"), jnp.concatenate(sections, axis=0))
    turned = []
    for pair in range(pairs):
        lanes = slice(pair * LANES, (pair + 1) * LANES)
        real, imag = section[:CONTRIB, lanes], section[CONTRIB:, lanes]
        turned.append(
            jnp.concatenate(
                [real * turn_real - imag * turn_imag, real * turn_imag + imag * turn_real],
                axis=1,
            )
        )
    inner = times_table(jnp.concatenate(turned, axis=0), pair_at("inner"))
    spectrum = jnp.concatenate(
        [
            jnp.concatenate(
                [
                    inner[pair * CONTRIB : (pair + 1) * CONTRIB, part * LANES : (part + 1) * LANES]
                    for pair in range(pairs)
                ],
                axis=1,
            )
            for part in range(2)
        ],
        axis=0,
    )
    inside = dot_split(spectrum, pick_inside)
    beyond = dot_split(spectrum, pick_beyond)
    kappa = within(iota((2 * CONTRIB, width), 0), CONTRIB)
    cutout = jnp.where(kappa >= residue, inside, beyond)
    piece = times_table(cutout.T, pair_at("piece"))
    straight, crossed = shift_rows(residue, pair_at("shift"))
    out_ref[...] = (piece * straight + swap_halves(piece) * crossed).astype(BF16)


def in_first_half():
    return 2 * lax.axis_index("group") < lax.axis_size("group")


def early_kernel(
    offsets, cells, values, weights, flags, strips, plain_table, paired_table,
    out_ref, packed_ref, places_ref, spread_ref,
    offsets_ref, cells_ref, values_ref, weights_ref, flags_ref, strips_ref, plain_ref, paired_ref,
    real_ref, imag_ref, small_semaphores, semaphores, *, plain, paired, share,
):
    small = start_all(
        (offsets, cells, values, weights, flags),
        (offsets_ref, cells_ref, values_ref, weights_ref, flags_ref),
        small_semaphores,
    )

    def large():
        sources, targets = (strips, plain_table, paired_table), (strips_ref, plain_ref, paired_ref)
        return [
            pltpu.make_async_copy(source, target, semaphores.at[i])
            for i, (source, target) in enumerate(zip(sources, targets))
        ]

    @pl.when(in_first_half())
    def _():
        for copy in large():
            copy.start()

    for copy in small:
        copy.wait()
    for t in range(cells_ref.shape[0]):
        rows = [
            cells_ref[t, 0:1, :].astype(F32) * SUBGRID + cells_ref[t, 1:2, :].astype(F32),
            weights_ref[t] * flags_ref[t].astype(F32),
            values_ref[t],
        ]
        packed_ref[4 * t : 4 * t + 4, :] = jnp.concatenate(rows, axis=0)
    places_ref[...] = offsets_on_lanes(offsets_ref, share, PLACE_ORDER)
    spread_ref[...] = offsets_on_lanes(offsets_ref, strips_ref.shape[1], SEND_ORDER)

    @pl.when(in_first_half())
    def _():
        predict(
            spread_ref[...], large(), strips_ref, plain_ref, paired_ref, (real_ref, imag_ref),
            out_ref, plain, paired,
        )


def late_kernel(
    early_ref, spread_ref, strips_ref, plain_ref, paired_ref, out_ref, real_ref, imag_ref,
    *, plain, paired,
):
    @pl.when(in_first_half())
    def _():
        out_ref[...] = early_ref[...]

    @pl.when(jnp.logical_not(in_first_half()))
    def _():
        predict(
            spread_ref[...], (), strips_ref, plain_ref, paired_ref, (real_ref, imag_ref), out_ref,
            plain, paired,
        )


def prepare_kernel(places_ref, shift_ref, *refs, columns, share, blocks):
    samples_refs, outs = refs[:-5], refs[-5:]
    value_ref, weight_ref, put_ref, straight_ref, crossed_ref = outs
    fronts, samples = samples_refs[0].shape[0] // 4, samples_refs[0].shape[1]
    own = lax.axis_index("group")
    depth = FACET_ROWS * columns
    for spot in range(len(samples_refs) * fronts):
        step, t = spot // fronts, spot % fronts
        sample = samples_refs[step][4 * t : 4 * t + 4, :]
        cell = sample[0:1, :].astype(jnp.int32)
        row, col = over(cell, SUBGRID) - own * columns, within(cell, SUBGRID)
        inside = (row >= 0) & (row < columns)
        target = jnp.where(inside, within(col, FACET_ROWS) * columns + row, -1)
        pick = one_hot((depth, samples), target)
        mask = iota((HALF, samples), 0) == over(col, FACET_ROWS)
        factor = sample[1:2, :]
        highs, lows = [], []
        for term in (factor * sample[2:3, :], factor * sample[3:4, :], factor):
            high = term.astype(BF16).astype(F32)
            highs.append(jnp.where(mask, high, 0.0).astype(BF16))
            lows.append(jnp.where(mask, term - high, 0.0).astype(BF16))
        highs, lows = highs + highs[2:], lows + lows[2:]
        grid = dot(pick, jnp.concatenate(highs, axis=0), ((1,), (1,))) + dot(
            pick, jnp.concatenate(lows, axis=0), ((1,), (1,))
        )
        rows = slice(spot * depth, (spot + 1) * depth)
        value_ref[rows, :] = grid[:, :LANES]
        weight_ref[rows, :] = grid[:, LANES:]
    spread = places_ref[...]
    first_block, residue = over(spread, CONTRIB), within(spread, CONTRIB)
    straight_ref[...], crossed_ref[...] = shift_rows(residue, shift_ref)
    base = within(iota(spread.shape, 1), share) * blocks
    targets = jnp.concatenate([base + first_block, base + within(first_block + 1, blocks)], axis=1)
    put_ref[...] = one_hot(put_ref.shape, targets)


def subgrid_kernel(
    pieces_ref, value_ref, weight_ref, turn_ref, model_ref, back_ref, out_ref, held_ref,
    *, columns, bands,
):
    rows = pieces_ref.shape[0] // FACET_ROWS
    spots = range(rows // columns)
    depth = FACET_ROWS * columns
    share = columns // bands
    pieces = pieces_ref[...].astype(F32)
    sky = turned_eighths(
        [
            pieces[spot * rows : (spot + 1) * rows, :]
            for spot in (SEND_ORDER.index(i) for i in range(FACET_ROWS))
        ],
        -1.0,
    )
    sky = [
        value * turn_ref[0, i : i + 1, :] + swap_halves(value) * turn_ref[1, i : i + 1, :]
        for i, value in enumerate(sky)
    ]
    stacked = jnp.concatenate(
        [value[spot * columns : (spot + 1) * columns, :] for spot in spots for value in sky],
        axis=0,
    )
    grid = value_ref[...] - weight_ref[...] * times_table(stacked, model_ref)
    back = times_table(grid, back_ref)
    lines = []
    for i in range(FACET_ROWS):
        value = jnp.concatenate(
            [
                back[spot * depth + i * columns : spot * depth + (i + 1) * columns, :]
                for spot in spots
            ],
            axis=0,
        )
        lines.append(
            value * turn_ref[0, i : i + 1, :] - swap_halves(value) * turn_ref[1, i : i + 1, :]
        )
    lines = turned_eighths(lines, 1.0)
    for i in range(FACET_ROWS):
        for spot in spots:
            for b in range(bands):
                source = spot * columns + b * share
                place = return_order(bands).index((b, i))
                target = (place * len(spots) + spot) * share
                held_ref[target : target + share, :] = lines[i][source : source + share, :]
    out_ref[...] = held_ref[...].astype(BF16)


def return_kernel(
    places_ref, pieces_ref, straight_ref, crossed_ref, put_ref, window_ref, turn_ref, partial_ref,
    inner_ref, outer_ref, out_ref, *line_refs, bands,
):
    columns, _, length = out_ref.shape
    blocks = length // CONTRIB
    groups = length // LANES
    pairs = (columns + 1) // 2
    width = pieces_ref.shape[0] // bands
    pieces = pieces_ref[...].astype(F32)
    order, rows = return_order(bands), width // FACET_ROWS

    def of_band(b):
        begins = [order.index((b, member)) * rows for member in PLACE_ORDER]
        return jnp.concatenate([pieces[begin : begin + rows, :] for begin in begins], axis=0)

    summed = of_band(0)
    for b in range(1, bands):
        summed += of_band(b)
    summed = summed * straight_ref[...] - swap_halves(summed) * crossed_ref[...]
    residues = table_times(partial_ref, summed, ((1,), (1,)))
    kappa = within(iota((2 * CONTRIB, width), 0), CONTRIB)
    inside = kappa >= within(places_ref[...], CONTRIB)
    both = jnp.concatenate(
        [jnp.where(inside, residues, 0.0), jnp.where(inside, 0.0, residues)], axis=1
    )
    spectrum = dot_split(both, put_ref[...], ((1,), (1,)))
    inner = times_table(
        jnp.concatenate(
            [
                jnp.concatenate(
                    [
                        spectrum[:CONTRIB, pair * LANES : (pair + 1) * LANES],
                        spectrum[CONTRIB:, pair * LANES : (pair + 1) * LANES],
                    ],
                    axis=1,
                )
                for pair in range(pairs)
            ],
            axis=0,
        ),
        inner_ref,
    )
    reals, imags = [], []
    for pair in range(pairs):
        rows = slice(pair * CONTRIB, (pair + 1) * CONTRIB)
        real, imag = inner[rows, :LANES], inner[rows, LANES:]
        reals.append(real * turn_ref[0] + imag * turn_ref[1])
        imags.append(imag * turn_ref[0] - real * turn_ref[1])
    lines = table_times(
        outer_ref,
        jnp.concatenate(
            [jnp.concatenate(reals, axis=1), jnp.concatenate(imags, axis=1)], axis=0
        ),
    )
    window = window_ref[...]
    low_half = iota((blocks, LANES), 1) < HALF
    for pair in range(pairs):
        lanes = slice(pair * LANES, (pair + 1) * LANES)
        even, odd = lines[:blocks, lanes], lines[blocks:, lanes]
        line_refs[2 * pair][...] = jnp.where(low_half, even, swap_halves(odd)) * window
        if 2 * pair + 1 < columns:
            line_refs[2 * pair + 1][...] = jnp.where(low_half, swap_halves(even), odd) * window
    for column in range(columns):
        for group in range(groups):
            out_ref[column, :, group * LANES : (group + 1) * LANES] = line_refs[column][
                2 * group : 2 * group + 2, :
            ]


def kernel_call(kernel, name, out_shape, spaces, scratch, *operands, flops=0):
    return pl.pallas_call(
        kernel,
        out_shape=out_shape,
        in_specs=[pl.BlockSpec(memory_space=space) for space in spaces],
        out_specs=jax.tree.map(lambda _: pl.BlockSpec(memory_space=pltpu.VMEM), out_shape),
        scratch_shapes=scratch,
        compiler_params=pltpu.CompilerParams(vmem_limit_bytes=VMEM_LIMIT),
        cost_estimate=pl.CostEstimate(flops=flops, bytes_accessed=0, transcendentals=0)
        if flops
        else None,
        name=name,
    )(*operands)


def wide(rows):
    return pltpu.VMEM((rows, LANES), F32)


def local(groups, bands, strips, offsets, cells, values, weights, flags):
    columns, length = strips.shape[-2:]
    fronts = offsets.shape[0]
    share = columns // bands
    facets = groups * FACET_ROWS
    rows = facets * fronts * columns
    width = facets * fronts * share
    made = tables(length)
    plain, plain_places = made.pop("plain")
    paired, paired_places = made.pop("paired")
    made = {key: jnp.asarray(value) for key, value in made.items()}
    held = length // LANES * columns
    small = [offsets, cells[0, :, 0], values[0, :, 0], weights[0], flags[0]]
    large = [strips[0, 0], jnp.asarray(plain), jnp.asarray(paired)]

    def landing(arrays):
        return [
            (pltpu.SMEM if array is offsets else pltpu.VMEM)(array.shape, array.dtype)
            for array in arrays
        ]

    def in_hbm(arrays):
        return [pltpu.with_memory_space_constraint(array, pltpu.HBM) for array in arrays]

    def semaphores(count):
        return pltpu.SemaphoreType.DMA((count,))

    early, packed, places, spread = kernel_call(
        functools.partial(early_kernel, plain=plain_places, paired=paired_places, share=share),
        "early",
        [
            jax.ShapeDtypeStruct((rows, LANES), BF16),
            jax.ShapeDtypeStruct((4 * fronts, cells.shape[-1]), F32),
            jax.ShapeDtypeStruct((1, width), jnp.int32),
            jax.ShapeDtypeStruct((1, rows), jnp.int32),
        ],
        [pltpu.HBM] * 8,
        landing(small + large) + [wide(held)] * 2 + [semaphores(5), semaphores(3)],
        *in_hbm(small + large), flops=EARLY_FLOPS,
    )
    pieces = kernel_call(
        functools.partial(late_kernel, plain=plain_places, paired=paired_places), "late",
        jax.ShapeDtypeStruct((rows, LANES), BF16), [pltpu.VMEM] * 5, [wide(held)] * 2,
        early, spread, *large, flops=LATE_FLOPS,
    )
    gathered = [packed]
    for step in range(1, groups):
        moves = [((group + step) % groups, group) for group in range(groups)]
        gathered.append(lax.ppermute(packed, "group", moves))
    arrived = lax.all_to_all(
        pieces, "member", split_axis=0, concat_axis=0, tiled=True,
        axis_index_groups=[list(SEND_ORDER)],
    )
    blocks = length // CONTRIB
    value, weight, put, straight, crossed = kernel_call(
        functools.partial(prepare_kernel, columns=columns, share=share, blocks=blocks), "prepare",
        [jax.ShapeDtypeStruct((rows, LANES), F32)] * 2
        + [jax.ShapeDtypeStruct(((share + share % 2) * blocks, 2 * width), BF16)]
        + [jax.ShapeDtypeStruct((width, LANES), F32)] * 2,
        [pltpu.VMEM] * (2 + len(gathered)), [],
        places, made["shift"], *gathered, flops=PREPARE_FLOPS,
    )
    returned = kernel_call(
        functools.partial(subgrid_kernel, columns=columns, bands=bands), "subgrid",
        jax.ShapeDtypeStruct((rows, LANES), BF16), [pltpu.VMEM] * 6, [wide(rows)],
        arrived, value, weight, made["grid_turn"], made["model"], made["back"],
    )
    delivered = lax.all_to_all(
        returned, ("band", "member"), split_axis=0, concat_axis=0, tiled=True,
        axis_index_groups=[
            [b * FACET_ROWS + member for b, member in return_order(bands)]
        ],
    )
    lines = kernel_call(
        functools.partial(return_kernel, bands=bands), "lines",
        jax.ShapeDtypeStruct((share, 2, length), F32), [pltpu.VMEM] * 10,
        [wide(2 * length // LANES)] * share,
        places, delivered, straight, crossed, put, made["window"], made["turn"],
        made["partial"], made["inner_plus"], made["outer_plus"],
    )
    return lines[None]


def solution(mesh):
    bands = mesh.shape["band"]
    groups = mesh.shape["facet"] // FACET_ROWS
    split_mesh = Mesh(
        mesh.devices.reshape(groups, FACET_ROWS, bands), ("group", "member", "band")
    )
    facet = ("group", "member")
    placed = (
        P("band", facet, None, None, None),
        P(),
        P("band", None, facet, None, None),
        P("band", None, facet, None, None),
        P("band", None, facet, None),
        P("band", None, facet, None),
    )
    return jax.shard_map(
        functools.partial(local, groups, bands),
        mesh=split_mesh,
        in_specs=placed,
        out_specs=P(facet, "band", None, None),
        check_vma=False,
    )
```

```python
import functools
import math

import jax
import jax.numpy as jnp
import ml_dtypes
import numpy as np
from jax import lax
from jax.experimental import pallas as pl
from jax.experimental.pallas import tpu as pltpu
from jax.sharding import Mesh
from jax.sharding import PartitionSpec as P

CONTRIB = 64
FACET_ROWS = 8
SUBGRID = FACET_ROWS * CONTRIB
SEND_ORDER = (FACET_ROWS - 1, *range(FACET_ROWS - 1))
PLACE_ORDER = tuple(range(FACET_ROWS))
LANES = 128
HALF = LANES // 2
EARLY_FLOPS = 10**10
LATE_FLOPS = 10**10
PREPARE_FLOPS = 2 * 10**10
VMEM_LIMIT = 48 * 1024 * 1024
F32 = jnp.float32
BF16 = jnp.bfloat16


def phases(rows, cols, length, rotation):
    product = np.outer(rows, cols) % length
    return np.exp(rotation * 2j * np.pi * product / length)


def from_left(matrix):
    return np.block([[matrix.real, -matrix.imag], [matrix.imag, matrix.real]])


def from_right(matrix):
    return np.block([[matrix.real, matrix.imag], [-matrix.imag, matrix.real]])


def high_low(table):
    high = table.astype(ml_dtypes.bfloat16)
    low = (table - high.astype(np.float64)).astype(ml_dtypes.bfloat16)
    return np.stack([high, low])


def side_by_side(values):
    straight = np.concatenate([values.real, values.real], axis=-1)
    crossed = np.concatenate([-values.imag, values.imag], axis=-1)
    return np.stack([straight, crossed])


def stack_tables(named):
    places, blocks, begin = {}, [], 0
    for name, table in named.items():
        count = table.shape[1] // LANES
        places[name] = (begin, table.shape[0], count)
        blocks += [table[:, i * LANES : (i + 1) * LANES] for i in range(count)]
        begin += table.shape[0] * count
    return np.concatenate(blocks, axis=0), places


def stack_pairs(named):
    return stack_tables(
        {(name, i): table for name, pair in named.items() for i, table in enumerate(pair)}
    )


def tables(length):
    blocks = length // CONTRIB
    short = np.arange(CONTRIB)
    outer = np.concatenate([np.arange(0, blocks, 2), np.arange(1, blocks, 2)])
    window = 1.0 + 0.5 * np.cos(np.arange(length) * (2.0 * math.pi / length))
    window = (window * length**-0.5).reshape(length // LANES, LANES).astype(np.float32)
    turn = np.tile(phases(short, short, length, -1), (1, 2))
    turn = np.stack([turn.real, turn.imag]).astype(np.float32)
    pair = np.eye(2)
    shift = high_low(np.concatenate(side_by_side(phases(short, short, CONTRIB, -1)), axis=1))
    outer_minus = from_left(phases(short, outer, blocks, -1))
    inner_minus = from_right(np.kron(pair, phases(short, short, CONTRIB, -1)))
    piece = from_right(phases(short, short, CONTRIB, 1)) * CONTRIB**-0.5
    return dict(
        plain=stack_tables(dict(window=window, real=turn[0], imag=turn[1])),
        paired=stack_pairs(
            dict(
                shift=shift,
                outer=high_low(outer_minus),
                inner=high_low(inner_minus),
                piece=high_low(piece),
            )
        ),
        window=np.repeat(window, 2, axis=0),
        turn=turn,
        shift=shift,
        inner_plus=high_low(from_right(np.kron(pair, phases(short, short, CONTRIB, 1)))),
        outer_plus=high_low(
            from_left(phases(outer, short, blocks, 1))
            .reshape(2, blocks, 2 * CONTRIB)
            .transpose(1, 0, 2)
            .reshape(2 * blocks, 2 * CONTRIB)
        ),
        partial=high_low(from_right(phases(short, short, CONTRIB, -1)).T * CONTRIB**-0.5),
        grid_turn=side_by_side(phases(np.arange(FACET_ROWS), short, SUBGRID, -1)).astype(
            np.float32
        ),
        model=high_low(from_right(phases(short, short, CONTRIB, -1)) * SUBGRID**-0.5),
        back=high_low(from_right(phases(short, short, CONTRIB, 1)) * SUBGRID**-0.5),
    )


def return_order(bands):
    order = [(b, member) for b in range(bands) for member in PLACE_ORDER]
    return order[-1:] + order[:-1]


def split(values):
    high = values.astype(BF16)
    return high, (values - high.astype(F32)).astype(BF16)


def dot(left, right, dims=((1,), (0,))):
    return lax.dot_general(left, right, (dims, ((), ())), preferred_element_type=F32)


def dot_split(values, right, dims=((1,), (0,))):
    rows = values.shape[0]
    both = dot(jnp.concatenate(split(values), axis=0), right, dims)
    return both[:rows] + both[rows:]


def times_table(values, table):
    return dot_split(values, table[0]) + dot(values.astype(BF16), table[1])


def table_times(table, values, dims=((1,), (0,))):
    high, low = split(values)
    rows = table[0].shape[0]
    both = dot(jnp.concatenate([table[0], table[1]], axis=0), high, dims)
    return both[:rows] + both[rows:] + dot(table[0], low, dims)


def iota(shape, dimension):
    return lax.broadcasted_iota(jnp.int32, shape, dimension)


def over(values, size):
    return lax.shift_right_logical(values, jnp.full_like(values, size.bit_length() - 1))


def within(values, size):
    return values & (size - 1)


def swap_halves(values):
    return pltpu.roll(values, HALF, 1)


def table_at(ref, place):
    begin, rows, blocks = place
    parts = [ref[begin + i * rows : begin + (i + 1) * rows, :] for i in range(blocks)]
    return parts[0] if blocks == 1 else jnp.concatenate(parts, axis=1)


def offsets_on_lanes(offsets_ref, columns, order):
    fronts, owners = offsets_ref.shape
    groups = owners // FACET_ROWS
    own = lax.axis_index("group")
    begins = []
    for step in range(groups):
        group = own + step
        begins.append(jnp.where(group >= groups, group - groups, group) * FACET_ROWS)
    spread = iota((1, fronts * owners * columns), 1)
    place_of = over(spread, columns)
    for place in range(fronts * owners):
        t, step, spot = place % fronts, place // fronts % groups, place // (fronts * groups)
        member = order[spot]
        spread = jnp.where(place_of == place, offsets_ref[t, begins[step] + member], spread)
    return spread


def shift_rows(residue, table):
    pick = jnp.where(iota((CONTRIB, residue.shape[1]), 0) == residue, 1.0, 0.0).T.astype(BF16)
    rows = dot(pick, table[0]) + dot(pick, table[1])
    return rows[:, :LANES], rows[:, LANES:]


def one_hot(shape, targets):
    return jnp.where(iota(shape, 0) == targets, 1.0, 0.0).astype(BF16)


def turned_eighths(values, rotation):
    sign = jnp.where(iota(values[0].shape, 1) < HALF, -rotation, rotation).astype(F32)

    def quarter_turn(value):
        return swap_halves(value) * sign

    def four(a, b, c, d):
        even_sum, even_diff = a + c, a - c
        odd_sum, odd_diff = b + d, quarter_turn(b - d)
        return even_sum + odd_sum, even_diff + odd_diff, even_sum - odd_sum, even_diff - odd_diff

    even = four(*values[0::2])
    odd = four(*values[1::2])
    root = math.sqrt(0.5)
    turned = (
        odd[0],
        (odd[1] + quarter_turn(odd[1])) * root,
        quarter_turn(odd[2]),
        (quarter_turn(odd[3]) - odd[3]) * root,
    )
    return [e + o for e, o in zip(even, turned)] + [e - o for e, o in zip(even, turned)]


def pack_samples(cells_ref, values_ref, weights_ref, flags_ref, out_ref):
    for t in range(cells_ref.shape[0]):
        rows = [
            cells_ref[t, 0:1, :].astype(F32) * SUBGRID + cells_ref[t, 1:2, :].astype(F32),
            weights_ref[t] * flags_ref[t].astype(F32),
            values_ref[t],
        ]
        out_ref[4 * t : 4 * t + 4, :] = jnp.concatenate(rows, axis=0)


def start_all(sources, targets, semaphores):
    copies = [
        pltpu.make_async_copy(source, target, semaphores.at[i])
        for i, (source, target) in enumerate(zip(sources, targets))
    ]
    for copy in copies:
        copy.start()
    return copies


def predict(spread, copies, strips_ref, plain_ref, paired_ref, held_refs, out_ref, plain, paired):
    columns, length = strips_ref.shape[1:]
    groups = length // LANES
    pairs = columns // 2
    blocks = length // CONTRIB
    width = spread.shape[1]
    first_block, residue = over(spread, CONTRIB), within(spread, CONTRIB)
    base = within(iota(spread.shape, 1), columns) * blocks
    shape = (columns * blocks, width)
    pick_inside = one_hot(shape, base + first_block)
    pick_beyond = one_hot(shape, base + within(first_block + 1, blocks))
    for copy in copies[:2]:
        copy.wait()

    def pair_at(name):
        return [table_at(paired_ref, paired[name, i]) for i in range(2)]

    window = table_at(plain_ref, plain["window"])
    turn_real, turn_imag = table_at(plain_ref, plain["real"]), table_at(plain_ref, plain["imag"])
    low_half = iota((groups, LANES), 1) < HALF
    sections = []
    for part, held in enumerate(held_refs):
        for group in range(groups):
            held[group * columns : (group + 1) * columns, :] = strips_ref[
                part, :, group * LANES : (group + 1) * LANES
            ]
        even, odd = [], []
        for pair in range(pairs):
            first = held[pl.ds(2 * pair, groups, stride=columns), :] * window
            second = held[pl.ds(2 * pair + 1, groups, stride=columns), :] * window
            even.append(jnp.where(low_half, first, swap_halves(second)))
            odd.append(jnp.where(low_half, swap_halves(first), second))
        sections += [jnp.concatenate(even, axis=1), jnp.concatenate(odd, axis=1)]
    for copy in copies[2:]:
        copy.wait()
    section = table_times(pair_at("outer"), jnp.concatenate(sections, axis=0))
    turned = []
    for pair in range(pairs):
        lanes = slice(pair * LANES, (pair + 1) * LANES)
        real, imag = section[:CONTRIB, lanes], section[CONTRIB:, lanes]
        turned.append(
            jnp.concatenate(
                [real * turn_real - imag * turn_imag, real * turn_imag + imag * turn_real],
                axis=1,
            )
        )
    inner = times_table(jnp.concatenate(turned, axis=0), pair_at("inner"))
    spectrum = jnp.concatenate(
        [
            jnp.concatenate(
                [
                    inner[pair * CONTRIB : (pair + 1) * CONTRIB, part * LANES : (part + 1) * LANES]
                    for pair in range(pairs)
                ],
                axis=1,
            )
            for part in range(2)
        ],
        axis=0,
    )
    inside = dot_split(spectrum, pick_inside)
    beyond = dot_split(spectrum, pick_beyond)
    kappa = within(iota((2 * CONTRIB, width), 0), CONTRIB)
    cutout = jnp.where(kappa >= residue, inside, beyond)
    piece = times_table(cutout.T, pair_at("piece"))
    straight, crossed = shift_rows(residue, pair_at("shift"))
    out_ref[...] = (piece * straight + swap_halves(piece) * crossed).astype(BF16)


def in_first_half():
    return 2 * lax.axis_index("group") < lax.axis_size("group")


def early_kernel(
    offsets, cells, values, weights, flags, strips, plain_table, paired_table,
    out_ref, packed_ref, places_ref, spread_ref,
    offsets_ref, cells_ref, values_ref, weights_ref, flags_ref, strips_ref, plain_ref, paired_ref,
    real_ref, imag_ref, small_semaphores, semaphores, *, plain, paired, share,
):
    small = start_all(
        (offsets, cells, values, weights, flags),
        (offsets_ref, cells_ref, values_ref, weights_ref, flags_ref),
        small_semaphores,
    )

    def large():
        sources, targets = (strips, plain_table, paired_table), (strips_ref, plain_ref, paired_ref)
        return [
            pltpu.make_async_copy(source, target, semaphores.at[i])
            for i, (source, target) in enumerate(zip(sources, targets))
        ]

    @pl.when(in_first_half())
    def _():
        for copy in large():
            copy.start()

    for copy in small:
        copy.wait()
    for t in range(cells_ref.shape[0]):
        rows = [
            cells_ref[t, 0:1, :].astype(F32) * SUBGRID + cells_ref[t, 1:2, :].astype(F32),
            weights_ref[t] * flags_ref[t].astype(F32),
            values_ref[t],
        ]
        packed_ref[4 * t : 4 * t + 4, :] = jnp.concatenate(rows, axis=0)
    places_ref[...] = offsets_on_lanes(offsets_ref, share, PLACE_ORDER)
    spread_ref[...] = offsets_on_lanes(offsets_ref, strips_ref.shape[1], SEND_ORDER)

    @pl.when(in_first_half())
    def _():
        predict(
            spread_ref[...], large(), strips_ref, plain_ref, paired_ref, (real_ref, imag_ref),
            out_ref, plain, paired,
        )


def late_kernel(
    early_ref, spread_ref, strips_ref, plain_ref, paired_ref, out_ref, real_ref, imag_ref,
    *, plain, paired,
):
    @pl.when(in_first_half())
    def _():
        out_ref[...] = early_ref[...]

    @pl.when(jnp.logical_not(in_first_half()))
    def _():
        predict(
            spread_ref[...], (), strips_ref, plain_ref, paired_ref, (real_ref, imag_ref), out_ref,
            plain, paired,
        )


def prepare_kernel(places_ref, shift_ref, *refs, columns, share, blocks):
    samples_refs, outs = refs[:-5], refs[-5:]
    value_ref, weight_ref, put_ref, straight_ref, crossed_ref = outs
    fronts, samples = samples_refs[0].shape[0] // 4, samples_refs[0].shape[1]
    own = lax.axis_index("group")
    depth = FACET_ROWS * columns
    for spot in range(len(samples_refs) * fronts):
        step, t = spot // fronts, spot % fronts
        sample = samples_refs[step][4 * t : 4 * t + 4, :]
        cell = sample[0:1, :].astype(jnp.int32)
        row, col = over(cell, SUBGRID) - own * columns, within(cell, SUBGRID)
        inside = (row >= 0) & (row < columns)
        target = jnp.where(inside, within(col, FACET_ROWS) * columns + row, -1)
        pick = one_hot((depth, samples), target)
        mask = iota((HALF, samples), 0) == over(col, FACET_ROWS)
        factor = sample[1:2, :]
        highs, lows = [], []
        for term in (factor * sample[2:3, :], factor * sample[3:4, :], factor):
            high = term.astype(BF16).astype(F32)
            highs.append(jnp.where(mask, high, 0.0).astype(BF16))
            lows.append(jnp.where(mask, term - high, 0.0).astype(BF16))
        highs, lows = highs + highs[2:], lows + lows[2:]
        grid = dot(pick, jnp.concatenate(highs, axis=0), ((1,), (1,))) + dot(
            pick, jnp.concatenate(lows, axis=0), ((1,), (1,))
        )
        rows = slice(spot * depth, (spot + 1) * depth)
        value_ref[rows, :] = grid[:, :LANES]
        weight_ref[rows, :] = grid[:, LANES:]
    spread = places_ref[...]
    first_block, residue = over(spread, CONTRIB), within(spread, CONTRIB)
    straight_ref[...], crossed_ref[...] = shift_rows(residue, shift_ref)
    base = within(iota(spread.shape, 1), share) * blocks
    targets = jnp.concatenate([base + first_block, base + within(first_block + 1, blocks)], axis=1)
    put_ref[...] = one_hot(put_ref.shape, targets)


def subgrid_kernel(
    pieces_ref, value_ref, weight_ref, turn_ref, model_ref, back_ref, out_ref, held_ref,
    *, columns, bands,
):
    rows = pieces_ref.shape[0] // FACET_ROWS
    spots = range(rows // columns)
    depth = FACET_ROWS * columns
    share = columns // bands
    pieces = pieces_ref[...].astype(F32)
    sky = turned_eighths(
        [
            pieces[spot * rows : (spot + 1) * rows, :]
            for spot in (SEND_ORDER.index(i) for i in range(FACET_ROWS))
        ],
        -1.0,
    )
    sky = [
        value * turn_ref[0, i : i + 1, :] + swap_halves(value) * turn_ref[1, i : i + 1, :]
        for i, value in enumerate(sky)
    ]
    stacked = jnp.concatenate(
        [value[spot * columns : (spot + 1) * columns, :] for spot in spots for value in sky],
        axis=0,
    )
    grid = value_ref[...] - weight_ref[...] * times_table(stacked, model_ref)
    back = times_table(grid, back_ref)
    lines = []
    for i in range(FACET_ROWS):
        value = jnp.concatenate(
            [
                back[spot * depth + i * columns : spot * depth + (i + 1) * columns, :]
                for spot in spots
            ],
            axis=0,
        )
        lines.append(
            value * turn_ref[0, i : i + 1, :] - swap_halves(value) * turn_ref[1, i : i + 1, :]
        )
    lines = turned_eighths(lines, 1.0)
    for i in range(FACET_ROWS):
        for spot in spots:
            for b in range(bands):
                source = spot * columns + b * share
                place = return_order(bands).index((b, i))
                target = (place * len(spots) + spot) * share
                held_ref[target : target + share, :] = lines[i][source : source + share, :]
    out_ref[...] = held_ref[...].astype(BF16)


def return_kernel(
    places_ref, pieces_ref, straight_ref, crossed_ref, put_ref, window_ref, turn_ref, partial_ref,
    inner_ref, outer_ref, out_ref, *, bands,
):
    columns, _, length = out_ref.shape
    blocks = length // CONTRIB
    groups = length // LANES
    pairs = (columns + 1) // 2
    width = pieces_ref.shape[0] // bands
    pieces = pieces_ref[...].astype(F32)
    order, rows = return_order(bands), width // FACET_ROWS

    def of_band(b):
        begins = [order.index((b, member)) * rows for member in PLACE_ORDER]
        return jnp.concatenate([pieces[begin : begin + rows, :] for begin in begins], axis=0)

    summed = of_band(0)
    for b in range(1, bands):
        summed += of_band(b)
    summed = summed * straight_ref[...] - swap_halves(summed) * crossed_ref[...]
    residues = table_times(partial_ref, summed, ((1,), (1,)))
    kappa = within(iota((2 * CONTRIB, width), 0), CONTRIB)
    inside = kappa >= within(places_ref[...], CONTRIB)
    both = jnp.concatenate(
        [jnp.where(inside, residues, 0.0), jnp.where(inside, 0.0, residues)], axis=1
    )
    spectrum = dot_split(both, put_ref[...], ((1,), (1,)))
    inner = times_table(
        jnp.concatenate(
            [
                jnp.concatenate(
                    [
                        spectrum[:CONTRIB, pair * LANES : (pair + 1) * LANES],
                        spectrum[CONTRIB:, pair * LANES : (pair + 1) * LANES],
                    ],
                    axis=1,
                )
                for pair in range(pairs)
            ],
            axis=0,
        ),
        inner_ref,
    )
    reals, imags = [], []
    for pair in range(pairs):
        rows = slice(pair * CONTRIB, (pair + 1) * CONTRIB)
        real, imag = inner[rows, :LANES], inner[rows, LANES:]
        reals.append(real * turn_ref[0] + imag * turn_ref[1])
        imags.append(imag * turn_ref[0] - real * turn_ref[1])
    lines = table_times(
        outer_ref,
        jnp.concatenate(
            [jnp.concatenate(reals, axis=1), jnp.concatenate(imags, axis=1)], axis=0
        ),
    )
    window = window_ref[...]
    low_half = iota((blocks, LANES), 1) < HALF
    for pair in range(pairs):
        lanes = slice(pair * LANES, (pair + 1) * LANES)
        even, odd = lines[:blocks, lanes], lines[blocks:, lanes]
        both = (
            jnp.where(low_half, even, swap_halves(odd)) * window,
            jnp.where(low_half, swap_halves(even), odd) * window,
        )
        for column in range(2 * pair, min(2 * pair + 2, columns)):
            line = both[column - 2 * pair]
            for group in range(groups):
                out_ref[column, :, group * LANES : (group + 1) * LANES] = line[
                    2 * group : 2 * group + 2, :
                ]


def kernel_call(kernel, name, out_shape, spaces, scratch, *operands, flops=0):
    return pl.pallas_call(
        kernel,
        out_shape=out_shape,
        in_specs=[pl.BlockSpec(memory_space=space) for space in spaces],
        out_specs=jax.tree.map(lambda _: pl.BlockSpec(memory_space=pltpu.VMEM), out_shape),
        scratch_shapes=scratch,
        compiler_params=pltpu.CompilerParams(vmem_limit_bytes=VMEM_LIMIT),
        cost_estimate=pl.CostEstimate(flops=flops, bytes_accessed=0, transcendentals=0)
        if flops
        else None,
        name=name,
    )(*operands)


def wide(rows):
    return pltpu.VMEM((rows, LANES), F32)


def local(groups, bands, strips, offsets, cells, values, weights, flags):
    columns, length = strips.shape[-2:]
    fronts = offsets.shape[0]
    share = columns // bands
    facets = groups * FACET_ROWS
    rows = facets * fronts * columns
    width = facets * fronts * share
    made = tables(length)
    plain, plain_places = made.pop("plain")
    paired, paired_places = made.pop("paired")
    made = {key: jnp.asarray(value) for key, value in made.items()}
    held = length // LANES * columns
    small = [offsets, cells[0, :, 0], values[0, :, 0], weights[0], flags[0]]
    large = [strips[0, 0], jnp.asarray(plain), jnp.asarray(paired)]

    def landing(arrays):
        return [
            (pltpu.SMEM if array is offsets else pltpu.VMEM)(array.shape, array.dtype)
            for array in arrays
        ]

    def in_hbm(arrays):
        return [pltpu.with_memory_space_constraint(array, pltpu.HBM) for array in arrays]

    def semaphores(count):
        return pltpu.SemaphoreType.DMA((count,))

    early, packed, places, spread = kernel_call(
        functools.partial(early_kernel, plain=plain_places, paired=paired_places, share=share),
        "early",
        [
            jax.ShapeDtypeStruct((rows, LANES), BF16),
            jax.ShapeDtypeStruct((4 * fronts, cells.shape[-1]), F32),
            jax.ShapeDtypeStruct((1, width), jnp.int32),
            jax.ShapeDtypeStruct((1, rows), jnp.int32),
        ],
        [pltpu.HBM] * 8,
        landing(small + large) + [wide(held)] * 2 + [semaphores(5), semaphores(3)],
        *in_hbm(small + large), flops=EARLY_FLOPS,
    )
    pieces = kernel_call(
        functools.partial(late_kernel, plain=plain_places, paired=paired_places), "late",
        jax.ShapeDtypeStruct((rows, LANES), BF16), [pltpu.VMEM] * 5, [wide(held)] * 2,
        early, spread, *large, flops=LATE_FLOPS,
    )
    gathered = [packed]
    for step in range(1, groups):
        moves = [((group + step) % groups, group) for group in range(groups)]
        gathered.append(lax.ppermute(packed, "group", moves))
    arrived = lax.all_to_all(
        pieces, "member", split_axis=0, concat_axis=0, tiled=True,
        axis_index_groups=[list(SEND_ORDER)],
    )
    blocks = length // CONTRIB
    value, weight, put, straight, crossed = kernel_call(
        functools.partial(prepare_kernel, columns=columns, share=share, blocks=blocks), "prepare",
        [jax.ShapeDtypeStruct((rows, LANES), F32)] * 2
        + [jax.ShapeDtypeStruct(((share + share % 2) * blocks, 2 * width), BF16)]
        + [jax.ShapeDtypeStruct((width, LANES), F32)] * 2,
        [pltpu.VMEM] * (2 + len(gathered)), [],
        places, made["shift"], *gathered, flops=PREPARE_FLOPS,
    )
    returned = kernel_call(
        functools.partial(subgrid_kernel, columns=columns, bands=bands), "subgrid",
        jax.ShapeDtypeStruct((rows, LANES), BF16), [pltpu.VMEM] * 6, [wide(rows)],
        arrived, value, weight, made["grid_turn"], made["model"], made["back"],
    )
    delivered = lax.all_to_all(
        returned, ("band", "member"), split_axis=0, concat_axis=0, tiled=True,
        axis_index_groups=[
            [b * FACET_ROWS + member for b, member in return_order(bands)]
        ],
    )
    lines = kernel_call(
        functools.partial(return_kernel, bands=bands), "lines",
        jax.ShapeDtypeStruct((share, 2, length), F32), [pltpu.VMEM] * 10,
        [],
        places, delivered, straight, crossed, put, made["window"], made["turn"],
        made["partial"], made["inner_plus"], made["outer_plus"],
    )
    return lines[None]


def solution(mesh):
    bands = mesh.shape["band"]
    groups = mesh.shape["facet"] // FACET_ROWS
    split_mesh = Mesh(
        mesh.devices.reshape(groups, FACET_ROWS, bands), ("group", "member", "band")
    )
    facet = ("group", "member")
    placed = (
        P("band", facet, None, None, None),
        P(),
        P("band", None, facet, None, None),
        P("band", None, facet, None, None),
        P("band", None, facet, None),
        P("band", None, facet, None),
    )
    return jax.shard_map(
        functools.partial(local, groups, bands),
        mesh=split_mesh,
        in_specs=placed,
        out_specs=P(facet, "band", None, None),
        check_vma=False,
    )
```
